32 devices in a mesh: gz: 8 (over z, x), gx: 4 (over y, core).
Axes of the slice: x: 2, y: 2, z: 4, core: 2. Of those that a mesh axis runs over, the one named last changes fastest.
Arguments:
- strength: float32 [3, 16384], P(None, ('gz', 'gx')), may hold values from -6 to 6
- offsets: float32 [3, 16384], P(None, ('gz', 'gx')), may hold values from -0.5 to 0.5
- cell_index: int32 [16384], P(('gz', 'gx')), may hold values from 0 to 131071
- migrate_count: int32 [8, 4, 2], P('gz', 'gx'), may hold values from 32 to 64, as said below
- ambient: float32 [3, 64, 256, 256], P(None, 'gz', 'gx'), may hold values from -2.5 to 2.5
Outputs:
- velocity: float32 [3, 64, 256, 256], P(None, 'gz', 'gx')
- vorticity: float32 [3, 64, 256, 256], P(None, 'gz', 'gx')
The draws below stay inside these ranges and needn't reach their ends.
Inputs may be any that keep to these rules, and one draw needn't show every extreme that they name: `migrate_count`: some device has 64 in the first entry and some device has 64 in the second.
All inputs are finite; a program needn't handle non-finite values.
Results may differ from the reference program's by a relative error of at most 0.0003.
Values sent between devices are 32-bit elements; how exact they have to be, the bound alone decides.
No kernel may reach another device: no remote copies, remote signals or barrier semaphores. Data moves between devices by JAX's collectives and lax.ppermute only.
A program may use at most 128 MiB of HBM per device.

```python
import jax
import jax.numpy as jnp

NX = 256
NY = 256
CZ = 8
NZ = 64
CX = 64
PART = 512
MIG = 64
PTOTAL = 16384
N_GZ = 8
N_GX = 4


def draw_migrate_count(key, part):
    first, second = jax.random.split(key)
    owners = N_GZ * N_GX
    counts = jax.random.randint(first, (owners, 2), MIG // 2, MIG + 1)
    chosen = jax.random.randint(second, (2,), 0, owners)
    rows_at = jnp.arange(owners)[:, None]
    counts = jnp.where(rows_at == chosen[None, :], MIG, counts)
    return counts.reshape(N_GZ, N_GX, 2).astype(jnp.int32)


def draw_ambient(key, part):
    extent = (3, NZ, NX, NY)
    return jnp.clip(0.5 * jax.random.normal(key, extent, jnp.float32), -2.5, 2.5)


def touch_ends(array, own_key, least, high):
    longest = array.shape.index(max(array.shape))
    spots = []
    for shift in (0, 1):
        where = [jax.random.randint(jax.random.fold_in(own_key, axis), (), 0, length) for axis, length in enumerate(array.shape)]
        where[longest] = (where[longest] + shift) % array.shape[longest]
        spots.append(tuple(where))
    return array.at[spots[0]].set(least).at[spots[1]].set(high)


def levels(rng, dims, cuts, low, high):
    loudness, own = 1.0, jax.random.fold_in(rng, 6)
    for axis_at, blocks in cuts:
        heights = jnp.exp(jax.random.uniform(jax.random.fold_in(own, axis_at), (blocks,), jnp.float32, low / len(cuts), high / len(cuts)))
        loudness = loudness * jnp.repeat(heights, dims[axis_at] // blocks).reshape([-1 if axis == axis_at else 1 for axis in range(len(dims))])
    return loudness


def gaussian(key, shape, width, limit, cuts=(), kind=jnp.bfloat16):
    level = levels(key, shape, cuts, -0.22, 0.18) if cuts else 1.0
    entries = jax.random.normal(key, shape, jnp.float32) * width * level
    return jnp.minimum(jnp.maximum(entries, -limit), limit).astype(kind)


def setup_inputs(seed: int = 0) -> dict:
    streams_of = jax.random.split(jax.random.key(seed), 6)
    strength = gaussian(streams_of[0], (3, PTOTAL), 1.0, 6.0, ((1, 32),), jnp.float32)
    offsets = jnp.clip(jax.random.uniform(streams_of[1], (3, PTOTAL), jnp.float32, -0.5, 0.5) * levels(streams_of[1], (3, PTOTAL), ((1, 32),), -0.4, 0.0), -0.5, 0.5)
    cell_index = touch_ends(jax.random.randint(streams_of[2], (PTOTAL,), 0, CZ * CX * NY), jax.random.fold_in(streams_of[2], 1), 0, (CZ * CX * NY) - 1).astype(jnp.int32)
    migrate_count = draw_migrate_count(jax.random.fold_in(streams_of[5], 71), 0)
    ambient = draw_ambient(jax.random.fold_in(streams_of[5], 71), 0)
    return dict(strength=strength, offsets=offsets, cell_index=cell_index, migrate_count=migrate_count, ambient=ambient)


def kernel_weight(distance):
    radius = jnp.abs(distance)
    near_part = 1.0 - 2.5 * radius * radius + 1.5 * radius * radius * radius
    far_part = 0.5 * (2.0 - radius) * (2.0 - radius) * (1.0 - radius)
    return jnp.where(radius < 1.0, near_part, jnp.where(radius < 2.0, far_part, 0.0))


def wave_of(position, extent):
    signed = jnp.where(position < extent // 2, position, position - extent)
    return 2.0 * jnp.pi * signed.astype(jnp.float32) / extent


def central(values, axis_number):
    return (jnp.roll(values, -1, axis=axis_number) - jnp.roll(values, 1, axis=axis_number)) * 0.5


def reference(strength, offsets, cell_index, migrate_count, ambient):
    owners = N_GZ * N_GX
    slot_index = jnp.arange(PART, dtype=jnp.int32)[None, :]
    counts = migrate_count.reshape(owners, 2)
    up_count = counts[:, 0:1]
    down_count = counts[:, 1:2]
    moves = jnp.where(slot_index < up_count, 1, jnp.where(slot_index < up_count + down_count, -1, 0)).astype(jnp.int32)
    owner = jnp.arange(owners, dtype=jnp.int32)[:, None]
    slab = (owner // N_GX + moves) % N_GZ
    cell_ids = cell_index.reshape(owners, PART)
    z_cell = (slab * CZ + cell_ids // (CX * NY)).reshape(-1)
    x_cell = ((owner % N_GX) * CX + (cell_ids // NY) % CX).reshape(-1)
    y_cell = (cell_ids % NY).reshape(-1)
    taps = jnp.arange(5, dtype=jnp.int32) - 2
    tap_float = taps.astype(jnp.float32)
    weight_z = kernel_weight(tap_float[None, :] - offsets[0][:, None])
    weight_x = kernel_weight(tap_float[None, :] - offsets[1][:, None])
    weight_y = kernel_weight(tap_float[None, :] - offsets[2][:, None])
    values = (strength[:, :, None] * weight_z[None])[:, :, :, None] * weight_x[None, :, None, :]
    values = values[:, :, :, :, None] * weight_y[None, :, None, None, :]
    index_z = (z_cell[:, None] + taps[None, :]) % NZ
    index_x = (x_cell[:, None] + taps[None, :]) % NX
    index_y = (y_cell[:, None] + taps[None, :]) % NY
    flat = (index_z[:, :, None, None] * NX + index_x[:, None, :, None]) * NY + index_y[:, None, None, :]
    deposited = jnp.zeros((3, NZ * NX * NY), jnp.float32).at[:, flat.reshape(-1)].add(values.reshape(3, -1))
    vorticity_mesh = ambient + deposited.reshape(3, NZ, NX, NY)
    spectrum = jnp.fft.fftn(vorticity_mesh, axes=(1, 2, 3))
    z_index = jnp.arange(NZ, dtype=jnp.int32)[:, None, None]
    x_index = jnp.arange(NX, dtype=jnp.int32)[None, :, None]
    y_index = jnp.arange(NY, dtype=jnp.int32)[None, None, :]
    wave_z = wave_of(z_index, NZ)
    wave_x = wave_of(x_index, NX)
    wave_y = wave_of(y_index, NY)
    anchor = (z_index == 0) & (x_index == 0) & (y_index == 0)
    wave_sq = wave_z * wave_z + wave_x * wave_x + wave_y * wave_y
    inverse_sq = jnp.where(anchor, 0.0, 1.0 / jnp.where(anchor, 1.0, wave_sq))
    stream = spectrum * inverse_sq
    crossed = jnp.stack([wave_x * stream[2] - wave_y * stream[1],
                         wave_y * stream[0] - wave_z * stream[2],
                         wave_z * stream[1] - wave_x * stream[0]])
    velocity = jnp.real(jnp.fft.ifftn(1j * crossed, axes=(1, 2, 3))).astype(jnp.float32)
    stretch = vorticity_mesh[0] * central(velocity, 1) + vorticity_mesh[1] * central(velocity, 2) + vorticity_mesh[2] * central(velocity, 3)
    return velocity, vorticity_mesh + 0.25 * stretch
```

```python
import functools
import math

import jax
import jax.numpy as jnp
import ml_dtypes
import numpy as np
from jax import lax
from jax.experimental import pallas as pl
from jax.experimental.pallas import tpu as pltpu
from jax.sharding import PartitionSpec as P

MIG = 64
LANES = 128
RIM = 8
TIME_STEP = 0.25
VMEM = 48 * 1024 * 1024
F32 = jnp.float32
BF16 = jnp.bfloat16


def split_table(table):
    high = table.astype(np.float32).astype(ml_dtypes.bfloat16)
    low = (table - high.astype(np.float64)).astype(np.float32).astype(ml_dtypes.bfloat16)
    return high, low


def angles(rows, columns, extent):
    return 2.0 * np.pi * (np.multiply.outer(rows, columns) % extent) / extent


def y_tables(ny, pencils, scale):
    modes = ny // (2 * pencils)
    position = np.arange(ny)
    angle = angles(position, np.arange(ny // 2), ny)
    real, imag = np.cos(angle), -np.sin(angle)
    imag[:, 0] = 1.0 - 2.0 * (position % 2)
    weight = np.where(np.arange(ny // 2) == 0, 1.0, 2.0) * scale
    ahead = np.zeros((2, ny, pencils, 2, 2, modes))
    back = np.zeros((pencils, 2, 2, modes, 2, ny))
    for parity in range(2):
        for part, values in enumerate((real, imag)):
            ahead[parity, :, :, part, parity] = values.reshape(ny, pencils, modes)
            back[:, part, parity, :, parity] = (values * weight).T.reshape(pencils, modes, ny)
    return ahead.reshape(2 * ny, -1), back.reshape(-1, 2 * ny)


def wave_order(nx, slabs):
    half = nx // 2
    ahead = np.arange(half).reshape(slabs, 1, half // slabs)
    behind = np.where(ahead == 0, half, (nx - ahead) % nx)
    return np.concatenate([ahead, behind], axis=1).reshape(-1)


def x_tables(nx, cols, pencils, slabs):
    order = wave_order(nx, slabs)
    angle = angles(order, np.arange(nx), nx)
    ahead = np.concatenate([np.cos(angle), np.sin(angle)], axis=0)
    row = np.arange(cols + RIM)
    offset = np.where(row <= cols, row, -1)
    used = ((row <= cols) | (row == cols + RIM - 1)).astype(np.float64)
    place = (np.arange(pencils)[:, None] * cols + offset[None, :]) % nx
    angle = angles(place.reshape(-1), order, nx)
    mask = np.tile(used, pencils)[:, None]
    back = np.concatenate([np.cos(angle) * mask, np.sin(angle) * mask], axis=0)
    return ahead, back


def split(values):
    high = values.astype(BF16)
    return high, (values - high.astype(F32)).astype(BF16)


def dot(left, right):
    return jnp.dot(left, right, preferred_element_type=F32)


def table_left(high, low, values):
    v_high, v_low = split(values)
    return dot(high, v_high) + (dot(high, v_low) + dot(low, v_high))


def table_right(values, high, low):
    v_high, v_low = split(values)
    return dot(v_high, high) + (dot(v_low, high) + dot(v_high, low))


def lane_of():
    return lax.broadcasted_iota(jnp.int32, (1, LANES), 1)


def times_i(values):
    half = LANES // 2
    sign = jnp.where(lane_of() < half, -1.0, 1.0).astype(F32)
    return pltpu.roll(values, half, 1) * sign


def parity_swap(values):
    quarter = LANES // 4
    even = (lane_of() // quarter) % 2 == 0
    return jnp.where(
        even, pltpu.roll(values, LANES - quarter, 1), pltpu.roll(values, quarter, 1)
    )


def kernel_weight(distance):
    radius = jnp.abs(distance)
    near = 1.0 - 2.5 * radius * radius + 1.5 * radius * radius * radius
    far = 0.5 * (2.0 - radius) * (2.0 - radius) * (1.0 - radius)
    return jnp.where(radius < 1.0, near, jnp.where(radius < 2.0, far, 0.0))


def turned(values, wave, extent, sign):
    real = math.cos(2.0 * math.pi * wave / extent)
    imag = sign * math.sin(2.0 * math.pi * wave / extent)
    if wave == 0:
        return values
    if 4 * wave == extent:
        return times_i(values) * imag
    return values * real + times_i(values) * imag


def fft(values, sign):
    count = len(values)
    if count == 1:
        return values
    even, odd = fft(values[::2], sign), fft(values[1::2], sign)
    odd = [turned(v, k, count, sign) for k, v in enumerate(odd)]
    return [a + b for a, b in zip(even, odd)] + [a - b for a, b in zip(even, odd)]


def deposit_kernel(
    chunks, own, up1, down1, up2, down2, ambient, t_high, t_low, mesh, rim_high, rim_low, *rest
):
    parts, total = rest[: len(chunks)], rest[len(chunks)]
    _, planes, cols, ny = ambient.shape
    rows = cols + RIM
    movers = up2.shape[1]
    count = own.shape[1]

    def decode(ref, start, stop, shift):
        packet = ref[:, start:stop]
        cell = packet[6:7].astype(jnp.int32)
        move = packet[7:8].astype(jnp.int32)
        z_cell = lax.div(cell, cols * ny) + planes * (move + shift)
        x_cell = lax.rem(lax.div(cell, ny), cols)
        return packet[0:6], z_cell, x_cell, lax.rem(cell, ny)

    def joined(pieces):
        return [jnp.concatenate(p, axis=1) if len(p) > 1 else p[0] for p in zip(*pieces)]

    def add_block(pieces, first, used):
        values, z_cell, x_cell, y_cell = joined(pieces)
        width = values.shape[1]
        z_at = lax.broadcasted_iota(jnp.int32, (8, width), 0) + first
        w_z = kernel_weight((z_at - z_cell).astype(F32) - values[3:4])
        row = lax.broadcasted_iota(jnp.int32, (rows, width), 0)
        x_at = jnp.where(row < cols + 2, row, jnp.where(row >= rows - 2, row - rows, 4 * rows))
        w_x = kernel_weight((x_at - x_cell).astype(F32) - values[4:5])
        y_at = lax.broadcasted_iota(jnp.int32, (ny, width), 0)
        y_off = lax.rem(y_at - y_cell + (ny + ny // 2), ny) - ny // 2
        w_y = kernel_weight(y_off.astype(F32) - values[5:6])
        y_high, y_low = split(w_y)
        right = jnp.concatenate([y_high, y_high, y_low], axis=1)
        for c in range(3):
            s_z = values[c : c + 1] * w_z
            left = jnp.concatenate([s_z[k : k + 1] * w_x for k in range(used)], axis=0)
            l_high, l_low = split(left)
            left = jnp.concatenate([l_high, l_low, l_high], axis=1)
            added = lax.dot_general(
                left, right, (((1,), (1,)), ((), ())), preferred_element_type=F32
            )
            total[c, first : first + used] += added.reshape(used, rows, ny)

    total[:, :, 0:cols] = ambient[...]
    total[:, :, cols:rows] = jnp.zeros((3, planes, RIM, ny), F32)
    step = 256
    for at in range(0, count, step):
        add_block([decode(own, at, min(at + step, count), 0)], 0, planes)
    add_block([decode(up1, 0, movers, 1), decode(down1, 0, movers, -1)], 0, planes)
    for near, far, shift, first in ((up1, up2, 1, planes - 2), (down1, down2, -1, 0)):
        whole = [decode(near, movers, count, shift), decode(far, 0, movers, 2 * shift)]
        values, z_cell, x_cell, y_cell = joined(whole)
        for at in range(0, count, step):
            to = min(at + step, count)
            block = (values[:, at:to], z_cell[:, at:to], x_cell[:, at:to], y_cell[:, at:to])
            add_block([block], first, 2)

    for c in range(3):
        for z in range(planes):
            at = 2 * (c * planes + z)
            mesh[c, z] = total[c, z, 0:cols]
            rim_high[at : at + 2] = total[c, z, cols : cols + 2]
            rim_low[at : at + 2] = total[c, z, rows - 2 : rows]
    for pairs, part in zip(chunks, parts):
        groups = [(c, pair) for c in range(3) for pair in pairs]
        left = jnp.concatenate(
            [
                jnp.concatenate([total[c, 2 * p], total[c, 2 * p + 1]], axis=1)
                for c, p in groups
            ],
            axis=0,
        )
        wide = table_right(left, t_high[...], t_low[...])
        for n in range(len(groups)):
            for g in range(part.shape[0]):
                part[g, :, n * LANES : (n + 1) * LANES] = wide[
                    n * rows : (n + 1) * rows, g * LANES : (g + 1) * LANES
                ]


def x_ahead_kernel(part, t_high, t_low, out):
    pencils, rows, width = part.shape
    cols = rows - RIM
    row = lax.broadcasted_iota(jnp.int32, (RIM, width), 0)
    pieces = []
    for h in range(pencils):
        from_low = part[(h - 1) % pencils, cols:rows]
        from_high = part[(h + 1) % pencils, cols:rows]
        pieces.append(part[h, 0:RIM] + jnp.where(row < 2, from_low, 0.0))
        pieces.append(part[h, RIM : cols - RIM])
        pieces.append(part[h, cols - RIM : cols] + jnp.where(row >= RIM - 2, from_high, 0.0))
    both = table_left(t_high[...], t_low[...], jnp.concatenate(pieces, axis=0))
    half = both.shape[0] // 2
    for n in range(width // LANES):
        lanes = slice(n * LANES, (n + 1) * LANES)
        out[:, lanes] = both[:half, lanes] - times_i(both[half:, lanes])


def x_back_kernel(part, t_high, t_low, out):
    pencils, rows, width = out.shape
    both = table_left(t_high[...], t_low[...], part[...])
    half = both.shape[0] // 2
    for n in range(width // LANES):
        lanes = slice(n * LANES, (n + 1) * LANES)
        made = both[:half, lanes] + times_i(both[half:, lanes])
        out[:, :, lanes] = made.reshape(pencils, rows, LANES)


def wake_kernel(chunks, nx, ny, place, *refs):
    count = len(chunks)
    parts, outs = refs[:count], refs[count : 2 * count]
    spectrum, curled = refs[2 * count :]
    slabs, block, _ = parts[0].shape
    pairs = sum(len(c) for c in chunks)
    extent = 2 * pairs * slabs
    length = extent // 2
    reach = block // 2
    tile = min(8, reach)
    modes = LANES // 4
    lane = lane_of()
    odd = (lane // modes) % 2 == 1
    odd_float = odd.astype(F32)
    butterfly = 1.0 - 2.0 * odd_float
    slot = {p: (n, i) for n, chunk in enumerate(chunks) for i, p in enumerate(chunk)}

    def lanes_at(c, pair):
        n, i = slot[pair]
        return n, pl.ds(pl.multiple_of((c * len(chunks[n]) + i) * LANES, LANES), LANES)

    def odd_turned(values, k, sign):
        if k == 0:
            return values
        real = math.cos(2.0 * math.pi * k / extent)
        imag = sign * math.sin(2.0 * math.pi * k / extent)
        return values * (1.0 + odd_float * (real - 1.0)) + times_i(values) * (odd_float * imag)

    def ahead(c, carry):
        for side in range(2):
            for top in range(0, reach, tile):
                rows = slice(side * reach + top, side * reach + top + tile)
                values = []
                for s in range(slabs):
                    for pair in range(pairs):
                        n, lanes = lanes_at(c, pair)
                        values.append(parts[n][s, rows, lanes])
                for k, v in enumerate(fft(values, -1.0)):
                    v = odd_turned(v, k, -1.0)
                    spectrum[c, side, k, top : top + tile] = v * butterfly + parity_swap(v)
        return carry

    lax.fori_loop(0, 3, ahead, 0)

    slab_at, pencil_at = place[0], place[1]
    j = lax.broadcasted_iota(jnp.int32, (reach, LANES), 0)
    wave_number = slab_at * reach + j
    mode = jnp.broadcast_to(lane % modes, (reach, LANES)) + pencil_at * modes
    wave_y = mode.astype(F32) * (2.0 * math.pi / ny)
    packed = mode == 0
    alone = wave_number == 0
    conjugate = jnp.where(lane < LANES // 2, 1.0, -1.0).astype(F32)
    pi_sq = math.pi * math.pi

    def curl_at(k, with_mirror):
        z_wave = k - length * odd.astype(jnp.int32)
        z_base = jnp.broadcast_to(z_wave, (reach, LANES)).astype(F32) * (2.0 * math.pi / extent)
        z_trim = jnp.where(z_wave == -length, 0.0, z_base)
        opposite = lax.rem(length - k, length)
        for side in range(2):
            if side == 0:
                x_base = wave_number.astype(F32) * (2.0 * math.pi / nx)
                x_trim = x_base
            else:
                x_base = jnp.where(alone, math.pi, wave_number.astype(F32) * (-2.0 * math.pi / nx))
                x_trim = jnp.where(alone, 0.0, x_base)
            base = z_base * z_base + x_base * x_base
            full = base + wave_y * wave_y
            empty = full == 0.0
            inverse = jnp.where(empty, 0.0, 1.0 / jnp.where(empty, 1.0, full))
            if with_mirror:
                other = 1.0 / (base + pi_sq)
                mirror = jnp.where(packed, 0.5 * (inverse - other), 0.0) * conjugate
                inverse = jnp.where(packed, 0.5 * (inverse + other), inverse)
            stream = []
            for c in range(3):
                value = spectrum[c, side, k] * inverse
                if with_mirror:
                    across = jnp.where(
                        alone, spectrum[c, side, opposite], spectrum[c, 1 - side, opposite]
                    )
                    across = jnp.where(k == 0, across, parity_swap(across))
                    value = value + mirror * across
                stream.append(value)
            curled[0, side, k] = times_i(x_trim * stream[2] - wave_y * stream[1])
            curled[1, side, k] = times_i(wave_y * stream[0] - z_trim * stream[2])
            curled[2, side, k] = times_i(z_trim * stream[1] - x_trim * stream[0])

    def curl_all(with_mirror):
        def body(k, carry):
            curl_at(k, with_mirror)
            return carry

        lax.fori_loop(0, length, body, 0)

    @pl.when(pencil_at == 0)
    def _():
        curl_all(True)

    @pl.when(pencil_at != 0)
    def _():
        curl_all(False)

    def back(c, carry):
        for side in range(2):
            for top in range(0, reach, tile):
                rows = slice(side * reach + top, side * reach + top + tile)
                values = []
                for k in range(length):
                    v = curled[c, side, k, top : top + tile]
                    values.append(odd_turned(v * butterfly + parity_swap(v), k, 1.0))
                for z, v in enumerate(fft(values, 1.0)):
                    n, lanes = lanes_at(c, z % pairs)
                    outs[n][z // pairs, rows, lanes] = v
        return carry

    lax.fori_loop(0, 3, back, 0)


def planes_of(part, pairs, t_high, t_low):
    pencils, rows, _ = part.shape
    ny = t_high.shape[1] // 2
    groups = [(c, pair) for c in range(3) for pair in pairs]
    left = jnp.concatenate(
        [
            jnp.concatenate(
                [part[h, :, n * LANES : (n + 1) * LANES] for h in range(pencils)], axis=1
            )
            for n in range(len(groups))
        ],
        axis=0,
    )
    wide = table_right(left, t_high[...], t_low[...])
    made = {}
    for n, (c, pair) in enumerate(groups):
        for parity in range(2):
            made[c, 2 * pair + parity] = wide[
                n * rows : (n + 1) * rows, parity * ny : (parity + 1) * ny
            ]
    return made


def edge_kernel(pairs, part, t_high, t_low, out, first, last):
    listed = [2 * pair + parity for pair in pairs for parity in range(2)]
    cols = first.shape[1]
    made = planes_of(part, pairs, t_high, t_low)
    for c in range(3):
        for n, z in enumerate(listed):
            out[c, n] = made[c, z]
        first[c] = made[c, listed[0]][0:cols]
        last[c] = made[c, listed[-1]][0:cols]


def stretch_kernel(
    edge_pairs, pairs, edges, part, before, after, mesh, low_rim, high_rim, t_high, t_low,
    velocity, vorticity, held
):
    _, planes, cols, ny = velocity.shape
    rows = cols + RIM

    def hold(c, z, value):
        velocity[c, z] = value[0:cols]
        held[c, z, RIM : RIM + rows] = value
        held[c, z, 0:RIM] = value[cols:rows]

    listed = [2 * pair + parity for pair in edge_pairs for parity in range(2)]
    for c in range(3):
        for n, z in enumerate(listed):
            hold(c, z, edges[c, n])
    for (c, z), value in planes_of(part, pairs, t_high, t_low).items():
        hold(c, z, value)
    for z in range(planes):
        for c in range(3):
            at = 2 * (c * planes + z)
            vorticity[c, z] = mesh[c, z]
            vorticity[c, z, 0:2] += low_rim[at : at + 2]
            vorticity[c, z, cols - 2 : cols] += high_rim[at : at + 2]
        omega = [vorticity[c, z] for c in range(3)]
        for c in range(3):
            value = velocity[c, z]
            ahead = velocity[c, z + 1] if z + 1 < planes else after[c]
            behind = velocity[c, z - 1] if z > 0 else before[c]
            along_z = (ahead - behind) * 0.5
            along_x = (
                held[c, z, RIM + 1 : RIM + 1 + cols] - held[c, z, RIM - 1 : RIM - 1 + cols]
            ) * 0.5
            along_y = (pltpu.roll(value, ny - 1, 1) - pltpu.roll(value, 1, 1)) * 0.5
            stretch = omega[0] * along_z + omega[1] * along_x + omega[2] * along_y
            vorticity[c, z] = omega[c] + TIME_STEP * stretch


def call(kernel, outs, scratch=(), scalars=0, inputs=0):
    vmem = pl.BlockSpec(memory_space=pltpu.VMEM)
    smem = pl.BlockSpec(memory_space=pltpu.SMEM)
    return pl.pallas_call(
        kernel,
        out_shape=[jax.ShapeDtypeStruct(shape, F32) for shape in outs],
        in_specs=[smem] * scalars + [vmem] * inputs,
        out_specs=[vmem] * len(outs),
        scratch_shapes=[pltpu.VMEM(shape, F32) for shape in scratch],
        compiler_params=pltpu.CompilerParams(vmem_limit_bytes=VMEM),
    )


def ring(axis, step):
    count = lax.axis_size(axis)
    return [(i, (i + step) % count) for i in range(count)]


def exchange(values, axis):
    return lax.all_to_all(values, axis, split_axis=0, concat_axis=0, tiled=True)


def on_device(strength, offsets, cell_index, migrate_count, ambient):
    _, planes, cols, ny = ambient.shape
    slabs, pencils = lax.axis_size("gz"), lax.axis_size("gx")
    nx, nz, rows = cols * pencils, planes * slabs, cols + RIM
    pair_count = planes // 2
    edge = tuple(sorted({0, pair_count - 1}))
    chunks = (edge, tuple(range(1, pair_count - 1)))
    widths = [3 * len(c) * LANES for c in chunks]

    y_ahead, y_back = [
        split_table(t) for t in y_tables(ny, pencils, 1.0 / (float(nx) * ny * nz))
    ]
    x_ahead, x_back = [split_table(t) for t in x_tables(nx, cols, pencils, slabs)]

    slot = jnp.arange(strength.shape[1], dtype=jnp.int32)
    up_count = migrate_count[0, 0, 0]
    both_count = up_count + migrate_count[0, 0, 1]
    move = jnp.where(slot < up_count, 1.0, jnp.where(slot < both_count, -1.0, 0.0))
    packet = jnp.concatenate(
        [strength, offsets, cell_index.astype(F32)[None], move.astype(F32)[None]], axis=0
    )
    movers = packet[:, : 2 * MIG]
    up1 = lax.ppermute(packet, "gz", ring("gz", -1))
    down1 = lax.ppermute(packet, "gz", ring("gz", 1))
    up2 = lax.ppermute(movers, "gz", ring("gz", -2))
    down2 = lax.ppermute(movers, "gz", ring("gz", 2))

    rim = (6 * planes, ny)
    mesh, rim_high, rim_low, *parts = call(
        functools.partial(deposit_kernel, chunks),
        [ambient.shape, rim, rim] + [(pencils, rows, w) for w in widths],
        [(3, planes, rows, ny)],
        inputs=8,
    )(packet, up1, down1, up2, down2, ambient, *y_ahead)
    low_rim = lax.ppermute(rim_high, "gx", ring("gx", 1))
    high_rim = lax.ppermute(rim_low, "gx", ring("gx", -1))

    spectra = []
    for part, width in zip(parts, widths):
        part = exchange(part, "gx")
        (part,) = call(x_ahead_kernel, [(nx, width)], inputs=3)(part, *x_ahead)
        spectra.append(exchange(part.reshape(slabs, nx // slabs, width), "gz"))
    place = jnp.stack([lax.axis_index("gz"), lax.axis_index("gx")]).astype(jnp.int32)
    held = (3, 2, nz // 2, nx // (2 * slabs), LANES)
    spectra = call(
        functools.partial(wake_kernel, chunks, nx, ny),
        [s.shape for s in spectra],
        [held, held],
        scalars=1,
        inputs=len(spectra),
    )(place, *spectra)
    parts = []
    for part, width in zip(spectra, widths):
        part = exchange(part, "gz").reshape(nx, width)
        (part,) = call(x_back_kernel, [(pencils, rows, width)], inputs=3)(part, *x_back)
        parts.append(exchange(part, "gx"))
    plane = (3, cols, ny)
    edges, first, last = call(
        functools.partial(edge_kernel, chunks[0]),
        [(3, 2 * len(edge), rows, ny), plane, plane],
        inputs=3,
    )(parts[0], *y_back)
    after = lax.ppermute(first, "gz", ring("gz", -1))
    before = lax.ppermute(last, "gz", ring("gz", 1))
    return tuple(
        call(
            functools.partial(stretch_kernel, *chunks),
            [ambient.shape, ambient.shape],
            [(3, planes, cols + 2 * RIM, ny)],
            inputs=9,
        )(edges, parts[1], before, after, mesh, low_rim, high_rim, *y_back)
    )


def solution(mesh):
    placed = (
        P(None, ("gz", "gx")),
        P(None, ("gz", "gx")),
        P(("gz", "gx")),
        P("gz", "gx", None),
        P(None, "gz", "gx", None),
    )
    return jax.shard_map(
        on_device,
        mesh=mesh,
        in_specs=placed,
        out_specs=(P(None, "gz", "gx", None), P(None, "gz", "gx", None)),
        check_vma=False,
    )
```

```python
import functools
import math

import jax
import jax.numpy as jnp
import ml_dtypes
import numpy as np
from jax import lax
from jax.experimental import pallas as pl
from jax.experimental.pallas import tpu as pltpu
from jax.sharding import PartitionSpec as P

MIG = 64
LANES = 128
RIM = 8
TIME_STEP = 0.25
VMEM = 48 * 1024 * 1024
F32 = jnp.float32
BF16 = jnp.bfloat16


def split_table(table):
    high = table.astype(np.float32).astype(ml_dtypes.bfloat16)
    low = (table - high.astype(np.float64)).astype(np.float32).astype(ml_dtypes.bfloat16)
    return high, low


def angles(rows, columns, extent):
    return 2.0 * np.pi * (np.multiply.outer(rows, columns) % extent) / extent


def y_tables(ny, pencils, scale):
    modes = ny // (2 * pencils)
    position = np.arange(ny)
    angle = angles(position, np.arange(ny // 2), ny)
    real, imag = np.cos(angle), -np.sin(angle)
    imag[:, 0] = 1.0 - 2.0 * (position % 2)
    weight = np.where(np.arange(ny // 2) == 0, 1.0, 2.0) * scale
    ahead = np.zeros((2, ny, pencils, 2, 2, modes))
    back = np.zeros((pencils, 2, 2, modes, 2, ny))
    for parity in range(2):
        for part, values in enumerate((real, imag)):
            ahead[parity, :, :, part, parity] = values.reshape(ny, pencils, modes)
            back[:, part, parity, :, parity] = (values * weight).T.reshape(pencils, modes, ny)
    return ahead.reshape(2 * ny, -1), back.reshape(-1, 2 * ny)


def wave_order(nx, slabs):
    half = nx // 2
    ahead = np.arange(half).reshape(slabs, 1, half // slabs)
    behind = np.where(ahead == 0, half, (nx - ahead) % nx)
    return np.concatenate([ahead, behind], axis=1).reshape(-1)


def x_tables(nx, cols, pencils, slabs):
    order = wave_order(nx, slabs)
    angle = angles(order, np.arange(nx), nx)
    ahead = np.concatenate([np.cos(angle), np.sin(angle)], axis=0)
    row = np.arange(cols + RIM)
    offset = np.where(row <= cols, row, -1)
    used = ((row <= cols) | (row == cols + RIM - 1)).astype(np.float64)
    place = (np.arange(pencils)[:, None] * cols + offset[None, :]) % nx
    angle = angles(place.reshape(-1), order, nx)
    mask = np.tile(used, pencils)[:, None]
    back = np.concatenate([np.cos(angle) * mask, np.sin(angle) * mask], axis=0)
    return ahead, back


def split(values):
    high = values.astype(BF16)
    return high, (values - high.astype(F32)).astype(BF16)


def dot(left, right):
    return jnp.dot(left, right, preferred_element_type=F32)


def table_left(high, low, values):
    v_high, v_low = split(values)
    return dot(high, v_high) + (dot(high, v_low) + dot(low, v_high))


def table_right(values, high, low):
    v_high, v_low = split(values)
    return dot(v_high, high) + (dot(v_low, high) + dot(v_high, low))


def lane_of():
    return lax.broadcasted_iota(jnp.int32, (1, LANES), 1)


def times_i(values):
    half = LANES // 2
    sign = jnp.where(lane_of() < half, -1.0, 1.0).astype(F32)
    return pltpu.roll(values, half, 1) * sign


def kernel_weight(distance):
    radius = jnp.abs(distance)
    near = 1.0 - 2.5 * radius * radius + 1.5 * radius * radius * radius
    far = 0.5 * (2.0 - radius) * (2.0 - radius) * (1.0 - radius)
    return jnp.where(radius < 1.0, near, jnp.where(radius < 2.0, far, 0.0))


def turned(value, wave, extent, sign):
    wave = wave % extent
    real, imag = value
    if wave == 0:
        return value
    if 2 * wave == extent:
        return -real, -imag
    if 4 * wave == extent:
        return (-imag, real) if sign > 0 else (imag, -real)
    if 4 * wave == 3 * extent:
        return (imag, -real) if sign > 0 else (-imag, real)
    a = math.cos(2.0 * math.pi * wave / extent)
    b = sign * math.sin(2.0 * math.pi * wave / extent)
    return real * a - imag * b, real * b + imag * a


def fft(values, sign):
    count = len(values)
    if count == 1:
        return values
    even, odd = fft(values[::2], sign), fft(values[1::2], sign)
    odd = [turned(v, k, count, sign) for k, v in enumerate(odd)]
    plus = [(a[0] + b[0], a[1] + b[1]) for a, b in zip(even, odd)]
    minus = [(a[0] - b[0], a[1] - b[1]) for a, b in zip(even, odd)]
    return plus + minus


def blocks_of(refs, at):
    if len(refs) == 1:
        return [(d, refs[0].at[d]) for d in range(refs[0].shape[0])]
    return [(at ^ k, ref) for k, ref in enumerate(refs)]


def gather_blocks(refs, held, at):
    for d, ref in blocks_of(refs, at):
        held[d] = ref[...]


def packet_kernel(counts, strength, offsets, cells, packet, movers):
    slot = lax.broadcasted_iota(jnp.int32, (1, strength.shape[1]), 1)
    up, both = counts[0], counts[0] + counts[1]
    packet[0:3] = strength[...]
    packet[3:6] = offsets[...]
    packet[6:7] = cells[...].astype(F32)
    packet[7:8] = jnp.where(slot < up, 1.0, jnp.where(slot < both, -1.0, 0.0))
    movers[...] = packet[:, : movers.shape[1]]


def deposit_kernel(
    pairs, place, own, up1, down1, up2, down2, ambient, table_high, table_low, *refs
):
    mesh, rim_high, rim_low = refs[:3]
    total, t_high, t_low, made, sems = refs[-5:]
    outs = refs[3:-5]
    _, planes, cols, ny = ambient.shape
    rows = cols + RIM
    movers = up2.shape[1]
    count = own.shape[1]
    listed = [2 * pair + parity for pair in pairs for parity in range(2)]
    fetches = [
        pltpu.make_async_copy(
            ambient.at[:, z], total.at[:, n, pl.ds(0, cols)], sems.at[n]
        )
        for n, z in enumerate(listed)
    ]
    tables = [
        pltpu.make_async_copy(table_high, t_high, sems.at[len(listed)]),
        pltpu.make_async_copy(table_low, t_low, sems.at[len(listed) + 1]),
    ]
    for fetch in fetches + tables:
        fetch.start()

    def decode(ref, start, stop, shift):
        packet = ref[:, start:stop]
        cell = packet[6:7].astype(jnp.int32)
        move = packet[7:8].astype(jnp.int32)
        z_cell = lax.div(cell, cols * ny) + planes * (move + shift)
        x_cell = lax.rem(lax.div(cell, ny), cols)
        return packet[0:6], z_cell, x_cell, lax.rem(cell, ny)

    def joined(pieces):
        return [jnp.concatenate(p, axis=1) if len(p) > 1 else p[0] for p in zip(*pieces)]

    def add_block(pieces, wanted, waits=()):
        values, z_cell, x_cell, y_cell = joined(pieces)
        width = values.shape[1]
        z_at = lax.broadcasted_iota(jnp.int32, (planes, width), 0)
        w_z = kernel_weight((z_at - z_cell).astype(F32) - values[3:4])
        row = lax.broadcasted_iota(jnp.int32, (rows, width), 0)
        x_at = jnp.where(row < cols + 2, row, jnp.where(row >= rows - 2, row - rows, 4 * rows))
        w_x = kernel_weight((x_at - x_cell).astype(F32) - values[4:5])
        y_at = lax.broadcasted_iota(jnp.int32, (ny, width), 0)
        y_off = lax.rem(y_at - y_cell + (ny + ny // 2), ny) - ny // 2
        w_y = kernel_weight(y_off.astype(F32) - values[5:6])
        y_high, y_low = split(w_y)
        right = jnp.concatenate([y_high, y_high, y_low], axis=1)
        for wait in waits:
            wait.wait()
        at = [listed.index(z) for z in wanted]
        for c in range(3):
            s_z = values[c : c + 1] * w_z
            left = jnp.concatenate([s_z[z : z + 1] * w_x for z in wanted], axis=0)
            l_high, l_low = split(left)
            left = jnp.concatenate([l_high, l_low, l_high], axis=1)
            added = lax.dot_general(
                left, right, (((1,), (1,)), ((), ())), preferred_element_type=F32
            )
            total[c, at[0] : at[-1] + 1] += added.reshape(len(wanted), rows, ny)

    total[:, :, cols:rows] = jnp.zeros((3, len(listed), RIM, ny), F32)
    step = 256
    for at in range(0, count, step):
        waits = fetches if at == 0 else ()
        add_block([decode(own, at, min(at + step, count), 0)], listed, waits)
    add_block([decode(up1, 0, movers, 1), decode(down1, 0, movers, -1)], listed)
    sides = ((up1, up2, 1, (planes - 2, planes - 1)), (down1, down2, -1, (0, 1)))
    for near, far, shift, wanted in sides:
        if not set(wanted) <= set(listed):
            continue
        whole = [decode(near, movers, count, shift), decode(far, 0, movers, 2 * shift)]
        values, z_cell, x_cell, y_cell = joined(whole)
        for at in range(0, count, step):
            to = min(at + step, count)
            block = (values[:, at:to], z_cell[:, at:to], x_cell[:, at:to], y_cell[:, at:to])
            add_block([block], wanted)

    keep = pltpu.make_async_copy(total.at[:, :, pl.ds(0, cols)], mesh, sems.at[0])
    keep.start()
    for n in range(3 * len(listed)):
        c, i = n // len(listed), n % len(listed)
        rim_high[2 * n : 2 * n + 2] = total[c, i, cols : cols + 2]
        rim_low[2 * n : 2 * n + 2] = total[c, i, rows - 2 : rows]
    groups = [(c, 2 * n) for c in range(3) for n in range(len(pairs))]
    left = jnp.concatenate(
        [jnp.concatenate([total[c, n], total[c, n + 1]], axis=1) for c, n in groups], axis=0
    )
    for table in tables:
        table.wait()
    wide = table_right(left, t_high[...], t_low[...])
    for n in range(len(groups)):
        for g in range(made.shape[0]):
            made[g, :, n * LANES : (n + 1) * LANES] = wide[
                n * rows : (n + 1) * rows, g * LANES : (g + 1) * LANES
            ]
    for d, out in blocks_of(outs, place[1]):
        out[...] = made[d]
    keep.wait()


def x_ahead_kernel(sends, place, t_high, t_low, *refs):
    held, made = refs[-2:]
    outs, parts = refs[-2 - sends : -2], refs[: -2 - sends]
    gather_blocks(parts, held, place[1])
    pencils, rows, width = held.shape
    cols = rows - RIM
    row = lax.broadcasted_iota(jnp.int32, (RIM, width), 0)
    pieces = []
    for h in range(pencils):
        from_low = held[(h - 1) % pencils, cols:rows]
        from_high = held[(h + 1) % pencils, cols:rows]
        pieces.append(held[h, 0:RIM] + jnp.where(row < 2, from_low, 0.0))
        pieces.append(held[h, RIM : cols - RIM])
        pieces.append(held[h, cols - RIM : cols] + jnp.where(row >= RIM - 2, from_high, 0.0))
    both = table_left(t_high[...], t_low[...], jnp.concatenate(pieces, axis=0))
    half = both.shape[0] // 2
    for n in range(width // LANES):
        lanes = slice(n * LANES, (n + 1) * LANES)
        value = both[:half, lanes] - times_i(both[half:, lanes])
        made[:, :, lanes] = value.reshape(made.shape[0], made.shape[1], LANES)
    for d, out in blocks_of(outs, place[0]):
        out[...] = made[d]


def x_back_kernel(sends, place, t_high, t_low, *refs):
    held, made = refs[-2:]
    outs, parts = refs[-2 - sends : -2], refs[: -2 - sends]
    gather_blocks(parts, held, place[0])
    pencils, rows, width = made.shape
    both = table_left(t_high[...], t_low[...], held[...].reshape(-1, width))
    half = both.shape[0] // 2
    for n in range(width // LANES):
        lanes = slice(n * LANES, (n + 1) * LANES)
        value = both[:half, lanes] + times_i(both[half:, lanes])
        made[:, :, lanes] = value.reshape(pencils, rows, LANES)
    for d, out in blocks_of(outs, place[1]):
        out[...] = made[d]


def wake_kernel(chunks, nx, ny, place, *refs):
    data, spectrum = refs[-2:]
    each = (len(refs) - 2) // (2 * len(chunks))
    parts = [refs[n * each : (n + 1) * each] for n in range(len(chunks))]
    outs = [refs[(n + len(chunks)) * each :][:each] for n in range(len(chunks))]
    _, _, planes, slabs, tile, _ = data.shape
    nz = planes * slabs
    lane = lane_of()
    modes = LANES // 4
    low_half = lane < LANES // 2
    first = (lane // modes) % 2 == 0
    half, quarter = LANES // 2, LANES // 4
    slab_at, pencil_at = place[0], place[1]

    def roll(values, shift):
        return pltpu.roll(values, shift, 1)

    def cross_half(a, b):
        return jnp.where(low_half, a, roll(b, half)), jnp.where(low_half, roll(a, half), b)

    def cross_quarter(a, b):
        return (
            jnp.where(first, a, roll(b, quarter)),
            jnp.where(first, roll(a, LANES - quarter), b),
        )

    def lanes_at(c, chunk, i):
        return pl.ds(pl.multiple_of((c * len(chunk) + i) * LANES, LANES), LANES)

    def enter(c, carry):
        for chunk, refs_in in zip(chunks, parts):
            for i, pair in enumerate(chunk):
                lanes = lanes_at(c, chunk, i)
                for s, ref in blocks_of(refs_in, slab_at):
                    quad = [ref[q * tile : (q + 1) * tile, lanes] for q in range(4)]
                    real0, imag0 = cross_half(quad[0], quad[2])
                    real1, imag1 = cross_half(quad[1], quad[3])
                    for part, (a, b) in enumerate(((real0, real1), (imag0, imag1))):
                        even, odd = cross_quarter(a, b)
                        data[c, part, 2 * pair, s] = even
                        data[c, part, 2 * pair + 1, s] = odd
        return carry

    def leave(c, carry):
        for chunk, refs_out in zip(chunks, outs):
            for i, pair in enumerate(chunk):
                lanes = lanes_at(c, chunk, i)
                for s, ref in blocks_of(refs_out, slab_at):
                    real0, real1 = cross_quarter(data[c, 0, 2 * pair, s], data[c, 0, 2 * pair + 1, s])
                    imag0, imag1 = cross_quarter(data[c, 1, 2 * pair, s], data[c, 1, 2 * pair + 1, s])
                    quad = [None] * 4
                    quad[0], quad[2] = cross_half(real0, imag0)
                    quad[1], quad[3] = cross_half(real1, imag1)
                    for q in range(4):
                        ref[q * tile : (q + 1) * tile, lanes] = quad[q]
        return carry

    def across_slabs(c, carry):
        for l in range(planes):
            line = [(data[c, 0, l, s], data[c, 1, l, s]) for s in range(slabs)]
            for k, v in enumerate(fft(line, -1.0)):
                v = turned(v, l * k, nz, -1.0)
                data[c, 0, l, k], data[c, 1, l, k] = v
        return carry

    def back_across_slabs(c, carry):
        for l in range(planes):
            line = [
                turned((data[c, 0, l, k], data[c, 1, l, k]), l * k, nz, 1.0) for k in range(slabs)
            ]
            for s, v in enumerate(fft(line, 1.0)):
                data[c, 0, l, s], data[c, 1, l, s] = v
        return carry

    def across_planes(k, carry):
        for c in range(3):
            line = [(data[c, 0, l, k], data[c, 1, l, k]) for l in range(planes)]
            for n, v in enumerate(fft(line, -1.0)):
                spectrum[c, 0, k + slabs * n], spectrum[c, 1, k + slabs * n] = v
        return carry

    reach = 2 * tile
    row = lax.broadcasted_iota(jnp.int32, (tile, LANES), 0)
    lane_all = lax.broadcasted_iota(jnp.int32, (tile, LANES), 1)
    number = slab_at * reach + (lane_all // modes) % 2 * tile + row
    ahead = lane_all < half
    mode = lane_all % modes + pencil_at * modes
    alone = number == 0
    number = number.astype(F32) * (2.0 * math.pi / nx)
    x_base = jnp.where(ahead, number, jnp.where(alone, math.pi, -number))
    x_trim = jnp.where(ahead, number, jnp.where(alone, 0.0, -number))
    wave_y = mode.astype(F32) * (2.0 * math.pi / ny)
    packed = mode == 0
    x_sq = x_base * x_base
    lateral = x_sq + wave_y * wave_y

    def curl_at(k, with_mirror):
        z_wave = jnp.where(k < nz // 2, k, k - nz).astype(F32) * (2.0 * math.pi / nz)
        z_trim = jnp.where(k == nz // 2, 0.0, z_wave)
        full = lateral + z_wave * z_wave
        empty = full == 0.0
        inverse = jnp.where(empty, 0.0, 1.0 / jnp.where(empty, 1.0, full))
        if with_mirror:
            other = 1.0 / (x_sq + (z_wave * z_wave + math.pi * math.pi))
            mirror = jnp.where(packed, 0.5 * (inverse - other), 0.0)
            inverse = jnp.where(packed, 0.5 * (inverse + other), inverse)
            opposite = lax.rem(nz - k, nz)
        stream = []
        for c in range(3):
            value = [spectrum[c, part, k] * inverse for part in range(2)]
            if with_mirror:
                for part, sign in enumerate((1.0, -1.0)):
                    there = spectrum[c, part, opposite]
                    there = jnp.where(alone, there, roll(there, half))
                    value[part] = value[part] + (mirror * sign) * there
            stream.append(value)
        made = []
        for part in range(2):
            s = [value[part] for value in stream]
            made.append(
                (
                    x_trim * s[2] - wave_y * s[1],
                    wave_y * s[0] - z_trim * s[2],
                    z_trim * s[1] - x_trim * s[0],
                )
            )
        return [(-made[1][c], made[0][c]) for c in range(3)]

    def curl_all(with_mirror):
        def body(k, carry):
            made = [curl_at(k + slabs * n, with_mirror) for n in range(planes)]
            for c in range(3):
                for l, v in enumerate(fft([m[c] for m in made], 1.0)):
                    data[c, 0, l, k], data[c, 1, l, k] = v
            return carry

        lax.fori_loop(0, slabs, body, 0)

    lax.fori_loop(0, 3, enter, 0)
    lax.fori_loop(0, 3, across_slabs, 0)
    lax.fori_loop(0, slabs, across_planes, 0)

    @pl.when(pencil_at == 0)
    def _():
        curl_all(True)

    @pl.when(pencil_at != 0)
    def _():
        curl_all(False)

    lax.fori_loop(0, 3, back_across_slabs, 0)
    lax.fori_loop(0, 3, leave, 0)


def planes_of(held, pairs, t_high, t_low):
    pencils, rows, _ = held.shape
    ny = t_high.shape[1] // 2
    groups = [(c, pair) for c in range(3) for pair in pairs]
    left = jnp.concatenate(
        [
            jnp.concatenate(
                [held[h, :, n * LANES : (n + 1) * LANES] for h in range(pencils)], axis=1
            )
            for n in range(len(groups))
        ],
        axis=0,
    )
    wide = table_right(left, t_high[...], t_low[...])
    made = {}
    for n, (c, pair) in enumerate(groups):
        for parity in range(2):
            made[c, 2 * pair + parity] = wide[
                n * rows : (n + 1) * rows, parity * ny : (parity + 1) * ny
            ]
    return made


def edge_kernel(pairs, place, t_high, t_low, *refs):
    out, first, last, held, made, sem = refs[-6:]
    gather_blocks(refs[:-6], held, place[1])
    listed = [2 * pair + parity for pair in pairs for parity in range(2)]
    cols = first.shape[1]
    values = planes_of(held, pairs, t_high, t_low)
    for c in range(3):
        for n, z in enumerate(listed):
            made[c, n] = values[c, z]
    keep = pltpu.make_async_copy(made, out, sem.at[0])
    keep.start()
    for c in range(3):
        first[c] = values[c, listed[0]][0:cols]
        last[c] = values[c, listed[-1]][0:cols]
    keep.wait()


def stretch_kernel(chunks, place, t_high, t_low, edges, before, after, *refs):
    meshes, rims, refs = refs[:2], refs[2:6], refs[6:]
    velocity, vorticity, held, tall, omega, sems = refs[-6:]
    parts = refs[:-6]
    _, planes, cols, ny = velocity.shape
    rows = cols + RIM
    lists = [[2 * pair + parity for pair in chunk for parity in range(2)] for chunk in chunks]
    copies, used = [], 0
    for chunk, mesh in zip(lists, meshes):
        for n, z in enumerate(chunk):
            copies.append(pltpu.make_async_copy(mesh.at[:, n], omega.at[:, z], sems.at[used]))
            used += 1
    for n, z in enumerate(lists[0]):
        copies.append(
            pltpu.make_async_copy(
                edges.at[:, n], tall.at[:, z, pl.ds(RIM, rows)], sems.at[used]
            )
        )
        copies.append(
            pltpu.make_async_copy(
                edges.at[:, n, pl.ds(cols, RIM)], tall.at[:, z, pl.ds(0, RIM)], sems.at[used + 1]
            )
        )
        used += 2
    for copy in copies:
        copy.start()
    gather_blocks(parts, held, place[1])
    for (c, z), value in planes_of(held, chunks[1], t_high, t_low).items():
        tall[c, z, RIM : RIM + rows] = value
        tall[c, z, 0:RIM] = value[cols:rows]
    for copy in copies:
        copy.wait()
    sent = []
    for z in range(planes):
        sent.append(
            pltpu.make_async_copy(tall.at[:, z, pl.ds(RIM, cols)], velocity.at[:, z], sems.at[z])
        )
        sent[-1].start()
    for z in range(planes):
        which = 0 if z in lists[0] else 1
        n, size = lists[which].index(z), len(lists[which])
        low_rim, high_rim = rims[2 * which], rims[2 * which + 1]
        for c in range(3):
            at = 2 * (c * size + n)
            omega[c, z, 0:2] += low_rim[at : at + 2]
            omega[c, z, cols - 2 : cols] += high_rim[at : at + 2]
        mesh = [omega[c, z] for c in range(3)]
        for c in range(3):
            value = tall[c, z, RIM : RIM + cols]
            above = tall[c, z + 1, RIM : RIM + cols] if z + 1 < planes else after[c]
            below = tall[c, z - 1, RIM : RIM + cols] if z > 0 else before[c]
            along_z = (above - below) * 0.5
            along_x = (
                tall[c, z, RIM + 1 : RIM + 1 + cols] - tall[c, z, RIM - 1 : RIM - 1 + cols]
            ) * 0.5
            along_y = (pltpu.roll(value, ny - 1, 1) - pltpu.roll(value, 1, 1)) * 0.5
            stretch = mesh[0] * along_z + mesh[1] * along_x + mesh[2] * along_y
            omega[c, z] = mesh[c] + TIME_STEP * stretch
        sent.append(
            pltpu.make_async_copy(omega.at[:, z], vorticity.at[:, z], sems.at[planes + z])
        )
        sent[-1].start()
    for copy in sent:
        copy.wait()


VM = pl.BlockSpec(memory_space=pltpu.VMEM)
SM = pl.BlockSpec(memory_space=pltpu.SMEM)
HB = pl.BlockSpec(memory_space=pltpu.HBM)


def call(kernel, ins, outs, scratch=(), sems=0, micros=2.0):
    extra = [pltpu.SemaphoreType.DMA((sems,))] if sems else []
    return pl.pallas_call(
        kernel,
        out_shape=[jax.ShapeDtypeStruct(shape, F32) for _, shape in outs],
        in_specs=[spec for spec, _ in ins],
        out_specs=[spec for spec, _ in outs],
        scratch_shapes=[pltpu.VMEM(shape, kind) for shape, kind in scratch] + extra,
        compiler_params=pltpu.CompilerParams(vmem_limit_bytes=VMEM),
        cost_estimate=pl.CostEstimate(
            flops=int(micros * 1.0e9), bytes_accessed=int(micros * 3.0e6), transcendentals=0
        ),
    )(*[value for _, value in ins])


def ring(axis, step):
    count = lax.axis_size(axis)
    return [(i, (i + step) % count) for i in range(count)]


def spread(axis):
    count = lax.axis_size(axis)
    return count <= 8 and count & (count - 1) == 0


def sent_shapes(axis, rows, width):
    count = lax.axis_size(axis)
    return [(rows, width)] * count if spread(axis) else [(count, rows, width)]


def exchange(blocks, axis):
    if not spread(axis):
        return [lax.all_to_all(blocks[0], axis, split_axis=0, concat_axis=0, tiled=True)]
    count = lax.axis_size(axis)
    moved = [blocks[0]] + [None] * (count - 1)
    for k in range(count - 1, 0, -1):
        moved[k] = lax.ppermute(blocks[k], axis, [(i, i ^ k) for i in range(count)])
    return moved


def on_device(strength, offsets, cell_index, migrate_count, ambient):
    _, planes, cols, ny = ambient.shape
    slabs, pencils = lax.axis_size("gz"), lax.axis_size("gx")
    nx, nz, rows = cols * pencils, planes * slabs, cols + RIM
    count = strength.shape[1]
    pair_count = planes // 2
    chunks = ((0, pair_count - 1), tuple(range(1, pair_count - 1)))
    widths = [3 * len(c) * LANES for c in chunks]
    block = nx // slabs

    y_ahead, y_back = [split_table(t) for t in y_tables(ny, pencils, 1.0 / (float(nx) * ny * nz))]
    x_ahead, x_back = [split_table(t) for t in x_tables(nx, cols, pencils, slabs)]
    place = jnp.stack([lax.axis_index("gz"), lax.axis_index("gx")]).astype(jnp.int32)
    here = (SM, place)

    packet, movers = call(
        packet_kernel,
        [
            (SM, migrate_count.reshape(2)),
            (VM, strength),
            (VM, offsets),
            (VM, cell_index.reshape(1, count)),
        ],
        [(VM, (8, count)), (VM, (8, 2 * MIG))],
    )
    up1 = lax.ppermute(packet, "gz", ring("gz", -1))
    down1 = lax.ppermute(packet, "gz", ring("gz", 1))
    up2 = lax.ppermute(movers, "gz", ring("gz", -2))
    down2 = lax.ppermute(movers, "gz", ring("gz", 2))

    meshes, rims, parts = [], [], []
    for chunk, width in zip(chunks, widths):
        size = 2 * len(chunk)
        mesh, rim_high, rim_low, *part = call(
            functools.partial(deposit_kernel, chunk),
            [here]
            + [(VM, value) for value in (packet, up1, down1, up2, down2)]
            + [(HB, ambient), (HB, y_ahead[0]), (HB, y_ahead[1])],
            [(HB, (3, size, cols, ny)), (VM, (6 * size, ny)), (VM, (6 * size, ny))]
            + [(VM, shape) for shape in sent_shapes("gx", rows, width)],
            [
                ((3, size, rows, ny), F32),
                (y_ahead[0].shape, BF16),
                (y_ahead[0].shape, BF16),
                ((pencils, rows, width), F32),
            ],
            sems=size + 2,
            micros=6.0,
        )
        meshes.append(mesh)
        rims.append(lax.ppermute(rim_high, "gx", ring("gx", 1)))
        rims.append(lax.ppermute(rim_low, "gx", ring("gx", -1)))
        parts.append(exchange(part, "gx"))

    spectra = []
    for part, width in zip(parts, widths):
        shapes = sent_shapes("gz", block, width)
        part = call(
            functools.partial(x_ahead_kernel, len(shapes)),
            [here, (VM, x_ahead[0]), (VM, x_ahead[1])] + [(VM, p) for p in part],
            [(VM, shape) for shape in shapes],
            [((pencils, rows, width), F32), ((slabs, block, width), F32)],
        )
        spectra += exchange(part, "gz")
    tile = max(1, block // 4)
    spectra = call(
        functools.partial(wake_kernel, chunks, nx, ny),
        [here] + [(VM, s) for s in spectra],
        [(VM, s.shape) for s in spectra],
        [((3, 2, planes, slabs, tile, LANES), F32), ((3, 2, nz, tile, LANES), F32)],
        micros=6.0,
    )
    each = len(spectra) // len(chunks)
    parts = []
    for n, width in enumerate(widths):
        part = exchange(spectra[n * each : (n + 1) * each], "gz")
        shapes = sent_shapes("gx", rows, width)
        part = call(
            functools.partial(x_back_kernel, len(shapes)),
            [here, (VM, x_back[0]), (VM, x_back[1])] + [(VM, p) for p in part],
            [(VM, shape) for shape in shapes],
            [((slabs, block, width), F32), ((pencils, rows, width), F32)],
        )
        parts.append(exchange(part, "gx"))
    plane = (3, cols, ny)
    tables = [(VM, y_back[0]), (VM, y_back[1])]
    size = 2 * len(chunks[0])
    edges, first, last = call(
        functools.partial(edge_kernel, chunks[0]),
        [here] + tables + [(VM, p) for p in parts[0]],
        [(HB, (3, size, rows, ny)), (VM, plane), (VM, plane)],
        [((pencils, rows, widths[0]), F32), ((3, size, rows, ny), F32)],
        sems=1,
    )
    after = lax.ppermute(first, "gz", ring("gz", -1))
    before = lax.ppermute(last, "gz", ring("gz", 1))
    return tuple(
        call(
            functools.partial(stretch_kernel, chunks),
            [here]
            + tables
            + [(HB, edges), (VM, before), (VM, after)]
            + [(HB, mesh) for mesh in meshes]
            + [(VM, rim) for rim in rims]
            + [(VM, p) for p in parts[1]],
            [(HB, ambient.shape), (HB, ambient.shape)],
            [
                ((pencils, rows, widths[1]), F32),
                ((3, planes, cols + 2 * RIM, ny), F32),
                ((3, planes, cols, ny), F32),
            ],
            sems=4 * planes,
            micros=4.0,
        )
    )


def solution(mesh):
    placed = (
        P(None, ("gz", "gx")),
        P(None, ("gz", "gx")),
        P(("gz", "gx")),
        P("gz", "gx", None),
        P(None, "gz", "gx", None),
    )
    return jax.shard_map(
        on_device,
        mesh=mesh,
        in_specs=placed,
        out_specs=(P(None, "gz", "gx", None), P(None, "gz", "gx", None)),
        check_vma=False,
    )
```

```python
import functools
import math

import jax
import jax.numpy as jnp
import ml_dtypes
import numpy as np
from jax import lax
from jax.experimental import pallas as pl
from jax.experimental.pallas import tpu as pltpu
from jax.sharding import PartitionSpec as P

MIG = 64
LANES = 128
RIM = 8
TIME_STEP = 0.25
VMEM = 24 * 1024 * 1024
F32 = jnp.float32
BF16 = jnp.bfloat16


def split_table(table):
    high = table.astype(np.float32).astype(ml_dtypes.bfloat16)
    low = (table - high.astype(np.float64)).astype(np.float32).astype(ml_dtypes.bfloat16)
    return high, low


def angles(rows, columns, extent):
    return 2.0 * np.pi * (np.multiply.outer(rows, columns) % extent) / extent


def y_tables(ny, pencils, scale):
    modes = ny // (2 * pencils)
    position = np.arange(ny)
    angle = angles(position, np.arange(ny // 2), ny)
    real, imag = np.cos(angle), -np.sin(angle)
    imag[:, 0] = 1.0 - 2.0 * (position % 2)
    weight = np.where(np.arange(ny // 2) == 0, 1.0, 2.0) * scale
    ahead = np.zeros((2, ny, pencils, 2, 2, modes))
    back = np.zeros((pencils, 2, 2, modes, 2, ny))
    for parity in range(2):
        for part, values in enumerate((real, imag)):
            ahead[parity, :, :, part, parity] = values.reshape(ny, pencils, modes)
            back[:, part, parity, :, parity] = (values * weight).T.reshape(pencils, modes, ny)
    return ahead.reshape(2 * ny, -1), back.reshape(-1, 2 * ny)


def wave_order(nx, slabs):
    half = nx // 2
    ahead = np.arange(half).reshape(slabs, 1, half // slabs)
    behind = np.where(ahead == 0, half, (nx - ahead) % nx)
    return np.concatenate([ahead, behind], axis=1).reshape(-1)


def x_tables(nx, cols, pencils, slabs):
    order = wave_order(nx, slabs)
    angle = angles(order, np.arange(nx), nx)
    ahead = np.concatenate([np.cos(angle), np.sin(angle)], axis=0)
    row = np.arange(cols + RIM)
    offset = np.where(row <= cols, row, -1)
    used = ((row <= cols) | (row == cols + RIM - 1)).astype(np.float64)
    place = (np.arange(pencils)[:, None] * cols + offset[None, :]) % nx
    angle = angles(place.reshape(-1), order, nx)
    mask = np.tile(used, pencils)[:, None]
    back = np.concatenate([np.cos(angle) * mask, np.sin(angle) * mask], axis=0)
    return ahead, back


def split(values):
    high = values.astype(BF16)
    return high, (values - high.astype(F32)).astype(BF16)


def dot(left, right):
    return jnp.dot(left, right, preferred_element_type=F32)


def table_left(high, low, values):
    v_high, v_low = split(values)
    return dot(high, v_high) + (dot(high, v_low) + dot(low, v_high))


def table_right(values, high, low):
    v_high, v_low = split(values)
    return dot(v_high, high) + (dot(v_low, high) + dot(v_high, low))


def lane_of():
    return lax.broadcasted_iota(jnp.int32, (1, LANES), 1)


def times_i(values):
    half = LANES // 2
    sign = jnp.where(lane_of() < half, -1.0, 1.0).astype(F32)
    return pltpu.roll(values, half, 1) * sign


def kernel_weight(distance):
    radius = jnp.abs(distance)
    near = 1.0 - 2.5 * radius * radius + 1.5 * radius * radius * radius
    far = 0.5 * (2.0 - radius) * (2.0 - radius) * (1.0 - radius)
    return jnp.where(radius < 1.0, near, jnp.where(radius < 2.0, far, 0.0))


def turned(value, wave, extent, sign):
    wave = wave % extent
    real, imag = value
    if wave == 0:
        return value
    if 2 * wave == extent:
        return -real, -imag
    if 4 * wave == extent:
        return (-imag, real) if sign > 0 else (imag, -real)
    if 4 * wave == 3 * extent:
        return (imag, -real) if sign > 0 else (-imag, real)
    a = math.cos(2.0 * math.pi * wave / extent)
    b = sign * math.sin(2.0 * math.pi * wave / extent)
    return real * a - imag * b, real * b + imag * a


def fft(values, sign):
    count = len(values)
    if count == 1:
        return values
    even, odd = fft(values[::2], sign), fft(values[1::2], sign)
    odd = [turned(v, k, count, sign) for k, v in enumerate(odd)]
    plus = [(a[0] + b[0], a[1] + b[1]) for a, b in zip(even, odd)]
    minus = [(a[0] - b[0], a[1] - b[1]) for a, b in zip(even, odd)]
    return plus + minus


def offset_order(count):
    if count < 4:
        return list(range(count))
    far, near = list(range(count // 2, count)), list(range(1, count // 2))
    order = [0, far.pop(0)]
    while far or near:
        order += far[:1] + near[:1]
        far, near = far[1:], near[1:]
    return order


def blocks_of(refs, at):
    if len(refs) == 1:
        return [(d, refs[0].at[d]) for d in range(refs[0].shape[0])]
    return [(at ^ k, ref) for k, ref in zip(offset_order(len(refs)), refs)]


def gather_blocks(refs, held, at):
    for d, ref in blocks_of(refs, at):
        held[d] = ref[...]


def packet_kernel(
    counts, strength, offsets, cells, packet, movers, near_counts, near_cells, sems
):
    copies = [
        pltpu.make_async_copy(counts, near_counts, sems.at[0]),
        pltpu.make_async_copy(cells, near_cells, sems.at[1]),
        pltpu.make_async_copy(strength, packet.at[pl.ds(0, 3)], sems.at[2]),
        pltpu.make_async_copy(offsets, packet.at[pl.ds(3, 3)], sems.at[3]),
    ]
    for copy in copies:
        copy.start()
    for copy in copies:
        copy.wait()
    slot = lax.broadcasted_iota(jnp.int32, (1, packet.shape[1]), 1)
    up = near_counts[0:1, 0:1]
    both = up + near_counts[0:1, 1:2]
    packet[6:7] = near_cells[...].astype(F32)
    packet[7:8] = jnp.where(slot < up, 1.0, jnp.where(slot < both, -1.0, 0.0))
    movers[...] = packet[:, : movers.shape[1]]


def deposit_kernel(
    pairs, rims_before, place, own, up1, down1, up2, down2, ambient, t_high, t_low, *refs
):
    rims, refs = refs[:rims_before], refs[rims_before:]
    mesh, rim_high, rim_low = refs[:3]
    total, made = refs[-2:]
    outs = refs[3:-2]
    _, planes, cols, ny = ambient.shape
    rows = cols + RIM
    movers = up2.shape[1]
    count = own.shape[1]
    listed = [2 * pair + parity for pair in pairs for parity in range(2)]

    def decode(ref, start, stop, shift):
        packet = ref[:, start:stop]
        cell = packet[6:7].astype(jnp.int32)
        move = packet[7:8].astype(jnp.int32)
        z_cell = lax.div(cell, cols * ny) + planes * (move + shift)
        x_cell = lax.rem(lax.div(cell, ny), cols)
        return packet[0:6], z_cell, x_cell, lax.rem(cell, ny)

    def joined(pieces):
        return [jnp.concatenate(p, axis=1) if len(p) > 1 else p[0] for p in zip(*pieces)]

    def add_block(pieces, wanted):
        values, z_cell, x_cell, y_cell = joined(pieces)
        width = values.shape[1]
        z_at = lax.broadcasted_iota(jnp.int32, (planes, width), 0)
        w_z = kernel_weight((z_at - z_cell).astype(F32) - values[3:4])
        row = lax.broadcasted_iota(jnp.int32, (rows, width), 0)
        x_at = jnp.where(row < cols + 2, row, jnp.where(row >= rows - 2, row - rows, 4 * rows))
        w_x = kernel_weight((x_at - x_cell).astype(F32) - values[4:5])
        y_at = lax.broadcasted_iota(jnp.int32, (ny, width), 0)
        y_off = lax.rem(y_at - y_cell + (ny + ny // 2), ny) - ny // 2
        w_y = kernel_weight(y_off.astype(F32) - values[5:6])
        y_high, y_low = split(w_y)
        right = jnp.concatenate([y_high, y_high, y_low], axis=1)
        at = [listed.index(z) for z in wanted]
        for c in range(3):
            s_z = values[c : c + 1] * w_z
            left = jnp.concatenate([s_z[z : z + 1] * w_x for z in wanted], axis=0)
            l_high, l_low = split(left)
            left = jnp.concatenate([l_high, l_low, l_high], axis=1)
            added = lax.dot_general(
                left, right, (((1,), (1,)), ((), ())), preferred_element_type=F32
            )
            total[c, at[0] : at[-1] + 1] += added.reshape(len(wanted), rows, ny)

    for n, z in enumerate(listed):
        total[:, n, 0:cols] = ambient[:, z]
    total[:, :, cols:rows] = jnp.zeros((3, len(listed), RIM, ny), F32)
    step = 256
    for at in range(0, count, step):
        add_block([decode(own, at, min(at + step, count), 0)], listed)
    add_block([decode(up1, 0, movers, 1), decode(down1, 0, movers, -1)], listed)
    sides = ((up1, up2, 1, (planes - 2, planes - 1)), (down1, down2, -1, (0, 1)))
    for near, far, shift, wanted in sides:
        if not set(wanted) <= set(listed):
            continue
        whole = [decode(near, movers, count, shift), decode(far, 0, movers, 2 * shift)]
        values, z_cell, x_cell, y_cell = joined(whole)
        for at in range(0, count, step):
            to = min(at + step, count)
            block = (values[:, at:to], z_cell[:, at:to], x_cell[:, at:to], y_cell[:, at:to])
            add_block([block], wanted)

    mesh[...] = total[:, :, 0:cols]
    at = 0
    if rims:
        at = rims[0].shape[0]
        rim_high[0:at] = rims[0][...]
        rim_low[0:at] = rims[1][...]
    for n in range(3 * len(listed)):
        c, i = n // len(listed), n % len(listed)
        rim_high[at + 2 * n : at + 2 * n + 2] = total[c, i, cols : cols + 2]
        rim_low[at + 2 * n : at + 2 * n + 2] = total[c, i, rows - 2 : rows]
    groups = [(c, 2 * n) for c in range(3) for n in range(len(pairs))]
    left = jnp.concatenate(
        [jnp.concatenate([total[c, n], total[c, n + 1]], axis=1) for c, n in groups], axis=0
    )
    wide = table_right(left, t_high[...], t_low[...])
    for n in range(len(groups)):
        for g in range(made.shape[0]):
            made[g, :, n * LANES : (n + 1) * LANES] = wide[
                n * rows : (n + 1) * rows, g * LANES : (g + 1) * LANES
            ]
    for d, out in blocks_of(outs, place[1]):
        out[...] = made[d]


def x_ahead_kernel(sends, place, t_high, t_low, *refs):
    held, made = refs[-2:]
    outs, parts = refs[-2 - sends : -2], refs[: -2 - sends]
    gather_blocks(parts, held, place[1])
    pencils, rows, width = held.shape
    cols = rows - RIM
    row = lax.broadcasted_iota(jnp.int32, (RIM, width), 0)
    pieces = []
    for h in range(pencils):
        from_low = held[(h - 1) % pencils, cols:rows]
        from_high = held[(h + 1) % pencils, cols:rows]
        pieces.append(held[h, 0:RIM] + jnp.where(row < 2, from_low, 0.0))
        pieces.append(held[h, RIM : cols - RIM])
        pieces.append(held[h, cols - RIM : cols] + jnp.where(row >= RIM - 2, from_high, 0.0))
    both = table_left(t_high[...], t_low[...], jnp.concatenate(pieces, axis=0))
    half = both.shape[0] // 2
    for n in range(width // LANES):
        lanes = slice(n * LANES, (n + 1) * LANES)
        value = both[:half, lanes] - times_i(both[half:, lanes])
        made[:, :, lanes] = value.reshape(made.shape[0], made.shape[1], LANES)
    for d, out in blocks_of(outs, place[0]):
        out[...] = made[d]


def x_back_kernel(sends, place, t_high, t_low, *refs):
    held, made = refs[-2:]
    outs, parts = refs[-2 - sends : -2], refs[: -2 - sends]
    gather_blocks(parts, held, place[0])
    pencils, rows, width = made.shape
    both = table_left(t_high[...], t_low[...], held[...].reshape(-1, width))
    half = both.shape[0] // 2
    for n in range(width // LANES):
        lanes = slice(n * LANES, (n + 1) * LANES)
        value = both[:half, lanes] + times_i(both[half:, lanes])
        made[:, :, lanes] = value.reshape(pencils, rows, LANES)
    for d, out in blocks_of(outs, place[1]):
        out[...] = made[d]


def wave_lanes():
    lane = lane_of()
    return lane < LANES // 2, (lane // (LANES // 4)) % 2 == 0


def roll(values, shift):
    return pltpu.roll(values, shift, 1)


def cross_half(a, b):
    low, _ = wave_lanes()
    half = LANES // 2
    return jnp.where(low, a, roll(b, half)), jnp.where(low, roll(a, half), b)


def cross_quarter(a, b):
    _, first = wave_lanes()
    quarter = LANES // 4
    return (
        jnp.where(first, a, roll(b, quarter)),
        jnp.where(first, roll(a, LANES - quarter), b),
    )


def lanes_at(c, count, i):
    return pl.ds(pl.multiple_of((c * count + i) * LANES, LANES), LANES)


def enter_kernel(pairs, nz, place, *refs):
    parts, data = refs[:-1], refs[-1]
    _, _, _, slabs, tile, _ = data.shape

    def body(c, carry):
        for i, pair in enumerate(pairs):
            lanes = lanes_at(c, len(pairs), i)
            for s, ref in blocks_of(parts, place[0]):
                quad = [ref[q * tile : (q + 1) * tile, lanes] for q in range(4)]
                real0, imag0 = cross_half(quad[0], quad[2])
                real1, imag1 = cross_half(quad[1], quad[3])
                for part, (a, b) in enumerate(((real0, real1), (imag0, imag1))):
                    even, odd = cross_quarter(a, b)
                    data[c, part, 2 * i, s] = even
                    data[c, part, 2 * i + 1, s] = odd
            for parity in range(2):
                at = 2 * i + parity
                line = [(data[c, 0, at, s], data[c, 1, at, s]) for s in range(slabs)]
                for k, v in enumerate(fft(line, -1.0)):
                    v = turned(v, (2 * pair + parity) * k, nz, -1.0)
                    data[c, 0, at, k], data[c, 1, at, k] = v
        return carry

    lax.fori_loop(0, 3, body, 0)


def leave_kernel(pairs, nz, place, source, *refs):
    outs, data = refs[:-1], refs[-1]
    _, _, _, slabs, tile, _ = source.shape

    def body(c, carry):
        for i, pair in enumerate(pairs):
            lanes = lanes_at(c, len(pairs), i)
            for parity in range(2):
                at = 2 * i + parity
                line = [
                    turned(
                        (source[c, 0, at, k], source[c, 1, at, k]),
                        (2 * pair + parity) * k,
                        nz,
                        1.0,
                    )
                    for k in range(slabs)
                ]
                for s, v in enumerate(fft(line, 1.0)):
                    data[c, 0, at, s], data[c, 1, at, s] = v
            for s, ref in blocks_of(outs, place[0]):
                real0, real1 = cross_quarter(data[c, 0, 2 * i, s], data[c, 0, 2 * i + 1, s])
                imag0, imag1 = cross_quarter(data[c, 1, 2 * i, s], data[c, 1, 2 * i + 1, s])
                quad = [None] * 4
                quad[0], quad[2] = cross_half(real0, imag0)
                quad[1], quad[3] = cross_half(real1, imag1)
                for q in range(4):
                    ref[q * tile : (q + 1) * tile, lanes] = quad[q]
        return carry

    lax.fori_loop(0, 3, body, 0)


def curl_kernel(chunks, nx, ny, place, low_rim, high_rim, *refs):
    sources, outs = refs[: len(chunks)], refs[len(chunks) : 2 * len(chunks)]
    spectrum = refs[-1]
    _, _, nz, tile, _ = spectrum.shape
    slabs = sources[0].shape[3]
    planes = nz // slabs
    modes, half = LANES // 4, LANES // 2
    slab_at, pencil_at = place[0], place[1]
    spot = {}
    for n, chunk in enumerate(chunks):
        for i, pair in enumerate(chunk):
            spot[2 * pair], spot[2 * pair + 1] = (n, 2 * i), (n, 2 * i + 1)

    def across_planes(k, carry):
        for c in range(3):
            line = []
            for l in range(planes):
                n, i = spot[l]
                line.append((sources[n][c, 0, i, k], sources[n][c, 1, i, k]))
            for n, v in enumerate(fft(line, -1.0)):
                spectrum[c, 0, k + slabs * n], spectrum[c, 1, k + slabs * n] = v
        return carry

    reach = 2 * tile
    row = lax.broadcasted_iota(jnp.int32, (tile, LANES), 0)
    lane = lax.broadcasted_iota(jnp.int32, (tile, LANES), 1)
    number = slab_at * reach + (lane // modes) % 2 * tile + row
    ahead = lane < half
    mode = lane % modes + pencil_at * modes
    alone = number == 0
    number = number.astype(F32) * (2.0 * math.pi / nx)
    x_base = jnp.where(ahead, number, jnp.where(alone, math.pi, -number))
    x_trim = jnp.where(ahead, number, jnp.where(alone, 0.0, -number))
    wave_y = mode.astype(F32) * (2.0 * math.pi / ny)
    packed = mode == 0
    x_sq = x_base * x_base
    lateral = x_sq + wave_y * wave_y

    def curl_at(k, with_mirror):
        z_wave = jnp.where(k < nz // 2, k, k - nz).astype(F32) * (2.0 * math.pi / nz)
        z_trim = jnp.where(k == nz // 2, 0.0, z_wave)
        full = lateral + z_wave * z_wave
        empty = full == 0.0
        inverse = jnp.where(empty, 0.0, 1.0 / jnp.where(empty, 1.0, full))
        if with_mirror:
            other = 1.0 / (x_sq + (z_wave * z_wave + math.pi * math.pi))
            mirror = jnp.where(packed, 0.5 * (inverse - other), 0.0)
            inverse = jnp.where(packed, 0.5 * (inverse + other), inverse)
            opposite = lax.rem(nz - k, nz)
        stream = []
        for c in range(3):
            value = [spectrum[c, part, k] * inverse for part in range(2)]
            if with_mirror:
                for part, sign in enumerate((1.0, -1.0)):
                    there = spectrum[c, part, opposite]
                    there = jnp.where(alone, there, roll(there, half))
                    value[part] = value[part] + (mirror * sign) * there
            stream.append(value)
        made = []
        for part in range(2):
            s = [value[part] for value in stream]
            made.append(
                (
                    x_trim * s[2] - wave_y * s[1],
                    wave_y * s[0] - z_trim * s[2],
                    z_trim * s[1] - x_trim * s[0],
                )
            )
        return [(-made[1][c], made[0][c]) for c in range(3)]

    def curl_all(with_mirror):
        def body(k, carry):
            made = [curl_at(k + slabs * n, with_mirror) for n in range(planes)]
            for c in range(3):
                for l, v in enumerate(fft([m[c] for m in made], 1.0)):
                    n, i = spot[l]
                    outs[n][c, 0, i, k], outs[n][c, 1, i, k] = v
            return carry

        lax.fori_loop(0, slabs, body, 0)

    lax.fori_loop(0, slabs, across_planes, 0)

    @pl.when(pencil_at == 0)
    def _():
        curl_all(True)

    @pl.when(pencil_at != 0)
    def _():
        curl_all(False)


def planes_of(held, pairs, t_high, t_low):
    pencils, rows, _ = held.shape
    ny = t_high.shape[1] // 2
    groups = [(c, pair) for c in range(3) for pair in pairs]
    left = jnp.concatenate(
        [
            jnp.concatenate(
                [held[h, :, n * LANES : (n + 1) * LANES] for h in range(pencils)], axis=1
            )
            for n in range(len(groups))
        ],
        axis=0,
    )
    wide = table_right(left, t_high[...], t_low[...])
    made = {}
    for n, (c, pair) in enumerate(groups):
        for parity in range(2):
            made[c, 2 * pair + parity] = wide[
                n * rows : (n + 1) * rows, parity * ny : (parity + 1) * ny
            ]
    return made


def hold(tall, c, n, value):
    rows = value.shape[0]
    tall[c, n, RIM : RIM + rows] = value
    tall[c, n, 0:RIM] = value[rows - RIM : rows]


def edge_kernel(pairs, place, t_high, t_low, *refs):
    tall, first, last, held = refs[-4:]
    gather_blocks(refs[:-4], held, place[1])
    listed = [2 * pair + parity for pair in pairs for parity in range(2)]
    cols = first.shape[1]
    values = planes_of(held, pairs, t_high, t_low)
    for c in range(3):
        for n, z in enumerate(listed):
            hold(tall, c, n, values[c, z])
        first[c] = values[c, listed[0]][0:cols]
        last[c] = values[c, listed[-1]][0:cols]


def stretch_kernel(
    chunks, place, t_high, t_low, edges, before, after, low_rim, high_rim, *refs
):
    meshes, refs = refs[:2], refs[2:]
    velocity, vorticity, held, inner, omega, sems = refs[-6:]
    _, planes, cols, ny = velocity.shape
    spot = {}
    for n, chunk in enumerate(chunks):
        for i, pair in enumerate(chunk):
            spot[2 * pair], spot[2 * pair + 1] = (n, 2 * i), (n, 2 * i + 1)
    talls = (edges, inner)
    sent = []

    def send(source, target):
        sent.append(pltpu.make_async_copy(source, target, sems.at[len(sent)]))
        sent[-1].start()

    def send_velocity(z):
        n, i = spot[z]
        send(talls[n].at[:, i, pl.ds(RIM, cols)], velocity.at[:, z])

    def rows_of(c, z, start=RIM):
        n, i = spot[z]
        return talls[n][c, i, start : start + cols]

    for z in range(planes):
        if spot[z][0] == 0:
            send_velocity(z)
    gather_blocks(refs[:-6], held, place[1])
    for (c, z), value in planes_of(held, chunks[1], t_high, t_low).items():
        hold(inner, c, spot[z][1], value)
    for z in range(planes):
        if spot[z][0] == 1:
            send_velocity(z)
    rim_at = 0
    for which, mesh in enumerate(meshes):
        size = mesh.shape[1]
        for z in range(planes):
            n, i = spot[z]
            if n != which:
                continue
            for c in range(3):
                at = rim_at + 2 * (c * size + i)
                omega[c, z] = mesh[c, i]
                omega[c, z, 0:2] += low_rim[at : at + 2]
                omega[c, z, cols - 2 : cols] += high_rim[at : at + 2]
            omega_z = [omega[c, z] for c in range(3)]
            for c in range(3):
                value = rows_of(c, z)
                above = rows_of(c, z + 1) if z + 1 < planes else after[c]
                below = rows_of(c, z - 1) if z > 0 else before[c]
                along_z = (above - below) * 0.5
                along_x = (rows_of(c, z, RIM + 1) - rows_of(c, z, RIM - 1)) * 0.5
                along_y = (pltpu.roll(value, ny - 1, 1) - pltpu.roll(value, 1, 1)) * 0.5
                stretch = omega_z[0] * along_z + omega_z[1] * along_x + omega_z[2] * along_y
                omega[c, z] = omega_z[c] + TIME_STEP * stretch
            send(omega.at[:, z], vorticity.at[:, z])
        rim_at += 6 * size
    for copy in sent:
        copy.wait()


VM = pl.BlockSpec(memory_space=pltpu.VMEM)
SM = pl.BlockSpec(memory_space=pltpu.SMEM)
AN = pl.BlockSpec(memory_space=pl.ANY)


def call(kernel, ins, outs, scratch=(), sems=0, micros=2.0, vmem=VMEM):
    extra = [pltpu.SemaphoreType.DMA((sems,))] if sems else []
    return pl.pallas_call(
        kernel,
        out_shape=[jax.ShapeDtypeStruct(shape, F32) for _, shape in outs],
        in_specs=[spec for spec, _ in ins],
        out_specs=[spec for spec, _ in outs],
        scratch_shapes=[pltpu.VMEM(shape, kind) for shape, kind in scratch] + extra,
        compiler_params=pltpu.CompilerParams(vmem_limit_bytes=vmem),
        cost_estimate=pl.CostEstimate(
            flops=int(micros * 1.0e9), bytes_accessed=int(micros * 3.0e6), transcendentals=0
        ),
    )(*[value for _, value in ins])


def ring(axis, step):
    count = lax.axis_size(axis)
    return [(i, (i + step) % count) for i in range(count)]


def spread(axis):
    count = lax.axis_size(axis)
    return count <= 8 and count & (count - 1) == 0


def sent_shapes(axis, rows, width, whole=False):
    count = lax.axis_size(axis)
    return [(count, rows, width)] if whole or not spread(axis) else [(rows, width)] * count


def exchange(blocks, axis):
    if len(blocks) == 1:
        return [lax.all_to_all(blocks[0], axis, split_axis=0, concat_axis=0, tiled=True)]
    count = lax.axis_size(axis)
    order = offset_order(count)
    return [blocks[0]] + [
        lax.ppermute(block, axis, [(i, i ^ k) for i in range(count)])
        for k, block in zip(order[1:], blocks[1:])
    ]


def on_device(strength, offsets, cell_index, migrate_count, ambient):
    _, planes, cols, ny = ambient.shape
    slabs, pencils = lax.axis_size("gz"), lax.axis_size("gx")
    nx, nz, rows = cols * pencils, planes * slabs, cols + RIM
    count = strength.shape[1]
    pair_count = planes // 2
    chunks = ((0, pair_count - 1), tuple(range(1, pair_count - 1)))
    widths = [3 * len(c) * LANES for c in chunks]
    block = nx // slabs

    y_ahead, y_back = [split_table(t) for t in y_tables(ny, pencils, 1.0 / (float(nx) * ny * nz))]
    x_ahead, x_back = [split_table(t) for t in x_tables(nx, cols, pencils, slabs)]
    place = jnp.stack([lax.axis_index("gz"), lax.axis_index("gx")]).astype(jnp.int32)
    here = (SM, place)

    packet, movers = call(
        packet_kernel,
        [
            (AN, migrate_count.reshape(1, 2)),
            (AN, strength),
            (AN, offsets),
            (AN, cell_index.reshape(1, count)),
        ],
        [(VM, (8, count)), (VM, (8, 2 * MIG))],
        [((1, 2), jnp.int32), ((1, count), jnp.int32)],
        sems=4,
        micros=1.0,
        vmem=63 * 1024 * 1024,
    )
    up1 = lax.ppermute(packet, "gz", ring("gz", -1))
    down1 = lax.ppermute(packet, "gz", ring("gz", 1))
    up2 = lax.ppermute(movers, "gz", ring("gz", -2))
    down2 = lax.ppermute(movers, "gz", ring("gz", 2))

    meshes, rims, parts = [], [], []
    for chunk, width in zip(chunks, widths):
        size = 2 * len(chunk)
        rim = (6 * size + (rims[0].shape[0] if rims else 0), ny)
        mesh, rim_high, rim_low, *part = call(
            functools.partial(deposit_kernel, chunk, len(rims)),
            [here]
            + [(VM, value) for value in (packet, up1, down1, up2, down2)]
            + [(VM, ambient), (VM, y_ahead[0]), (VM, y_ahead[1])]
            + [(VM, value) for value in rims],
            [(VM, (3, size, cols, ny)), (VM, rim), (VM, rim)]
            + [(VM, shape) for shape in sent_shapes("gx", rows, width)],
            [((3, size, rows, ny), F32), ((pencils, rows, width), F32)],
            micros=5.0,
        )
        meshes.append(mesh)
        rims = [rim_high, rim_low]
        parts.append(exchange(part, "gx"))
    low_rim = lax.ppermute(rims[0], "gx", ring("gx", 1))
    high_rim = lax.ppermute(rims[1], "gx", ring("gx", -1))

    tile = max(1, block // 4)
    data = []
    for chunk, part, width in zip(chunks, parts, widths):
        shapes = sent_shapes("gz", block, width)
        part = call(
            functools.partial(x_ahead_kernel, len(shapes)),
            [here, (VM, x_ahead[0]), (VM, x_ahead[1])] + [(VM, p) for p in part],
            [(VM, shape) for shape in shapes],
            [((pencils, rows, width), F32), ((slabs, block, width), F32)],
        )
        (entered,) = call(
            functools.partial(enter_kernel, chunk, nz),
            [here] + [(VM, p) for p in exchange(part, "gz")],
            [(VM, (3, 2, 2 * len(chunk), slabs, tile, LANES))],
        )
        data.append(entered)
    data = call(
        functools.partial(curl_kernel, chunks, nx, ny),
        [here, (VM, low_rim), (VM, high_rim)] + [(VM, d) for d in data],
        [(VM, d.shape) for d in data],
        [((3, 2, nz, tile, LANES), F32)],
        micros=5.0,
    )
    parts = []
    for chunk, source, width in zip(chunks, data, widths):
        part = call(
            functools.partial(leave_kernel, chunk, nz),
            [here, (VM, source)],
            [(VM, shape) for shape in sent_shapes("gz", block, width)],
            [(source.shape, F32)],
        )
        part = exchange(part, "gz")
        shapes = sent_shapes("gx", rows, width, whole=not parts)
        part = call(
            functools.partial(x_back_kernel, len(shapes)),
            [here, (VM, x_back[0]), (VM, x_back[1])] + [(VM, p) for p in part],
            [(VM, shape) for shape in shapes],
            [((slabs, block, width), F32), ((pencils, rows, width), F32)],
        )
        parts.append(exchange(part, "gx"))
    plane = (3, cols, ny)
    tables = [(VM, y_back[0]), (VM, y_back[1])]
    tall = [(3, 2 * len(chunk), cols + 2 * RIM, ny) for chunk in chunks]
    edges, first, last = call(
        functools.partial(edge_kernel, chunks[0]),
        [here] + tables + [(VM, p) for p in parts[0]],
        [(VM, tall[0]), (VM, plane), (VM, plane)],
        [((pencils, rows, widths[0]), F32)],
    )
    after = lax.ppermute(first, "gz", ring("gz", -1))
    before = lax.ppermute(last, "gz", ring("gz", 1))
    return tuple(
        call(
            functools.partial(stretch_kernel, chunks),
            [here]
            + tables
            + [(VM, v) for v in (edges, before, after, low_rim, high_rim, *meshes)]
            + [(VM, p) for p in parts[1]],
            [(AN, ambient.shape), (AN, ambient.shape)],
            [
                ((pencils, rows, widths[1]), F32),
                (tall[1], F32),
                ((3, planes, cols, ny), F32),
            ],
            sems=2 * planes,
            micros=4.0,
        )
    )


def solution(mesh):
    placed = (
        P(None, ("gz", "gx")),
        P(None, ("gz", "gx")),
        P(("gz", "gx")),
        P("gz", "gx", None),
        P(None, "gz", "gx", None),
    )
    return jax.shard_map(
        on_device,
        mesh=mesh,
        in_specs=placed,
        out_specs=(P(None, "gz", "gx", None), P(None, "gz", "gx", None)),
        check_vma=False,
    )
```

```python
import functools
import math

import jax
import jax.numpy as jnp
import ml_dtypes
import numpy as np
from jax import lax
from jax.experimental import pallas as pl
from jax.experimental.pallas import tpu as pltpu
from jax.sharding import PartitionSpec as P

MIG = 64
LANES = 128
RIM = 8
TIME_STEP = 0.25
VMEM = 24 * 1024 * 1024
F32 = jnp.float32
BF16 = jnp.bfloat16


def split_table(table):
    high = table.astype(np.float32).astype(ml_dtypes.bfloat16)
    low = (table - high.astype(np.float64)).astype(np.float32).astype(ml_dtypes.bfloat16)
    return high, low


def angles(rows, columns, extent):
    return 2.0 * np.pi * (np.multiply.outer(rows, columns) % extent) / extent


def y_tables(ny, pencils, scale):
    modes = ny // (2 * pencils)
    position = np.arange(ny)
    angle = angles(position, np.arange(ny // 2), ny)
    real, imag = np.cos(angle), -np.sin(angle)
    imag[:, 0] = 1.0 - 2.0 * (position % 2)
    weight = np.where(np.arange(ny // 2) == 0, 1.0, 2.0) * scale
    ahead = np.zeros((2, ny, pencils, 2, 2, modes))
    back = np.zeros((pencils, 2, 2, modes, 2, ny))
    for parity in range(2):
        for part, values in enumerate((real, imag)):
            ahead[parity, :, :, part, parity] = values.reshape(ny, pencils, modes)
            back[:, part, parity, :, parity] = (values * weight).T.reshape(pencils, modes, ny)
    return ahead.reshape(2 * ny, -1), back.reshape(-1, 2 * ny)


def wave_order(nx, slabs):
    half = nx // 2
    ahead = np.arange(half).reshape(slabs, 1, half // slabs)
    behind = np.where(ahead == 0, half, (nx - ahead) % nx)
    return np.concatenate([ahead, behind], axis=1).reshape(-1)


def x_tables(nx, cols, pencils, slabs):
    order = wave_order(nx, slabs)
    angle = angles(order, np.arange(nx), nx)
    ahead = np.concatenate([np.cos(angle), np.sin(angle)], axis=0)
    row = np.arange(cols + RIM)
    offset = np.where(row <= cols, row, -1)
    used = ((row <= cols) | (row == cols + RIM - 1)).astype(np.float64)
    place = (np.arange(pencils)[:, None] * cols + offset[None, :]) % nx
    angle = angles(place.reshape(-1), order, nx)
    mask = np.tile(used, pencils)[:, None]
    back = np.concatenate([np.cos(angle) * mask, np.sin(angle) * mask], axis=0)
    return ahead, back


def split(values):
    high = values.astype(BF16)
    return high, (values - high.astype(F32)).astype(BF16)


def dot(left, right):
    return jnp.dot(left, right, preferred_element_type=F32)


def table_left(high, low, values):
    v_high, v_low = split(values)
    return dot(high, v_high) + (dot(high, v_low) + dot(low, v_high))


def table_right(values, high, low):
    v_high, v_low = split(values)
    return dot(v_high, high) + (dot(v_low, high) + dot(v_high, low))


def lane_of():
    return lax.broadcasted_iota(jnp.int32, (1, LANES), 1)


def times_i(values):
    half = LANES // 2
    sign = jnp.where(lane_of() < half, -1.0, 1.0).astype(F32)
    return pltpu.roll(values, half, 1) * sign


def kernel_weight(distance):
    radius = jnp.abs(distance)
    near = 1.0 - 2.5 * radius * radius + 1.5 * radius * radius * radius
    far = 0.5 * (2.0 - radius) * (2.0 - radius) * (1.0 - radius)
    return jnp.where(radius < 1.0, near, jnp.where(radius < 2.0, far, 0.0))


def turned(value, wave, extent, sign):
    wave = wave % extent
    real, imag = value
    if wave == 0:
        return value
    if 2 * wave == extent:
        return -real, -imag
    if 4 * wave == extent:
        return (-imag, real) if sign > 0 else (imag, -real)
    if 4 * wave == 3 * extent:
        return (imag, -real) if sign > 0 else (-imag, real)
    a = math.cos(2.0 * math.pi * wave / extent)
    b = sign * math.sin(2.0 * math.pi * wave / extent)
    return real * a - imag * b, real * b + imag * a


def fft(values, sign):
    count = len(values)
    if count == 1:
        return values
    even, odd = fft(values[::2], sign), fft(values[1::2], sign)
    odd = [turned(v, k, count, sign) for k, v in enumerate(odd)]
    plus = [(a[0] + b[0], a[1] + b[1]) for a, b in zip(even, odd)]
    minus = [(a[0] - b[0], a[1] - b[1]) for a, b in zip(even, odd)]
    return plus + minus


def offset_order(count):
    if count < 4:
        return list(range(count))
    far, near = list(range(count // 2, count)), list(range(1, count // 2))
    order = [0, far.pop(0)]
    while far or near:
        order += far[:1] + near[:1]
        far, near = far[1:], near[1:]
    return order


def blocks_of(refs, at):
    if len(refs) == 1:
        return [(d, refs[0].at[d]) for d in range(refs[0].shape[0])]
    return [(at ^ k, ref) for k, ref in zip(offset_order(len(refs)), refs)]


def gather_blocks(refs, held, at):
    for d, ref in blocks_of(refs, at):
        held[d] = ref[...]


def packet_kernel(
    counts, strength, offsets, cells, packet, movers, near_counts, near_cells, sems
):
    copies = [
        pltpu.make_async_copy(counts, near_counts, sems.at[0]),
        pltpu.make_async_copy(cells, near_cells, sems.at[1]),
        pltpu.make_async_copy(strength, packet.at[pl.ds(0, 3)], sems.at[2]),
        pltpu.make_async_copy(offsets, packet.at[pl.ds(3, 3)], sems.at[3]),
    ]
    for copy in copies:
        copy.start()
    for copy in copies:
        copy.wait()
    slot = lax.broadcasted_iota(jnp.int32, (1, packet.shape[1]), 1)
    up = near_counts[0:1, 0:1]
    both = up + near_counts[0:1, 1:2]
    packet[6:7] = near_cells[...].astype(F32)
    packet[7:8] = jnp.where(slot < up, 1.0, jnp.where(slot < both, -1.0, 0.0))
    movers[...] = packet[:, : movers.shape[1]]


def deposit_kernel(
    pairs, rims_before, place, own, up1, down1, up2, down2, ambient, t_high, t_low, *refs
):
    rims, refs = refs[:rims_before], refs[rims_before:]
    mesh, rim_high, rim_low = refs[:3]
    total, made = refs[-2:]
    outs = refs[3:-2]
    _, planes, cols, ny = ambient.shape
    rows = cols + RIM
    movers = up2.shape[1]
    count = own.shape[1]
    listed = [2 * pair + parity for pair in pairs for parity in range(2)]

    def decode(ref, start, stop, shift):
        packet = ref[:, start:stop]
        cell = packet[6:7].astype(jnp.int32)
        move = packet[7:8].astype(jnp.int32)
        z_cell = lax.div(cell, cols * ny) + planes * (move + shift)
        x_cell = lax.rem(lax.div(cell, ny), cols)
        return packet[0:6], z_cell, x_cell, lax.rem(cell, ny)

    def joined(pieces):
        return [jnp.concatenate(p, axis=1) if len(p) > 1 else p[0] for p in zip(*pieces)]

    def add_block(pieces, wanted):
        values, z_cell, x_cell, y_cell = joined(pieces)
        width = values.shape[1]
        z_at = lax.broadcasted_iota(jnp.int32, (planes, width), 0)
        w_z = kernel_weight((z_at - z_cell).astype(F32) - values[3:4])
        row = lax.broadcasted_iota(jnp.int32, (rows, width), 0)
        x_at = jnp.where(row < cols + 2, row, jnp.where(row >= rows - 2, row - rows, 4 * rows))
        w_x = kernel_weight((x_at - x_cell).astype(F32) - values[4:5])
        y_at = lax.broadcasted_iota(jnp.int32, (ny, width), 0)
        y_off = lax.rem(y_at - y_cell + (ny + ny // 2), ny) - ny // 2
        w_y = kernel_weight(y_off.astype(F32) - values[5:6])
        y_high, y_low = split(w_y)
        right = jnp.concatenate([y_high, y_high, y_low], axis=1)
        at = [listed.index(z) for z in wanted]
        for c in range(3):
            s_z = values[c : c + 1] * w_z
            left = jnp.concatenate([s_z[z : z + 1] * w_x for z in wanted], axis=0)
            l_high, l_low = split(left)
            left = jnp.concatenate([l_high, l_low, l_high], axis=1)
            added = lax.dot_general(
                left, right, (((1,), (1,)), ((), ())), preferred_element_type=F32
            )
            total[c, at[0] : at[-1] + 1] += added.reshape(len(wanted), rows, ny)

    for n, z in enumerate(listed):
        total[:, n, 0:cols] = ambient[:, z]
    total[:, :, cols:rows] = jnp.zeros((3, len(listed), RIM, ny), F32)
    step = 256
    for at in range(0, count, step):
        add_block([decode(own, at, min(at + step, count), 0)], listed)
    add_block([decode(up1, 0, movers, 1), decode(down1, 0, movers, -1)], listed)
    sides = ((up1, up2, 1, (planes - 2, planes - 1)), (down1, down2, -1, (0, 1)))
    for near, far, shift, wanted in sides:
        if not set(wanted) <= set(listed):
            continue
        whole = [decode(near, movers, count, shift), decode(far, 0, movers, 2 * shift)]
        values, z_cell, x_cell, y_cell = joined(whole)
        for at in range(0, count, step):
            to = min(at + step, count)
            block = (values[:, at:to], z_cell[:, at:to], x_cell[:, at:to], y_cell[:, at:to])
            add_block([block], wanted)

    mesh[...] = total[:, :, 0:cols]
    at = 0
    if rims:
        at = rims[0].shape[0]
        rim_high[0:at] = rims[0][...]
        rim_low[0:at] = rims[1][...]
    for n in range(3 * len(listed)):
        c, i = n // len(listed), n % len(listed)
        rim_high[at + 2 * n : at + 2 * n + 2] = total[c, i, cols : cols + 2]
        rim_low[at + 2 * n : at + 2 * n + 2] = total[c, i, rows - 2 : rows]
    groups = [(c, 2 * n) for c in range(3) for n in range(len(pairs))]
    left = jnp.concatenate(
        [jnp.concatenate([total[c, n], total[c, n + 1]], axis=1) for c, n in groups], axis=0
    )
    wide = table_right(left, t_high[...], t_low[...])
    for n in range(len(groups)):
        for g in range(made.shape[0]):
            made[g, :, n * LANES : (n + 1) * LANES] = wide[
                n * rows : (n + 1) * rows, g * LANES : (g + 1) * LANES
            ]
    for d, out in blocks_of(outs, place[1]):
        out[...] = made[d]


def x_ahead_kernel(sends, place, t_high, t_low, *refs):
    held, made = refs[-2:]
    outs, parts = refs[-2 - sends : -2], refs[: -2 - sends]
    gather_blocks(parts, held, place[1])
    pencils, rows, width = held.shape
    cols = rows - RIM
    row = lax.broadcasted_iota(jnp.int32, (RIM, width), 0)
    pieces = []
    for h in range(pencils):
        from_low = held[(h - 1) % pencils, cols:rows]
        from_high = held[(h + 1) % pencils, cols:rows]
        pieces.append(held[h, 0:RIM] + jnp.where(row < 2, from_low, 0.0))
        pieces.append(held[h, RIM : cols - RIM])
        pieces.append(held[h, cols - RIM : cols] + jnp.where(row >= RIM - 2, from_high, 0.0))
    both = table_left(t_high[...], t_low[...], jnp.concatenate(pieces, axis=0))
    half = both.shape[0] // 2
    for n in range(width // LANES):
        lanes = slice(n * LANES, (n + 1) * LANES)
        value = both[:half, lanes] - times_i(both[half:, lanes])
        made[:, :, lanes] = value.reshape(made.shape[0], made.shape[1], LANES)
    for d, out in blocks_of(outs, place[0]):
        out[...] = made[d]


def x_back_kernel(sends, place, last_left, t_high, t_low, *refs):
    held, made = refs[-2:]
    outs, parts = refs[-2 - sends : -2], refs[: -2 - sends]
    gather_blocks(parts, held, place[0])
    pencils, rows, width = made.shape
    both = table_left(t_high[...], t_low[...], held[...].reshape(-1, width))
    half = both.shape[0] // 2
    for n in range(width // LANES):
        lanes = slice(n * LANES, (n + 1) * LANES)
        value = both[:half, lanes] + times_i(both[half:, lanes])
        made[:, :, lanes] = value.reshape(pencils, rows, LANES)
    for d, out in blocks_of(outs, place[1]):
        out[...] = made[d]


def wave_lanes():
    lane = lane_of()
    return lane < LANES // 2, (lane // (LANES // 4)) % 2 == 0


def roll(values, shift):
    return pltpu.roll(values, shift, 1)


def cross_half(a, b):
    low, _ = wave_lanes()
    half = LANES // 2
    return jnp.where(low, a, roll(b, half)), jnp.where(low, roll(a, half), b)


def cross_quarter(a, b):
    _, first = wave_lanes()
    quarter = LANES // 4
    return (
        jnp.where(first, a, roll(b, quarter)),
        jnp.where(first, roll(a, LANES - quarter), b),
    )


def lanes_at(c, count, i):
    return pl.ds(pl.multiple_of((c * count + i) * LANES, LANES), LANES)


def enter_kernel(pairs, nz, place, *refs):
    parts, data = refs[:-1], refs[-1]
    _, _, _, slabs, tile, _ = data.shape

    def body(c, carry):
        for i, pair in enumerate(pairs):
            lanes = lanes_at(c, len(pairs), i)
            for s, ref in blocks_of(parts, place[0]):
                quad = [ref[q * tile : (q + 1) * tile, lanes] for q in range(4)]
                real0, imag0 = cross_half(quad[0], quad[2])
                real1, imag1 = cross_half(quad[1], quad[3])
                for part, (a, b) in enumerate(((real0, real1), (imag0, imag1))):
                    even, odd = cross_quarter(a, b)
                    data[c, part, 2 * i, s] = even
                    data[c, part, 2 * i + 1, s] = odd
            for parity in range(2):
                at = 2 * i + parity
                line = [(data[c, 0, at, s], data[c, 1, at, s]) for s in range(slabs)]
                for k, v in enumerate(fft(line, -1.0)):
                    v = turned(v, (2 * pair + parity) * k, nz, -1.0)
                    data[c, 0, at, k], data[c, 1, at, k] = v
        return carry

    lax.fori_loop(0, 3, body, 0)


def leave_kernel(pairs, nz, place, source, *refs):
    outs, data = refs[:-1], refs[-1]
    _, _, _, slabs, tile, _ = source.shape

    def body(c, carry):
        for i, pair in enumerate(pairs):
            lanes = lanes_at(c, len(pairs), i)
            for parity in range(2):
                at = 2 * i + parity
                line = [
                    turned(
                        (source[c, 0, at, k], source[c, 1, at, k]),
                        (2 * pair + parity) * k,
                        nz,
                        1.0,
                    )
                    for k in range(slabs)
                ]
                for s, v in enumerate(fft(line, 1.0)):
                    data[c, 0, at, s], data[c, 1, at, s] = v
            for s, ref in blocks_of(outs, place[0]):
                real0, real1 = cross_quarter(data[c, 0, 2 * i, s], data[c, 0, 2 * i + 1, s])
                imag0, imag1 = cross_quarter(data[c, 1, 2 * i, s], data[c, 1, 2 * i + 1, s])
                quad = [None] * 4
                quad[0], quad[2] = cross_half(real0, imag0)
                quad[1], quad[3] = cross_half(real1, imag1)
                for q in range(4):
                    ref[q * tile : (q + 1) * tile, lanes] = quad[q]
        return carry

    lax.fori_loop(0, 3, body, 0)


def curl_kernel(chunks, nx, ny, place, low_rim, high_rim, *refs):
    sources, outs = refs[: len(chunks)], refs[len(chunks) : 2 * len(chunks)]
    spectrum = refs[-1]
    _, _, nz, tile, _ = spectrum.shape
    slabs = sources[0].shape[3]
    planes = nz // slabs
    modes, half = LANES // 4, LANES // 2
    slab_at, pencil_at = place[0], place[1]
    spot = {}
    for n, chunk in enumerate(chunks):
        for i, pair in enumerate(chunk):
            spot[2 * pair], spot[2 * pair + 1] = (n, 2 * i), (n, 2 * i + 1)

    def across_planes(k, carry):
        for c in range(3):
            line = []
            for l in range(planes):
                n, i = spot[l]
                line.append((sources[n][c, 0, i, k], sources[n][c, 1, i, k]))
            for n, v in enumerate(fft(line, -1.0)):
                spectrum[c, 0, k + slabs * n], spectrum[c, 1, k + slabs * n] = v
        return carry

    reach = 2 * tile
    row = lax.broadcasted_iota(jnp.int32, (tile, LANES), 0)
    lane = lax.broadcasted_iota(jnp.int32, (tile, LANES), 1)
    number = slab_at * reach + (lane // modes) % 2 * tile + row
    ahead = lane < half
    mode = lane % modes + pencil_at * modes
    alone = number == 0
    number = number.astype(F32) * (2.0 * math.pi / nx)
    x_base = jnp.where(ahead, number, jnp.where(alone, math.pi, -number))
    x_trim = jnp.where(ahead, number, jnp.where(alone, 0.0, -number))
    wave_y = mode.astype(F32) * (2.0 * math.pi / ny)
    packed = mode == 0
    x_sq = x_base * x_base
    lateral = x_sq + wave_y * wave_y

    def curl_at(k, with_mirror):
        z_wave = jnp.where(k < nz // 2, k, k - nz).astype(F32) * (2.0 * math.pi / nz)
        z_trim = jnp.where(k == nz // 2, 0.0, z_wave)
        full = lateral + z_wave * z_wave
        empty = full == 0.0
        inverse = jnp.where(empty, 0.0, 1.0 / jnp.where(empty, 1.0, full))
        if with_mirror:
            other = 1.0 / (x_sq + (z_wave * z_wave + math.pi * math.pi))
            mirror = jnp.where(packed, 0.5 * (inverse - other), 0.0)
            inverse = jnp.where(packed, 0.5 * (inverse + other), inverse)
            opposite = lax.rem(nz - k, nz)
        stream = []
        for c in range(3):
            value = [spectrum[c, part, k] * inverse for part in range(2)]
            if with_mirror:
                for part, sign in enumerate((1.0, -1.0)):
                    there = spectrum[c, part, opposite]
                    there = jnp.where(alone, there, roll(there, half))
                    value[part] = value[part] + (mirror * sign) * there
            stream.append(value)
        made = []
        for part in range(2):
            s = [value[part] for value in stream]
            made.append(
                (
                    x_trim * s[2] - wave_y * s[1],
                    wave_y * s[0] - z_trim * s[2],
                    z_trim * s[1] - x_trim * s[0],
                )
            )
        return [(-made[1][c], made[0][c]) for c in range(3)]

    def curl_all(with_mirror):
        def body(k, carry):
            made = [curl_at(k + slabs * n, with_mirror) for n in range(planes)]
            for c in range(3):
                for l, v in enumerate(fft([m[c] for m in made], 1.0)):
                    n, i = spot[l]
                    outs[n][c, 0, i, k], outs[n][c, 1, i, k] = v
            return carry

        lax.fori_loop(0, slabs, body, 0)

    lax.fori_loop(0, slabs, across_planes, 0)

    @pl.when(pencil_at == 0)
    def _():
        curl_all(True)

    @pl.when(pencil_at != 0)
    def _():
        curl_all(False)


def planes_of(held, pairs, t_high, t_low):
    pencils, rows, _ = held.shape
    ny = t_high.shape[1] // 2
    groups = [(c, pair) for c in range(3) for pair in pairs]
    left = jnp.concatenate(
        [
            jnp.concatenate(
                [held[h, :, n * LANES : (n + 1) * LANES] for h in range(pencils)], axis=1
            )
            for n in range(len(groups))
        ],
        axis=0,
    )
    wide = table_right(left, t_high[...], t_low[...])
    made = {}
    for n, (c, pair) in enumerate(groups):
        for parity in range(2):
            made[c, 2 * pair + parity] = wide[
                n * rows : (n + 1) * rows, parity * ny : (parity + 1) * ny
            ]
    return made


def hold(tall, c, n, value):
    rows = value.shape[0]
    tall[c, n, RIM : RIM + rows] = value
    tall[c, n, 0:RIM] = value[rows - RIM : rows]


def edge_kernel(pairs, place, t_high, t_low, *refs):
    tall, first, last, held = refs[-4:]
    gather_blocks(refs[:-4], held, place[1])
    listed = [2 * pair + parity for pair in pairs for parity in range(2)]
    cols = first.shape[1]
    values = planes_of(held, pairs, t_high, t_low)
    for c in range(3):
        for n, z in enumerate(listed):
            hold(tall, c, n, values[c, z])
        first[c] = values[c, listed[0]][0:cols]
        last[c] = values[c, listed[-1]][0:cols]


def stretch_kernel(
    chunks, place, t_high, t_low, edges, before, after, low_rim, high_rim, *refs
):
    meshes, refs = refs[:2], refs[2:]
    velocity, vorticity, held, inner, omega, sems = refs[-6:]
    _, planes, cols, ny = velocity.shape
    spot = {}
    for n, chunk in enumerate(chunks):
        for i, pair in enumerate(chunk):
            spot[2 * pair], spot[2 * pair + 1] = (n, 2 * i), (n, 2 * i + 1)
    talls = (edges, inner)
    sent = []

    def send(source, target):
        sent.append(pltpu.make_async_copy(source, target, sems.at[len(sent)]))
        sent[-1].start()

    def send_velocity(z):
        n, i = spot[z]
        send(talls[n].at[:, i, pl.ds(RIM, cols)], velocity.at[:, z])

    def rows_of(c, z, start=RIM):
        n, i = spot[z]
        return talls[n][c, i, start : start + cols]

    for z in range(planes):
        if spot[z][0] == 0:
            send_velocity(z)
    gather_blocks(refs[:-6], held, place[1])
    for (c, z), value in planes_of(held, chunks[1], t_high, t_low).items():
        hold(inner, c, spot[z][1], value)
    for z in range(planes):
        if spot[z][0] == 1:
            send_velocity(z)
    rim_at = 0
    for which, mesh in enumerate(meshes):
        size = mesh.shape[1]
        for z in range(planes):
            n, i = spot[z]
            if n != which:
                continue
            for c in range(3):
                at = rim_at + 2 * (c * size + i)
                omega[c, z] = mesh[c, i]
                omega[c, z, 0:2] += low_rim[at : at + 2]
                omega[c, z, cols - 2 : cols] += high_rim[at : at + 2]
            omega_z = [omega[c, z] for c in range(3)]
            for c in range(3):
                value = rows_of(c, z)
                above = rows_of(c, z + 1) if z + 1 < planes else after[c]
                below = rows_of(c, z - 1) if z > 0 else before[c]
                along_z = (above - below) * 0.5
                along_x = (rows_of(c, z, RIM + 1) - rows_of(c, z, RIM - 1)) * 0.5
                along_y = (pltpu.roll(value, ny - 1, 1) - pltpu.roll(value, 1, 1)) * 0.5
                stretch = omega_z[0] * along_z + omega_z[1] * along_x + omega_z[2] * along_y
                omega[c, z] = omega_z[c] + TIME_STEP * stretch
            send(omega.at[:, z], vorticity.at[:, z])
        rim_at += 6 * size
    for copy in sent:
        copy.wait()


VM = pl.BlockSpec(memory_space=pltpu.VMEM)
SM = pl.BlockSpec(memory_space=pltpu.SMEM)
AN = pl.BlockSpec(memory_space=pl.ANY)


def call(kernel, ins, outs, scratch=(), sems=0, micros=2.0, moved=None):
    extra = [pltpu.SemaphoreType.DMA((sems,))] if sems else []
    return pl.pallas_call(
        kernel,
        out_shape=[jax.ShapeDtypeStruct(shape, F32) for _, shape in outs],
        in_specs=[spec for spec, _ in ins],
        out_specs=[spec for spec, _ in outs],
        scratch_shapes=[pltpu.VMEM(shape, kind) for shape, kind in scratch] + extra,
        compiler_params=pltpu.CompilerParams(vmem_limit_bytes=VMEM),
        cost_estimate=pl.CostEstimate(
            flops=int(micros * 1.0e9),
            bytes_accessed=int(micros * 3.0e6) if moved is None else moved,
            transcendentals=0,
        ),
    )(*[value for _, value in ins])


def ring(axis, step):
    count = lax.axis_size(axis)
    return [(i, (i + step) % count) for i in range(count)]


def spread(axis):
    count = lax.axis_size(axis)
    return count <= 8 and count & (count - 1) == 0


def sent_shapes(axis, rows, width, whole=False):
    count = lax.axis_size(axis)
    return [(count, rows, width)] if whole or not spread(axis) else [(rows, width)] * count


def exchange(blocks, axis):
    if len(blocks) == 1:
        return [lax.all_to_all(blocks[0], axis, split_axis=0, concat_axis=0, tiled=True)]
    count = lax.axis_size(axis)
    order = offset_order(count)
    return [blocks[0]] + [
        lax.ppermute(block, axis, [(i, i ^ k) for i in range(count)])
        for k, block in zip(order[1:], blocks[1:])
    ]


def on_device(strength, offsets, cell_index, migrate_count, ambient):
    _, planes, cols, ny = ambient.shape
    slabs, pencils = lax.axis_size("gz"), lax.axis_size("gx")
    nx, nz, rows = cols * pencils, planes * slabs, cols + RIM
    count = strength.shape[1]
    pair_count = planes // 2
    chunks = ((0, pair_count - 1), tuple(range(1, pair_count - 1)))
    widths = [3 * len(c) * LANES for c in chunks]
    block = nx // slabs

    y_ahead, y_back = [split_table(t) for t in y_tables(ny, pencils, 1.0 / (float(nx) * ny * nz))]
    x_ahead, x_back = [split_table(t) for t in x_tables(nx, cols, pencils, slabs)]
    place = jnp.stack([lax.axis_index("gz"), lax.axis_index("gx")]).astype(jnp.int32)
    here = (SM, place)

    packet, movers = call(
        packet_kernel,
        [
            (AN, migrate_count.reshape(1, 2)),
            (AN, strength),
            (AN, offsets),
            (AN, cell_index.reshape(1, count)),
        ],
        [(VM, (8, count)), (VM, (8, 2 * MIG))],
        [((1, 2), jnp.int32), ((1, count), jnp.int32)],
        sems=4,
        micros=1.0,
        moved=1000,
    )
    up1 = lax.ppermute(packet, "gz", ring("gz", -1))
    down1 = lax.ppermute(packet, "gz", ring("gz", 1))
    up2 = lax.ppermute(movers, "gz", ring("gz", -2))
    down2 = lax.ppermute(movers, "gz", ring("gz", 2))

    meshes, rims, parts = [], [], []
    for chunk, width in zip(chunks, widths):
        size = 2 * len(chunk)
        rim = (6 * size + (rims[0].shape[0] if rims else 0), ny)
        mesh, rim_high, rim_low, *part = call(
            functools.partial(deposit_kernel, chunk, len(rims)),
            [here]
            + [(VM, value) for value in (packet, up1, down1, up2, down2)]
            + [(VM, ambient), (VM, y_ahead[0]), (VM, y_ahead[1])]
            + [(VM, value) for value in rims],
            [(VM, (3, size, cols, ny)), (VM, rim), (VM, rim)]
            + [(VM, shape) for shape in sent_shapes("gx", rows, width)],
            [((3, size, rows, ny), F32), ((pencils, rows, width), F32)],
            micros=5.0,
        )
        meshes.append(mesh)
        rims = [rim_high, rim_low]
        parts.append(exchange(part, "gx"))
    low_rim = lax.ppermute(rims[0], "gx", ring("gx", 1))
    high_rim = lax.ppermute(rims[1], "gx", ring("gx", -1))

    tile = max(1, block // 4)
    data = []
    for chunk, part, width in zip(chunks, parts, widths):
        shapes = sent_shapes("gz", block, width)
        part = call(
            functools.partial(x_ahead_kernel, len(shapes)),
            [here, (VM, x_ahead[0]), (VM, x_ahead[1])] + [(VM, p) for p in part],
            [(VM, shape) for shape in shapes],
            [((pencils, rows, width), F32), ((slabs, block, width), F32)],
        )
        (entered,) = call(
            functools.partial(enter_kernel, chunk, nz),
            [here] + [(VM, p) for p in exchange(part, "gz")],
            [(VM, (3, 2, 2 * len(chunk), slabs, tile, LANES))],
        )
        data.append(entered)
    data = call(
        functools.partial(curl_kernel, chunks, nx, ny),
        [here, (VM, low_rim), (VM, high_rim)] + [(VM, d) for d in data],
        [(VM, d.shape) for d in data],
        [((3, 2, nz, tile, LANES), F32)],
        micros=5.0,
    )
    left = [
        call(
            functools.partial(leave_kernel, chunk, nz),
            [here, (VM, source)],
            [(VM, shape) for shape in sent_shapes("gz", block, width)],
            [(source.shape, F32)],
        )
        for chunk, source, width in zip(chunks, data, widths)
    ]
    parts = []
    for part, width in zip(left, widths):
        part = exchange(part, "gz")
        shapes = sent_shapes("gx", rows, width, whole=not parts)
        part = call(
            functools.partial(x_back_kernel, len(shapes)),
            [here, (AN, left[-1][0]), (VM, x_back[0]), (VM, x_back[1])] + [(VM, p) for p in part],
            [(VM, shape) for shape in shapes],
            [((slabs, block, width), F32), ((pencils, rows, width), F32)],
        )
        parts.append(exchange(part, "gx"))
    plane = (3, cols, ny)
    tables = [(VM, y_back[0]), (VM, y_back[1])]
    tall = [(3, 2 * len(chunk), cols + 2 * RIM, ny) for chunk in chunks]
    edges, first, last = call(
        functools.partial(edge_kernel, chunks[0]),
        [here] + tables + [(VM, p) for p in parts[0]],
        [(VM, tall[0]), (VM, plane), (VM, plane)],
        [((pencils, rows, widths[0]), F32)],
    )
    after = lax.ppermute(first, "gz", ring("gz", -1))
    before = lax.ppermute(last, "gz", ring("gz", 1))
    return tuple(
        call(
            functools.partial(stretch_kernel, chunks),
            [here]
            + tables
            + [(VM, v) for v in (edges, before, after, low_rim, high_rim, *meshes)]
            + [(VM, p) for p in parts[1]],
            [(AN, ambient.shape), (AN, ambient.shape)],
            [
                ((pencils, rows, widths[1]), F32),
                (tall[1], F32),
                ((3, planes, cols, ny), F32),
            ],
            sems=2 * planes,
            micros=4.0,
        )
    )


def solution(mesh):
    placed = (
        P(None, ("gz", "gx")),
        P(None, ("gz", "gx")),
        P(("gz", "gx")),
        P("gz", "gx", None),
        P(None, "gz", "gx", None),
    )
    return jax.shard_map(
        on_device,
        mesh=mesh,
        in_specs=placed,
        out_specs=(P(None, "gz", "gx", None), P(None, "gz", "gx", None)),
        check_vma=False,
    )
```

```python
import functools
import math

import jax
import jax.numpy as jnp
import ml_dtypes
import numpy as np
from jax import lax
from jax.experimental import pallas as pl
from jax.experimental.pallas import tpu as pltpu
from jax.sharding import PartitionSpec as P

MIG = 64
LANES = 128
RIM = 8
TIME_STEP = 0.25
VMEM = 24 * 1024 * 1024
F32 = jnp.float32
BF16 = jnp.bfloat16


def split_table(table):
    high = table.astype(np.float32).astype(ml_dtypes.bfloat16)
    low = (table - high.astype(np.float64)).astype(np.float32).astype(ml_dtypes.bfloat16)
    return high, low


def angles(rows, columns, extent):
    return 2.0 * np.pi * (np.multiply.outer(rows, columns) % extent) / extent


def y_tables(ny, pencils, scale):
    modes = ny // (2 * pencils)
    position = np.arange(ny)
    angle = angles(position, np.arange(ny // 2), ny)
    real, imag = np.cos(angle), -np.sin(angle)
    imag[:, 0] = 1.0 - 2.0 * (position % 2)
    weight = np.where(np.arange(ny // 2) == 0, 1.0, 2.0) * scale
    ahead = np.zeros((2, ny, pencils, 2, 2, modes))
    back = np.zeros((pencils, 2, 2, modes, 2, ny))
    for parity in range(2):
        for part, values in enumerate((real, imag)):
            ahead[parity, :, :, part, parity] = values.reshape(ny, pencils, modes)
            back[:, part, parity, :, parity] = (values * weight).T.reshape(pencils, modes, ny)
    return ahead.reshape(2 * ny, -1), back.reshape(-1, 2 * ny)


def wave_order(nx, slabs):
    half = nx // 2
    ahead = np.arange(half).reshape(slabs, 1, half // slabs)
    behind = np.where(ahead == 0, half, (nx - ahead) % nx)
    return np.concatenate([ahead, behind], axis=1).reshape(-1)


def x_tables(nx, cols, pencils, slabs):
    order = wave_order(nx, slabs)
    angle = angles(order, np.arange(nx), nx)
    ahead = np.concatenate([np.cos(angle), np.sin(angle)], axis=0)
    row = np.arange(cols + RIM)
    offset = np.where(row <= cols, row, -1)
    used = ((row <= cols) | (row == cols + RIM - 1)).astype(np.float64)
    place = (np.arange(pencils)[:, None] * cols + offset[None, :]) % nx
    angle = angles(place.reshape(-1), order, nx)
    mask = np.tile(used, pencils)[:, None]
    back = np.concatenate([np.cos(angle) * mask, np.sin(angle) * mask], axis=0)
    return ahead, back


def split(values):
    high = values.astype(BF16)
    return high, (values - high.astype(F32)).astype(BF16)


def dot(left, right):
    return jnp.dot(left, right, preferred_element_type=F32)


def table_left(high, low, values):
    v_high, v_low = split(values)
    return dot(high, v_high) + (dot(high, v_low) + dot(low, v_high))


def table_right(values, high, low):
    v_high, v_low = split(values)
    return dot(v_high, high) + (dot(v_low, high) + dot(v_high, low))


def lane_of():
    return lax.broadcasted_iota(jnp.int32, (1, LANES), 1)


def times_i(values):
    half = LANES // 2
    sign = jnp.where(lane_of() < half, -1.0, 1.0).astype(F32)
    return pltpu.roll(values, half, 1) * sign


def kernel_weight(distance):
    radius = jnp.abs(distance)
    near = 1.0 - 2.5 * radius * radius + 1.5 * radius * radius * radius
    far = 0.5 * (2.0 - radius) * (2.0 - radius) * (1.0 - radius)
    return jnp.where(radius < 1.0, near, jnp.where(radius < 2.0, far, 0.0))


def turned(value, wave, extent, sign):
    wave = wave % extent
    real, imag = value
    if wave == 0:
        return value
    if 2 * wave == extent:
        return -real, -imag
    if 4 * wave == extent:
        return (-imag, real) if sign > 0 else (imag, -real)
    if 4 * wave == 3 * extent:
        return (imag, -real) if sign > 0 else (-imag, real)
    a = math.cos(2.0 * math.pi * wave / extent)
    b = sign * math.sin(2.0 * math.pi * wave / extent)
    return real * a - imag * b, real * b + imag * a


def fft(values, sign):
    count = len(values)
    if count == 1:
        return values
    even, odd = fft(values[::2], sign), fft(values[1::2], sign)
    odd = [turned(v, k, count, sign) for k, v in enumerate(odd)]
    plus = [(a[0] + b[0], a[1] + b[1]) for a, b in zip(even, odd)]
    minus = [(a[0] - b[0], a[1] - b[1]) for a, b in zip(even, odd)]
    return plus + minus


def offset_order(count):
    if count < 4:
        return list(range(count))
    far, near = list(range(count // 2, count)), list(range(1, count // 2))
    order = [0, far.pop(0)]
    while far or near:
        order += far[:1] + near[:1]
        far, near = far[1:], near[1:]
    return order


def blocks_of(refs, at):
    if len(refs) == 1:
        return [(d, refs[0].at[d]) for d in range(refs[0].shape[0])]
    return [(at ^ k, ref) for k, ref in zip(offset_order(len(refs)), refs)]


def gather_blocks(refs, held, at):
    for d, ref in blocks_of(refs, at):
        held[d] = ref[...]


def packet_kernel(
    counts, strength, offsets, cells, packet, movers, near_counts, near_cells, sems
):
    copies = [
        pltpu.make_async_copy(counts, near_counts, sems.at[0]),
        pltpu.make_async_copy(cells, near_cells, sems.at[1]),
        pltpu.make_async_copy(strength, packet.at[pl.ds(0, 3)], sems.at[2]),
        pltpu.make_async_copy(offsets, packet.at[pl.ds(3, 3)], sems.at[3]),
    ]
    for copy in copies:
        copy.start()
    for copy in copies:
        copy.wait()
    slot = lax.broadcasted_iota(jnp.int32, (1, packet.shape[1]), 1)
    up = near_counts[0:1, 0:1]
    both = up + near_counts[0:1, 1:2]
    packet[6:7] = near_cells[...].astype(F32)
    packet[7:8] = jnp.where(slot < up, 1.0, jnp.where(slot < both, -1.0, 0.0))
    movers[...] = packet[:, : movers.shape[1]]


def deposit_kernel(
    pairs, rims_before, place, own, up1, down1, up2, down2, ambient, t_high, t_low, *refs
):
    rims, refs = refs[:rims_before], refs[rims_before:]
    mesh, rim_high, rim_low = refs[:3]
    total, made, sems = refs[-3:]
    outs = refs[3:-3]
    _, planes, cols, ny = ambient.shape
    rows = cols + RIM
    movers = up2.shape[1]
    count = own.shape[1]
    listed = [2 * pair + parity for pair in pairs for parity in range(2)]

    def decode(ref, start, stop, shift):
        packet = ref[:, start:stop]
        cell = packet[6:7].astype(jnp.int32)
        move = packet[7:8].astype(jnp.int32)
        z_cell = lax.div(cell, cols * ny) + planes * (move + shift)
        x_cell = lax.rem(lax.div(cell, ny), cols)
        return packet[0:6], z_cell, x_cell, lax.rem(cell, ny)

    def joined(pieces):
        return [jnp.concatenate(p, axis=1) if len(p) > 1 else p[0] for p in zip(*pieces)]

    def add_block(pieces, wanted):
        values, z_cell, x_cell, y_cell = joined(pieces)
        width = values.shape[1]
        z_at = lax.broadcasted_iota(jnp.int32, (planes, width), 0)
        w_z = kernel_weight((z_at - z_cell).astype(F32) - values[3:4])
        row = lax.broadcasted_iota(jnp.int32, (rows, width), 0)
        x_at = jnp.where(row < cols + 2, row, jnp.where(row >= rows - 2, row - rows, 4 * rows))
        w_x = kernel_weight((x_at - x_cell).astype(F32) - values[4:5])
        y_at = lax.broadcasted_iota(jnp.int32, (ny, width), 0)
        y_off = lax.rem(y_at - y_cell + (ny + ny // 2), ny) - ny // 2
        w_y = kernel_weight(y_off.astype(F32) - values[5:6])
        y_high, y_low = split(w_y)
        right = jnp.concatenate([y_high, y_high, y_low], axis=1)
        at = [listed.index(z) for z in wanted]
        for c in range(3):
            s_z = values[c : c + 1] * w_z
            left = jnp.concatenate([s_z[z : z + 1] * w_x for z in wanted], axis=0)
            l_high, l_low = split(left)
            left = jnp.concatenate([l_high, l_low, l_high], axis=1)
            added = lax.dot_general(
                left, right, (((1,), (1,)), ((), ())), preferred_element_type=F32
            )
            total[c, at[0] : at[-1] + 1] += added.reshape(len(wanted), rows, ny)

    for n, z in enumerate(listed):
        total[:, n, 0:cols] = ambient[:, z]
    total[:, :, cols:rows] = jnp.zeros((3, len(listed), RIM, ny), F32)
    step = 256
    for at in range(0, count, step):
        add_block([decode(own, at, min(at + step, count), 0)], listed)
    add_block([decode(up1, 0, movers, 1), decode(down1, 0, movers, -1)], listed)
    sides = ((up1, up2, 1, (planes - 2, planes - 1)), (down1, down2, -1, (0, 1)))
    for near, far, shift, wanted in sides:
        if not set(wanted) <= set(listed):
            continue
        whole = [decode(near, movers, count, shift), decode(far, 0, movers, 2 * shift)]
        values, z_cell, x_cell, y_cell = joined(whole)
        for at in range(0, count, step):
            to = min(at + step, count)
            block = (values[:, at:to], z_cell[:, at:to], x_cell[:, at:to], y_cell[:, at:to])
            add_block([block], wanted)

    keep = pltpu.make_async_copy(total.at[:, :, pl.ds(0, cols)], mesh, sems.at[0])
    keep.start()
    at = 0
    if rims:
        at = rims[0].shape[0]
        rim_high[0:at] = rims[0][...]
        rim_low[0:at] = rims[1][...]
    for n in range(3 * len(listed)):
        c, i = n // len(listed), n % len(listed)
        rim_high[at + 2 * n : at + 2 * n + 2] = total[c, i, cols : cols + 2]
        rim_low[at + 2 * n : at + 2 * n + 2] = total[c, i, rows - 2 : rows]
    groups = [(c, 2 * n) for c in range(3) for n in range(len(pairs))]
    left = jnp.concatenate(
        [jnp.concatenate([total[c, n], total[c, n + 1]], axis=1) for c, n in groups], axis=0
    )
    wide = table_right(left, t_high[...], t_low[...])
    for n in range(len(groups)):
        for g in range(made.shape[0]):
            made[g, :, n * LANES : (n + 1) * LANES] = wide[
                n * rows : (n + 1) * rows, g * LANES : (g + 1) * LANES
            ]
    for d, out in blocks_of(outs, place[1]):
        out[...] = made[d]
    keep.wait()


def x_ahead_kernel(sends, place, t_high, t_low, *refs):
    held, made = refs[-2:]
    outs, parts = refs[-2 - sends : -2], refs[: -2 - sends]
    gather_blocks(parts, held, place[1])
    pencils, rows, width = held.shape
    cols = rows - RIM
    row = lax.broadcasted_iota(jnp.int32, (RIM, width), 0)
    pieces = []
    for h in range(pencils):
        from_low = held[(h - 1) % pencils, cols:rows]
        from_high = held[(h + 1) % pencils, cols:rows]
        pieces.append(held[h, 0:RIM] + jnp.where(row < 2, from_low, 0.0))
        pieces.append(held[h, RIM : cols - RIM])
        pieces.append(held[h, cols - RIM : cols] + jnp.where(row >= RIM - 2, from_high, 0.0))
    both = table_left(t_high[...], t_low[...], jnp.concatenate(pieces, axis=0))
    half = both.shape[0] // 2
    for n in range(width // LANES):
        lanes = slice(n * LANES, (n + 1) * LANES)
        value = both[:half, lanes] - times_i(both[half:, lanes])
        made[:, :, lanes] = value.reshape(made.shape[0], made.shape[1], LANES)
    for d, out in blocks_of(outs, place[0]):
        out[...] = made[d]


def x_back_kernel(sends, tables, place, last_left, *refs):
    held, made = refs[-2:]
    outs, parts = refs[-2 - sends : -2], refs[: -2 - sends]
    gather_blocks(parts, held, place[0])
    pencils, rows, width = made.shape
    both = table_left(*tables(), held[...].reshape(-1, width))
    half = both.shape[0] // 2
    for n in range(width // LANES):
        lanes = slice(n * LANES, (n + 1) * LANES)
        value = both[:half, lanes] + times_i(both[half:, lanes])
        made[:, :, lanes] = value.reshape(pencils, rows, LANES)
    for d, out in blocks_of(outs, place[1]):
        out[...] = made[d]


def wave_lanes():
    lane = lane_of()
    return lane < LANES // 2, (lane // (LANES // 4)) % 2 == 0


def roll(values, shift):
    return pltpu.roll(values, shift, 1)


def cross_half(a, b):
    low, _ = wave_lanes()
    half = LANES // 2
    return jnp.where(low, a, roll(b, half)), jnp.where(low, roll(a, half), b)


def cross_quarter(a, b):
    _, first = wave_lanes()
    quarter = LANES // 4
    return (
        jnp.where(first, a, roll(b, quarter)),
        jnp.where(first, roll(a, LANES - quarter), b),
    )


def lanes_at(c, count, i):
    return pl.ds(pl.multiple_of((c * count + i) * LANES, LANES), LANES)


def enter_kernel(pairs, nz, place, *refs):
    parts, data = refs[:-1], refs[-1]
    _, _, _, slabs, tile, _ = data.shape

    def body(c, carry):
        for i, pair in enumerate(pairs):
            lanes = lanes_at(c, len(pairs), i)
            for s, ref in blocks_of(parts, place[0]):
                quad = [ref[q * tile : (q + 1) * tile, lanes] for q in range(4)]
                real0, imag0 = cross_half(quad[0], quad[2])
                real1, imag1 = cross_half(quad[1], quad[3])
                for part, (a, b) in enumerate(((real0, real1), (imag0, imag1))):
                    even, odd = cross_quarter(a, b)
                    data[c, part, 2 * i, s] = even
                    data[c, part, 2 * i + 1, s] = odd
            for parity in range(2):
                at = 2 * i + parity
                line = [(data[c, 0, at, s], data[c, 1, at, s]) for s in range(slabs)]
                for k, v in enumerate(fft(line, -1.0)):
                    v = turned(v, (2 * pair + parity) * k, nz, -1.0)
                    data[c, 0, at, k], data[c, 1, at, k] = v
        return carry

    lax.fori_loop(0, 3, body, 0)


def leave_kernel(pairs, nz, place, source, *refs):
    outs, data = refs[:-1], refs[-1]
    _, _, _, slabs, tile, _ = source.shape

    def body(c, carry):
        for i, pair in enumerate(pairs):
            lanes = lanes_at(c, len(pairs), i)
            for parity in range(2):
                at = 2 * i + parity
                line = [
                    turned(
                        (source[c, 0, at, k], source[c, 1, at, k]),
                        (2 * pair + parity) * k,
                        nz,
                        1.0,
                    )
                    for k in range(slabs)
                ]
                for s, v in enumerate(fft(line, 1.0)):
                    data[c, 0, at, s], data[c, 1, at, s] = v
            for s, ref in blocks_of(outs, place[0]):
                real0, real1 = cross_quarter(data[c, 0, 2 * i, s], data[c, 0, 2 * i + 1, s])
                imag0, imag1 = cross_quarter(data[c, 1, 2 * i, s], data[c, 1, 2 * i + 1, s])
                quad = [None] * 4
                quad[0], quad[2] = cross_half(real0, imag0)
                quad[1], quad[3] = cross_half(real1, imag1)
                for q in range(4):
                    ref[q * tile : (q + 1) * tile, lanes] = quad[q]
        return carry

    lax.fori_loop(0, 3, body, 0)


def curl_kernel(chunks, nx, ny, place, low_rim, high_rim, *refs):
    sources, outs = refs[: len(chunks)], refs[len(chunks) : 2 * len(chunks)]
    spectrum = refs[-1]
    _, _, nz, tile, _ = spectrum.shape
    slabs = sources[0].shape[3]
    planes = nz // slabs
    modes, half = LANES // 4, LANES // 2
    slab_at, pencil_at = place[0], place[1]
    spot = {}
    for n, chunk in enumerate(chunks):
        for i, pair in enumerate(chunk):
            spot[2 * pair], spot[2 * pair + 1] = (n, 2 * i), (n, 2 * i + 1)

    def across_planes(k, carry):
        for c in range(3):
            line = []
            for l in range(planes):
                n, i = spot[l]
                line.append((sources[n][c, 0, i, k], sources[n][c, 1, i, k]))
            for n, v in enumerate(fft(line, -1.0)):
                spectrum[c, 0, k + slabs * n], spectrum[c, 1, k + slabs * n] = v
        return carry

    reach = 2 * tile
    row = lax.broadcasted_iota(jnp.int32, (tile, LANES), 0)
    lane = lax.broadcasted_iota(jnp.int32, (tile, LANES), 1)
    number = slab_at * reach + (lane // modes) % 2 * tile + row
    ahead = lane < half
    mode = lane % modes + pencil_at * modes
    alone = number == 0
    number = number.astype(F32) * (2.0 * math.pi / nx)
    x_base = jnp.where(ahead, number, jnp.where(alone, math.pi, -number))
    x_trim = jnp.where(ahead, number, jnp.where(alone, 0.0, -number))
    wave_y = mode.astype(F32) * (2.0 * math.pi / ny)
    packed = mode == 0
    x_sq = x_base * x_base
    lateral = x_sq + wave_y * wave_y

    def curl_at(k, with_mirror):
        z_wave = jnp.where(k < nz // 2, k, k - nz).astype(F32) * (2.0 * math.pi / nz)
        z_trim = jnp.where(k == nz // 2, 0.0, z_wave)
        full = lateral + z_wave * z_wave
        empty = full == 0.0
        inverse = jnp.where(empty, 0.0, 1.0 / jnp.where(empty, 1.0, full))
        if with_mirror:
            other = 1.0 / (x_sq + (z_wave * z_wave + math.pi * math.pi))
            mirror = jnp.where(packed, 0.5 * (inverse - other), 0.0)
            inverse = jnp.where(packed, 0.5 * (inverse + other), inverse)
            opposite = lax.rem(nz - k, nz)
        stream = []
        for c in range(3):
            value = [spectrum[c, part, k] * inverse for part in range(2)]
            if with_mirror:
                for part, sign in enumerate((1.0, -1.0)):
                    there = spectrum[c, part, opposite]
                    there = jnp.where(alone, there, roll(there, half))
                    value[part] = value[part] + (mirror * sign) * there
            stream.append(value)
        made = []
        for part in range(2):
            s = [value[part] for value in stream]
            made.append(
                (
                    x_trim * s[2] - wave_y * s[1],
                    wave_y * s[0] - z_trim * s[2],
                    z_trim * s[1] - x_trim * s[0],
                )
            )
        return [(-made[1][c], made[0][c]) for c in range(3)]

    def curl_all(with_mirror):
        def body(k, carry):
            made = [curl_at(k + slabs * n, with_mirror) for n in range(planes)]
            for c in range(3):
                for l, v in enumerate(fft([m[c] for m in made], 1.0)):
                    n, i = spot[l]
                    outs[n][c, 0, i, k], outs[n][c, 1, i, k] = v
            return carry

        lax.fori_loop(0, slabs, body, 0)

    lax.fori_loop(0, slabs, across_planes, 0)

    @pl.when(pencil_at == 0)
    def _():
        curl_all(True)

    @pl.when(pencil_at != 0)
    def _():
        curl_all(False)


def planes_of(held, pairs, tables):
    pencils, rows, _ = held.shape
    groups = [(c, pair) for c in range(3) for pair in pairs]
    left = jnp.concatenate(
        [
            jnp.concatenate(
                [held[h, :, n * LANES : (n + 1) * LANES] for h in range(pencils)], axis=1
            )
            for n in range(len(groups))
        ],
        axis=0,
    )
    t_high, t_low = tables()
    ny = t_high.shape[1] // 2
    wide = table_right(left, t_high, t_low)
    made = {}
    for n, (c, pair) in enumerate(groups):
        for parity in range(2):
            made[c, 2 * pair + parity] = wide[
                n * rows : (n + 1) * rows, parity * ny : (parity + 1) * ny
            ]
    return made


def hold(tall, c, n, value):
    rows = value.shape[0]
    tall[c, n, RIM : RIM + rows] = value
    tall[c, n, 0:RIM] = value[rows - RIM : rows]


def edge_kernel(pairs, tables, place, *refs):
    tall, first, last, held = refs[-4:]
    gather_blocks(refs[:-4], held, place[1])
    listed = [2 * pair + parity for pair in pairs for parity in range(2)]
    cols = first.shape[1]
    values = planes_of(held, pairs, tables)
    for c in range(3):
        for n, z in enumerate(listed):
            hold(tall, c, n, values[c, z])
        first[c] = values[c, listed[0]][0:cols]
        last[c] = values[c, listed[-1]][0:cols]


def stretch_kernel(
    chunks, place, table_high, table_low, edges, before, after, low_rim, high_rim, *refs
):
    meshes, refs = refs[:2], refs[2:]
    velocity, vorticity, held, inner, omega, t_high, t_low, sems = refs[-8:]
    _, planes, cols, ny = velocity.shape
    spot = {}
    for n, chunk in enumerate(chunks):
        for i, pair in enumerate(chunk):
            spot[2 * pair], spot[2 * pair + 1] = (n, 2 * i), (n, 2 * i + 1)
    talls = (edges, inner)
    sent = []
    fetched = {}
    table_copies = [
        pltpu.make_async_copy(table_high, t_high, sems.at[3 * planes]),
        pltpu.make_async_copy(table_low, t_low, sems.at[3 * planes + 1]),
    ]
    for copy in table_copies:
        copy.start()

    def tables():
        for copy in table_copies:
            copy.wait()
        return t_high[...], t_low[...]

    for z in range(planes):
        n, i = spot[z]
        fetched[z] = pltpu.make_async_copy(
            meshes[n].at[:, i], omega.at[:, z], sems.at[2 * planes + z]
        )
        fetched[z].start()

    def send(source, target):
        sent.append(pltpu.make_async_copy(source, target, sems.at[len(sent)]))
        sent[-1].start()

    def send_velocity(z):
        n, i = spot[z]
        send(talls[n].at[:, i, pl.ds(RIM, cols)], velocity.at[:, z])

    def rows_of(c, z, start=RIM):
        n, i = spot[z]
        return talls[n][c, i, start : start + cols]

    for z in range(planes):
        if spot[z][0] == 0:
            send_velocity(z)
    gather_blocks(refs[:-8], held, place[1])
    for (c, z), value in planes_of(held, chunks[1], tables).items():
        hold(inner, c, spot[z][1], value)
    for z in range(planes):
        if spot[z][0] == 1:
            send_velocity(z)
    rim_at = 0
    for which in (1, 0):
        size = meshes[which].shape[1]
        for z in range(planes):
            n, i = spot[z]
            if n != which:
                continue
            fetched[z].wait()
            for c in range(3):
                at = rim_at + 2 * (c * size + i)
                omega[c, z, 0:2] += low_rim[at : at + 2]
                omega[c, z, cols - 2 : cols] += high_rim[at : at + 2]
            omega_z = [omega[c, z] for c in range(3)]
            for c in range(3):
                value = rows_of(c, z)
                above = rows_of(c, z + 1) if z + 1 < planes else after[c]
                below = rows_of(c, z - 1) if z > 0 else before[c]
                along_z = (above - below) * 0.5
                along_x = (rows_of(c, z, RIM + 1) - rows_of(c, z, RIM - 1)) * 0.5
                along_y = (pltpu.roll(value, ny - 1, 1) - pltpu.roll(value, 1, 1)) * 0.5
                stretch = omega_z[0] * along_z + omega_z[1] * along_x + omega_z[2] * along_y
                omega[c, z] = omega_z[c] + TIME_STEP * stretch
            send(omega.at[:, z], vorticity.at[:, z])
        rim_at += 6 * size
    for copy in sent:
        copy.wait()


VM = pl.BlockSpec(memory_space=pltpu.VMEM)
SM = pl.BlockSpec(memory_space=pltpu.SMEM)
AN = pl.BlockSpec(memory_space=pl.ANY)
HB = pl.BlockSpec(memory_space=pltpu.HBM)


def kept(values):
    return pltpu.with_memory_space_constraint(values, pltpu.HBM)


def copied(kernel, count):
    def run(place, *refs):
        tables, refs = refs[:count], refs[count:]
        scratch, sems = refs[-count - 1 : -1], refs[-1]
        copies = [
            pltpu.make_async_copy(source, target, sems.at[n])
            for n, (source, target) in enumerate(zip(tables, scratch))
        ]
        for copy in copies:
            copy.start()

        def ready():
            for copy in copies:
                copy.wait()
            return [target[...] for target in scratch]

        kernel(ready, place, *refs[: -count - 1])

    return run


def call(kernel, ins, outs, scratch=(), sems=0, micros=2.0, moved=None):
    extra = [pltpu.SemaphoreType.DMA((sems,))] if sems else []
    return pl.pallas_call(
        kernel,
        out_shape=[
            pltpu.HBM(shape, F32) if spec is HB else jax.ShapeDtypeStruct(shape, F32)
            for spec, shape in outs
        ],
        in_specs=[spec for spec, _ in ins],
        out_specs=[spec for spec, _ in outs],
        scratch_shapes=[pltpu.VMEM(shape, kind) for shape, kind in scratch] + extra,
        compiler_params=pltpu.CompilerParams(vmem_limit_bytes=VMEM),
        cost_estimate=pl.CostEstimate(
            flops=int(micros * 1.0e9),
            bytes_accessed=int(micros * 3.0e6) if moved is None else moved,
            transcendentals=0,
        ),
    )(*[value for _, value in ins])


def ring(axis, step):
    count = lax.axis_size(axis)
    return [(i, (i + step) % count) for i in range(count)]


def spread(axis):
    count = lax.axis_size(axis)
    return count <= 8 and count & (count - 1) == 0


def sent_shapes(axis, rows, width, whole=False):
    count = lax.axis_size(axis)
    return [(count, rows, width)] if whole or not spread(axis) else [(rows, width)] * count


def exchange(blocks, axis):
    if len(blocks) == 1:
        return [lax.all_to_all(blocks[0], axis, split_axis=0, concat_axis=0, tiled=True)]
    count = lax.axis_size(axis)
    order = offset_order(count)
    return [blocks[0]] + [
        lax.ppermute(block, axis, [(i, i ^ k) for i in range(count)])
        for k, block in zip(order[1:], blocks[1:])
    ]


def on_device(strength, offsets, cell_index, migrate_count, ambient):
    _, planes, cols, ny = ambient.shape
    slabs, pencils = lax.axis_size("gz"), lax.axis_size("gx")
    nx, nz, rows = cols * pencils, planes * slabs, cols + RIM
    count = strength.shape[1]
    pair_count = planes // 2
    chunks = ((0, pair_count - 1), tuple(range(1, pair_count - 1)))
    widths = [3 * len(c) * LANES for c in chunks]
    block = nx // slabs

    y_ahead, y_back = [split_table(t) for t in y_tables(ny, pencils, 1.0 / (float(nx) * ny * nz))]
    x_ahead, x_back = [split_table(t) for t in x_tables(nx, cols, pencils, slabs)]
    place = jnp.stack([lax.axis_index("gz"), lax.axis_index("gx")]).astype(jnp.int32)
    here = (SM, place)

    packet, movers = call(
        packet_kernel,
        [
            (HB, kept(migrate_count.reshape(1, 2))),
            (HB, kept(strength)),
            (HB, kept(offsets)),
            (HB, kept(cell_index.reshape(1, count))),
        ],
        [(VM, (8, count)), (VM, (8, 2 * MIG))],
        [((1, 2), jnp.int32), ((1, count), jnp.int32)],
        sems=4,
        micros=1.0,
        moved=1000,
    )
    up1 = lax.ppermute(packet, "gz", ring("gz", -1))
    down1 = lax.ppermute(packet, "gz", ring("gz", 1))
    up2 = lax.ppermute(movers, "gz", ring("gz", -2))
    down2 = lax.ppermute(movers, "gz", ring("gz", 2))

    meshes, rims, parts = [None, None], [], [None, None]
    for n in (1, 0):
        chunk, width = chunks[n], widths[n]
        size = 2 * len(chunk)
        rim = (6 * size + (rims[0].shape[0] if rims else 0), ny)
        mesh, rim_high, rim_low, *part = call(
            functools.partial(deposit_kernel, chunk, len(rims)),
            [here]
            + [(VM, value) for value in (packet, up1, down1, up2, down2)]
            + [(VM, ambient), (VM, y_ahead[0]), (VM, y_ahead[1])]
            + [(VM, value) for value in rims],
            [(HB, (3, size, cols, ny)), (VM, rim), (VM, rim)]
            + [(VM, shape) for shape in sent_shapes("gx", rows, width)],
            [((3, size, rows, ny), F32), ((pencils, rows, width), F32)],
            sems=1,
            micros=5.0,
        )
        meshes[n] = mesh
        rims = [rim_high, rim_low]
        parts[n] = exchange(part, "gx")
    low_rim = lax.ppermute(rims[0], "gx", ring("gx", 1))
    high_rim = lax.ppermute(rims[1], "gx", ring("gx", -1))

    tile = max(1, block // 4)
    data = [None, None]
    for n in (1, 0):
        chunk, part, width = chunks[n], parts[n], widths[n]
        shapes = sent_shapes("gz", block, width)
        part = call(
            functools.partial(x_ahead_kernel, len(shapes)),
            [here, (VM, x_ahead[0]), (VM, x_ahead[1])] + [(VM, p) for p in part],
            [(VM, shape) for shape in shapes],
            [((pencils, rows, width), F32), ((slabs, block, width), F32)],
        )
        (entered,) = call(
            functools.partial(enter_kernel, chunk, nz),
            [here] + [(VM, p) for p in exchange(part, "gz")],
            [(VM, (3, 2, 2 * len(chunk), slabs, tile, LANES))],
        )
        data[n] = entered
    data = call(
        functools.partial(curl_kernel, chunks, nx, ny),
        [here, (VM, low_rim), (VM, high_rim)] + [(VM, d) for d in data],
        [(VM, d.shape) for d in data],
        [((3, 2, nz, tile, LANES), F32)],
        micros=5.0,
    )
    left = [
        call(
            functools.partial(leave_kernel, chunk, nz),
            [here, (VM, source)],
            [(VM, shape) for shape in sent_shapes("gz", block, width, whole)],
            [(source.shape, F32)],
        )
        for chunk, source, width, whole in zip(chunks, data, widths, (False, True))
    ]
    parts = []
    for part, width in zip(left, widths):
        part = exchange(part, "gz")
        shapes = sent_shapes("gx", rows, width)
        part = call(
            copied(functools.partial(x_back_kernel, len(shapes)), 2),
            [here]
            + [(HB, kept(t)) for t in x_back]
            + [(AN, left[-1][0])]
            + [(VM, p) for p in part],
            [(VM, shape) for shape in shapes],
            [((slabs, block, width), F32), ((pencils, rows, width), F32)]
            + [(t.shape, BF16) for t in x_back],
            sems=2,
        )
        parts.append(exchange(part, "gx"))
    plane = (3, cols, ny)
    tables = [(HB, kept(t)) for t in y_back]
    near = [(t.shape, BF16) for t in y_back]
    tall = [(3, 2 * len(chunk), cols + 2 * RIM, ny) for chunk in chunks]
    edges, first, last = call(
        copied(functools.partial(edge_kernel, chunks[0]), 2),
        [here] + tables + [(VM, p) for p in parts[0]],
        [(VM, tall[0]), (VM, plane), (VM, plane)],
        [((pencils, rows, widths[0]), F32)] + near,
        sems=2,
    )
    after = lax.ppermute(first, "gz", ring("gz", -1))
    before = lax.ppermute(last, "gz", ring("gz", 1))
    return tuple(
        call(
            functools.partial(stretch_kernel, chunks),
            [here]
            + tables
            + [(VM, v) for v in (edges, before, after, low_rim, high_rim)]
            + [(HB, mesh) for mesh in meshes]
            + [(VM, p) for p in parts[1]],
            [(AN, ambient.shape), (AN, ambient.shape)],
            [
                ((pencils, rows, widths[1]), F32),
                (tall[1], F32),
                ((3, planes, cols, ny), F32),
            ]
            + near,
            sems=3 * planes + 2,
            micros=4.0,
        )
    )


def solution(mesh):
    placed = (
        P(None, ("gz", "gx")),
        P(None, ("gz", "gx")),
        P(("gz", "gx")),
        P("gz", "gx", None),
        P(None, "gz", "gx", None),
    )
    return jax.shard_map(
        on_device,
        mesh=mesh,
        in_specs=placed,
        out_specs=(P(None, "gz", "gx", None), P(None, "gz", "gx", None)),
        check_vma=False,
    )
```

```python
import functools
import math

import jax
import jax.numpy as jnp
import ml_dtypes
import numpy as np
from jax import lax
from jax.experimental import pallas as pl
from jax.experimental.pallas import tpu as pltpu
from jax.sharding import PartitionSpec as P

MIG = 64
LANES = 128
RIM = 8
LATE = 3
TIME_STEP = 0.25
VMEM = 24 * 1024 * 1024
F32 = jnp.float32
BF16 = jnp.bfloat16


def split_table(table):
    high = table.astype(np.float32).astype(ml_dtypes.bfloat16)
    low = (table - high.astype(np.float64)).astype(np.float32).astype(ml_dtypes.bfloat16)
    return high, low


def angles(rows, columns, extent):
    return 2.0 * np.pi * (np.multiply.outer(rows, columns) % extent) / extent


def y_tables(ny, pencils, scale):
    modes = ny // (2 * pencils)
    position = np.arange(ny)
    angle = angles(position, np.arange(ny // 2), ny)
    real, imag = np.cos(angle), -np.sin(angle)
    imag[:, 0] = 1.0 - 2.0 * (position % 2)
    weight = np.where(np.arange(ny // 2) == 0, 1.0, 2.0) * scale
    ahead = np.zeros((2, ny, pencils, 2, 2, modes))
    back = np.zeros((pencils, 2, 2, modes, 2, ny))
    for parity in range(2):
        for part, values in enumerate((real, imag)):
            ahead[parity, :, :, part, parity] = values.reshape(ny, pencils, modes)
            back[:, part, parity, :, parity] = (values * weight).T.reshape(pencils, modes, ny)
    return ahead.reshape(2 * ny, -1), back.reshape(-1, 2 * ny)


def wave_order(nx, slabs):
    half = nx // 2
    ahead = np.arange(half).reshape(slabs, 1, half // slabs)
    behind = np.where(ahead == 0, half, (nx - ahead) % nx)
    return np.concatenate([ahead, behind], axis=1).reshape(-1)


def x_tables(nx, cols, pencils, slabs):
    order = wave_order(nx, slabs)
    angle = angles(order, np.arange(nx), nx)
    ahead = np.concatenate([np.cos(angle), np.sin(angle)], axis=0)
    row = np.arange(cols + RIM)
    offset = np.where(row <= cols, row, -1)
    used = ((row <= cols) | (row == cols + RIM - 1)).astype(np.float64)
    place = (np.arange(pencils)[:, None] * cols + offset[None, :]) % nx
    angle = angles(place.reshape(-1), order, nx)
    mask = np.tile(used, pencils)[:, None]
    back = np.concatenate([np.cos(angle) * mask, np.sin(angle) * mask], axis=0)
    return ahead, back


def split(values):
    high = values.astype(BF16)
    return high, (values - high.astype(F32)).astype(BF16)


def dot(left, right):
    return jnp.dot(left, right, preferred_element_type=F32)


def table_left(high, low, values):
    v_high, v_low = split(values)
    return dot(high, v_high) + (dot(high, v_low) + dot(low, v_high))


def table_right(values, high, low):
    v_high, v_low = split(values)
    return dot(v_high, high) + (dot(v_low, high) + dot(v_high, low))


def lane_of():
    return lax.broadcasted_iota(jnp.int32, (1, LANES), 1)


def times_i(values):
    half = LANES // 2
    sign = jnp.where(lane_of() < half, -1.0, 1.0).astype(F32)
    return pltpu.roll(values, half, 1) * sign


def kernel_weight(distance):
    radius = jnp.abs(distance)
    near = 1.0 - 2.5 * radius * radius + 1.5 * radius * radius * radius
    far = 0.5 * (2.0 - radius) * (2.0 - radius) * (1.0 - radius)
    return jnp.where(radius < 1.0, near, jnp.where(radius < 2.0, far, 0.0))


def turned(value, wave, extent, sign):
    wave = wave % extent
    real, imag = value
    if wave == 0:
        return value
    if 2 * wave == extent:
        return -real, -imag
    if 4 * wave == extent:
        return (-imag, real) if sign > 0 else (imag, -real)
    if 4 * wave == 3 * extent:
        return (imag, -real) if sign > 0 else (-imag, real)
    a = math.cos(2.0 * math.pi * wave / extent)
    b = sign * math.sin(2.0 * math.pi * wave / extent)
    return real * a - imag * b, real * b + imag * a


def fft(values, sign):
    count = len(values)
    if count == 1:
        return values
    even, odd = fft(values[::2], sign), fft(values[1::2], sign)
    odd = [turned(v, k, count, sign) for k, v in enumerate(odd)]
    plus = [(a[0] + b[0], a[1] + b[1]) for a, b in zip(even, odd)]
    minus = [(a[0] - b[0], a[1] - b[1]) for a, b in zip(even, odd)]
    return plus + minus


def offset_order(count):
    if count < 4:
        return list(range(count))
    far, near = list(range(count // 2, count)), list(range(1, count // 2))
    order = [0]
    while far or near:
        order += far[:1] + near[:1]
        far, near = far[1:], near[1:]
    return order


def blocks_of(refs, at):
    if len(refs) == 1:
        return [(d, refs[0].at[d]) for d in range(refs[0].shape[0])]
    return [(at ^ k, ref) for k, ref in zip(offset_order(len(refs)), refs)]


def gather_blocks(refs, held, at):
    for d, ref in blocks_of(refs, at):
        held[d] = ref[...]


def packet_kernel(
    counts, strength, offsets, cells, packet, movers, near_counts, near_cells, sems
):
    copies = [
        pltpu.make_async_copy(counts, near_counts, sems.at[0]),
        pltpu.make_async_copy(cells, near_cells, sems.at[1]),
        pltpu.make_async_copy(strength, packet.at[pl.ds(0, 3)], sems.at[2]),
        pltpu.make_async_copy(offsets, packet.at[pl.ds(3, 3)], sems.at[3]),
    ]
    for copy in copies:
        copy.start()
    for copy in copies:
        copy.wait()
    slot = lax.broadcasted_iota(jnp.int32, (1, packet.shape[1]), 1)
    up = near_counts[0:1, 0:1]
    both = up + near_counts[0:1, 1:2]
    packet[6:7] = near_cells[...].astype(F32)
    packet[7:8] = jnp.where(slot < up, 1.0, jnp.where(slot < both, -1.0, 0.0))
    movers[...] = packet[:, : movers.shape[1]]


def deposit_kernel(
    pairs, rims_before, place, own, up1, down1, up2, down2, ambient, t_high, t_low, *refs
):
    rims, refs = refs[:rims_before], refs[rims_before:]
    mesh, rim_high, rim_low = refs[:3]
    total, made = refs[-2:]
    outs = refs[3:-2]
    _, planes, cols, ny = ambient.shape
    rows = cols + RIM
    movers = up2.shape[1]
    count = own.shape[1]
    listed = [2 * pair + parity for pair in pairs for parity in range(2)]

    def decode(ref, start, stop, shift):
        packet = ref[:, start:stop]
        cell = packet[6:7].astype(jnp.int32)
        move = packet[7:8].astype(jnp.int32)
        z_cell = lax.div(cell, cols * ny) + planes * (move + shift)
        x_cell = lax.rem(lax.div(cell, ny), cols)
        return packet[0:6], z_cell, x_cell, lax.rem(cell, ny)

    def joined(pieces):
        return [jnp.concatenate(p, axis=1) if len(p) > 1 else p[0] for p in zip(*pieces)]

    def add_block(pieces, wanted):
        values, z_cell, x_cell, y_cell = joined(pieces)
        width = values.shape[1]
        z_at = lax.broadcasted_iota(jnp.int32, (planes, width), 0)
        w_z = kernel_weight((z_at - z_cell).astype(F32) - values[3:4])
        row = lax.broadcasted_iota(jnp.int32, (rows, width), 0)
        x_at = jnp.where(row < cols + 2, row, jnp.where(row >= rows - 2, row - rows, 4 * rows))
        w_x = kernel_weight((x_at - x_cell).astype(F32) - values[4:5])
        y_at = lax.broadcasted_iota(jnp.int32, (ny, width), 0)
        y_off = lax.rem(y_at - y_cell + (ny + ny // 2), ny) - ny // 2
        w_y = kernel_weight(y_off.astype(F32) - values[5:6])
        y_high, y_low = split(w_y)
        right = jnp.concatenate([y_high, y_high, y_low], axis=1)
        at = [listed.index(z) for z in wanted]
        for c in range(3):
            s_z = values[c : c + 1] * w_z
            left = jnp.concatenate([s_z[z : z + 1] * w_x for z in wanted], axis=0)
            l_high, l_low = split(left)
            left = jnp.concatenate([l_high, l_low, l_high], axis=1)
            added = lax.dot_general(
                left, right, (((1,), (1,)), ((), ())), preferred_element_type=F32
            )
            total[c, at[0] : at[-1] + 1] += added.reshape(len(wanted), rows, ny)

    for n, z in enumerate(listed):
        total[:, n, 0:cols] = ambient[:, z]
    total[:, :, cols:rows] = jnp.zeros((3, len(listed), RIM, ny), F32)
    step = 256
    for at in range(0, count, step):
        add_block([decode(own, at, min(at + step, count), 0)], listed)
    add_block([decode(up1, 0, movers, 1), decode(down1, 0, movers, -1)], listed)
    sides = ((up1, up2, 1, (planes - 2, planes - 1)), (down1, down2, -1, (0, 1)))
    for near, far, shift, wanted in sides:
        if not set(wanted) <= set(listed):
            continue
        whole = [decode(near, movers, count, shift), decode(far, 0, movers, 2 * shift)]
        values, z_cell, x_cell, y_cell = joined(whole)
        for at in range(0, count, step):
            to = min(at + step, count)
            block = (values[:, at:to], z_cell[:, at:to], x_cell[:, at:to], y_cell[:, at:to])
            add_block([block], wanted)

    mesh[...] = total[:, :, 0:cols]
    at = 0
    if rims:
        at = rims[0].shape[0]
        rim_high[0:at] = rims[0][...]
        rim_low[0:at] = rims[1][...]
    for n in range(3 * len(listed)):
        c, i = n // len(listed), n % len(listed)
        rim_high[at + 2 * n : at + 2 * n + 2] = total[c, i, cols : cols + 2]
        rim_low[at + 2 * n : at + 2 * n + 2] = total[c, i, rows - 2 : rows]
    groups = [(c, 2 * n) for c in range(3) for n in range(len(pairs))]
    left = jnp.concatenate(
        [jnp.concatenate([total[c, n], total[c, n + 1]], axis=1) for c, n in groups], axis=0
    )
    wide = table_right(left, t_high[...], t_low[...])
    for n in range(len(groups)):
        for g in range(made.shape[0]):
            made[g, :, n * LANES : (n + 1) * LANES] = wide[
                n * rows : (n + 1) * rows, g * LANES : (g + 1) * LANES
            ]
    for d, out in blocks_of(outs, place[1]):
        out[...] = made[d]


def x_ahead_kernel(sends, place, t_high, t_low, *refs):
    held, made = refs[-2:]
    outs, parts = refs[-2 - sends : -2], refs[: -2 - sends]
    gather_blocks(parts, held, place[1])
    pencils, rows, width = held.shape
    cols = rows - RIM
    row = lax.broadcasted_iota(jnp.int32, (RIM, width), 0)
    pieces = []
    for h in range(pencils):
        from_low = held[(h - 1) % pencils, cols:rows]
        from_high = held[(h + 1) % pencils, cols:rows]
        pieces.append(held[h, 0:RIM] + jnp.where(row < 2, from_low, 0.0))
        pieces.append(held[h, RIM : cols - RIM])
        pieces.append(held[h, cols - RIM : cols] + jnp.where(row >= RIM - 2, from_high, 0.0))
    both = table_left(t_high[...], t_low[...], jnp.concatenate(pieces, axis=0))
    half = both.shape[0] // 2
    for n in range(width // LANES):
        lanes = slice(n * LANES, (n + 1) * LANES)
        value = both[:half, lanes] - times_i(both[half:, lanes])
        made[:, :, lanes] = value.reshape(made.shape[0], made.shape[1], LANES)
    for d, out in blocks_of(outs, place[0]):
        out[...] = made[d]


def x_back_kernel(sends, tables, place, *refs):
    held, made = refs[-2:]
    outs, parts = refs[-2 - sends : -2], refs[: -2 - sends]
    gather_blocks(parts, held, place[0])
    pencils, rows, width = made.shape
    both = table_left(tables[0][...], tables[1][...], held[...].reshape(-1, width))
    half = both.shape[0] // 2
    for n in range(width // LANES):
        lanes = slice(n * LANES, (n + 1) * LANES)
        value = both[:half, lanes] + times_i(both[half:, lanes])
        made[:, :, lanes] = value.reshape(pencils, rows, LANES)
    for d, out in blocks_of(outs, place[1]):
        out[...] = made[d]


def wave_lanes():
    lane = lane_of()
    return lane < LANES // 2, (lane // (LANES // 4)) % 2 == 0


def roll(values, shift):
    return pltpu.roll(values, shift, 1)


def cross_half(a, b):
    low, _ = wave_lanes()
    half = LANES // 2
    return jnp.where(low, a, roll(b, half)), jnp.where(low, roll(a, half), b)


def cross_quarter(a, b):
    _, first = wave_lanes()
    quarter = LANES // 4
    return (
        jnp.where(first, a, roll(b, quarter)),
        jnp.where(first, roll(a, LANES - quarter), b),
    )


def lanes_at(c, count, i):
    return pl.ds(pl.multiple_of((c * count + i) * LANES, LANES), LANES)


def enter_kernel(pairs, nz, place, *refs):
    parts, data = refs[:-1], refs[-1]
    _, _, _, slabs, tile, _ = data.shape

    def body(c, carry):
        for i, pair in enumerate(pairs):
            lanes = lanes_at(c, len(pairs), i)
            for s, ref in blocks_of(parts, place[0]):
                quad = [ref[q * tile : (q + 1) * tile, lanes] for q in range(4)]
                real0, imag0 = cross_half(quad[0], quad[2])
                real1, imag1 = cross_half(quad[1], quad[3])
                for part, (a, b) in enumerate(((real0, real1), (imag0, imag1))):
                    even, odd = cross_quarter(a, b)
                    data[c, part, 2 * i, s] = even
                    data[c, part, 2 * i + 1, s] = odd
            for parity in range(2):
                at = 2 * i + parity
                line = [(data[c, 0, at, s], data[c, 1, at, s]) for s in range(slabs)]
                for k, v in enumerate(fft(line, -1.0)):
                    v = turned(v, (2 * pair + parity) * k, nz, -1.0)
                    data[c, 0, at, k], data[c, 1, at, k] = v
        return carry

    lax.fori_loop(0, 3, body, 0)


def pass_kernel(before, *refs):
    for source, target in zip(refs[: len(refs) // 2], refs[len(refs) // 2 :]):
        target[...] = source[...]


def leave_kernel(pairs, nz, place, source, *refs):
    outs, data = refs[:-1], refs[-1]
    _, _, _, slabs, tile, _ = source.shape

    def body(c, carry):
        for i, pair in enumerate(pairs):
            lanes = lanes_at(c, len(pairs), i)
            for parity in range(2):
                at = 2 * i + parity
                line = [
                    turned(
                        (source[c, 0, at, k], source[c, 1, at, k]),
                        (2 * pair + parity) * k,
                        nz,
                        1.0,
                    )
                    for k in range(slabs)
                ]
                for s, v in enumerate(fft(line, 1.0)):
                    data[c, 0, at, s], data[c, 1, at, s] = v
            for s, ref in blocks_of(outs, place[0]):
                real0, real1 = cross_quarter(data[c, 0, 2 * i, s], data[c, 0, 2 * i + 1, s])
                imag0, imag1 = cross_quarter(data[c, 1, 2 * i, s], data[c, 1, 2 * i + 1, s])
                quad = [None] * 4
                quad[0], quad[2] = cross_half(real0, imag0)
                quad[1], quad[3] = cross_half(real1, imag1)
                for q in range(4):
                    ref[q * tile : (q + 1) * tile, lanes] = quad[q]
        return carry

    lax.fori_loop(0, 3, body, 0)


def curl_kernel(chunks, nx, ny, place, low_rim, high_rim, *refs):
    sources, outs = refs[: len(chunks)], refs[len(chunks) : 2 * len(chunks)]
    spectrum = refs[-1]
    _, _, nz, tile, _ = spectrum.shape
    slabs = sources[0].shape[3]
    planes = nz // slabs
    modes, half = LANES // 4, LANES // 2
    slab_at, pencil_at = place[0], place[1]
    spot = {}
    for n, chunk in enumerate(chunks):
        for i, pair in enumerate(chunk):
            spot[2 * pair], spot[2 * pair + 1] = (n, 2 * i), (n, 2 * i + 1)

    def across_planes(k, carry):
        for c in range(3):
            line = []
            for l in range(planes):
                n, i = spot[l]
                line.append((sources[n][c, 0, i, k], sources[n][c, 1, i, k]))
            for n, v in enumerate(fft(line, -1.0)):
                spectrum[c, 0, k + slabs * n], spectrum[c, 1, k + slabs * n] = v
        return carry

    reach = 2 * tile
    row = lax.broadcasted_iota(jnp.int32, (tile, LANES), 0)
    lane = lax.broadcasted_iota(jnp.int32, (tile, LANES), 1)
    number = slab_at * reach + (lane // modes) % 2 * tile + row
    ahead = lane < half
    mode = lane % modes + pencil_at * modes
    alone = number == 0
    number = number.astype(F32) * (2.0 * math.pi / nx)
    x_base = jnp.where(ahead, number, jnp.where(alone, math.pi, -number))
    x_trim = jnp.where(ahead, number, jnp.where(alone, 0.0, -number))
    wave_y = mode.astype(F32) * (2.0 * math.pi / ny)
    packed = mode == 0
    x_sq = x_base * x_base
    lateral = x_sq + wave_y * wave_y

    def curl_at(k, with_mirror):
        z_wave = jnp.where(k < nz // 2, k, k - nz).astype(F32) * (2.0 * math.pi / nz)
        z_trim = jnp.where(k == nz // 2, 0.0, z_wave)
        full = lateral + z_wave * z_wave
        empty = full == 0.0
        inverse = jnp.where(empty, 0.0, 1.0 / jnp.where(empty, 1.0, full))
        if with_mirror:
            other = 1.0 / (x_sq + (z_wave * z_wave + math.pi * math.pi))
            mirror = jnp.where(packed, 0.5 * (inverse - other), 0.0)
            inverse = jnp.where(packed, 0.5 * (inverse + other), inverse)
            opposite = lax.rem(nz - k, nz)
        stream = []
        for c in range(3):
            value = [spectrum[c, part, k] * inverse for part in range(2)]
            if with_mirror:
                for part, sign in enumerate((1.0, -1.0)):
                    there = spectrum[c, part, opposite]
                    there = jnp.where(alone, there, roll(there, half))
                    value[part] = value[part] + (mirror * sign) * there
            stream.append(value)
        made = []
        for part in range(2):
            s = [value[part] for value in stream]
            made.append(
                (
                    x_trim * s[2] - wave_y * s[1],
                    wave_y * s[0] - z_trim * s[2],
                    z_trim * s[1] - x_trim * s[0],
                )
            )
        return [(-made[1][c], made[0][c]) for c in range(3)]

    def curl_all(with_mirror):
        def body(k, carry):
            made = [curl_at(k + slabs * n, with_mirror) for n in range(planes)]
            for c in range(3):
                for l, v in enumerate(fft([m[c] for m in made], 1.0)):
                    n, i = spot[l]
                    outs[n][c, 0, i, k], outs[n][c, 1, i, k] = v
            return carry

        lax.fori_loop(0, slabs, body, 0)

    lax.fori_loop(0, slabs, across_planes, 0)

    @pl.when(pencil_at == 0)
    def _():
        curl_all(True)

    @pl.when(pencil_at != 0)
    def _():
        curl_all(False)


def planes_of(held, pairs, tables):
    pencils, rows, _ = held.shape
    groups = [(c, pair) for c in range(3) for pair in pairs]
    left = jnp.concatenate(
        [
            jnp.concatenate(
                [held[h, :, n * LANES : (n + 1) * LANES] for h in range(pencils)], axis=1
            )
            for n in range(len(groups))
        ],
        axis=0,
    )
    ny = tables[0].shape[1] // 2
    wide = table_right(left, tables[0][...], tables[1][...])
    made = {}
    for n, (c, pair) in enumerate(groups):
        for parity in range(2):
            made[c, 2 * pair + parity] = wide[
                n * rows : (n + 1) * rows, parity * ny : (parity + 1) * ny
            ]
    return made


def hold(tall, c, n, value):
    rows = value.shape[0]
    tall[c, n, RIM : RIM + rows] = value
    tall[c, n, 0:RIM] = value[rows - RIM : rows]


def edge_kernel(pairs, tables, place, *refs):
    tall, first, last, held = refs[-4:]
    gather_blocks(refs[:-4], held, place[1])
    listed = [2 * pair + parity for pair in pairs for parity in range(2)]
    cols = first.shape[1]
    values = planes_of(held, pairs, tables)
    for c in range(3):
        for n, z in enumerate(listed):
            hold(tall, c, n, values[c, z])
        first[c] = values[c, listed[0]][0:cols]
        last[c] = values[c, listed[-1]][0:cols]


def stretch_kernel(
    chunks, tables, place, edges, before, after, low_rim, high_rim, *refs
):
    meshes, refs = refs[:2], refs[2:]
    velocity, vorticity, held, inner, omega, sems = refs[-6:]
    _, planes, cols, ny = velocity.shape
    spot = {}
    for n, chunk in enumerate(chunks):
        for i, pair in enumerate(chunk):
            spot[2 * pair], spot[2 * pair + 1] = (n, 2 * i), (n, 2 * i + 1)
    talls = (edges, inner)
    sent = []

    def send(source, target):
        sent.append(pltpu.make_async_copy(source, target, sems.at[len(sent)]))
        sent[-1].start()

    def send_velocity(z):
        n, i = spot[z]
        send(talls[n].at[:, i, pl.ds(RIM, cols)], velocity.at[:, z])

    def rows_of(c, z, start=RIM):
        n, i = spot[z]
        return talls[n][c, i, start : start + cols]

    for z in range(planes):
        if spot[z][0] == 0:
            send_velocity(z)
    gather_blocks(refs[:-6], held, place[1])
    for (c, z), value in planes_of(held, chunks[1], tables).items():
        hold(inner, c, spot[z][1], value)
    for z in range(planes):
        if spot[z][0] == 1:
            send_velocity(z)
    rim_at = 0
    for which in (1, 0):
        size = meshes[which].shape[1]
        for z in range(planes):
            n, i = spot[z]
            if n != which:
                continue
            for c in range(3):
                at = rim_at + 2 * (c * size + i)
                omega[c, z] = meshes[which][c, i]
                omega[c, z, 0:2] += low_rim[at : at + 2]
                omega[c, z, cols - 2 : cols] += high_rim[at : at + 2]
            omega_z = [omega[c, z] for c in range(3)]
            for c in range(3):
                value = rows_of(c, z)
                above = rows_of(c, z + 1) if z + 1 < planes else after[c]
                below = rows_of(c, z - 1) if z > 0 else before[c]
                along_z = (above - below) * 0.5
                along_x = (rows_of(c, z, RIM + 1) - rows_of(c, z, RIM - 1)) * 0.5
                along_y = (pltpu.roll(value, ny - 1, 1) - pltpu.roll(value, 1, 1)) * 0.5
                stretch = omega_z[0] * along_z + omega_z[1] * along_x + omega_z[2] * along_y
                omega[c, z] = omega_z[c] + TIME_STEP * stretch
            send(omega.at[:, z], vorticity.at[:, z])
        rim_at += 6 * size
    for copy in sent:
        copy.wait()


VM = pl.BlockSpec(memory_space=pltpu.VMEM)
SM = pl.BlockSpec(memory_space=pltpu.SMEM)
AN = pl.BlockSpec(memory_space=pl.ANY)
HB = pl.BlockSpec(memory_space=pltpu.HBM)


def kept(values):
    return pltpu.with_memory_space_constraint(values, pltpu.HBM)


def loaded(kernel):
    def run(place, t_high, t_low, *refs):
        kernel((t_high, t_low), place, *refs)

    return run


def call(kernel, ins, outs, scratch=(), sems=0, micros=2.0, moved=None):
    extra = [pltpu.SemaphoreType.DMA((sems,))] if sems else []
    return pl.pallas_call(
        kernel,
        out_shape=[jax.ShapeDtypeStruct(shape, F32) for _, shape in outs],
        in_specs=[spec for spec, _ in ins],
        out_specs=[spec for spec, _ in outs],
        scratch_shapes=[pltpu.VMEM(shape, kind) for shape, kind in scratch] + extra,
        compiler_params=pltpu.CompilerParams(vmem_limit_bytes=VMEM),
        cost_estimate=pl.CostEstimate(
            flops=int(micros * 1.0e9),
            bytes_accessed=int(micros * 3.0e6) if moved is None else moved,
            transcendentals=0,
        ),
    )(*[value for _, value in ins])


def ring(axis, step):
    count = lax.axis_size(axis)
    return [(i, (i + step) % count) for i in range(count)]


def spread(axis):
    count = lax.axis_size(axis)
    return count <= 8 and count & (count - 1) == 0


def sent_shapes(axis, rows, width, whole=False):
    count = lax.axis_size(axis)
    return [(count, rows, width)] if whole or not spread(axis) else [(rows, width)] * count


def exchange(blocks, axis, start=0):
    if not spread(axis):
        return [lax.all_to_all(blocks[0], axis, split_axis=0, concat_axis=0, tiled=True)]
    count = lax.axis_size(axis)
    return [
        lax.ppermute(block, axis, [(i, i ^ k) for i in range(count)]) if k else block
        for k, block in zip(offset_order(count)[start:], blocks)
    ]


def on_device(strength, offsets, cell_index, migrate_count, ambient):
    _, planes, cols, ny = ambient.shape
    slabs, pencils = lax.axis_size("gz"), lax.axis_size("gx")
    nx, nz, rows = cols * pencils, planes * slabs, cols + RIM
    count = strength.shape[1]
    pair_count = planes // 2
    chunks = ((0, pair_count - 1), tuple(range(1, pair_count - 1)))
    widths = [3 * len(c) * LANES for c in chunks]
    block = nx // slabs

    y_ahead, y_back = [split_table(t) for t in y_tables(ny, pencils, 1.0 / (float(nx) * ny * nz))]
    x_ahead, x_back = [split_table(t) for t in x_tables(nx, cols, pencils, slabs)]
    place = jnp.stack([lax.axis_index("gz"), lax.axis_index("gx")]).astype(jnp.int32)
    here = (SM, place)

    packet, movers = call(
        packet_kernel,
        [
            (HB, kept(migrate_count.reshape(1, 2))),
            (HB, kept(strength)),
            (HB, kept(offsets)),
            (HB, kept(cell_index.reshape(1, count))),
        ],
        [(VM, (8, count)), (VM, (8, 2 * MIG))],
        [((1, 2), jnp.int32), ((1, count), jnp.int32)],
        sems=4,
        micros=1.0,
        moved=1000,
    )
    up1 = lax.ppermute(packet, "gz", ring("gz", -1))
    down1 = lax.ppermute(packet, "gz", ring("gz", 1))
    up2 = lax.ppermute(movers, "gz", ring("gz", -2))
    down2 = lax.ppermute(movers, "gz", ring("gz", 2))

    meshes, rims, parts = [None, None], [], [None, None]
    for n in (1, 0):
        chunk, width = chunks[n], widths[n]
        size = 2 * len(chunk)
        rim = (6 * size + (rims[0].shape[0] if rims else 0), ny)
        mesh, rim_high, rim_low, *part = call(
            functools.partial(deposit_kernel, chunk, len(rims)),
            [here]
            + [(VM, value) for value in (packet, up1, down1, up2, down2)]
            + [(VM, ambient), (VM, y_ahead[0]), (VM, y_ahead[1])]
            + [(VM, value) for value in rims],
            [(VM, (3, size, cols, ny)), (VM, rim), (VM, rim)]
            + [(VM, shape) for shape in sent_shapes("gx", rows, width)],
            [((3, size, rows, ny), F32), ((pencils, rows, width), F32)],
            micros=5.0,
        )
        meshes[n] = mesh
        rims = [rim_high, rim_low]
        parts[n] = exchange(part, "gx")
    low_rim = lax.ppermute(rims[0], "gx", ring("gx", 1))
    high_rim = lax.ppermute(rims[1], "gx", ring("gx", -1))

    tile = max(1, block // 4)
    data = [None, None]
    for n in (1, 0):
        chunk, part, width = chunks[n], parts[n], widths[n]
        shapes = sent_shapes("gz", block, width)
        part = call(
            functools.partial(x_ahead_kernel, len(shapes)),
            [here, (VM, x_ahead[0]), (VM, x_ahead[1])] + [(VM, p) for p in part],
            [(VM, shape) for shape in shapes],
            [((pencils, rows, width), F32), ((slabs, block, width), F32)],
        )
        (entered,) = call(
            functools.partial(enter_kernel, chunk, nz),
            [here] + [(VM, p) for p in exchange(part, "gz")],
            [(VM, (3, 2, 2 * len(chunk), slabs, tile, LANES))],
        )
        data[n] = entered
    data = call(
        functools.partial(curl_kernel, chunks, nx, ny),
        [here, (VM, low_rim), (VM, high_rim)] + [(VM, d) for d in data],
        [(VM, d.shape) for d in data],
        [((3, 2, nz, tile, LANES), F32)],
        micros=5.0,
    )
    plane = (3, cols, ny)
    tables = [(VM, t) for t in y_back]
    tall = [(3, 2 * len(chunk), cols + 2 * RIM, ny) for chunk in chunks]
    left = [
        call(
            functools.partial(leave_kernel, chunk, nz),
            [here, (VM, source)],
            [(VM, shape) for shape in sent_shapes("gz", block, width)],
            [(source.shape, F32)],
        )
        for chunk, source, width in zip(chunks, data, widths)
    ]

    def back(part, width):
        shapes = sent_shapes("gx", rows, width)
        part = call(
            loaded(functools.partial(x_back_kernel, len(shapes))),
            [here] + [(VM, t) for t in x_back] + [(VM, p) for p in part],
            [(VM, shape) for shape in shapes],
            [((slabs, block, width), F32), ((pencils, rows, width), F32)],
        )
        return exchange(part, "gx")

    early = max(1, len(left[1]) - LATE)
    second = exchange(left[1][:early], "gz")
    parts = [back(exchange(left[0], "gz"), widths[0])]
    edges, first, last = call(
        loaded(functools.partial(edge_kernel, chunks[0])),
        [here] + tables + [(VM, p) for p in parts[0]],
        [(VM, tall[0]), (VM, plane), (VM, plane)],
        [((pencils, rows, widths[0]), F32)],
    )
    if early < len(left[1]):
        late = call(
            pass_kernel,
            [(AN, parts[0][0])] + [(VM, p) for p in left[1][early:]],
            [(VM, p.shape) for p in left[1][early:]],
            micros=0.3,
        )
        second += exchange(late, "gz", early)
    parts.append(back(second, widths[1]))
    after = lax.ppermute(first, "gz", ring("gz", -1))
    before = lax.ppermute(last, "gz", ring("gz", 1))
    return tuple(
        call(
            loaded(functools.partial(stretch_kernel, chunks)),
            [here]
            + tables
            + [(VM, v) for v in (edges, before, after, low_rim, high_rim, *meshes)]
            + [(VM, p) for p in parts[1]],
            [(AN, ambient.shape), (AN, ambient.shape)],
            [
                ((pencils, rows, widths[1]), F32),
                (tall[1], F32),
                ((3, planes, cols, ny), F32),
            ],
            sems=2 * planes,
            micros=4.0,
        )
    )


def solution(mesh):
    placed = (
        P(None, ("gz", "gx")),
        P(None, ("gz", "gx")),
        P(("gz", "gx")),
        P("gz", "gx", None),
        P(None, "gz", "gx", None),
    )
    return jax.shard_map(
        on_device,
        mesh=mesh,
        in_specs=placed,
        out_specs=(P(None, "gz", "gx", None), P(None, "gz", "gx", None)),
        check_vma=False,
    )
```

```python
import functools
import math

import jax
import jax.numpy as jnp
import ml_dtypes
import numpy as np
from jax import lax
from jax.experimental import pallas as pl
from jax.experimental.pallas import tpu as pltpu
from jax.sharding import PartitionSpec as P

MIG = 64
LANES = 128
RIM = 8
LATE = 3
TIME_STEP = 0.25
VMEM = 24 * 1024 * 1024
F32 = jnp.float32
BF16 = jnp.bfloat16


def split_table(table):
    high = table.astype(np.float32).astype(ml_dtypes.bfloat16)
    low = (table - high.astype(np.float64)).astype(np.float32).astype(ml_dtypes.bfloat16)
    return high, low


def angles(rows, columns, extent):
    return 2.0 * np.pi * (np.multiply.outer(rows, columns) % extent) / extent


def y_tables(ny, pencils, scale):
    modes = ny // (2 * pencils)
    position = np.arange(ny)
    angle = angles(position, np.arange(ny // 2), ny)
    real, imag = np.cos(angle), -np.sin(angle)
    imag[:, 0] = 1.0 - 2.0 * (position % 2)
    weight = np.where(np.arange(ny // 2) == 0, 1.0, 2.0) * scale
    ahead = np.zeros((2, ny, pencils, 2, 2, modes))
    back = np.zeros((pencils, 2, 2, modes, 2, ny))
    for parity in range(2):
        for part, values in enumerate((real, imag)):
            ahead[parity, :, :, part, parity] = values.reshape(ny, pencils, modes)
            back[:, part, parity, :, parity] = (values * weight).T.reshape(pencils, modes, ny)
    return ahead.reshape(2 * ny, -1), back.reshape(-1, 2 * ny)


def wave_order(nx, slabs):
    half = nx // 2
    ahead = np.arange(half).reshape(slabs, 1, half // slabs)
    behind = np.where(ahead == 0, half, (nx - ahead) % nx)
    return np.concatenate([ahead, behind], axis=1).reshape(-1)


def x_tables(nx, cols, pencils, slabs):
    order = wave_order(nx, slabs)
    angle = angles(order, np.arange(nx), nx)
    ahead = np.concatenate([np.cos(angle), np.sin(angle)], axis=0)
    row = np.arange(cols + RIM)
    offset = np.where(row <= cols, row, -1)
    used = ((row <= cols) | (row == cols + RIM - 1)).astype(np.float64)
    place = (np.arange(pencils)[:, None] * cols + offset[None, :]) % nx
    angle = angles(place.reshape(-1), order, nx)
    mask = np.tile(used, pencils)[:, None]
    back = np.concatenate([np.cos(angle) * mask, np.sin(angle) * mask], axis=0)
    return ahead, back


def split(values):
    high = values.astype(BF16)
    return high, (values - high.astype(F32)).astype(BF16)


def dot(left, right):
    return jnp.dot(left, right, preferred_element_type=F32)


def table_left(high, low, values):
    v_high, v_low = split(values)
    return dot(high, v_high) + (dot(high, v_low) + dot(low, v_high))


def table_right(values, high, low):
    v_high, v_low = split(values)
    return dot(v_high, high) + (dot(v_low, high) + dot(v_high, low))


def lane_of():
    return lax.broadcasted_iota(jnp.int32, (1, LANES), 1)


def times_i(values):
    half = LANES // 2
    sign = jnp.where(lane_of() < half, -1.0, 1.0).astype(F32)
    return pltpu.roll(values, half, 1) * sign


def kernel_weight(distance):
    radius = jnp.abs(distance)
    near = 1.0 - 2.5 * radius * radius + 1.5 * radius * radius * radius
    far = 0.5 * (2.0 - radius) * (2.0 - radius) * (1.0 - radius)
    return jnp.where(radius < 1.0, near, jnp.where(radius < 2.0, far, 0.0))


def turned(value, wave, extent, sign):
    wave = wave % extent
    real, imag = value
    if wave == 0:
        return value
    if 2 * wave == extent:
        return -real, -imag
    if 4 * wave == extent:
        return (-imag, real) if sign > 0 else (imag, -real)
    if 4 * wave == 3 * extent:
        return (imag, -real) if sign > 0 else (-imag, real)
    a = math.cos(2.0 * math.pi * wave / extent)
    b = sign * math.sin(2.0 * math.pi * wave / extent)
    return real * a - imag * b, real * b + imag * a


def fft(values, sign):
    count = len(values)
    if count == 1:
        return values
    even, odd = fft(values[::2], sign), fft(values[1::2], sign)
    odd = [turned(v, k, count, sign) for k, v in enumerate(odd)]
    plus = [(a[0] + b[0], a[1] + b[1]) for a, b in zip(even, odd)]
    minus = [(a[0] - b[0], a[1] - b[1]) for a, b in zip(even, odd)]
    return plus + minus


def offset_order(count):
    if count < 4:
        return list(range(count))
    far, near = list(range(count // 2, count)), list(range(1, count // 2))
    order = [0]
    while far or near:
        order += far[:2] + near[:2]
        far, near = far[2:], near[2:]
    return order


def blocks_of(refs, at):
    if len(refs) == 1:
        return [(d, refs[0].at[d]) for d in range(refs[0].shape[0])]
    return [(at ^ k, ref) for k, ref in zip(offset_order(len(refs)), refs)]


def gather_blocks(refs, held, at):
    for d, ref in blocks_of(refs, at):
        held[d] = ref[...]


def packet_kernel(
    counts, strength, offsets, cells, packet, movers, near_counts, near_cells, sems
):
    copies = [
        pltpu.make_async_copy(counts, near_counts, sems.at[0]),
        pltpu.make_async_copy(cells, near_cells, sems.at[1]),
        pltpu.make_async_copy(strength, packet.at[pl.ds(0, 3)], sems.at[2]),
        pltpu.make_async_copy(offsets, packet.at[pl.ds(3, 3)], sems.at[3]),
    ]
    for copy in copies:
        copy.start()
    for copy in copies:
        copy.wait()
    slot = lax.broadcasted_iota(jnp.int32, (1, packet.shape[1]), 1)
    up = near_counts[0:1, 0:1]
    both = up + near_counts[0:1, 1:2]
    packet[6:7] = near_cells[...].astype(F32)
    packet[7:8] = jnp.where(slot < up, 1.0, jnp.where(slot < both, -1.0, 0.0))
    movers[...] = packet[:, : movers.shape[1]]


def deposit_kernel(
    pairs, rims_before, place, own, up1, down1, up2, down2, ambient, t_high, t_low, *refs
):
    rims, refs = refs[:rims_before], refs[rims_before:]
    mesh, rim_high, rim_low = refs[:3]
    total, made = refs[-2:]
    outs = refs[3:-2]
    _, planes, cols, ny = ambient.shape
    rows = cols + RIM
    movers = up2.shape[1]
    count = own.shape[1]
    listed = [2 * pair + parity for pair in pairs for parity in range(2)]

    def decode(ref, start, stop, shift):
        packet = ref[:, start:stop]
        cell = packet[6:7].astype(jnp.int32)
        move = packet[7:8].astype(jnp.int32)
        z_cell = lax.div(cell, cols * ny) + planes * (move + shift)
        x_cell = lax.rem(lax.div(cell, ny), cols)
        return packet[0:6], z_cell, x_cell, lax.rem(cell, ny)

    def joined(pieces):
        return [jnp.concatenate(p, axis=1) if len(p) > 1 else p[0] for p in zip(*pieces)]

    def add_block(pieces, wanted):
        values, z_cell, x_cell, y_cell = joined(pieces)
        width = values.shape[1]
        z_at = lax.broadcasted_iota(jnp.int32, (planes, width), 0)
        w_z = kernel_weight((z_at - z_cell).astype(F32) - values[3:4])
        row = lax.broadcasted_iota(jnp.int32, (rows, width), 0)
        x_at = jnp.where(row < cols + 2, row, jnp.where(row >= rows - 2, row - rows, 4 * rows))
        w_x = kernel_weight((x_at - x_cell).astype(F32) - values[4:5])
        y_at = lax.broadcasted_iota(jnp.int32, (ny, width), 0)
        y_off = lax.rem(y_at - y_cell + (ny + ny // 2), ny) - ny // 2
        w_y = kernel_weight(y_off.astype(F32) - values[5:6])
        y_high, y_low = split(w_y)
        right = jnp.concatenate([y_high, y_high, y_low], axis=1)
        at = [listed.index(z) for z in wanted]
        for c in range(3):
            s_z = values[c : c + 1] * w_z
            left = jnp.concatenate([s_z[z : z + 1] * w_x for z in wanted], axis=0)
            l_high, l_low = split(left)
            left = jnp.concatenate([l_high, l_low, l_high], axis=1)
            added = lax.dot_general(
                left, right, (((1,), (1,)), ((), ())), preferred_element_type=F32
            )
            total[c, at[0] : at[-1] + 1] += added.reshape(len(wanted), rows, ny)

    for n, z in enumerate(listed):
        total[:, n, 0:cols] = ambient[:, z]
    total[:, :, cols:rows] = jnp.zeros((3, len(listed), RIM, ny), F32)
    step = 256
    for at in range(0, count, step):
        add_block([decode(own, at, min(at + step, count), 0)], listed)
    add_block([decode(up1, 0, movers, 1), decode(down1, 0, movers, -1)], listed)
    sides = ((up1, up2, 1, (planes - 2, planes - 1)), (down1, down2, -1, (0, 1)))
    for near, far, shift, wanted in sides:
        if not set(wanted) <= set(listed):
            continue
        whole = [decode(near, movers, count, shift), decode(far, 0, movers, 2 * shift)]
        values, z_cell, x_cell, y_cell = joined(whole)
        for at in range(0, count, step):
            to = min(at + step, count)
            block = (values[:, at:to], z_cell[:, at:to], x_cell[:, at:to], y_cell[:, at:to])
            add_block([block], wanted)

    mesh[...] = total[:, :, 0:cols]
    at = 0
    if rims:
        at = rims[0].shape[0]
        rim_high[0:at] = rims[0][...]
        rim_low[0:at] = rims[1][...]
    for n in range(3 * len(listed)):
        c, i = n // len(listed), n % len(listed)
        rim_high[at + 2 * n : at + 2 * n + 2] = total[c, i, cols : cols + 2]
        rim_low[at + 2 * n : at + 2 * n + 2] = total[c, i, rows - 2 : rows]
    groups = [(c, 2 * n) for c in range(3) for n in range(len(pairs))]
    left = jnp.concatenate(
        [jnp.concatenate([total[c, n], total[c, n + 1]], axis=1) for c, n in groups], axis=0
    )
    wide = table_right(left, t_high[...], t_low[...])
    for n in range(len(groups)):
        for g in range(made.shape[0]):
            made[g, :, n * LANES : (n + 1) * LANES] = wide[
                n * rows : (n + 1) * rows, g * LANES : (g + 1) * LANES
            ]
    for d, out in blocks_of(outs, place[1]):
        out[...] = made[d]


def x_ahead_kernel(sends, place, t_high, t_low, *refs):
    held, made = refs[-2:]
    outs, parts = refs[-2 - sends : -2], refs[: -2 - sends]
    gather_blocks(parts, held, place[1])
    pencils, rows, width = held.shape
    cols = rows - RIM
    row = lax.broadcasted_iota(jnp.int32, (RIM, width), 0)
    pieces = []
    for h in range(pencils):
        from_low = held[(h - 1) % pencils, cols:rows]
        from_high = held[(h + 1) % pencils, cols:rows]
        pieces.append(held[h, 0:RIM] + jnp.where(row < 2, from_low, 0.0))
        pieces.append(held[h, RIM : cols - RIM])
        pieces.append(held[h, cols - RIM : cols] + jnp.where(row >= RIM - 2, from_high, 0.0))
    both = table_left(t_high[...], t_low[...], jnp.concatenate(pieces, axis=0))
    half = both.shape[0] // 2
    for n in range(width // LANES):
        lanes = slice(n * LANES, (n + 1) * LANES)
        value = both[:half, lanes] - times_i(both[half:, lanes])
        made[:, :, lanes] = value.reshape(made.shape[0], made.shape[1], LANES)
    for d, out in blocks_of(outs, place[0]):
        out[...] = made[d]


def x_back_kernel(sends, passed, tables, place, *refs):
    held, made = refs[-2:]
    outs, parts = refs[-2 - sends : -2], refs[passed : -2 - sends]
    gather_blocks(parts, held, place[0])
    pencils, rows, width = made.shape
    both = table_left(tables[0][...], tables[1][...], held[...].reshape(-1, width))
    half = both.shape[0] // 2
    for n in range(width // LANES):
        lanes = slice(n * LANES, (n + 1) * LANES)
        value = both[:half, lanes] + times_i(both[half:, lanes])
        made[:, :, lanes] = value.reshape(pencils, rows, LANES)
    for d, out in blocks_of(outs, place[1]):
        out[...] = made[d]


def wave_lanes():
    lane = lane_of()
    return lane < LANES // 2, (lane // (LANES // 4)) % 2 == 0


def roll(values, shift):
    return pltpu.roll(values, shift, 1)


def cross_half(a, b):
    low, _ = wave_lanes()
    half = LANES // 2
    return jnp.where(low, a, roll(b, half)), jnp.where(low, roll(a, half), b)


def cross_quarter(a, b):
    _, first = wave_lanes()
    quarter = LANES // 4
    return (
        jnp.where(first, a, roll(b, quarter)),
        jnp.where(first, roll(a, LANES - quarter), b),
    )


def lanes_at(c, count, i):
    return pl.ds(pl.multiple_of((c * count + i) * LANES, LANES), LANES)


def enter_kernel(pairs, nz, place, *refs):
    parts, data = refs[:-1], refs[-1]
    _, _, _, slabs, tile, _ = data.shape

    def body(c, carry):
        for i, pair in enumerate(pairs):
            lanes = lanes_at(c, len(pairs), i)
            for s, ref in blocks_of(parts, place[0]):
                quad = [ref[q * tile : (q + 1) * tile, lanes] for q in range(4)]
                real0, imag0 = cross_half(quad[0], quad[2])
                real1, imag1 = cross_half(quad[1], quad[3])
                for part, (a, b) in enumerate(((real0, real1), (imag0, imag1))):
                    even, odd = cross_quarter(a, b)
                    data[c, part, 2 * i, s] = even
                    data[c, part, 2 * i + 1, s] = odd
            for parity in range(2):
                at = 2 * i + parity
                line = [(data[c, 0, at, s], data[c, 1, at, s]) for s in range(slabs)]
                for k, v in enumerate(fft(line, -1.0)):
                    v = turned(v, (2 * pair + parity) * k, nz, -1.0)
                    data[c, 0, at, k], data[c, 1, at, k] = v
        return carry

    lax.fori_loop(0, 3, body, 0)


def pass_kernel(before, *refs):
    half = LATE
    for source, target in zip(refs[-2 * half : -half], refs[-half:]):
        target[...] = source[...]


def leave_kernel(pairs, nz, place, source, *refs):
    outs, data = refs[:-1], refs[-1]
    _, _, _, slabs, tile, _ = source.shape

    def body(c, carry):
        for i, pair in enumerate(pairs):
            lanes = lanes_at(c, len(pairs), i)
            for parity in range(2):
                at = 2 * i + parity
                line = [
                    turned(
                        (source[c, 0, at, k], source[c, 1, at, k]),
                        (2 * pair + parity) * k,
                        nz,
                        1.0,
                    )
                    for k in range(slabs)
                ]
                for s, v in enumerate(fft(line, 1.0)):
                    data[c, 0, at, s], data[c, 1, at, s] = v
            for s, ref in blocks_of(outs, place[0]):
                real0, real1 = cross_quarter(data[c, 0, 2 * i, s], data[c, 0, 2 * i + 1, s])
                imag0, imag1 = cross_quarter(data[c, 1, 2 * i, s], data[c, 1, 2 * i + 1, s])
                quad = [None] * 4
                quad[0], quad[2] = cross_half(real0, imag0)
                quad[1], quad[3] = cross_half(real1, imag1)
                for q in range(4):
                    ref[q * tile : (q + 1) * tile, lanes] = quad[q]
        return carry

    lax.fori_loop(0, 3, body, 0)


def curl_kernel(chunks, nx, ny, place, low_rim, high_rim, *refs):
    sources, outs = refs[: len(chunks)], refs[len(chunks) : 2 * len(chunks)]
    spectrum = refs[-1]
    _, _, nz, tile, _ = spectrum.shape
    slabs = sources[0].shape[3]
    planes = nz // slabs
    modes, half = LANES // 4, LANES // 2
    slab_at, pencil_at = place[0], place[1]
    spot = {}
    for n, chunk in enumerate(chunks):
        for i, pair in enumerate(chunk):
            spot[2 * pair], spot[2 * pair + 1] = (n, 2 * i), (n, 2 * i + 1)

    def across_planes(k, carry):
        for c in range(3):
            line = []
            for l in range(planes):
                n, i = spot[l]
                line.append((sources[n][c, 0, i, k], sources[n][c, 1, i, k]))
            for n, v in enumerate(fft(line, -1.0)):
                spectrum[c, 0, k + slabs * n], spectrum[c, 1, k + slabs * n] = v
        return carry

    reach = 2 * tile
    row = lax.broadcasted_iota(jnp.int32, (tile, LANES), 0)
    lane = lax.broadcasted_iota(jnp.int32, (tile, LANES), 1)
    number = slab_at * reach + (lane // modes) % 2 * tile + row
    ahead = lane < half
    mode = lane % modes + pencil_at * modes
    alone = number == 0
    number = number.astype(F32) * (2.0 * math.pi / nx)
    x_base = jnp.where(ahead, number, jnp.where(alone, math.pi, -number))
    x_trim = jnp.where(ahead, number, jnp.where(alone, 0.0, -number))
    wave_y = mode.astype(F32) * (2.0 * math.pi / ny)
    packed = mode == 0
    x_sq = x_base * x_base
    lateral = x_sq + wave_y * wave_y

    def curl_at(k, with_mirror):
        z_wave = jnp.where(k < nz // 2, k, k - nz).astype(F32) * (2.0 * math.pi / nz)
        z_trim = jnp.where(k == nz // 2, 0.0, z_wave)
        full = lateral + z_wave * z_wave
        empty = full == 0.0
        inverse = jnp.where(empty, 0.0, 1.0 / jnp.where(empty, 1.0, full))
        if with_mirror:
            other = 1.0 / (x_sq + (z_wave * z_wave + math.pi * math.pi))
            mirror = jnp.where(packed, 0.5 * (inverse - other), 0.0)
            inverse = jnp.where(packed, 0.5 * (inverse + other), inverse)
            opposite = lax.rem(nz - k, nz)
        stream = []
        for c in range(3):
            value = [spectrum[c, part, k] * inverse for part in range(2)]
            if with_mirror:
                for part, sign in enumerate((1.0, -1.0)):
                    there = spectrum[c, part, opposite]
                    there = jnp.where(alone, there, roll(there, half))
                    value[part] = value[part] + (mirror * sign) * there
            stream.append(value)
        made = []
        for part in range(2):
            s = [value[part] for value in stream]
            made.append(
                (
                    x_trim * s[2] - wave_y * s[1],
                    wave_y * s[0] - z_trim * s[2],
                    z_trim * s[1] - x_trim * s[0],
                )
            )
        return [(-made[1][c], made[0][c]) for c in range(3)]

    def curl_all(with_mirror):
        def body(k, carry):
            made = [curl_at(k + slabs * n, with_mirror) for n in range(planes)]
            for c in range(3):
                for l, v in enumerate(fft([m[c] for m in made], 1.0)):
                    n, i = spot[l]
                    outs[n][c, 0, i, k], outs[n][c, 1, i, k] = v
            return carry

        lax.fori_loop(0, slabs, body, 0)

    lax.fori_loop(0, slabs, across_planes, 0)

    @pl.when(pencil_at == 0)
    def _():
        curl_all(True)

    @pl.when(pencil_at != 0)
    def _():
        curl_all(False)


def planes_of(held, pairs, tables):
    pencils, rows, _ = held.shape
    groups = [(c, pair) for c in range(3) for pair in pairs]
    left = jnp.concatenate(
        [
            jnp.concatenate(
                [held[h, :, n * LANES : (n + 1) * LANES] for h in range(pencils)], axis=1
            )
            for n in range(len(groups))
        ],
        axis=0,
    )
    ny = tables[0].shape[1] // 2
    wide = table_right(left, tables[0][...], tables[1][...])
    made = {}
    for n, (c, pair) in enumerate(groups):
        for parity in range(2):
            made[c, 2 * pair + parity] = wide[
                n * rows : (n + 1) * rows, parity * ny : (parity + 1) * ny
            ]
    return made


def hold(tall, c, n, value):
    rows = value.shape[0]
    tall[c, n, RIM : RIM + rows] = value
    tall[c, n, 0:RIM] = value[rows - RIM : rows]


def edge_kernel(pairs, tables, place, *refs):
    tall, first, last, held = refs[-4:]
    gather_blocks(refs[:-4], held, place[1])
    listed = [2 * pair + parity for pair in pairs for parity in range(2)]
    cols = first.shape[1]
    values = planes_of(held, pairs, tables)
    for c in range(3):
        for n, z in enumerate(listed):
            hold(tall, c, n, values[c, z])
        first[c] = values[c, listed[0]][0:cols]
        last[c] = values[c, listed[-1]][0:cols]


def where_planes(chunks):
    spot = {}
    for n, chunk in enumerate(chunks):
        for i, pair in enumerate(chunk):
            spot[2 * pair], spot[2 * pair + 1] = (n, 2 * i), (n, 2 * i + 1)
    return spot


def rim_start(meshes, which, c, i):
    before = 6 * meshes[1].shape[1] if which == 0 else 0
    return before + 2 * (c * meshes[which].shape[1] + i)


def stretch_plane(out, mesh, rims, at, rows_of, above, below):
    cols, ny = out[0].shape
    low_rim, high_rim = rims
    for c in range(3):
        out[c][...] = mesh[c][...]
        out[c][0:2] += low_rim[at[c] : at[c] + 2]
        out[c][cols - 2 : cols] += high_rim[at[c] : at[c] + 2]
    omega = [ref[...] for ref in out]
    for c in range(3):
        value = rows_of(c, RIM)
        along_z = (above(c) - below(c)) * 0.5
        along_x = (rows_of(c, RIM + 1) - rows_of(c, RIM - 1)) * 0.5
        along_y = (pltpu.roll(value, ny - 1, 1) - pltpu.roll(value, 1, 1)) * 0.5
        stretch = omega[0] * along_z + omega[1] * along_x + omega[2] * along_y
        out[c][...] = omega[c] + TIME_STEP * stretch


def ends_kernel(chunks, edges, before, after, low_rim, high_rim, *refs):
    meshes, out = refs[:-1], refs[-1]
    cols = before.shape[1]
    size = edges.shape[1]

    def rows_of(i):
        return lambda c, start=RIM: edges[c, i, start : start + cols]

    for n, i in enumerate((0, size - 1)):
        stretch_plane(
            [out.at[c, n] for c in range(3)],
            [meshes[0].at[c, i] for c in range(3)],
            (low_rim, high_rim),
            [rim_start(meshes, 0, c, i) for c in range(3)],
            rows_of(i),
            (lambda c: after[c]) if i else rows_of(1),
            rows_of(size - 2) if i else (lambda c: before[c]),
        )


def stretch_kernel(chunks, tables, place, edges, ends, low_rim, high_rim, *refs):
    meshes, refs = refs[:2], refs[2:]
    velocity, vorticity, held, inner, omega, sems = refs[-6:]
    _, planes, cols, ny = velocity.shape
    spot = where_planes(chunks)
    talls = (edges, inner)
    sent = []

    def send(source, target):
        sent.append(pltpu.make_async_copy(source, target, sems.at[len(sent)]))
        sent[-1].start()

    def rows_of(z):
        n, i = spot[z]
        return lambda c, start=RIM: talls[n][c, i, start : start + cols]

    def send_velocity(which):
        for z in range(planes):
            n, i = spot[z]
            if n == which:
                send(talls[n].at[:, i, pl.ds(RIM, cols)], velocity.at[:, z])

    send_velocity(0)
    send(ends.at[:, 0], vorticity.at[:, 0])
    send(ends.at[:, 1], vorticity.at[:, planes - 1])
    gather_blocks(refs[:-6], held, place[1])
    for (c, z), value in planes_of(held, chunks[1], tables).items():
        hold(inner, c, spot[z][1], value)
    send_velocity(1)
    for z in range(1, planes - 1):
        which, i = spot[z]
        stretch_plane(
            [omega.at[c, z] for c in range(3)],
            [meshes[which].at[c, i] for c in range(3)],
            (low_rim, high_rim),
            [rim_start(meshes, which, c, i) for c in range(3)],
            rows_of(z),
            rows_of(z + 1),
            rows_of(z - 1),
        )
        send(omega.at[:, z], vorticity.at[:, z])
    for copy in sent:
        copy.wait()


VM = pl.BlockSpec(memory_space=pltpu.VMEM)
SM = pl.BlockSpec(memory_space=pltpu.SMEM)
AN = pl.BlockSpec(memory_space=pl.ANY)
HB = pl.BlockSpec(memory_space=pltpu.HBM)


def kept(values):
    return pltpu.with_memory_space_constraint(values, pltpu.HBM)


def loaded(kernel):
    def run(place, t_high, t_low, *refs):
        kernel((t_high, t_low), place, *refs)

    return run


def call(kernel, ins, outs, scratch=(), sems=0, micros=2.0, moved=None):
    extra = [pltpu.SemaphoreType.DMA((sems,))] if sems else []
    return pl.pallas_call(
        kernel,
        out_shape=[jax.ShapeDtypeStruct(shape, F32) for _, shape in outs],
        in_specs=[spec for spec, _ in ins],
        out_specs=[spec for spec, _ in outs],
        scratch_shapes=[pltpu.VMEM(shape, kind) for shape, kind in scratch] + extra,
        compiler_params=pltpu.CompilerParams(vmem_limit_bytes=VMEM),
        cost_estimate=pl.CostEstimate(
            flops=int(micros * 1.0e9),
            bytes_accessed=int(micros * 3.0e6) if moved is None else moved,
            transcendentals=0,
        ),
    )(*[value for _, value in ins])


def ring(axis, step):
    count = lax.axis_size(axis)
    return [(i, (i + step) % count) for i in range(count)]


def spread(axis):
    count = lax.axis_size(axis)
    return count <= 8 and count & (count - 1) == 0


def sent_shapes(axis, rows, width, whole=False):
    count = lax.axis_size(axis)
    return [(count, rows, width)] if whole or not spread(axis) else [(rows, width)] * count


def exchange(blocks, axis, start=0):
    if not spread(axis):
        return [lax.all_to_all(blocks[0], axis, split_axis=0, concat_axis=0, tiled=True)]
    count = lax.axis_size(axis)
    return [
        lax.ppermute(block, axis, [(i, i ^ k) for i in range(count)]) if k else block
        for k, block in zip(offset_order(count)[start:], blocks)
    ]


def on_device(strength, offsets, cell_index, migrate_count, ambient):
    _, planes, cols, ny = ambient.shape
    slabs, pencils = lax.axis_size("gz"), lax.axis_size("gx")
    nx, nz, rows = cols * pencils, planes * slabs, cols + RIM
    count = strength.shape[1]
    pair_count = planes // 2
    chunks = ((0, pair_count - 1), tuple(range(1, pair_count - 1)))
    widths = [3 * len(c) * LANES for c in chunks]
    block = nx // slabs

    y_ahead, y_back = [split_table(t) for t in y_tables(ny, pencils, 1.0 / (float(nx) * ny * nz))]
    x_ahead, x_back = [split_table(t) for t in x_tables(nx, cols, pencils, slabs)]
    place = jnp.stack([lax.axis_index("gz"), lax.axis_index("gx")]).astype(jnp.int32)
    here = (SM, place)

    packet, movers = call(
        packet_kernel,
        [
            (HB, kept(migrate_count.reshape(1, 2))),
            (HB, kept(strength)),
            (HB, kept(offsets)),
            (HB, kept(cell_index.reshape(1, count))),
        ],
        [(VM, (8, count)), (VM, (8, 2 * MIG))],
        [((1, 2), jnp.int32), ((1, count), jnp.int32)],
        sems=4,
        micros=1.0,
        moved=1000,
    )
    up1 = lax.ppermute(packet, "gz", ring("gz", -1))
    down1 = lax.ppermute(packet, "gz", ring("gz", 1))
    up2 = lax.ppermute(movers, "gz", ring("gz", -2))
    down2 = lax.ppermute(movers, "gz", ring("gz", 2))

    meshes, rims, parts = [None, None], [], [None, None]
    for n in (1, 0):
        chunk, width = chunks[n], widths[n]
        size = 2 * len(chunk)
        rim = (6 * size + (rims[0].shape[0] if rims else 0), ny)
        mesh, rim_high, rim_low, *part = call(
            functools.partial(deposit_kernel, chunk, len(rims)),
            [here]
            + [(VM, value) for value in (packet, up1, down1, up2, down2)]
            + [(VM, ambient), (VM, y_ahead[0]), (VM, y_ahead[1])]
            + [(VM, value) for value in rims],
            [(VM, (3, size, cols, ny)), (VM, rim), (VM, rim)]
            + [(VM, shape) for shape in sent_shapes("gx", rows, width)],
            [((3, size, rows, ny), F32), ((pencils, rows, width), F32)],
            micros=5.0,
        )
        meshes[n] = mesh
        rims = [rim_high, rim_low]
        parts[n] = exchange(part, "gx")
    low_rim = lax.ppermute(rims[0], "gx", ring("gx", 1))
    high_rim = lax.ppermute(rims[1], "gx", ring("gx", -1))

    tile = max(1, block // 4)
    data = [None, None]
    for n in (1, 0):
        chunk, part, width = chunks[n], parts[n], widths[n]
        shapes = sent_shapes("gz", block, width)
        part = call(
            functools.partial(x_ahead_kernel, len(shapes)),
            [here, (VM, x_ahead[0]), (VM, x_ahead[1])] + [(VM, p) for p in part],
            [(VM, shape) for shape in shapes],
            [((pencils, rows, width), F32), ((slabs, block, width), F32)],
        )
        (entered,) = call(
            functools.partial(enter_kernel, chunk, nz),
            [here] + [(VM, p) for p in exchange(part, "gz")],
            [(VM, (3, 2, 2 * len(chunk), slabs, tile, LANES))],
        )
        data[n] = entered
    data = call(
        functools.partial(curl_kernel, chunks, nx, ny),
        [here, (VM, low_rim), (VM, high_rim)] + [(VM, d) for d in data],
        [(VM, d.shape) for d in data],
        [((3, 2, nz, tile, LANES), F32)],
        micros=5.0,
    )
    plane = (3, cols, ny)
    tables = [(VM, t) for t in y_back]
    tall = [(3, 2 * len(chunk), cols + 2 * RIM, ny) for chunk in chunks]
    left = [
        call(
            functools.partial(leave_kernel, chunk, nz),
            [here, (VM, source)],
            [(VM, shape) for shape in sent_shapes("gz", block, width)],
            [(source.shape, F32)],
        )
        for chunk, source, width in zip(chunks, data, widths)
    ]

    def back(part, width, before=()):
        shapes = sent_shapes("gx", rows, width)
        part = call(
            loaded(functools.partial(x_back_kernel, len(shapes), len(before))),
            [here]
            + [(VM, t) for t in x_back]
            + [(AN, b) for b in before]
            + [(VM, p) for p in part],
            [(VM, shape) for shape in shapes],
            [((slabs, block, width), F32), ((pencils, rows, width), F32)],
        )
        return exchange(part, "gx")

    early = max(1, len(left[1]) - LATE)
    second = exchange(left[1][:early], "gz")
    parts = [back(exchange(left[0], "gz"), widths[0])]
    edges, first, last = call(
        loaded(functools.partial(edge_kernel, chunks[0])),
        [here] + tables + [(VM, p) for p in parts[0]],
        [(VM, tall[0]), (VM, plane), (VM, plane)],
        [((pencils, rows, widths[0]), F32)],
    )
    if early < len(left[1]):
        late = call(
            pass_kernel,
            [(AN, parts[0][0])] + [(AN, p) for p in second[1:]] + [(VM, p) for p in left[1][early:]],
            [(VM, p.shape) for p in left[1][early:]],
            micros=0.3,
        )
        second += exchange(late, "gz", early)
    parts.append(back(second, widths[1], [first]))
    after = lax.ppermute(first, "gz", ring("gz", -1))
    before = lax.ppermute(last, "gz", ring("gz", 1))
    (ends,) = call(
        functools.partial(ends_kernel, chunks),
        [(VM, v) for v in (edges, before, after, low_rim, high_rim, *meshes)],
        [(VM, (3, 2, cols, ny))],
    )
    return tuple(
        call(
            loaded(functools.partial(stretch_kernel, chunks)),
            [here]
            + tables
            + [(VM, v) for v in (edges, ends, low_rim, high_rim, *meshes)]
            + [(VM, p) for p in parts[1]],
            [(AN, ambient.shape), (AN, ambient.shape)],
            [
                ((pencils, rows, widths[1]), F32),
                (tall[1], F32),
                ((3, planes, cols, ny), F32),
            ],
            sems=2 * planes,
            micros=4.0,
        )
    )


def solution(mesh):
    placed = (
        P(None, ("gz", "gx")),
        P(None, ("gz", "gx")),
        P(("gz", "gx")),
        P("gz", "gx", None),
        P(None, "gz", "gx", None),
    )
    return jax.shard_map(
        on_device,
        mesh=mesh,
        in_specs=placed,
        out_specs=(P(None, "gz", "gx", None), P(None, "gz", "gx", None)),
        check_vma=False,
    )
```

```python
import functools
import math

import jax
import jax.numpy as jnp
import ml_dtypes
import numpy as np
from jax import lax
from jax.experimental import pallas as pl
from jax.experimental.pallas import tpu as pltpu
from jax.sharding import PartitionSpec as P

MIG = 64
LANES = 128
RIM = 8
LATE = 3
TIME_STEP = 0.25
VMEM = 24 * 1024 * 1024
F32 = jnp.float32
BF16 = jnp.bfloat16


def split_table(table):
    high = table.astype(np.float32).astype(ml_dtypes.bfloat16)
    low = (table - high.astype(np.float64)).astype(np.float32).astype(ml_dtypes.bfloat16)
    return high, low


def angles(rows, columns, extent):
    return 2.0 * np.pi * (np.multiply.outer(rows, columns) % extent) / extent


def y_tables(ny, pencils, scale):
    modes = ny // (2 * pencils)
    position = np.arange(ny)
    angle = angles(position, np.arange(ny // 2), ny)
    real, imag = np.cos(angle), -np.sin(angle)
    imag[:, 0] = 1.0 - 2.0 * (position % 2)
    weight = np.where(np.arange(ny // 2) == 0, 1.0, 2.0) * scale
    ahead = np.zeros((2, ny, pencils, 2, 2, modes))
    back = np.zeros((pencils, 2, 2, modes, 2, ny))
    for parity in range(2):
        for part, values in enumerate((real, imag)):
            ahead[parity, :, :, part, parity] = values.reshape(ny, pencils, modes)
            back[:, part, parity, :, parity] = (values * weight).T.reshape(pencils, modes, ny)
    return ahead.reshape(2 * ny, -1), back.reshape(-1, 2 * ny)


def wave_order(nx, slabs):
    half = nx // 2
    ahead = np.arange(half).reshape(slabs, 1, half // slabs)
    behind = np.where(ahead == 0, half, (nx - ahead) % nx)
    return np.concatenate([ahead, behind], axis=1).reshape(-1)


def x_tables(nx, cols, pencils, slabs):
    order = wave_order(nx, slabs)
    angle = angles(order, np.arange(nx), nx)
    ahead = np.concatenate([np.cos(angle), np.sin(angle)], axis=0)
    row = np.arange(cols + RIM)
    offset = np.where(row <= cols, row, -1)
    used = ((row <= cols) | (row == cols + RIM - 1)).astype(np.float64)
    place = (np.arange(pencils)[:, None] * cols + offset[None, :]) % nx
    angle = angles(place.reshape(-1), order, nx)
    mask = np.tile(used, pencils)[:, None]
    back = np.concatenate([np.cos(angle) * mask, np.sin(angle) * mask], axis=0)
    return ahead, back


def split(values):
    high = values.astype(BF16)
    return high, (values - high.astype(F32)).astype(BF16)


def dot(left, right):
    return jnp.dot(left, right, preferred_element_type=F32)


def table_left(high, low, values):
    v_high, v_low = split(values)
    return dot(high, v_high) + (dot(high, v_low) + dot(low, v_high))


def table_right(values, high, low):
    v_high, v_low = split(values)
    return dot(v_high, high) + (dot(v_low, high) + dot(v_high, low))


def lane_of():
    return lax.broadcasted_iota(jnp.int32, (1, LANES), 1)


def times_i(values):
    half = LANES // 2
    sign = jnp.where(lane_of() < half, -1.0, 1.0).astype(F32)
    return pltpu.roll(values, half, 1) * sign


def kernel_weight(distance):
    radius = jnp.abs(distance)
    near = 1.0 - 2.5 * radius * radius + 1.5 * radius * radius * radius
    far = 0.5 * (2.0 - radius) * (2.0 - radius) * (1.0 - radius)
    return jnp.where(radius < 1.0, near, jnp.where(radius < 2.0, far, 0.0))


def turned(value, wave, extent, sign):
    wave = wave % extent
    real, imag = value
    if wave == 0:
        return value
    if 2 * wave == extent:
        return -real, -imag
    if 4 * wave == extent:
        return (-imag, real) if sign > 0 else (imag, -real)
    if 4 * wave == 3 * extent:
        return (imag, -real) if sign > 0 else (-imag, real)
    a = math.cos(2.0 * math.pi * wave / extent)
    b = sign * math.sin(2.0 * math.pi * wave / extent)
    return real * a - imag * b, real * b + imag * a


def fft(values, sign):
    count = len(values)
    if count == 1:
        return values
    even, odd = fft(values[::2], sign), fft(values[1::2], sign)
    odd = [turned(v, k, count, sign) for k, v in enumerate(odd)]
    plus = [(a[0] + b[0], a[1] + b[1]) for a, b in zip(even, odd)]
    minus = [(a[0] - b[0], a[1] - b[1]) for a, b in zip(even, odd)]
    return plus + minus


def offset_order(count):
    if count < 4:
        return list(range(count))
    far, near = list(range(count // 2, count)), list(range(1, count // 2))
    order = [0]
    while far or near:
        order += far[:1] + near[:1]
        far, near = far[1:], near[1:]
    return order


def blocks_of(refs, at):
    if len(refs) == 1:
        return [(d, refs[0].at[d]) for d in range(refs[0].shape[0])]
    return [(at ^ k, ref) for k, ref in zip(offset_order(len(refs)), refs)]


def gather_blocks(refs, held, at):
    for d, ref in blocks_of(refs, at):
        held[d] = ref[...]


def packet_kernel(
    counts, strength, offsets, cells, packet, movers, near_counts, near_cells, sems
):
    copies = [
        pltpu.make_async_copy(counts, near_counts, sems.at[0]),
        pltpu.make_async_copy(cells, near_cells, sems.at[1]),
        pltpu.make_async_copy(strength, packet.at[pl.ds(0, 3)], sems.at[2]),
        pltpu.make_async_copy(offsets, packet.at[pl.ds(3, 3)], sems.at[3]),
    ]
    for copy in copies:
        copy.start()
    for copy in copies:
        copy.wait()
    slot = lax.broadcasted_iota(jnp.int32, (1, packet.shape[1]), 1)
    up = near_counts[0:1, 0:1]
    both = up + near_counts[0:1, 1:2]
    packet[6:7] = near_cells[...].astype(F32)
    packet[7:8] = jnp.where(slot < up, 1.0, jnp.where(slot < both, -1.0, 0.0))
    movers[...] = packet[:, : movers.shape[1]]


def deposit_kernel(
    pairs, rims_before, place, own, up1, down1, up2, down2, ambient, t_high, t_low, *refs
):
    rims, refs = refs[:rims_before], refs[rims_before:]
    mesh, rim_high, rim_low = refs[:3]
    total, made = refs[-2:]
    outs = refs[3:-2]
    _, planes, cols, ny = ambient.shape
    rows = cols + RIM
    movers = up2.shape[1]
    count = own.shape[1]
    listed = [2 * pair + parity for pair in pairs for parity in range(2)]

    def decode(ref, start, stop, shift):
        packet = ref[:, start:stop]
        cell = packet[6:7].astype(jnp.int32)
        move = packet[7:8].astype(jnp.int32)
        z_cell = lax.div(cell, cols * ny) + planes * (move + shift)
        x_cell = lax.rem(lax.div(cell, ny), cols)
        return packet[0:6], z_cell, x_cell, lax.rem(cell, ny)

    def joined(pieces):
        return [jnp.concatenate(p, axis=1) if len(p) > 1 else p[0] for p in zip(*pieces)]

    def add_block(pieces, wanted):
        values, z_cell, x_cell, y_cell = joined(pieces)
        width = values.shape[1]
        z_at = lax.broadcasted_iota(jnp.int32, (planes, width), 0)
        w_z = kernel_weight((z_at - z_cell).astype(F32) - values[3:4])
        row = lax.broadcasted_iota(jnp.int32, (rows, width), 0)
        x_at = jnp.where(row < cols + 2, row, jnp.where(row >= rows - 2, row - rows, 4 * rows))
        w_x = kernel_weight((x_at - x_cell).astype(F32) - values[4:5])
        y_at = lax.broadcasted_iota(jnp.int32, (ny, width), 0)
        y_off = lax.rem(y_at - y_cell + (ny + ny // 2), ny) - ny // 2
        w_y = kernel_weight(y_off.astype(F32) - values[5:6])
        y_high, y_low = split(w_y)
        right = jnp.concatenate([y_high, y_high, y_low], axis=1)
        at = [listed.index(z) for z in wanted]
        for c in range(3):
            s_z = values[c : c + 1] * w_z
            left = jnp.concatenate([s_z[z : z + 1] * w_x for z in wanted], axis=0)
            l_high, l_low = split(left)
            left = jnp.concatenate([l_high, l_low, l_high], axis=1)
            added = lax.dot_general(
                left, right, (((1,), (1,)), ((), ())), preferred_element_type=F32
            )
            total[c, at[0] : at[-1] + 1] += added.reshape(len(wanted), rows, ny)

    for n, z in enumerate(listed):
        total[:, n, 0:cols] = ambient[:, z]
    total[:, :, cols:rows] = jnp.zeros((3, len(listed), RIM, ny), F32)
    step = 256
    for at in range(0, count, step):
        add_block([decode(own, at, min(at + step, count), 0)], listed)
    add_block([decode(up1, 0, movers, 1), decode(down1, 0, movers, -1)], listed)
    sides = ((up1, up2, 1, (planes - 2, planes - 1)), (down1, down2, -1, (0, 1)))
    for near, far, shift, wanted in sides:
        if not set(wanted) <= set(listed):
            continue
        whole = [decode(near, movers, count, shift), decode(far, 0, movers, 2 * shift)]
        values, z_cell, x_cell, y_cell = joined(whole)
        for at in range(0, count, step):
            to = min(at + step, count)
            block = (values[:, at:to], z_cell[:, at:to], x_cell[:, at:to], y_cell[:, at:to])
            add_block([block], wanted)

    mesh[...] = total[:, :, 0:cols]
    at = 0
    if rims:
        at = rims[0].shape[0]
        rim_high[0:at] = rims[0][...]
        rim_low[0:at] = rims[1][...]
    for n in range(3 * len(listed)):
        c, i = n // len(listed), n % len(listed)
        rim_high[at + 2 * n : at + 2 * n + 2] = total[c, i, cols : cols + 2]
        rim_low[at + 2 * n : at + 2 * n + 2] = total[c, i, rows - 2 : rows]
    groups = [(c, 2 * n) for c in range(3) for n in range(len(pairs))]
    left = jnp.concatenate(
        [jnp.concatenate([total[c, n], total[c, n + 1]], axis=1) for c, n in groups], axis=0
    )
    wide = table_right(left, t_high[...], t_low[...])
    for n in range(len(groups)):
        for g in range(made.shape[0]):
            made[g, :, n * LANES : (n + 1) * LANES] = wide[
                n * rows : (n + 1) * rows, g * LANES : (g + 1) * LANES
            ]
    for d, out in blocks_of(outs, place[1]):
        out[...] = made[d]


def x_ahead_kernel(sends, place, t_high, t_low, *refs):
    held, made = refs[-2:]
    outs, parts = refs[-2 - sends : -2], refs[: -2 - sends]
    gather_blocks(parts, held, place[1])
    pencils, rows, width = held.shape
    cols = rows - RIM
    row = lax.broadcasted_iota(jnp.int32, (RIM, width), 0)
    pieces = []
    for h in range(pencils):
        from_low = held[(h - 1) % pencils, cols:rows]
        from_high = held[(h + 1) % pencils, cols:rows]
        pieces.append(held[h, 0:RIM] + jnp.where(row < 2, from_low, 0.0))
        pieces.append(held[h, RIM : cols - RIM])
        pieces.append(held[h, cols - RIM : cols] + jnp.where(row >= RIM - 2, from_high, 0.0))
    both = table_left(t_high[...], t_low[...], jnp.concatenate(pieces, axis=0))
    half = both.shape[0] // 2
    for n in range(width // LANES):
        lanes = slice(n * LANES, (n + 1) * LANES)
        value = both[:half, lanes] - times_i(both[half:, lanes])
        made[:, :, lanes] = value.reshape(made.shape[0], made.shape[1], LANES)
    for d, out in blocks_of(outs, place[0]):
        out[...] = made[d]


def x_back_kernel(sends, tables, place, *refs):
    held, made = refs[-2:]
    outs, parts = refs[-2 - sends : -2], refs[: -2 - sends]
    gather_blocks(parts, held, place[0])
    pencils, rows, width = made.shape
    both = table_left(tables[0][...], tables[1][...], held[...].reshape(-1, width))
    half = both.shape[0] // 2
    for n in range(width // LANES):
        lanes = slice(n * LANES, (n + 1) * LANES)
        value = both[:half, lanes] + times_i(both[half:, lanes])
        made[:, :, lanes] = value.reshape(pencils, rows, LANES)
    for d, out in blocks_of(outs, place[1]):
        out[...] = made[d]


def wave_lanes():
    lane = lane_of()
    return lane < LANES // 2, (lane // (LANES // 4)) % 2 == 0


def roll(values, shift):
    return pltpu.roll(values, shift, 1)


def cross_half(a, b):
    low, _ = wave_lanes()
    half = LANES // 2
    return jnp.where(low, a, roll(b, half)), jnp.where(low, roll(a, half), b)


def cross_quarter(a, b):
    _, first = wave_lanes()
    quarter = LANES // 4
    return (
        jnp.where(first, a, roll(b, quarter)),
        jnp.where(first, roll(a, LANES - quarter), b),
    )


def lanes_at(c, count, i):
    return pl.ds(pl.multiple_of((c * count + i) * LANES, LANES), LANES)


def enter_kernel(pairs, nz, place, *refs):
    parts, data = refs[:-1], refs[-1]
    _, _, _, slabs, tile, _ = data.shape

    def body(c, carry):
        for i, pair in enumerate(pairs):
            lanes = lanes_at(c, len(pairs), i)
            for s, ref in blocks_of(parts, place[0]):
                quad = [ref[q * tile : (q + 1) * tile, lanes] for q in range(4)]
                real0, imag0 = cross_half(quad[0], quad[2])
                real1, imag1 = cross_half(quad[1], quad[3])
                for part, (a, b) in enumerate(((real0, real1), (imag0, imag1))):
                    even, odd = cross_quarter(a, b)
                    data[c, part, 2 * i, s] = even
                    data[c, part, 2 * i + 1, s] = odd
            for parity in range(2):
                at = 2 * i + parity
                line = [(data[c, 0, at, s], data[c, 1, at, s]) for s in range(slabs)]
                for k, v in enumerate(fft(line, -1.0)):
                    v = turned(v, (2 * pair + parity) * k, nz, -1.0)
                    data[c, 0, at, k], data[c, 1, at, k] = v
        return carry

    lax.fori_loop(0, 3, body, 0)


def pass_kernel(before, *refs):
    for source, target in zip(refs[: len(refs) // 2], refs[len(refs) // 2 :]):
        target[...] = source[...]


def leave_kernel(pairs, nz, place, source, *refs):
    outs, data = refs[:-1], refs[-1]
    _, _, _, slabs, tile, _ = source.shape

    def body(c, carry):
        for i, pair in enumerate(pairs):
            lanes = lanes_at(c, len(pairs), i)
            for parity in range(2):
                at = 2 * i + parity
                line = [
                    turned(
                        (source[c, 0, at, k], source[c, 1, at, k]),
                        (2 * pair + parity) * k,
                        nz,
                        1.0,
                    )
                    for k in range(slabs)
                ]
                for s, v in enumerate(fft(line, 1.0)):
                    data[c, 0, at, s], data[c, 1, at, s] = v
            for s, ref in blocks_of(outs, place[0]):
                real0, real1 = cross_quarter(data[c, 0, 2 * i, s], data[c, 0, 2 * i + 1, s])
                imag0, imag1 = cross_quarter(data[c, 1, 2 * i, s], data[c, 1, 2 * i + 1, s])
                quad = [None] * 4
                quad[0], quad[2] = cross_half(real0, imag0)
                quad[1], quad[3] = cross_half(real1, imag1)
                for q in range(4):
                    ref[q * tile : (q + 1) * tile, lanes] = quad[q]
        return carry

    lax.fori_loop(0, 3, body, 0)


def curl_kernel(chunks, nx, ny, place, low_rim, high_rim, *refs):
    sources, outs = refs[: len(chunks)], refs[len(chunks) : 2 * len(chunks)]
    spectrum = refs[-1]
    _, _, nz, tile, _ = spectrum.shape
    slabs = sources[0].shape[3]
    planes = nz // slabs
    modes, half = LANES // 4, LANES // 2
    slab_at, pencil_at = place[0], place[1]
    spot = {}
    for n, chunk in enumerate(chunks):
        for i, pair in enumerate(chunk):
            spot[2 * pair], spot[2 * pair + 1] = (n, 2 * i), (n, 2 * i + 1)

    def across_planes(k, carry):
        for c in range(3):
            line = []
            for l in range(planes):
                n, i = spot[l]
                line.append((sources[n][c, 0, i, k], sources[n][c, 1, i, k]))
            for n, v in enumerate(fft(line, -1.0)):
                spectrum[c, 0, k + slabs * n], spectrum[c, 1, k + slabs * n] = v
        return carry

    reach = 2 * tile
    row = lax.broadcasted_iota(jnp.int32, (tile, LANES), 0)
    lane = lax.broadcasted_iota(jnp.int32, (tile, LANES), 1)
    number = slab_at * reach + (lane // modes) % 2 * tile + row
    ahead = lane < half
    mode = lane % modes + pencil_at * modes
    alone = number == 0
    number = number.astype(F32) * (2.0 * math.pi / nx)
    x_base = jnp.where(ahead, number, jnp.where(alone, math.pi, -number))
    x_trim = jnp.where(ahead, number, jnp.where(alone, 0.0, -number))
    wave_y = mode.astype(F32) * (2.0 * math.pi / ny)
    packed = mode == 0
    x_sq = x_base * x_base
    lateral = x_sq + wave_y * wave_y

    def curl_at(k, with_mirror):
        z_wave = jnp.where(k < nz // 2, k, k - nz).astype(F32) * (2.0 * math.pi / nz)
        z_trim = jnp.where(k == nz // 2, 0.0, z_wave)
        full = lateral + z_wave * z_wave
        empty = full == 0.0
        inverse = jnp.where(empty, 0.0, 1.0 / jnp.where(empty, 1.0, full))
        if with_mirror:
            other = 1.0 / (x_sq + (z_wave * z_wave + math.pi * math.pi))
            mirror = jnp.where(packed, 0.5 * (inverse - other), 0.0)
            inverse = jnp.where(packed, 0.5 * (inverse + other), inverse)
            opposite = lax.rem(nz - k, nz)
        stream = []
        for c in range(3):
            value = [spectrum[c, part, k] * inverse for part in range(2)]
            if with_mirror:
                for part, sign in enumerate((1.0, -1.0)):
                    there = spectrum[c, part, opposite]
                    there = jnp.where(alone, there, roll(there, half))
                    value[part] = value[part] + (mirror * sign) * there
            stream.append(value)
        made = []
        for part in range(2):
            s = [value[part] for value in stream]
            made.append(
                (
                    x_trim * s[2] - wave_y * s[1],
                    wave_y * s[0] - z_trim * s[2],
                    z_trim * s[1] - x_trim * s[0],
                )
            )
        return [(-made[1][c], made[0][c]) for c in range(3)]

    def curl_all(with_mirror):
        def body(k, carry):
            made = [curl_at(k + slabs * n, with_mirror) for n in range(planes)]
            for c in range(3):
                for l, v in enumerate(fft([m[c] for m in made], 1.0)):
                    n, i = spot[l]
                    outs[n][c, 0, i, k], outs[n][c, 1, i, k] = v
            return carry

        lax.fori_loop(0, slabs, body, 0)

    lax.fori_loop(0, slabs, across_planes, 0)

    @pl.when(pencil_at == 0)
    def _():
        curl_all(True)

    @pl.when(pencil_at != 0)
    def _():
        curl_all(False)


def planes_of(held, pairs, tables):
    pencils, rows, _ = held.shape
    groups = [(c, pair) for c in range(3) for pair in pairs]
    left = jnp.concatenate(
        [
            jnp.concatenate(
                [held[h, :, n * LANES : (n + 1) * LANES] for h in range(pencils)], axis=1
            )
            for n in range(len(groups))
        ],
        axis=0,
    )
    ny = tables[0].shape[1] // 2
    wide = table_right(left, tables[0][...], tables[1][...])
    made = {}
    for n, (c, pair) in enumerate(groups):
        for parity in range(2):
            made[c, 2 * pair + parity] = wide[
                n * rows : (n + 1) * rows, parity * ny : (parity + 1) * ny
            ]
    return made


def hold(tall, c, n, value):
    rows = value.shape[0]
    tall[c, n, RIM : RIM + rows] = value
    tall[c, n, 0:RIM] = value[rows - RIM : rows]


def edge_kernel(pairs, tables, place, *refs):
    tall, first, last, held = refs[-4:]
    gather_blocks(refs[:-4], held, place[1])
    listed = [2 * pair + parity for pair in pairs for parity in range(2)]
    cols = first.shape[1]
    values = planes_of(held, pairs, tables)
    for c in range(3):
        for n, z in enumerate(listed):
            hold(tall, c, n, values[c, z])
        first[c] = values[c, listed[0]][0:cols]
        last[c] = values[c, listed[-1]][0:cols]


def where_planes(chunks):
    spot = {}
    for n, chunk in enumerate(chunks):
        for i, pair in enumerate(chunk):
            spot[2 * pair], spot[2 * pair + 1] = (n, 2 * i), (n, 2 * i + 1)
    return spot


def rim_start(meshes, which, c, i):
    before = 6 * meshes[1].shape[1] if which == 0 else 0
    return before + 2 * (c * meshes[which].shape[1] + i)


def stretch_plane(out, mesh, rims, at, rows_of, above, below):
    cols, ny = out[0].shape
    low_rim, high_rim = rims
    for c in range(3):
        out[c][...] = mesh[c][...]
        out[c][0:2] += low_rim[at[c] : at[c] + 2]
        out[c][cols - 2 : cols] += high_rim[at[c] : at[c] + 2]
    omega = [ref[...] for ref in out]
    for c in range(3):
        value = rows_of(c, RIM)
        along_z = (above(c) - below(c)) * 0.5
        along_x = (rows_of(c, RIM + 1) - rows_of(c, RIM - 1)) * 0.5
        along_y = (pltpu.roll(value, ny - 1, 1) - pltpu.roll(value, 1, 1)) * 0.5
        stretch = omega[0] * along_z + omega[1] * along_x + omega[2] * along_y
        out[c][...] = omega[c] + TIME_STEP * stretch


def ends_kernel(_, edges, before, after, low_rim, high_rim, *refs):
    meshes, vorticity, out, sems = refs[:-3], refs[-3], refs[-2], refs[-1]
    cols = before.shape[1]
    size = edges.shape[1]
    copies = []

    def rows_of(i):
        return lambda c, start=RIM: edges[c, i, start : start + cols]

    for n, i in enumerate((0, size - 1)):
        stretch_plane(
            [out.at[c, n] for c in range(3)],
            [meshes[0].at[c, i] for c in range(3)],
            (low_rim, high_rim),
            [rim_start(meshes, 0, c, i) for c in range(3)],
            rows_of(i),
            (lambda c: after[c]) if i else rows_of(1),
            rows_of(size - 2) if i else (lambda c: before[c]),
        )
        copies.append(
            pltpu.make_async_copy(
                out.at[:, n], vorticity.at[:, n * (vorticity.shape[1] - 1)], sems.at[n]
            )
        )
        copies[-1].start()
    for copy in copies:
        copy.wait()


def stretch_kernel(chunks, tables, place, edges, low_rim, high_rim, *refs):
    meshes, refs = refs[:2], refs[2:]
    velocity, vorticity, held, inner, omega, sems = refs[-6:]
    _, planes, cols, ny = velocity.shape
    spot = where_planes(chunks)
    talls = (edges, inner)
    sent = []

    def send(source, target):
        sent.append(pltpu.make_async_copy(source, target, sems.at[len(sent)]))
        sent[-1].start()

    def rows_of(z):
        n, i = spot[z]
        return lambda c, start=RIM: talls[n][c, i, start : start + cols]

    def send_velocity(which):
        for z in range(planes):
            n, i = spot[z]
            if n == which:
                send(talls[n].at[:, i, pl.ds(RIM, cols)], velocity.at[:, z])

    send_velocity(0)
    gather_blocks(refs[:-6], held, place[1])
    for (c, z), value in planes_of(held, chunks[1], tables).items():
        hold(inner, c, spot[z][1], value)
    send_velocity(1)
    for z in range(1, planes - 1):
        which, i = spot[z]
        stretch_plane(
            [omega.at[c, z] for c in range(3)],
            [meshes[which].at[c, i] for c in range(3)],
            (low_rim, high_rim),
            [rim_start(meshes, which, c, i) for c in range(3)],
            rows_of(z),
            rows_of(z + 1),
            rows_of(z - 1),
        )
        send(omega.at[:, z], vorticity.at[:, z])
    for copy in sent:
        copy.wait()


VM = pl.BlockSpec(memory_space=pltpu.VMEM)
SM = pl.BlockSpec(memory_space=pltpu.SMEM)
AN = pl.BlockSpec(memory_space=pl.ANY)
HB = pl.BlockSpec(memory_space=pltpu.HBM)


def kept(values):
    return pltpu.with_memory_space_constraint(values, pltpu.HBM)


def loaded(kernel):
    def run(place, t_high, t_low, *refs):
        kernel((t_high, t_low), place, *refs)

    return run


def call(kernel, ins, outs, scratch=(), sems=0, micros=2.0, moved=None, aliases=None):
    extra = [pltpu.SemaphoreType.DMA((sems,))] if sems else []
    return pl.pallas_call(
        kernel,
        out_shape=[jax.ShapeDtypeStruct(shape, F32) for _, shape in outs],
        in_specs=[spec for spec, _ in ins],
        out_specs=[spec for spec, _ in outs],
        scratch_shapes=[pltpu.VMEM(shape, kind) for shape, kind in scratch] + extra,
        compiler_params=pltpu.CompilerParams(vmem_limit_bytes=VMEM),
        input_output_aliases=aliases or {},
        cost_estimate=pl.CostEstimate(
            flops=int(micros * 1.0e9),
            bytes_accessed=int(micros * 3.0e6) if moved is None else moved,
            transcendentals=0,
        ),
    )(*[value for _, value in ins])


def ring(axis, step):
    count = lax.axis_size(axis)
    return [(i, (i + step) % count) for i in range(count)]


def spread(axis):
    count = lax.axis_size(axis)
    return count <= 8 and count & (count - 1) == 0


def sent_shapes(axis, rows, width, whole=False):
    count = lax.axis_size(axis)
    return [(count, rows, width)] if whole or not spread(axis) else [(rows, width)] * count


def exchange(blocks, axis, start=0):
    if not spread(axis):
        return [lax.all_to_all(blocks[0], axis, split_axis=0, concat_axis=0, tiled=True)]
    count = lax.axis_size(axis)
    return [
        lax.ppermute(block, axis, [(i, i ^ k) for i in range(count)]) if k else block
        for k, block in zip(offset_order(count)[start:], blocks)
    ]


def on_device(strength, offsets, cell_index, migrate_count, ambient):
    _, planes, cols, ny = ambient.shape
    slabs, pencils = lax.axis_size("gz"), lax.axis_size("gx")
    nx, nz, rows = cols * pencils, planes * slabs, cols + RIM
    count = strength.shape[1]
    pair_count = planes // 2
    chunks = ((0, pair_count - 1), tuple(range(1, pair_count - 1)))
    widths = [3 * len(c) * LANES for c in chunks]
    block = nx // slabs

    y_ahead, y_back = [split_table(t) for t in y_tables(ny, pencils, 1.0 / (float(nx) * ny * nz))]
    x_ahead, x_back = [split_table(t) for t in x_tables(nx, cols, pencils, slabs)]
    place = jnp.stack([lax.axis_index("gz"), lax.axis_index("gx")]).astype(jnp.int32)
    here = (SM, place)

    packet, movers = call(
        packet_kernel,
        [
            (HB, kept(migrate_count.reshape(1, 2))),
            (HB, kept(strength)),
            (HB, kept(offsets)),
            (HB, kept(cell_index.reshape(1, count))),
        ],
        [(VM, (8, count)), (VM, (8, 2 * MIG))],
        [((1, 2), jnp.int32), ((1, count), jnp.int32)],
        sems=4,
        micros=1.0,
        moved=1000,
    )
    up1 = lax.ppermute(packet, "gz", ring("gz", -1))
    down1 = lax.ppermute(packet, "gz", ring("gz", 1))
    up2 = lax.ppermute(movers, "gz", ring("gz", -2))
    down2 = lax.ppermute(movers, "gz", ring("gz", 2))

    meshes, rims, parts = [None, None], [], [None, None]
    for n in (1, 0):
        chunk, width = chunks[n], widths[n]
        size = 2 * len(chunk)
        rim = (6 * size + (rims[0].shape[0] if rims else 0), ny)
        mesh, rim_high, rim_low, *part = call(
            functools.partial(deposit_kernel, chunk, len(rims)),
            [here]
            + [(VM, value) for value in (packet, up1, down1, up2, down2)]
            + [(VM, ambient), (VM, y_ahead[0]), (VM, y_ahead[1])]
            + [(VM, value) for value in rims],
            [(VM, (3, size, cols, ny)), (VM, rim), (VM, rim)]
            + [(VM, shape) for shape in sent_shapes("gx", rows, width)],
            [((3, size, rows, ny), F32), ((pencils, rows, width), F32)],
            micros=5.0,
        )
        meshes[n] = mesh
        rims = [rim_high, rim_low]
        parts[n] = exchange(part, "gx")
    low_rim = lax.ppermute(rims[0], "gx", ring("gx", 1))
    high_rim = lax.ppermute(rims[1], "gx", ring("gx", -1))

    tile = max(1, block // 4)
    data = [None, None]
    for n in (1, 0):
        chunk, part, width = chunks[n], parts[n], widths[n]
        shapes = sent_shapes("gz", block, width)
        part = call(
            functools.partial(x_ahead_kernel, len(shapes)),
            [here, (VM, x_ahead[0]), (VM, x_ahead[1])] + [(VM, p) for p in part],
            [(VM, shape) for shape in shapes],
            [((pencils, rows, width), F32), ((slabs, block, width), F32)],
        )
        (entered,) = call(
            functools.partial(enter_kernel, chunk, nz),
            [here] + [(VM, p) for p in exchange(part, "gz")],
            [(VM, (3, 2, 2 * len(chunk), slabs, tile, LANES))],
        )
        data[n] = entered
    data = call(
        functools.partial(curl_kernel, chunks, nx, ny),
        [here, (VM, low_rim), (VM, high_rim)] + [(VM, d) for d in data],
        [(VM, d.shape) for d in data],
        [((3, 2, nz, tile, LANES), F32)],
        micros=5.0,
    )
    plane = (3, cols, ny)
    tables = [(VM, t) for t in y_back]
    tall = [(3, 2 * len(chunk), cols + 2 * RIM, ny) for chunk in chunks]
    left = [
        call(
            functools.partial(leave_kernel, chunk, nz),
            [here, (VM, source)],
            [(VM, shape) for shape in sent_shapes("gz", block, width)],
            [(source.shape, F32)],
        )
        for chunk, source, width in zip(chunks, data, widths)
    ]

    def back(part, width):
        shapes = sent_shapes("gx", rows, width)
        part = call(
            loaded(functools.partial(x_back_kernel, len(shapes))),
            [here]
            + [(VM, t) for t in x_back]
            + [(VM, p) for p in part],
            [(VM, shape) for shape in shapes],
            [((slabs, block, width), F32), ((pencils, rows, width), F32)],
        )
        return exchange(part, "gx")

    early = max(1, len(left[1]) - LATE)
    second = exchange(left[1][:early], "gz")
    parts = [back(exchange(left[0], "gz"), widths[0])]
    edges, first, last = call(
        loaded(functools.partial(edge_kernel, chunks[0])),
        [here] + tables + [(VM, p) for p in parts[0]],
        [(VM, tall[0]), (VM, plane), (VM, plane)],
        [((pencils, rows, widths[0]), F32)],
    )
    if early < len(left[1]):
        late = call(
            pass_kernel,
            [(AN, parts[0][0])] + [(VM, p) for p in left[1][early:]],
            [(VM, p.shape) for p in left[1][early:]],
            micros=0.3,
        )
        second += exchange(late, "gz", early)
    parts.append(back(second, widths[1]))
    after = lax.ppermute(first, "gz", ring("gz", -1))
    before = lax.ppermute(last, "gz", ring("gz", 1))
    velocity, vorticity = call(
        loaded(functools.partial(stretch_kernel, chunks)),
        [here]
        + tables
        + [(VM, v) for v in (edges, low_rim, high_rim, *meshes)]
        + [(VM, p) for p in parts[1]],
        [(AN, ambient.shape), (AN, ambient.shape)],
        [
            ((pencils, rows, widths[1]), F32),
            (tall[1], F32),
            ((3, planes, cols, ny), F32),
        ],
        sems=2 * planes,
        micros=4.0,
    )
    (vorticity,) = call(
        ends_kernel,
        [(AN, vorticity)]
        + [(VM, v) for v in (edges, before, after, low_rim, high_rim, *meshes)],
        [(AN, ambient.shape)],
        [((3, 2, cols, ny), F32)],
        sems=2,
        micros=1.0,
        aliases={0: 0},
    )
    return velocity, vorticity


def solution(mesh):
    placed = (
        P(None, ("gz", "gx")),
        P(None, ("gz", "gx")),
        P(("gz", "gx")),
        P("gz", "gx", None),
        P(None, "gz", "gx", None),
    )
    return jax.shard_map(
        on_device,
        mesh=mesh,
        in_specs=placed,
        out_specs=(P(None, "gz", "gx", None), P(None, "gz", "gx", None)),
        check_vma=False,
    )
```

```python
import functools
import math

import jax
import jax.numpy as jnp
import ml_dtypes
import numpy as np
from jax import lax
from jax.experimental import pallas as pl
from jax.experimental.pallas import tpu as pltpu
from jax.sharding import PartitionSpec as P

MIG = 64
LANES = 128
RIM = 8
LATE = 3
TIME_STEP = 0.25
VMEM = 24 * 1024 * 1024
F32 = jnp.float32
BF16 = jnp.bfloat16


def split_table(table):
    high = table.astype(np.float32).astype(ml_dtypes.bfloat16)
    low = (table - high.astype(np.float64)).astype(np.float32).astype(ml_dtypes.bfloat16)
    return high, low


def angles(rows, columns, extent):
    return 2.0 * np.pi * (np.multiply.outer(rows, columns) % extent) / extent


def y_tables(ny, pencils, scale):
    modes = ny // (2 * pencils)
    position = np.arange(ny)
    angle = angles(position, np.arange(ny // 2), ny)
    real, imag = np.cos(angle), -np.sin(angle)
    imag[:, 0] = 1.0 - 2.0 * (position % 2)
    weight = np.where(np.arange(ny // 2) == 0, 1.0, 2.0) * scale
    ahead = np.zeros((2, ny, pencils, 2, 2, modes))
    back = np.zeros((pencils, 2, 2, modes, 2, ny))
    for parity in range(2):
        for part, values in enumerate((real, imag)):
            ahead[parity, :, :, part, parity] = values.reshape(ny, pencils, modes)
            back[:, part, parity, :, parity] = (values * weight).T.reshape(pencils, modes, ny)
    return ahead.reshape(2 * ny, -1), back.reshape(-1, 2 * ny)


def wave_order(nx, slabs):
    half = nx // 2
    ahead = np.arange(half).reshape(slabs, 1, half // slabs)
    behind = np.where(ahead == 0, half, (nx - ahead) % nx)
    return np.concatenate([ahead, behind], axis=1).reshape(-1)


def x_tables(nx, cols, pencils, slabs):
    order = wave_order(nx, slabs)
    angle = angles(order, np.arange(nx), nx)
    ahead = np.concatenate([np.cos(angle), np.sin(angle)], axis=0)
    row = np.arange(cols + RIM)
    offset = np.where(row <= cols, row, -1)
    used = ((row <= cols) | (row == cols + RIM - 1)).astype(np.float64)
    place = (np.arange(pencils)[:, None] * cols + offset[None, :]) % nx
    angle = angles(place.reshape(-1), order, nx)
    mask = np.tile(used, pencils)[:, None]
    back = np.concatenate([np.cos(angle) * mask, np.sin(angle) * mask], axis=0)
    return ahead, back


def split(values):
    high = values.astype(BF16)
    return high, (values - high.astype(F32)).astype(BF16)


def dot(left, right):
    return jnp.dot(left, right, preferred_element_type=F32)


def table_left(high, low, values):
    v_high, v_low = split(values)
    return dot(high, v_high) + (dot(high, v_low) + dot(low, v_high))


def table_right(values, high, low):
    v_high, v_low = split(values)
    return dot(v_high, high) + (dot(v_low, high) + dot(v_high, low))


def lane_of():
    return lax.broadcasted_iota(jnp.int32, (1, LANES), 1)


def times_i(values):
    half = LANES // 2
    sign = jnp.where(lane_of() < half, -1.0, 1.0).astype(F32)
    return pltpu.roll(values, half, 1) * sign


def kernel_weight(distance):
    radius = jnp.abs(distance)
    near = 1.0 - 2.5 * radius * radius + 1.5 * radius * radius * radius
    far = 0.5 * (2.0 - radius) * (2.0 - radius) * (1.0 - radius)
    return jnp.where(radius < 1.0, near, jnp.where(radius < 2.0, far, 0.0))


def turned(value, wave, extent, sign):
    wave = wave % extent
    real, imag = value
    if wave == 0:
        return value
    if 2 * wave == extent:
        return -real, -imag
    if 4 * wave == extent:
        return (-imag, real) if sign > 0 else (imag, -real)
    if 4 * wave == 3 * extent:
        return (imag, -real) if sign > 0 else (-imag, real)
    a = math.cos(2.0 * math.pi * wave / extent)
    b = sign * math.sin(2.0 * math.pi * wave / extent)
    return real * a - imag * b, real * b + imag * a


def fft(values, sign):
    count = len(values)
    if count == 1:
        return values
    even, odd = fft(values[::2], sign), fft(values[1::2], sign)
    odd = [turned(v, k, count, sign) for k, v in enumerate(odd)]
    plus = [(a[0] + b[0], a[1] + b[1]) for a, b in zip(even, odd)]
    minus = [(a[0] - b[0], a[1] - b[1]) for a, b in zip(even, odd)]
    return plus + minus


def offset_order(count):
    if count < 4:
        return list(range(count))
    far, near = list(range(count // 2, count)), list(range(1, count // 2))
    order = [0]
    while far or near:
        order += far[:1] + near[:1]
        far, near = far[1:], near[1:]
    return order


def blocks_of(refs, at):
    if len(refs) == 1:
        return [(d, refs[0].at[d]) for d in range(refs[0].shape[0])]
    return [(at ^ k, ref) for k, ref in zip(offset_order(len(refs)), refs)]


def gather_blocks(refs, held, at):
    for d, ref in blocks_of(refs, at):
        held[d] = ref[...]


def packet_kernel(
    counts, strength, offsets, cells, packet, movers, near_counts, near_cells, sems
):
    copies = [
        pltpu.make_async_copy(counts, near_counts, sems.at[0]),
        pltpu.make_async_copy(cells, near_cells, sems.at[1]),
        pltpu.make_async_copy(strength, packet.at[pl.ds(0, 3)], sems.at[2]),
        pltpu.make_async_copy(offsets, packet.at[pl.ds(3, 3)], sems.at[3]),
    ]
    for copy in copies:
        copy.start()
    for copy in copies:
        copy.wait()
    slot = lax.broadcasted_iota(jnp.int32, (1, packet.shape[1]), 1)
    up = near_counts[0:1, 0:1]
    both = up + near_counts[0:1, 1:2]
    packet[6:7] = near_cells[...].astype(F32)
    packet[7:8] = jnp.where(slot < up, 1.0, jnp.where(slot < both, -1.0, 0.0))
    movers[...] = packet[:, : movers.shape[1]]


def deposit_kernel(
    pairs, rims_before, place, own, up1, down1, up2, down2, ambient, t_high, t_low, *refs
):
    rims, refs = refs[:rims_before], refs[rims_before:]
    mesh, rim_high, rim_low = refs[:3]
    total, made = refs[-2:]
    outs = refs[3:-2]
    _, planes, cols, ny = ambient.shape
    rows = cols + RIM
    movers = up2.shape[1]
    count = own.shape[1]
    listed = [2 * pair + parity for pair in pairs for parity in range(2)]

    def decode(ref, start, stop, shift):
        packet = ref[:, start:stop]
        cell = packet[6:7].astype(jnp.int32)
        move = packet[7:8].astype(jnp.int32)
        z_cell = lax.div(cell, cols * ny) + planes * (move + shift)
        x_cell = lax.rem(lax.div(cell, ny), cols)
        return packet[0:6], z_cell, x_cell, lax.rem(cell, ny)

    def joined(pieces):
        return [jnp.concatenate(p, axis=1) if len(p) > 1 else p[0] for p in zip(*pieces)]

    def add_block(pieces, wanted):
        values, z_cell, x_cell, y_cell = joined(pieces)
        width = values.shape[1]
        z_at = lax.broadcasted_iota(jnp.int32, (planes, width), 0)
        w_z = kernel_weight((z_at - z_cell).astype(F32) - values[3:4])
        row = lax.broadcasted_iota(jnp.int32, (rows, width), 0)
        x_at = jnp.where(row < cols + 2, row, jnp.where(row >= rows - 2, row - rows, 4 * rows))
        w_x = kernel_weight((x_at - x_cell).astype(F32) - values[4:5])
        y_at = lax.broadcasted_iota(jnp.int32, (ny, width), 0)
        y_off = lax.rem(y_at - y_cell + (ny + ny // 2), ny) - ny // 2
        w_y = kernel_weight(y_off.astype(F32) - values[5:6])
        y_high, y_low = split(w_y)
        right = jnp.concatenate([y_high, y_high, y_low], axis=1)
        at = [listed.index(z) for z in wanted]
        for c in range(3):
            s_z = values[c : c + 1] * w_z
            left = jnp.concatenate([s_z[z : z + 1] * w_x for z in wanted], axis=0)
            l_high, l_low = split(left)
            left = jnp.concatenate([l_high, l_low, l_high], axis=1)
            added = lax.dot_general(
                left, right, (((1,), (1,)), ((), ())), preferred_element_type=F32
            )
            total[c, at[0] : at[-1] + 1] += added.reshape(len(wanted), rows, ny)

    for n, z in enumerate(listed):
        total[:, n, 0:cols] = ambient[:, z]
    total[:, :, cols:rows] = jnp.zeros((3, len(listed), RIM, ny), F32)
    step = 256
    for at in range(0, count, step):
        add_block([decode(own, at, min(at + step, count), 0)], listed)
    add_block([decode(up1, 0, movers, 1), decode(down1, 0, movers, -1)], listed)
    sides = ((up1, up2, 1, (planes - 2, planes - 1)), (down1, down2, -1, (0, 1)))
    for near, far, shift, wanted in sides:
        if not set(wanted) <= set(listed):
            continue
        whole = [decode(near, movers, count, shift), decode(far, 0, movers, 2 * shift)]
        values, z_cell, x_cell, y_cell = joined(whole)
        for at in range(0, count, step):
            to = min(at + step, count)
            block = (values[:, at:to], z_cell[:, at:to], x_cell[:, at:to], y_cell[:, at:to])
            add_block([block], wanted)

    mesh[...] = total[:, :, 0:cols]
    at = 0
    if rims:
        at = rims[0].shape[0]
        rim_high[0:at] = rims[0][...]
        rim_low[0:at] = rims[1][...]
    for n in range(3 * len(listed)):
        c, i = n // len(listed), n % len(listed)
        rim_high[at + 2 * n : at + 2 * n + 2] = total[c, i, cols : cols + 2]
        rim_low[at + 2 * n : at + 2 * n + 2] = total[c, i, rows - 2 : rows]
    groups = [(c, 2 * n) for c in range(3) for n in range(len(pairs))]
    left = jnp.concatenate(
        [jnp.concatenate([total[c, n], total[c, n + 1]], axis=1) for c, n in groups], axis=0
    )
    wide = table_right(left, t_high[...], t_low[...])
    for n in range(len(groups)):
        for g in range(made.shape[0]):
            made[g, :, n * LANES : (n + 1) * LANES] = wide[
                n * rows : (n + 1) * rows, g * LANES : (g + 1) * LANES
            ]
    for d, out in blocks_of(outs, place[1]):
        out[...] = made[d]


def x_ahead_kernel(sends, passed, place, t_high, t_low, *refs):
    held, made = refs[-2:]
    outs, parts = refs[-2 - sends : -2], refs[passed : -2 - sends]
    gather_blocks(parts, held, place[1])
    pencils, rows, width = held.shape
    cols = rows - RIM
    row = lax.broadcasted_iota(jnp.int32, (RIM, width), 0)
    pieces = []
    for h in range(pencils):
        from_low = held[(h - 1) % pencils, cols:rows]
        from_high = held[(h + 1) % pencils, cols:rows]
        pieces.append(held[h, 0:RIM] + jnp.where(row < 2, from_low, 0.0))
        pieces.append(held[h, RIM : cols - RIM])
        pieces.append(held[h, cols - RIM : cols] + jnp.where(row >= RIM - 2, from_high, 0.0))
    both = table_left(t_high[...], t_low[...], jnp.concatenate(pieces, axis=0))
    half = both.shape[0] // 2
    for n in range(width // LANES):
        lanes = slice(n * LANES, (n + 1) * LANES)
        value = both[:half, lanes] - times_i(both[half:, lanes])
        made[:, :, lanes] = value.reshape(made.shape[0], made.shape[1], LANES)
    for d, out in blocks_of(outs, place[0]):
        out[...] = made[d]


def x_back_kernel(sends, tables, place, *refs):
    held, made = refs[-2:]
    outs, parts = refs[-2 - sends : -2], refs[: -2 - sends]
    gather_blocks(parts, held, place[0])
    pencils, rows, width = made.shape
    both = table_left(tables[0][...], tables[1][...], held[...].reshape(-1, width))
    half = both.shape[0] // 2
    for n in range(width // LANES):
        lanes = slice(n * LANES, (n + 1) * LANES)
        value = both[:half, lanes] + times_i(both[half:, lanes])
        made[:, :, lanes] = value.reshape(pencils, rows, LANES)
    for d, out in blocks_of(outs, place[1]):
        out[...] = made[d]


def wave_lanes():
    lane = lane_of()
    return lane < LANES // 2, (lane // (LANES // 4)) % 2 == 0


def roll(values, shift):
    return pltpu.roll(values, shift, 1)


def cross_half(a, b):
    low, _ = wave_lanes()
    half = LANES // 2
    return jnp.where(low, a, roll(b, half)), jnp.where(low, roll(a, half), b)


def cross_quarter(a, b):
    _, first = wave_lanes()
    quarter = LANES // 4
    return (
        jnp.where(first, a, roll(b, quarter)),
        jnp.where(first, roll(a, LANES - quarter), b),
    )


def lanes_at(c, count, i):
    return pl.ds(pl.multiple_of((c * count + i) * LANES, LANES), LANES)


def enter_kernel(pairs, nz, place, *refs):
    parts, data = refs[:-1], refs[-1]
    _, _, _, slabs, tile, _ = data.shape

    def body(c, carry):
        for i, pair in enumerate(pairs):
            lanes = lanes_at(c, len(pairs), i)
            for s, ref in blocks_of(parts, place[0]):
                quad = [ref[q * tile : (q + 1) * tile, lanes] for q in range(4)]
                real0, imag0 = cross_half(quad[0], quad[2])
                real1, imag1 = cross_half(quad[1], quad[3])
                for part, (a, b) in enumerate(((real0, real1), (imag0, imag1))):
                    even, odd = cross_quarter(a, b)
                    data[c, part, 2 * i, s] = even
                    data[c, part, 2 * i + 1, s] = odd
            for parity in range(2):
                at = 2 * i + parity
                line = [(data[c, 0, at, s], data[c, 1, at, s]) for s in range(slabs)]
                for k, v in enumerate(fft(line, -1.0)):
                    v = turned(v, (2 * pair + parity) * k, nz, -1.0)
                    data[c, 0, at, k], data[c, 1, at, k] = v
        return carry

    lax.fori_loop(0, 3, body, 0)


def pass_kernel(before, *refs):
    for source, target in zip(refs[: len(refs) // 2], refs[len(refs) // 2 :]):
        target[...] = source[...]


def leave_kernel(pairs, nz, place, source, *refs):
    outs, data = refs[:-1], refs[-1]
    _, _, _, slabs, tile, _ = source.shape

    def body(c, carry):
        for i, pair in enumerate(pairs):
            lanes = lanes_at(c, len(pairs), i)
            for parity in range(2):
                at = 2 * i + parity
                line = [
                    turned(
                        (source[c, 0, at, k], source[c, 1, at, k]),
                        (2 * pair + parity) * k,
                        nz,
                        1.0,
                    )
                    for k in range(slabs)
                ]
                for s, v in enumerate(fft(line, 1.0)):
                    data[c, 0, at, s], data[c, 1, at, s] = v
            for s, ref in blocks_of(outs, place[0]):
                real0, real1 = cross_quarter(data[c, 0, 2 * i, s], data[c, 0, 2 * i + 1, s])
                imag0, imag1 = cross_quarter(data[c, 1, 2 * i, s], data[c, 1, 2 * i + 1, s])
                quad = [None] * 4
                quad[0], quad[2] = cross_half(real0, imag0)
                quad[1], quad[3] = cross_half(real1, imag1)
                for q in range(4):
                    ref[q * tile : (q + 1) * tile, lanes] = quad[q]
        return carry

    lax.fori_loop(0, 3, body, 0)


def curl_kernel(chunks, nx, ny, place, low_rim, high_rim, *refs):
    sources, outs = refs[: len(chunks)], refs[len(chunks) : 2 * len(chunks)]
    spectrum = refs[-1]
    _, _, nz, tile, _ = spectrum.shape
    slabs = sources[0].shape[3]
    planes = nz // slabs
    modes, half = LANES // 4, LANES // 2
    slab_at, pencil_at = place[0], place[1]
    spot = {}
    for n, chunk in enumerate(chunks):
        for i, pair in enumerate(chunk):
            spot[2 * pair], spot[2 * pair + 1] = (n, 2 * i), (n, 2 * i + 1)

    def across_planes(k, carry):
        for c in range(3):
            line = []
            for l in range(planes):
                n, i = spot[l]
                line.append((sources[n][c, 0, i, k], sources[n][c, 1, i, k]))
            for n, v in enumerate(fft(line, -1.0)):
                spectrum[c, 0, k + slabs * n], spectrum[c, 1, k + slabs * n] = v
        return carry

    reach = 2 * tile
    row = lax.broadcasted_iota(jnp.int32, (tile, LANES), 0)
    lane = lax.broadcasted_iota(jnp.int32, (tile, LANES), 1)
    number = slab_at * reach + (lane // modes) % 2 * tile + row
    ahead = lane < half
    mode = lane % modes + pencil_at * modes
    alone = number == 0
    number = number.astype(F32) * (2.0 * math.pi / nx)
    x_base = jnp.where(ahead, number, jnp.where(alone, math.pi, -number))
    x_trim = jnp.where(ahead, number, jnp.where(alone, 0.0, -number))
    wave_y = mode.astype(F32) * (2.0 * math.pi / ny)
    packed = mode == 0
    x_sq = x_base * x_base
    lateral = x_sq + wave_y * wave_y

    def curl_at(k, with_mirror):
        z_wave = jnp.where(k < nz // 2, k, k - nz).astype(F32) * (2.0 * math.pi / nz)
        z_trim = jnp.where(k == nz // 2, 0.0, z_wave)
        full = lateral + z_wave * z_wave
        empty = full == 0.0
        inverse = jnp.where(empty, 0.0, 1.0 / jnp.where(empty, 1.0, full))
        if with_mirror:
            other = 1.0 / (x_sq + (z_wave * z_wave + math.pi * math.pi))
            mirror = jnp.where(packed, 0.5 * (inverse - other), 0.0)
            inverse = jnp.where(packed, 0.5 * (inverse + other), inverse)
            opposite = lax.rem(nz - k, nz)
        stream = []
        for c in range(3):
            value = [spectrum[c, part, k] * inverse for part in range(2)]
            if with_mirror:
                for part, sign in enumerate((1.0, -1.0)):
                    there = spectrum[c, part, opposite]
                    there = jnp.where(alone, there, roll(there, half))
                    value[part] = value[part] + (mirror * sign) * there
            stream.append(value)
        made = []
        for part in range(2):
            s = [value[part] for value in stream]
            made.append(
                (
                    x_trim * s[2] - wave_y * s[1],
                    wave_y * s[0] - z_trim * s[2],
                    z_trim * s[1] - x_trim * s[0],
                )
            )
        return [(-made[1][c], made[0][c]) for c in range(3)]

    def curl_all(with_mirror):
        def body(k, carry):
            made = [curl_at(k + slabs * n, with_mirror) for n in range(planes)]
            for c in range(3):
                for l, v in enumerate(fft([m[c] for m in made], 1.0)):
                    n, i = spot[l]
                    outs[n][c, 0, i, k], outs[n][c, 1, i, k] = v
            return carry

        lax.fori_loop(0, slabs, body, 0)

    lax.fori_loop(0, slabs, across_planes, 0)

    @pl.when(pencil_at == 0)
    def _():
        curl_all(True)

    @pl.when(pencil_at != 0)
    def _():
        curl_all(False)


def planes_of(held, pairs, tables):
    pencils, rows, _ = held.shape
    groups = [(c, pair) for c in range(3) for pair in pairs]
    left = jnp.concatenate(
        [
            jnp.concatenate(
                [held[h, :, n * LANES : (n + 1) * LANES] for h in range(pencils)], axis=1
            )
            for n in range(len(groups))
        ],
        axis=0,
    )
    ny = tables[0].shape[1] // 2
    wide = table_right(left, tables[0][...], tables[1][...])
    made = {}
    for n, (c, pair) in enumerate(groups):
        for parity in range(2):
            made[c, 2 * pair + parity] = wide[
                n * rows : (n + 1) * rows, parity * ny : (parity + 1) * ny
            ]
    return made


def hold(tall, c, n, value):
    rows = value.shape[0]
    tall[c, n, RIM : RIM + rows] = value
    tall[c, n, 0:RIM] = value[rows - RIM : rows]


def edge_kernel(pairs, tables, place, *refs):
    tall, first, last, held = refs[-4:]
    gather_blocks(refs[:-4], held, place[1])
    listed = [2 * pair + parity for pair in pairs for parity in range(2)]
    cols = first.shape[1]
    values = planes_of(held, pairs, tables)
    for c in range(3):
        for n, z in enumerate(listed):
            hold(tall, c, n, values[c, z])
        first[c] = values[c, listed[0]][0:cols]
        last[c] = values[c, listed[-1]][0:cols]


def where_planes(chunks):
    spot = {}
    for n, chunk in enumerate(chunks):
        for i, pair in enumerate(chunk):
            spot[2 * pair], spot[2 * pair + 1] = (n, 2 * i), (n, 2 * i + 1)
    return spot


def rim_start(meshes, which, c, i):
    before = 6 * meshes[1].shape[1] if which == 0 else 0
    return before + 2 * (c * meshes[which].shape[1] + i)


def stretch_plane(out, mesh, rims, at, rows_of, above, below):
    cols, ny = out[0].shape
    low_rim, high_rim = rims
    for c in range(3):
        out[c][...] = mesh[c][...]
        out[c][0:2] += low_rim[at[c] : at[c] + 2]
        out[c][cols - 2 : cols] += high_rim[at[c] : at[c] + 2]
    omega = [ref[...] for ref in out]
    for c in range(3):
        value = rows_of(c, RIM)
        along_z = (above(c) - below(c)) * 0.5
        along_x = (rows_of(c, RIM + 1) - rows_of(c, RIM - 1)) * 0.5
        along_y = (pltpu.roll(value, ny - 1, 1) - pltpu.roll(value, 1, 1)) * 0.5
        stretch = omega[0] * along_z + omega[1] * along_x + omega[2] * along_y
        out[c][...] = omega[c] + TIME_STEP * stretch


def ends_kernel(_, edges, before, after, low_rim, high_rim, *refs):
    meshes, vorticity, out, sems = refs[:-3], refs[-3], refs[-2], refs[-1]
    cols = before.shape[1]
    size = edges.shape[1]
    copies = []

    def rows_of(i):
        return lambda c, start=RIM: edges[c, i, start : start + cols]

    for n, i in enumerate((0, size - 1)):
        stretch_plane(
            [out.at[c, n] for c in range(3)],
            [meshes[0].at[c, i] for c in range(3)],
            (low_rim, high_rim),
            [rim_start(meshes, 0, c, i) for c in range(3)],
            rows_of(i),
            (lambda c: after[c]) if i else rows_of(1),
            rows_of(size - 2) if i else (lambda c: before[c]),
        )
        copies.append(
            pltpu.make_async_copy(
                out.at[:, n], vorticity.at[:, n * (vorticity.shape[1] - 1)], sems.at[n]
            )
        )
        copies[-1].start()
    for copy in copies:
        copy.wait()


def stretch_kernel(chunks, tables, place, edges, low_rim, high_rim, *refs):
    meshes, refs = refs[:2], refs[2:]
    velocity, vorticity, held, inner, omega, sems = refs[-6:]
    _, planes, cols, ny = velocity.shape
    spot = where_planes(chunks)
    talls = (edges, inner)
    sent = []

    def send(source, target):
        sent.append(pltpu.make_async_copy(source, target, sems.at[len(sent)]))
        sent[-1].start()

    def rows_of(z):
        n, i = spot[z]
        return lambda c, start=RIM: talls[n][c, i, start : start + cols]

    def send_velocity(which):
        for z in range(planes):
            n, i = spot[z]
            if n == which:
                send(talls[n].at[:, i, pl.ds(RIM, cols)], velocity.at[:, z])

    send_velocity(0)
    gather_blocks(refs[:-6], held, place[1])
    for (c, z), value in planes_of(held, chunks[1], tables).items():
        hold(inner, c, spot[z][1], value)
    send_velocity(1)
    for z in range(1, planes - 1):
        which, i = spot[z]
        stretch_plane(
            [omega.at[c, z] for c in range(3)],
            [meshes[which].at[c, i] for c in range(3)],
            (low_rim, high_rim),
            [rim_start(meshes, which, c, i) for c in range(3)],
            rows_of(z),
            rows_of(z + 1),
            rows_of(z - 1),
        )
        send(omega.at[:, z], vorticity.at[:, z])
    for copy in sent:
        copy.wait()


VM = pl.BlockSpec(memory_space=pltpu.VMEM)
SM = pl.BlockSpec(memory_space=pltpu.SMEM)
AN = pl.BlockSpec(memory_space=pl.ANY)
HB = pl.BlockSpec(memory_space=pltpu.HBM)


def kept(values):
    return pltpu.with_memory_space_constraint(values, pltpu.HBM)


def loaded(kernel):
    def run(place, t_high, t_low, *refs):
        kernel((t_high, t_low), place, *refs)

    return run


def call(kernel, ins, outs, scratch=(), sems=0, micros=2.0, moved=None, aliases=None):
    extra = [pltpu.SemaphoreType.DMA((sems,))] if sems else []
    return pl.pallas_call(
        kernel,
        out_shape=[jax.ShapeDtypeStruct(shape, F32) for _, shape in outs],
        in_specs=[spec for spec, _ in ins],
        out_specs=[spec for spec, _ in outs],
        scratch_shapes=[pltpu.VMEM(shape, kind) for shape, kind in scratch] + extra,
        compiler_params=pltpu.CompilerParams(vmem_limit_bytes=VMEM),
        input_output_aliases=aliases or {},
        cost_estimate=pl.CostEstimate(
            flops=int(micros * 1.0e9),
            bytes_accessed=int(micros * 3.0e6) if moved is None else moved,
            transcendentals=0,
        ),
    )(*[value for _, value in ins])


def ring(axis, step):
    count = lax.axis_size(axis)
    return [(i, (i + step) % count) for i in range(count)]


def spread(axis):
    count = lax.axis_size(axis)
    return count <= 8 and count & (count - 1) == 0


def sent_shapes(axis, rows, width, whole=False):
    count = lax.axis_size(axis)
    return [(count, rows, width)] if whole or not spread(axis) else [(rows, width)] * count


def exchange(blocks, axis, start=0):
    if not spread(axis):
        return [lax.all_to_all(blocks[0], axis, split_axis=0, concat_axis=0, tiled=True)]
    count = lax.axis_size(axis)
    return [
        lax.ppermute(block, axis, [(i, i ^ k) for i in range(count)]) if k else block
        for k, block in zip(offset_order(count)[start:], blocks)
    ]


def on_device(strength, offsets, cell_index, migrate_count, ambient):
    _, planes, cols, ny = ambient.shape
    slabs, pencils = lax.axis_size("gz"), lax.axis_size("gx")
    nx, nz, rows = cols * pencils, planes * slabs, cols + RIM
    count = strength.shape[1]
    pair_count = planes // 2
    chunks = ((0, pair_count - 1), tuple(range(1, pair_count - 1)))
    widths = [3 * len(c) * LANES for c in chunks]
    block = nx // slabs

    y_ahead, y_back = [split_table(t) for t in y_tables(ny, pencils, 1.0 / (float(nx) * ny * nz))]
    x_ahead, x_back = [split_table(t) for t in x_tables(nx, cols, pencils, slabs)]
    place = jnp.stack([lax.axis_index("gz"), lax.axis_index("gx")]).astype(jnp.int32)
    here = (SM, place)

    packet, movers = call(
        packet_kernel,
        [
            (HB, kept(migrate_count.reshape(1, 2))),
            (HB, kept(strength)),
            (HB, kept(offsets)),
            (HB, kept(cell_index.reshape(1, count))),
        ],
        [(VM, (8, count)), (VM, (8, 2 * MIG))],
        [((1, 2), jnp.int32), ((1, count), jnp.int32)],
        sems=4,
        micros=1.0,
        moved=1000,
    )
    up1 = lax.ppermute(packet, "gz", ring("gz", -1))
    down1 = lax.ppermute(packet, "gz", ring("gz", 1))
    up2 = lax.ppermute(movers, "gz", ring("gz", -2))
    down2 = lax.ppermute(movers, "gz", ring("gz", 2))

    meshes, rims, parts = [None, None], [], [None, None]
    for n in (1, 0):
        chunk, width = chunks[n], widths[n]
        size = 2 * len(chunk)
        rim = (6 * size + (rims[0].shape[0] if rims else 0), ny)
        mesh, rim_high, rim_low, *part = call(
            functools.partial(deposit_kernel, chunk, len(rims)),
            [here]
            + [(VM, value) for value in (packet, up1, down1, up2, down2)]
            + [(VM, ambient), (VM, y_ahead[0]), (VM, y_ahead[1])]
            + [(VM, value) for value in rims],
            [(VM, (3, size, cols, ny)), (VM, rim), (VM, rim)]
            + [(VM, shape) for shape in sent_shapes("gx", rows, width)],
            [((3, size, rows, ny), F32), ((pencils, rows, width), F32)],
            micros=5.0,
        )
        meshes[n] = mesh
        rims = [rim_high, rim_low]
        parts[n] = exchange(part, "gx")
    low_rim = lax.ppermute(rims[0], "gx", ring("gx", 1))
    high_rim = lax.ppermute(rims[1], "gx", ring("gx", -1))

    tile = max(1, block // 4)
    data, before = [None, None], []
    for n in (1, 0):
        chunk, part, width = chunks[n], parts[n], widths[n]
        shapes = sent_shapes("gz", block, width)
        part = call(
            functools.partial(x_ahead_kernel, len(shapes), len(before)),
            [here, (VM, x_ahead[0]), (VM, x_ahead[1])]
            + [(AN, b) for b in before]
            + [(VM, p) for p in part],
            [(VM, shape) for shape in shapes],
            [((pencils, rows, width), F32), ((slabs, block, width), F32)],
        )
        before = [part[0]]
        (entered,) = call(
            functools.partial(enter_kernel, chunk, nz),
            [here] + [(VM, p) for p in exchange(part, "gz")],
            [(VM, (3, 2, 2 * len(chunk), slabs, tile, LANES))],
        )
        data[n] = entered
    data = call(
        functools.partial(curl_kernel, chunks, nx, ny),
        [here, (VM, low_rim), (VM, high_rim)] + [(VM, d) for d in data],
        [(VM, d.shape) for d in data],
        [((3, 2, nz, tile, LANES), F32)],
        micros=5.0,
    )
    plane = (3, cols, ny)
    tables = [(VM, t) for t in y_back]
    tall = [(3, 2 * len(chunk), cols + 2 * RIM, ny) for chunk in chunks]
    left = [
        call(
            functools.partial(leave_kernel, chunk, nz),
            [here, (VM, source)],
            [(VM, shape) for shape in sent_shapes("gz", block, width)],
            [(source.shape, F32)],
        )
        for chunk, source, width in zip(chunks, data, widths)
    ]

    def back(part, width):
        shapes = sent_shapes("gx", rows, width)
        part = call(
            loaded(functools.partial(x_back_kernel, len(shapes))),
            [here]
            + [(VM, t) for t in x_back]
            + [(VM, p) for p in part],
            [(VM, shape) for shape in shapes],
            [((slabs, block, width), F32), ((pencils, rows, width), F32)],
        )
        return exchange(part, "gx")

    early = max(1, len(left[1]) - LATE)
    second = exchange(left[1][:early], "gz")
    parts = [back(exchange(left[0], "gz"), widths[0])]
    edges, first, last = call(
        loaded(functools.partial(edge_kernel, chunks[0])),
        [here] + tables + [(VM, p) for p in parts[0]],
        [(VM, tall[0]), (VM, plane), (VM, plane)],
        [((pencils, rows, widths[0]), F32)],
    )
    if early < len(left[1]):
        late = call(
            pass_kernel,
            [(AN, parts[0][0])] + [(VM, p) for p in left[1][early:]],
            [(VM, p.shape) for p in left[1][early:]],
            micros=0.3,
        )
        second += exchange(late, "gz", early)
    parts.append(back(second, widths[1]))
    after = lax.ppermute(first, "gz", ring("gz", -1))
    before = lax.ppermute(last, "gz", ring("gz", 1))
    velocity, vorticity = call(
        loaded(functools.partial(stretch_kernel, chunks)),
        [here]
        + tables
        + [(VM, v) for v in (edges, low_rim, high_rim, *meshes)]
        + [(VM, p) for p in parts[1]],
        [(AN, ambient.shape), (AN, ambient.shape)],
        [
            ((pencils, rows, widths[1]), F32),
            (tall[1], F32),
            ((3, planes, cols, ny), F32),
        ],
        sems=2 * planes,
        micros=4.0,
    )
    (vorticity,) = call(
        ends_kernel,
        [(AN, vorticity)]
        + [(VM, v) for v in (edges, before, after, low_rim, high_rim, *meshes)],
        [(AN, ambient.shape)],
        [((3, 2, cols, ny), F32)],
        sems=2,
        micros=1.0,
        aliases={0: 0},
    )
    return velocity, vorticity


def solution(mesh):
    placed = (
        P(None, ("gz", "gx")),
        P(None, ("gz", "gx")),
        P(("gz", "gx")),
        P("gz", "gx", None),
        P(None, "gz", "gx", None),
    )
    return jax.shard_map(
        on_device,
        mesh=mesh,
        in_specs=placed,
        out_specs=(P(None, "gz", "gx", None), P(None, "gz", "gx", None)),
        check_vma=False,
    )
```

```python
import functools
import math

import jax
import jax.numpy as jnp
import ml_dtypes
import numpy as np
from jax import lax
from jax.experimental import pallas as pl
from jax.experimental.pallas import tpu as pltpu
from jax.sharding import PartitionSpec as P

MIG = 64
LANES = 128
RIM = 8
LATE = 3
TIME_STEP = 0.25
VMEM = 24 * 1024 * 1024
F32 = jnp.float32
BF16 = jnp.bfloat16


def split_table(table):
    high = table.astype(np.float32).astype(ml_dtypes.bfloat16)
    low = (table - high.astype(np.float64)).astype(np.float32).astype(ml_dtypes.bfloat16)
    return high, low


def angles(rows, columns, extent):
    return 2.0 * np.pi * (np.multiply.outer(rows, columns) % extent) / extent


def y_tables(ny, pencils, scale):
    modes = ny // (2 * pencils)
    position = np.arange(ny)
    angle = angles(position, np.arange(ny // 2), ny)
    real, imag = np.cos(angle), -np.sin(angle)
    imag[:, 0] = 1.0 - 2.0 * (position % 2)
    weight = np.where(np.arange(ny // 2) == 0, 1.0, 2.0) * scale
    ahead = np.zeros((2, ny, pencils, 2, 2, modes))
    back = np.zeros((pencils, 2, 2, modes, 2, ny))
    for parity in range(2):
        for part, values in enumerate((real, imag)):
            ahead[parity, :, :, part, parity] = values.reshape(ny, pencils, modes)
            back[:, part, parity, :, parity] = (values * weight).T.reshape(pencils, modes, ny)
    return ahead.reshape(2 * ny, -1), back.reshape(-1, 2 * ny)


def wave_order(nx, slabs):
    half = nx // 2
    ahead = np.arange(half).reshape(slabs, 1, half // slabs)
    behind = np.where(ahead == 0, half, (nx - ahead) % nx)
    return np.concatenate([ahead, behind], axis=1).reshape(-1)


def x_tables(nx, cols, pencils, slabs):
    order = wave_order(nx, slabs)
    angle = angles(order, np.arange(nx), nx)
    ahead = np.concatenate([np.cos(angle), np.sin(angle)], axis=0)
    row = np.arange(cols + RIM)
    offset = np.where(row <= cols, row, -1)
    used = ((row <= cols) | (row == cols + RIM - 1)).astype(np.float64)
    place = (np.arange(pencils)[:, None] * cols + offset[None, :]) % nx
    angle = angles(place.reshape(-1), order, nx)
    mask = np.tile(used, pencils)[:, None]
    back = np.concatenate([np.cos(angle) * mask, np.sin(angle) * mask], axis=0)
    return ahead, back


def split(values):
    high = values.astype(BF16)
    return high, (values - high.astype(F32)).astype(BF16)


def dot(left, right):
    return jnp.dot(left, right, preferred_element_type=F32)


def table_left(high, low, values):
    v_high, v_low = split(values)
    return dot(high, v_high) + (dot(high, v_low) + dot(low, v_high))


def table_right(values, high, low):
    v_high, v_low = split(values)
    return dot(v_high, high) + (dot(v_low, high) + dot(v_high, low))


def lane_of():
    return lax.broadcasted_iota(jnp.int32, (1, LANES), 1)


def times_i(values):
    half = LANES // 2
    sign = jnp.where(lane_of() < half, -1.0, 1.0).astype(F32)
    return pltpu.roll(values, half, 1) * sign


def kernel_weight(distance):
    radius = jnp.abs(distance)
    near = 1.0 - 2.5 * radius * radius + 1.5 * radius * radius * radius
    far = 0.5 * (2.0 - radius) * (2.0 - radius) * (1.0 - radius)
    return jnp.where(radius < 1.0, near, jnp.where(radius < 2.0, far, 0.0))


def turned(value, wave, extent, sign):
    wave = wave % extent
    real, imag = value
    if wave == 0:
        return value
    if 2 * wave == extent:
        return -real, -imag
    if 4 * wave == extent:
        return (-imag, real) if sign > 0 else (imag, -real)
    if 4 * wave == 3 * extent:
        return (imag, -real) if sign > 0 else (-imag, real)
    a = math.cos(2.0 * math.pi * wave / extent)
    b = sign * math.sin(2.0 * math.pi * wave / extent)
    return real * a - imag * b, real * b + imag * a


def fft(values, sign):
    count = len(values)
    if count == 1:
        return values
    even, odd = fft(values[::2], sign), fft(values[1::2], sign)
    odd = [turned(v, k, count, sign) for k, v in enumerate(odd)]
    plus = [(a[0] + b[0], a[1] + b[1]) for a, b in zip(even, odd)]
    minus = [(a[0] - b[0], a[1] - b[1]) for a, b in zip(even, odd)]
    return plus + minus


def offset_order(count):
    if count < 4:
        return list(range(count))
    far, near = list(range(count // 2, count)), list(range(1, count // 2))
    order = [0]
    while far or near:
        order += far[:1] + near[:1]
        far, near = far[1:], near[1:]
    return order


def blocks_of(refs, at):
    if len(refs) == 1:
        return [(d, refs[0].at[d]) for d in range(refs[0].shape[0])]
    return [(at ^ k, ref) for k, ref in zip(offset_order(len(refs)), refs)]


def gather_blocks(refs, held, at):
    for d, ref in blocks_of(refs, at):
        held[d] = ref[...]


def packet_kernel(
    counts, strength, offsets, cells, packet, movers, near_counts, near_cells, sems
):
    copies = [
        pltpu.make_async_copy(counts, near_counts, sems.at[0]),
        pltpu.make_async_copy(cells, near_cells, sems.at[1]),
        pltpu.make_async_copy(strength, packet.at[pl.ds(0, 3)], sems.at[2]),
        pltpu.make_async_copy(offsets, packet.at[pl.ds(3, 3)], sems.at[3]),
    ]
    for copy in copies:
        copy.start()
    for copy in copies:
        copy.wait()
    slot = lax.broadcasted_iota(jnp.int32, (1, packet.shape[1]), 1)
    up = near_counts[0:1, 0:1]
    both = up + near_counts[0:1, 1:2]
    packet[6:7] = near_cells[...].astype(F32)
    packet[7:8] = jnp.where(slot < up, 1.0, jnp.where(slot < both, -1.0, 0.0))
    movers[...] = packet[:, : movers.shape[1]]


def deposit_kernel(
    pairs, rims_before, place, own, up1, down1, up2, down2, ambient, t_high, t_low, *refs
):
    rims, refs = refs[:rims_before], refs[rims_before:]
    mesh, rim_high, rim_low = refs[:3]
    total, made = refs[-2:]
    outs = refs[3:-2]
    _, planes, cols, ny = ambient.shape
    rows = cols + RIM
    movers = up2.shape[1]
    count = own.shape[1]
    listed = [2 * pair + parity for pair in pairs for parity in range(2)]

    def decode(ref, start, stop, shift):
        packet = ref[:, start:stop]
        cell = packet[6:7].astype(jnp.int32)
        move = packet[7:8].astype(jnp.int32)
        z_cell = lax.div(cell, cols * ny) + planes * (move + shift)
        x_cell = lax.rem(lax.div(cell, ny), cols)
        return packet[0:6], z_cell, x_cell, lax.rem(cell, ny)

    def joined(pieces):
        return [jnp.concatenate(p, axis=1) if len(p) > 1 else p[0] for p in zip(*pieces)]

    def add_block(pieces, wanted):
        values, z_cell, x_cell, y_cell = joined(pieces)
        width = values.shape[1]
        z_at = lax.broadcasted_iota(jnp.int32, (planes, width), 0)
        w_z = kernel_weight((z_at - z_cell).astype(F32) - values[3:4])
        row = lax.broadcasted_iota(jnp.int32, (rows, width), 0)
        x_at = jnp.where(row < cols + 2, row, jnp.where(row >= rows - 2, row - rows, 4 * rows))
        w_x = kernel_weight((x_at - x_cell).astype(F32) - values[4:5])
        y_at = lax.broadcasted_iota(jnp.int32, (ny, width), 0)
        y_off = lax.rem(y_at - y_cell + (ny + ny // 2), ny) - ny // 2
        w_y = kernel_weight(y_off.astype(F32) - values[5:6])
        y_high, y_low = split(w_y)
        right = jnp.concatenate([y_high, y_high, y_low], axis=1)
        at = [listed.index(z) for z in wanted]
        for c in range(3):
            s_z = values[c : c + 1] * w_z
            left = jnp.concatenate([s_z[z : z + 1] * w_x for z in wanted], axis=0)
            l_high, l_low = split(left)
            left = jnp.concatenate([l_high, l_low, l_high], axis=1)
            added = lax.dot_general(
                left, right, (((1,), (1,)), ((), ())), preferred_element_type=F32
            )
            total[c, at[0] : at[-1] + 1] += added.reshape(len(wanted), rows, ny)

    for n, z in enumerate(listed):
        total[:, n, 0:cols] = ambient[:, z]
    total[:, :, cols:rows] = jnp.zeros((3, len(listed), RIM, ny), F32)
    step = 256
    for at in range(0, count, step):
        add_block([decode(own, at, min(at + step, count), 0)], listed)
    add_block([decode(up1, 0, movers, 1), decode(down1, 0, movers, -1)], listed)
    sides = ((up1, up2, 1, (planes - 2, planes - 1)), (down1, down2, -1, (0, 1)))
    for near, far, shift, wanted in sides:
        if not set(wanted) <= set(listed):
            continue
        whole = [decode(near, movers, count, shift), decode(far, 0, movers, 2 * shift)]
        values, z_cell, x_cell, y_cell = joined(whole)
        for at in range(0, count, step):
            to = min(at + step, count)
            block = (values[:, at:to], z_cell[:, at:to], x_cell[:, at:to], y_cell[:, at:to])
            add_block([block], wanted)

    mesh[...] = total[:, :, 0:cols]
    at = 0
    if rims:
        at = rims[0].shape[0]
        rim_high[0:at] = rims[0][...]
        rim_low[0:at] = rims[1][...]
    for n in range(3 * len(listed)):
        c, i = n // len(listed), n % len(listed)
        rim_high[at + 2 * n : at + 2 * n + 2] = total[c, i, cols : cols + 2]
        rim_low[at + 2 * n : at + 2 * n + 2] = total[c, i, rows - 2 : rows]
    groups = [(c, 2 * n) for c in range(3) for n in range(len(pairs))]
    left = jnp.concatenate(
        [jnp.concatenate([total[c, n], total[c, n + 1]], axis=1) for c, n in groups], axis=0
    )
    wide = table_right(left, t_high[...], t_low[...])
    for n in range(len(groups)):
        for g in range(made.shape[0]):
            made[g, :, n * LANES : (n + 1) * LANES] = wide[
                n * rows : (n + 1) * rows, g * LANES : (g + 1) * LANES
            ]
    for d, out in blocks_of(outs, place[1]):
        out[...] = made[d]


def x_ahead_kernel(sends, passed, place, t_high, t_low, *refs):
    held, made = refs[-2:]
    outs, parts = refs[-2 - sends : -2], refs[passed : -2 - sends]
    gather_blocks(parts, held, place[1])
    pencils, rows, width = held.shape
    cols = rows - RIM
    row = lax.broadcasted_iota(jnp.int32, (RIM, width), 0)
    pieces = []
    for h in range(pencils):
        from_low = held[(h - 1) % pencils, cols:rows]
        from_high = held[(h + 1) % pencils, cols:rows]
        pieces.append(held[h, 0:RIM] + jnp.where(row < 2, from_low, 0.0))
        pieces.append(held[h, RIM : cols - RIM])
        pieces.append(held[h, cols - RIM : cols] + jnp.where(row >= RIM - 2, from_high, 0.0))
    both = table_left(t_high[...], t_low[...], jnp.concatenate(pieces, axis=0))
    half = both.shape[0] // 2
    for n in range(width // LANES):
        lanes = slice(n * LANES, (n + 1) * LANES)
        value = both[:half, lanes] - times_i(both[half:, lanes])
        made[:, :, lanes] = value.reshape(made.shape[0], made.shape[1], LANES)
    for d, out in blocks_of(outs, place[0]):
        out[...] = made[d]


def x_back_kernel(sends, tables, place, *refs):
    held, made = refs[-2:]
    outs, parts = refs[-2 - sends : -2], refs[: -2 - sends]
    gather_blocks(parts, held, place[0])
    pencils, rows, width = made.shape
    both = table_left(tables[0][...], tables[1][...], held[...].reshape(-1, width))
    half = both.shape[0] // 2
    for n in range(width // LANES):
        lanes = slice(n * LANES, (n + 1) * LANES)
        value = both[:half, lanes] + times_i(both[half:, lanes])
        made[:, :, lanes] = value.reshape(pencils, rows, LANES)
    for d, out in blocks_of(outs, place[1]):
        out[...] = made[d]


def wave_lanes():
    lane = lane_of()
    return lane < LANES // 2, (lane // (LANES // 4)) % 2 == 0


def roll(values, shift):
    return pltpu.roll(values, shift, 1)


def cross_half(a, b):
    low, _ = wave_lanes()
    half = LANES // 2
    return jnp.where(low, a, roll(b, half)), jnp.where(low, roll(a, half), b)


def cross_quarter(a, b):
    _, first = wave_lanes()
    quarter = LANES // 4
    return (
        jnp.where(first, a, roll(b, quarter)),
        jnp.where(first, roll(a, LANES - quarter), b),
    )


def lanes_at(c, count, i):
    return pl.ds(pl.multiple_of((c * count + i) * LANES, LANES), LANES)


def enter_kernel(pairs, nz, place, *refs):
    parts, data = refs[:-1], refs[-1]
    _, _, _, slabs, tile, _ = data.shape

    def body(c, carry):
        for i, pair in enumerate(pairs):
            lanes = lanes_at(c, len(pairs), i)
            for s, ref in blocks_of(parts, place[0]):
                quad = [ref[q * tile : (q + 1) * tile, lanes] for q in range(4)]
                real0, imag0 = cross_half(quad[0], quad[2])
                real1, imag1 = cross_half(quad[1], quad[3])
                for part, (a, b) in enumerate(((real0, real1), (imag0, imag1))):
                    even, odd = cross_quarter(a, b)
                    data[c, part, 2 * i, s] = even
                    data[c, part, 2 * i + 1, s] = odd
            for parity in range(2):
                at = 2 * i + parity
                line = [(data[c, 0, at, s], data[c, 1, at, s]) for s in range(slabs)]
                for k, v in enumerate(fft(line, -1.0)):
                    v = turned(v, (2 * pair + parity) * k, nz, -1.0)
                    data[c, 0, at, k], data[c, 1, at, k] = v
        return carry

    lax.fori_loop(0, 3, body, 0)


def pass_kernel(*_):
    pass


def leave_kernel(pairs, nz, place, source, *refs):
    outs, data = refs[:-1], refs[-1]
    _, _, _, slabs, tile, _ = source.shape

    def body(c, carry):
        for i, pair in enumerate(pairs):
            lanes = lanes_at(c, len(pairs), i)
            for parity in range(2):
                at = 2 * i + parity
                line = [
                    turned(
                        (source[c, 0, at, k], source[c, 1, at, k]),
                        (2 * pair + parity) * k,
                        nz,
                        1.0,
                    )
                    for k in range(slabs)
                ]
                for s, v in enumerate(fft(line, 1.0)):
                    data[c, 0, at, s], data[c, 1, at, s] = v
            for s, ref in blocks_of(outs, place[0]):
                real0, real1 = cross_quarter(data[c, 0, 2 * i, s], data[c, 0, 2 * i + 1, s])
                imag0, imag1 = cross_quarter(data[c, 1, 2 * i, s], data[c, 1, 2 * i + 1, s])
                quad = [None] * 4
                quad[0], quad[2] = cross_half(real0, imag0)
                quad[1], quad[3] = cross_half(real1, imag1)
                for q in range(4):
                    ref[q * tile : (q + 1) * tile, lanes] = quad[q]
        return carry

    lax.fori_loop(0, 3, body, 0)


def curl_kernel(chunks, nx, ny, place, low_rim, high_rim, *refs):
    sources, outs = refs[: len(chunks)], refs[len(chunks) : 2 * len(chunks)]
    spectrum = refs[-1]
    _, _, nz, tile, _ = spectrum.shape
    slabs = sources[0].shape[3]
    planes = nz // slabs
    modes, half = LANES // 4, LANES // 2
    slab_at, pencil_at = place[0], place[1]
    spot = {}
    for n, chunk in enumerate(chunks):
        for i, pair in enumerate(chunk):
            spot[2 * pair], spot[2 * pair + 1] = (n, 2 * i), (n, 2 * i + 1)

    def across_planes(k, carry):
        for c in range(3):
            line = []
            for l in range(planes):
                n, i = spot[l]
                line.append((sources[n][c, 0, i, k], sources[n][c, 1, i, k]))
            for n, v in enumerate(fft(line, -1.0)):
                spectrum[c, 0, k + slabs * n], spectrum[c, 1, k + slabs * n] = v
        return carry

    reach = 2 * tile
    row = lax.broadcasted_iota(jnp.int32, (tile, LANES), 0)
    lane = lax.broadcasted_iota(jnp.int32, (tile, LANES), 1)
    number = slab_at * reach + (lane // modes) % 2 * tile + row
    ahead = lane < half
    mode = lane % modes + pencil_at * modes
    alone = number == 0
    number = number.astype(F32) * (2.0 * math.pi / nx)
    x_base = jnp.where(ahead, number, jnp.where(alone, math.pi, -number))
    x_trim = jnp.where(ahead, number, jnp.where(alone, 0.0, -number))
    wave_y = mode.astype(F32) * (2.0 * math.pi / ny)
    packed = mode == 0
    x_sq = x_base * x_base
    lateral = x_sq + wave_y * wave_y

    def curl_at(k, with_mirror):
        z_wave = jnp.where(k < nz // 2, k, k - nz).astype(F32) * (2.0 * math.pi / nz)
        z_trim = jnp.where(k == nz // 2, 0.0, z_wave)
        full = lateral + z_wave * z_wave
        empty = full == 0.0
        inverse = jnp.where(empty, 0.0, 1.0 / jnp.where(empty, 1.0, full))
        if with_mirror:
            other = 1.0 / (x_sq + (z_wave * z_wave + math.pi * math.pi))
            mirror = jnp.where(packed, 0.5 * (inverse - other), 0.0)
            inverse = jnp.where(packed, 0.5 * (inverse + other), inverse)
            opposite = lax.rem(nz - k, nz)
        stream = []
        for c in range(3):
            value = [spectrum[c, part, k] * inverse for part in range(2)]
            if with_mirror:
                for part, sign in enumerate((1.0, -1.0)):
                    there = spectrum[c, part, opposite]
                    there = jnp.where(alone, there, roll(there, half))
                    value[part] = value[part] + (mirror * sign) * there
            stream.append(value)
        made = []
        for part in range(2):
            s = [value[part] for value in stream]
            made.append(
                (
                    x_trim * s[2] - wave_y * s[1],
                    wave_y * s[0] - z_trim * s[2],
                    z_trim * s[1] - x_trim * s[0],
                )
            )
        return [(-made[1][c], made[0][c]) for c in range(3)]

    def curl_all(with_mirror):
        def body(k, carry):
            made = [curl_at(k + slabs * n, with_mirror) for n in range(planes)]
            for c in range(3):
                for l, v in enumerate(fft([m[c] for m in made], 1.0)):
                    n, i = spot[l]
                    outs[n][c, 0, i, k], outs[n][c, 1, i, k] = v
            return carry

        lax.fori_loop(0, slabs, body, 0)

    lax.fori_loop(0, slabs, across_planes, 0)

    @pl.when(pencil_at == 0)
    def _():
        curl_all(True)

    @pl.when(pencil_at != 0)
    def _():
        curl_all(False)


def planes_of(held, pairs, tables):
    pencils, rows, _ = held.shape
    groups = [(c, pair) for c in range(3) for pair in pairs]
    left = jnp.concatenate(
        [
            jnp.concatenate(
                [held[h, :, n * LANES : (n + 1) * LANES] for h in range(pencils)], axis=1
            )
            for n in range(len(groups))
        ],
        axis=0,
    )
    ny = tables[0].shape[1] // 2
    wide = table_right(left, tables[0][...], tables[1][...])
    made = {}
    for n, (c, pair) in enumerate(groups):
        for parity in range(2):
            made[c, 2 * pair + parity] = wide[
                n * rows : (n + 1) * rows, parity * ny : (parity + 1) * ny
            ]
    return made


def hold(tall, c, n, value):
    rows = value.shape[0]
    tall[c, n, RIM : RIM + rows] = value
    tall[c, n, 0:RIM] = value[rows - RIM : rows]


def edge_kernel(pairs, tables, place, *refs):
    tall, first, last, held = refs[-4:]
    gather_blocks(refs[:-4], held, place[1])
    listed = [2 * pair + parity for pair in pairs for parity in range(2)]
    cols = first.shape[1]
    values = planes_of(held, pairs, tables)
    for c in range(3):
        for n, z in enumerate(listed):
            hold(tall, c, n, values[c, z])
        first[c] = values[c, listed[0]][0:cols]
        last[c] = values[c, listed[-1]][0:cols]


def where_planes(chunks):
    spot = {}
    for n, chunk in enumerate(chunks):
        for i, pair in enumerate(chunk):
            spot[2 * pair], spot[2 * pair + 1] = (n, 2 * i), (n, 2 * i + 1)
    return spot


def rim_start(meshes, which, c, i):
    before = 6 * meshes[1].shape[1] if which == 0 else 0
    return before + 2 * (c * meshes[which].shape[1] + i)


def stretch_plane(out, mesh, rims, at, rows_of, above, below):
    cols, ny = out[0].shape
    low_rim, high_rim = rims
    for c in range(3):
        out[c][...] = mesh[c][...]
        out[c][0:2] += low_rim[at[c] : at[c] + 2]
        out[c][cols - 2 : cols] += high_rim[at[c] : at[c] + 2]
    omega = [ref[...] for ref in out]
    for c in range(3):
        value = rows_of(c, RIM)
        along_z = (above(c) - below(c)) * 0.5
        along_x = (rows_of(c, RIM + 1) - rows_of(c, RIM - 1)) * 0.5
        along_y = (pltpu.roll(value, ny - 1, 1) - pltpu.roll(value, 1, 1)) * 0.5
        stretch = omega[0] * along_z + omega[1] * along_x + omega[2] * along_y
        out[c][...] = omega[c] + TIME_STEP * stretch


def ends_kernel(_, edges, before, after, low_rim, high_rim, *refs):
    meshes, vorticity, out, sems = refs[:-3], refs[-3], refs[-2], refs[-1]
    cols = before.shape[1]
    size = edges.shape[1]
    copies = []

    def rows_of(i):
        return lambda c, start=RIM: edges[c, i, start : start + cols]

    for n, i in enumerate((0, size - 1)):
        stretch_plane(
            [out.at[c, n] for c in range(3)],
            [meshes[0].at[c, i] for c in range(3)],
            (low_rim, high_rim),
            [rim_start(meshes, 0, c, i) for c in range(3)],
            rows_of(i),
            (lambda c: after[c]) if i else rows_of(1),
            rows_of(size - 2) if i else (lambda c: before[c]),
        )
        copies.append(
            pltpu.make_async_copy(
                out.at[:, n], vorticity.at[:, n * (vorticity.shape[1] - 1)], sems.at[n]
            )
        )
        copies[-1].start()
    for copy in copies:
        copy.wait()


def stretch_kernel(chunks, tables, place, edges, low_rim, high_rim, *refs):
    meshes, refs = refs[:2], refs[2:]
    velocity, vorticity, held, inner, omega, sems = refs[-6:]
    _, planes, cols, ny = velocity.shape
    spot = where_planes(chunks)
    talls = (edges, inner)
    sent = []

    def send(source, target):
        sent.append(pltpu.make_async_copy(source, target, sems.at[len(sent)]))
        sent[-1].start()

    def rows_of(z):
        n, i = spot[z]
        return lambda c, start=RIM: talls[n][c, i, start : start + cols]

    def send_velocity(which):
        for z in range(planes):
            n, i = spot[z]
            if n == which:
                send(talls[n].at[:, i, pl.ds(RIM, cols)], velocity.at[:, z])

    send_velocity(0)
    gather_blocks(refs[:-6], held, place[1])
    for (c, z), value in planes_of(held, chunks[1], tables).items():
        hold(inner, c, spot[z][1], value)
    send_velocity(1)
    for z in range(1, planes - 1):
        which, i = spot[z]
        stretch_plane(
            [omega.at[c, z] for c in range(3)],
            [meshes[which].at[c, i] for c in range(3)],
            (low_rim, high_rim),
            [rim_start(meshes, which, c, i) for c in range(3)],
            rows_of(z),
            rows_of(z + 1),
            rows_of(z - 1),
        )
        send(omega.at[:, z], vorticity.at[:, z])
    for copy in sent:
        copy.wait()


VM = pl.BlockSpec(memory_space=pltpu.VMEM)
SM = pl.BlockSpec(memory_space=pltpu.SMEM)
AN = pl.BlockSpec(memory_space=pl.ANY)
HB = pl.BlockSpec(memory_space=pltpu.HBM)


def kept(values):
    return pltpu.with_memory_space_constraint(values, pltpu.HBM)


def loaded(kernel):
    def run(place, t_high, t_low, *refs):
        kernel((t_high, t_low), place, *refs)

    return run


def call(kernel, ins, outs, scratch=(), sems=0, micros=2.0, moved=None, aliases=None):
    extra = [pltpu.SemaphoreType.DMA((sems,))] if sems else []
    return pl.pallas_call(
        kernel,
        out_shape=[jax.ShapeDtypeStruct(shape, F32) for _, shape in outs],
        in_specs=[spec for spec, _ in ins],
        out_specs=[spec for spec, _ in outs],
        scratch_shapes=[pltpu.VMEM(shape, kind) for shape, kind in scratch] + extra,
        compiler_params=pltpu.CompilerParams(vmem_limit_bytes=VMEM),
        input_output_aliases=aliases or {},
        cost_estimate=pl.CostEstimate(
            flops=int(micros * 1.0e9),
            bytes_accessed=int(micros * 3.0e6) if moved is None else moved,
            transcendentals=0,
        ),
    )(*[value for _, value in ins])


def ring(axis, step):
    count = lax.axis_size(axis)
    return [(i, (i + step) % count) for i in range(count)]


def spread(axis):
    count = lax.axis_size(axis)
    return count <= 8 and count & (count - 1) == 0


def sent_shapes(axis, rows, width, whole=False):
    count = lax.axis_size(axis)
    return [(count, rows, width)] if whole or not spread(axis) else [(rows, width)] * count


def held_back(blocks, before):
    return list(
        call(
            pass_kernel,
            [(AN, before)] + [(AN, b) for b in blocks],
            [(AN, b.shape) for b in blocks],
            micros=0.1,
            aliases={n + 1: n for n in range(len(blocks))},
        )
    )


def exchange(blocks, axis, start=0):
    if not spread(axis):
        return [lax.all_to_all(blocks[0], axis, split_axis=0, concat_axis=0, tiled=True)]
    count = lax.axis_size(axis)
    return [
        lax.ppermute(block, axis, [(i, i ^ k) for i in range(count)]) if k else block
        for k, block in zip(offset_order(count)[start:], blocks)
    ]


def on_device(strength, offsets, cell_index, migrate_count, ambient):
    _, planes, cols, ny = ambient.shape
    slabs, pencils = lax.axis_size("gz"), lax.axis_size("gx")
    nx, nz, rows = cols * pencils, planes * slabs, cols + RIM
    count = strength.shape[1]
    pair_count = planes // 2
    chunks = ((0, pair_count - 1), tuple(range(1, pair_count - 1)))
    widths = [3 * len(c) * LANES for c in chunks]
    block = nx // slabs

    y_ahead, y_back = [split_table(t) for t in y_tables(ny, pencils, 1.0 / (float(nx) * ny * nz))]
    x_ahead, x_back = [split_table(t) for t in x_tables(nx, cols, pencils, slabs)]
    place = jnp.stack([lax.axis_index("gz"), lax.axis_index("gx")]).astype(jnp.int32)
    here = (SM, place)

    packet, movers = call(
        packet_kernel,
        [
            (HB, kept(migrate_count.reshape(1, 2))),
            (HB, kept(strength)),
            (HB, kept(offsets)),
            (HB, kept(cell_index.reshape(1, count))),
        ],
        [(VM, (8, count)), (VM, (8, 2 * MIG))],
        [((1, 2), jnp.int32), ((1, count), jnp.int32)],
        sems=4,
        micros=1.0,
        moved=1000,
    )
    up1 = lax.ppermute(packet, "gz", ring("gz", -1))
    down1 = lax.ppermute(packet, "gz", ring("gz", 1))
    up2 = lax.ppermute(movers, "gz", ring("gz", -2))
    down2 = lax.ppermute(movers, "gz", ring("gz", 2))

    meshes, rims, parts = [None, None], [], [None, None]
    for n in (1, 0):
        chunk, width = chunks[n], widths[n]
        size = 2 * len(chunk)
        rim = (6 * size + (rims[0].shape[0] if rims else 0), ny)
        mesh, rim_high, rim_low, *part = call(
            functools.partial(deposit_kernel, chunk, len(rims)),
            [here]
            + [(VM, value) for value in (packet, up1, down1, up2, down2)]
            + [(VM, ambient), (VM, y_ahead[0]), (VM, y_ahead[1])]
            + [(VM, value) for value in rims],
            [(VM, (3, size, cols, ny)), (VM, rim), (VM, rim)]
            + [(VM, shape) for shape in sent_shapes("gx", rows, width)],
            [((3, size, rows, ny), F32), ((pencils, rows, width), F32)],
            micros=5.0,
        )
        meshes[n] = mesh
        rims = [rim_high, rim_low]
        parts[n] = part
    low_rim = lax.ppermute(rims[0], "gx", ring("gx", 1))
    high_rim = lax.ppermute(rims[1], "gx", ring("gx", -1))

    tile = max(1, block // 4)
    data, before = [None, None], []
    for n in (1, 0):
        chunk, part, width = chunks[n], exchange(parts[n], "gx"), widths[n]
        shapes = sent_shapes("gz", block, width)
        part = call(
            functools.partial(x_ahead_kernel, len(shapes), len(before)),
            [here, (VM, x_ahead[0]), (VM, x_ahead[1])]
            + [(AN, b) for b in before]
            + [(VM, p) for p in part],
            [(VM, shape) for shape in shapes],
            [((pencils, rows, width), F32), ((slabs, block, width), F32)],
        )
        if n:
            parts[0] = held_back(parts[0], part[0])
        part = exchange(part, "gz")
        before = part[1:4]
        (entered,) = call(
            functools.partial(enter_kernel, chunk, nz),
            [here] + [(VM, p) for p in part],
            [(VM, (3, 2, 2 * len(chunk), slabs, tile, LANES))],
        )
        data[n] = entered
    data = call(
        functools.partial(curl_kernel, chunks, nx, ny),
        [here, (VM, low_rim), (VM, high_rim)] + [(VM, d) for d in data],
        [(VM, d.shape) for d in data],
        [((3, 2, nz, tile, LANES), F32)],
        micros=5.0,
    )
    plane = (3, cols, ny)
    tables = [(VM, t) for t in y_back]
    tall = [(3, 2 * len(chunk), cols + 2 * RIM, ny) for chunk in chunks]
    left = [
        call(
            functools.partial(leave_kernel, chunk, nz),
            [here, (VM, source)],
            [(VM, shape) for shape in sent_shapes("gz", block, width)],
            [(source.shape, F32)],
        )
        for chunk, source, width in zip(chunks, data, widths)
    ]

    def back(part, width):
        shapes = sent_shapes("gx", rows, width)
        part = call(
            loaded(functools.partial(x_back_kernel, len(shapes))),
            [here]
            + [(VM, t) for t in x_back]
            + [(VM, p) for p in part],
            [(VM, shape) for shape in shapes],
            [((slabs, block, width), F32), ((pencils, rows, width), F32)],
        )
        return exchange(part, "gx")

    early = max(1, len(left[1]) - LATE)
    second = exchange(left[1][:early], "gz")
    parts = [back(exchange(left[0], "gz"), widths[0])]
    edges, first, last = call(
        loaded(functools.partial(edge_kernel, chunks[0])),
        [here] + tables + [(VM, p) for p in parts[0]],
        [(VM, tall[0]), (VM, plane), (VM, plane)],
        [((pencils, rows, widths[0]), F32)],
    )
    if early < len(left[1]):
        late = held_back(left[1][early:], parts[0][0])
        second += exchange(late, "gz", early)
    parts.append(back(second, widths[1]))
    after = lax.ppermute(first, "gz", ring("gz", -1))
    before = lax.ppermute(last, "gz", ring("gz", 1))
    velocity, vorticity = call(
        loaded(functools.partial(stretch_kernel, chunks)),
        [here]
        + tables
        + [(VM, v) for v in (edges, low_rim, high_rim, *meshes)]
        + [(VM, p) for p in parts[1]],
        [(AN, ambient.shape), (AN, ambient.shape)],
        [
            ((pencils, rows, widths[1]), F32),
            (tall[1], F32),
            ((3, planes, cols, ny), F32),
        ],
        sems=2 * planes,
        micros=4.0,
    )
    (vorticity,) = call(
        ends_kernel,
        [(AN, vorticity)]
        + [(VM, v) for v in (edges, before, after, low_rim, high_rim, *meshes)],
        [(AN, ambient.shape)],
        [((3, 2, cols, ny), F32)],
        sems=2,
        micros=1.0,
        aliases={0: 0},
    )
    return velocity, vorticity


def solution(mesh):
    placed = (
        P(None, ("gz", "gx")),
        P(None, ("gz", "gx")),
        P(("gz", "gx")),
        P("gz", "gx", None),
        P(None, "gz", "gx", None),
    )
    return jax.shard_map(
        on_device,
        mesh=mesh,
        in_specs=placed,
        out_specs=(P(None, "gz", "gx", None), P(None, "gz", "gx", None)),
        check_vma=False,
    )
```

```python
import functools
import math

import jax
import jax.numpy as jnp
import ml_dtypes
import numpy as np
from jax import lax
from jax.experimental import pallas as pl
from jax.experimental.pallas import tpu as pltpu
from jax.sharding import PartitionSpec as P

MIG = 64
LANES = 128
RIM = 8
LATE = 3
TIME_STEP = 0.25
VMEM = 24 * 1024 * 1024
F32 = jnp.float32
BF16 = jnp.bfloat16


def split_table(table):
    high = table.astype(np.float32).astype(ml_dtypes.bfloat16)
    low = (table - high.astype(np.float64)).astype(np.float32).astype(ml_dtypes.bfloat16)
    return high, low


def angles(rows, columns, extent):
    return 2.0 * np.pi * (np.multiply.outer(rows, columns) % extent) / extent


def y_tables(ny, pencils, scale):
    modes = ny // (2 * pencils)
    position = np.arange(ny)
    angle = angles(position, np.arange(ny // 2), ny)
    real, imag = np.cos(angle), -np.sin(angle)
    imag[:, 0] = 1.0 - 2.0 * (position % 2)
    weight = np.where(np.arange(ny // 2) == 0, 1.0, 2.0) * scale
    ahead = np.zeros((2, ny, pencils, 2, 2, modes))
    back = np.zeros((pencils, 2, 2, modes, 2, ny))
    for parity in range(2):
        for part, values in enumerate((real, imag)):
            ahead[parity, :, :, part, parity] = values.reshape(ny, pencils, modes)
            back[:, part, parity, :, parity] = (values * weight).T.reshape(pencils, modes, ny)
    return ahead.reshape(2 * ny, -1), back.reshape(-1, 2 * ny)


def wave_order(nx, slabs):
    half = nx // 2
    ahead = np.arange(half).reshape(slabs, 1, half // slabs)
    behind = np.where(ahead == 0, half, (nx - ahead) % nx)
    return np.concatenate([ahead, behind], axis=1).reshape(-1)


def x_tables(nx, cols, pencils, slabs):
    order = wave_order(nx, slabs)
    angle = angles(order, np.arange(nx), nx)
    ahead = np.concatenate([np.cos(angle), np.sin(angle)], axis=0)
    row = np.arange(cols + RIM)
    offset = np.where(row <= cols, row, -1)
    used = ((row <= cols) | (row == cols + RIM - 1)).astype(np.float64)
    place = (np.arange(pencils)[:, None] * cols + offset[None, :]) % nx
    angle = angles(place.reshape(-1), order, nx)
    mask = np.tile(used, pencils)[:, None]
    back = np.concatenate([np.cos(angle) * mask, np.sin(angle) * mask], axis=0)
    return ahead, back


def split(values):
    high = values.astype(BF16)
    return high, (values - high.astype(F32)).astype(BF16)


def dot(left, right):
    return jnp.dot(left, right, preferred_element_type=F32)


def table_left(high, low, values):
    v_high, v_low = split(values)
    return dot(high, v_high) + (dot(high, v_low) + dot(low, v_high))


def table_right(values, high, low):
    v_high, v_low = split(values)
    return dot(v_high, high) + (dot(v_low, high) + dot(v_high, low))


def lane_of():
    return lax.broadcasted_iota(jnp.int32, (1, LANES), 1)


def times_i(values):
    half = LANES // 2
    sign = jnp.where(lane_of() < half, -1.0, 1.0).astype(F32)
    return pltpu.roll(values, half, 1) * sign


def kernel_weight(distance):
    radius = jnp.abs(distance)
    near = 1.0 - 2.5 * radius * radius + 1.5 * radius * radius * radius
    far = 0.5 * (2.0 - radius) * (2.0 - radius) * (1.0 - radius)
    return jnp.where(radius < 1.0, near, jnp.where(radius < 2.0, far, 0.0))


def turned(value, wave, extent, sign):
    wave = wave % extent
    real, imag = value
    if wave == 0:
        return value
    if 2 * wave == extent:
        return -real, -imag
    if 4 * wave == extent:
        return (-imag, real) if sign > 0 else (imag, -real)
    if 4 * wave == 3 * extent:
        return (imag, -real) if sign > 0 else (-imag, real)
    a = math.cos(2.0 * math.pi * wave / extent)
    b = sign * math.sin(2.0 * math.pi * wave / extent)
    return real * a - imag * b, real * b + imag * a


def fft(values, sign):
    count = len(values)
    if count == 1:
        return values
    even, odd = fft(values[::2], sign), fft(values[1::2], sign)
    odd = [turned(v, k, count, sign) for k, v in enumerate(odd)]
    plus = [(a[0] + b[0], a[1] + b[1]) for a, b in zip(even, odd)]
    minus = [(a[0] - b[0], a[1] - b[1]) for a, b in zip(even, odd)]
    return plus + minus


def offset_order(count):
    if count < 4:
        return list(range(count))
    far, near = list(range(count // 2, count)), list(range(1, count // 2))
    order = [0]
    while far or near:
        order += far[:1] + near[:1]
        far, near = far[1:], near[1:]
    return order


def blocks_of(refs, at):
    if len(refs) == 1:
        return [(d, refs[0].at[d]) for d in range(refs[0].shape[0])]
    return [(at ^ k, ref) for k, ref in zip(offset_order(len(refs)), refs)]


def gather_blocks(refs, held, at):
    for d, ref in blocks_of(refs, at):
        held[d] = ref[...]


def packet_kernel(
    counts, strength, offsets, cells, packet, movers, near_counts, near_cells, sems
):
    copies = [
        pltpu.make_async_copy(counts, near_counts, sems.at[0]),
        pltpu.make_async_copy(cells, near_cells, sems.at[1]),
        pltpu.make_async_copy(strength, packet.at[pl.ds(0, 3)], sems.at[2]),
        pltpu.make_async_copy(offsets, packet.at[pl.ds(3, 3)], sems.at[3]),
    ]
    for copy in copies:
        copy.start()
    for copy in copies:
        copy.wait()
    slot = lax.broadcasted_iota(jnp.int32, (1, packet.shape[1]), 1)
    up = near_counts[0:1, 0:1]
    both = up + near_counts[0:1, 1:2]
    packet[6:7] = near_cells[...].astype(F32)
    packet[7:8] = jnp.where(slot < up, 1.0, jnp.where(slot < both, -1.0, 0.0))
    movers[...] = packet[:, : movers.shape[1]]


def deposit_kernel(
    pairs, rims_before, place, own, up1, down1, up2, down2, ambient, t_high, t_low, *refs
):
    rims, refs = refs[:rims_before], refs[rims_before:]
    mesh, rim_high, rim_low = refs[:3]
    total, made = refs[-2:]
    outs = refs[3:-2]
    _, planes, cols, ny = ambient.shape
    rows = cols + RIM
    movers = up2.shape[1]
    count = own.shape[1]
    listed = [2 * pair + parity for pair in pairs for parity in range(2)]

    def decode(ref, start, stop, shift):
        packet = ref[:, start:stop]
        cell = packet[6:7].astype(jnp.int32)
        move = packet[7:8].astype(jnp.int32)
        z_cell = lax.div(cell, cols * ny) + planes * (move + shift)
        x_cell = lax.rem(lax.div(cell, ny), cols)
        return packet[0:6], z_cell, x_cell, lax.rem(cell, ny)

    def joined(pieces):
        return [jnp.concatenate(p, axis=1) if len(p) > 1 else p[0] for p in zip(*pieces)]

    def add_block(pieces, wanted):
        values, z_cell, x_cell, y_cell = joined(pieces)
        width = values.shape[1]
        z_at = lax.broadcasted_iota(jnp.int32, (planes, width), 0)
        w_z = kernel_weight((z_at - z_cell).astype(F32) - values[3:4])
        row = lax.broadcasted_iota(jnp.int32, (rows, width), 0)
        x_at = jnp.where(row < cols + 2, row, jnp.where(row >= rows - 2, row - rows, 4 * rows))
        w_x = kernel_weight((x_at - x_cell).astype(F32) - values[4:5])
        y_at = lax.broadcasted_iota(jnp.int32, (ny, width), 0)
        y_off = lax.rem(y_at - y_cell + (ny + ny // 2), ny) - ny // 2
        w_y = kernel_weight(y_off.astype(F32) - values[5:6])
        y_high, y_low = split(w_y)
        right = jnp.concatenate([y_high, y_high, y_low], axis=1)
        at = [listed.index(z) for z in wanted]
        for c in range(3):
            s_z = values[c : c + 1] * w_z
            left = jnp.concatenate([s_z[z : z + 1] * w_x for z in wanted], axis=0)
            l_high, l_low = split(left)
            left = jnp.concatenate([l_high, l_low, l_high], axis=1)
            added = lax.dot_general(
                left, right, (((1,), (1,)), ((), ())), preferred_element_type=F32
            )
            total[c, at[0] : at[-1] + 1] += added.reshape(len(wanted), rows, ny)

    for n, z in enumerate(listed):
        total[:, n, 0:cols] = ambient[:, z]
    total[:, :, cols:rows] = jnp.zeros((3, len(listed), RIM, ny), F32)
    step = 256
    for at in range(0, count, step):
        add_block([decode(own, at, min(at + step, count), 0)], listed)
    add_block([decode(up1, 0, movers, 1), decode(down1, 0, movers, -1)], listed)
    sides = ((up1, up2, 1, (planes - 2, planes - 1)), (down1, down2, -1, (0, 1)))
    for near, far, shift, wanted in sides:
        if not set(wanted) <= set(listed):
            continue
        whole = [decode(near, movers, count, shift), decode(far, 0, movers, 2 * shift)]
        values, z_cell, x_cell, y_cell = joined(whole)
        for at in range(0, count, step):
            to = min(at + step, count)
            block = (values[:, at:to], z_cell[:, at:to], x_cell[:, at:to], y_cell[:, at:to])
            add_block([block], wanted)

    mesh[...] = total[:, :, 0:cols]
    at = 0
    if rims:
        at = rims[0].shape[0]
        rim_high[0:at] = rims[0][...]
        rim_low[0:at] = rims[1][...]
    for n in range(3 * len(listed)):
        c, i = n // len(listed), n % len(listed)
        rim_high[at + 2 * n : at + 2 * n + 2] = total[c, i, cols : cols + 2]
        rim_low[at + 2 * n : at + 2 * n + 2] = total[c, i, rows - 2 : rows]
    groups = [(c, 2 * n) for c in range(3) for n in range(len(pairs))]
    left = jnp.concatenate(
        [jnp.concatenate([total[c, n], total[c, n + 1]], axis=1) for c, n in groups], axis=0
    )
    wide = table_right(left, t_high[...], t_low[...])
    for n in range(len(groups)):
        for g in range(made.shape[0]):
            made[g, :, n * LANES : (n + 1) * LANES] = wide[
                n * rows : (n + 1) * rows, g * LANES : (g + 1) * LANES
            ]
    for d, out in blocks_of(outs, place[1]):
        out[...] = made[d]


def x_ahead_kernel(sends, place, t_high, t_low, *refs):
    held, made = refs[-2:]
    outs, parts = refs[-2 - sends : -2], refs[: -2 - sends]
    gather_blocks(parts, held, place[1])
    pencils, rows, width = held.shape
    cols = rows - RIM
    row = lax.broadcasted_iota(jnp.int32, (RIM, width), 0)
    pieces = []
    for h in range(pencils):
        from_low = held[(h - 1) % pencils, cols:rows]
        from_high = held[(h + 1) % pencils, cols:rows]
        pieces.append(held[h, 0:RIM] + jnp.where(row < 2, from_low, 0.0))
        pieces.append(held[h, RIM : cols - RIM])
        pieces.append(held[h, cols - RIM : cols] + jnp.where(row >= RIM - 2, from_high, 0.0))
    both = table_left(t_high[...], t_low[...], jnp.concatenate(pieces, axis=0))
    half = both.shape[0] // 2
    for n in range(width // LANES):
        lanes = slice(n * LANES, (n + 1) * LANES)
        value = both[:half, lanes] - times_i(both[half:, lanes])
        made[:, :, lanes] = value.reshape(made.shape[0], made.shape[1], LANES)
    for d, out in blocks_of(outs, place[0]):
        out[...] = made[d]


def x_back_kernel(sends, tables, place, *refs):
    held, made = refs[-2:]
    outs, parts = refs[-2 - sends : -2], refs[: -2 - sends]
    gather_blocks(parts, held, place[0])
    pencils, rows, width = made.shape
    both = table_left(tables[0][...], tables[1][...], held[...].reshape(-1, width))
    half = both.shape[0] // 2
    for n in range(width // LANES):
        lanes = slice(n * LANES, (n + 1) * LANES)
        value = both[:half, lanes] + times_i(both[half:, lanes])
        made[:, :, lanes] = value.reshape(pencils, rows, LANES)
    for d, out in blocks_of(outs, place[1]):
        out[...] = made[d]


def wave_lanes():
    lane = lane_of()
    return lane < LANES // 2, (lane // (LANES // 4)) % 2 == 0


def roll(values, shift):
    return pltpu.roll(values, shift, 1)


def cross_half(a, b):
    low, _ = wave_lanes()
    half = LANES // 2
    return jnp.where(low, a, roll(b, half)), jnp.where(low, roll(a, half), b)


def cross_quarter(a, b):
    _, first = wave_lanes()
    quarter = LANES // 4
    return (
        jnp.where(first, a, roll(b, quarter)),
        jnp.where(first, roll(a, LANES - quarter), b),
    )


def lanes_at(c, count, i):
    return pl.ds(pl.multiple_of((c * count + i) * LANES, LANES), LANES)


def enter_kernel(pairs, nz, place, *refs):
    parts, data = refs[:-1], refs[-1]
    _, _, _, slabs, tile, _ = data.shape

    def body(c, carry):
        for i, pair in enumerate(pairs):
            lanes = lanes_at(c, len(pairs), i)
            for s, ref in blocks_of(parts, place[0]):
                quad = [ref[q * tile : (q + 1) * tile, lanes] for q in range(4)]
                real0, imag0 = cross_half(quad[0], quad[2])
                real1, imag1 = cross_half(quad[1], quad[3])
                for part, (a, b) in enumerate(((real0, real1), (imag0, imag1))):
                    even, odd = cross_quarter(a, b)
                    data[c, part, 2 * i, s] = even
                    data[c, part, 2 * i + 1, s] = odd
            for parity in range(2):
                at = 2 * i + parity
                line = [(data[c, 0, at, s], data[c, 1, at, s]) for s in range(slabs)]
                for k, v in enumerate(fft(line, -1.0)):
                    v = turned(v, (2 * pair + parity) * k, nz, -1.0)
                    data[c, 0, at, k], data[c, 1, at, k] = v
        return carry

    lax.fori_loop(0, 3, body, 0)


def pass_kernel(before, *refs):
    for source, target in zip(refs[: len(refs) // 2], refs[len(refs) // 2 :]):
        target[...] = source[...]


def leave_kernel(pairs, nz, place, source, *refs):
    outs, data = refs[:-1], refs[-1]
    _, _, _, slabs, tile, _ = source.shape

    def body(c, carry):
        for i, pair in enumerate(pairs):
            lanes = lanes_at(c, len(pairs), i)
            for parity in range(2):
                at = 2 * i + parity
                line = [
                    turned(
                        (source[c, 0, at, k], source[c, 1, at, k]),
                        (2 * pair + parity) * k,
                        nz,
                        1.0,
                    )
                    for k in range(slabs)
                ]
                for s, v in enumerate(fft(line, 1.0)):
                    data[c, 0, at, s], data[c, 1, at, s] = v
            for s, ref in blocks_of(outs, place[0]):
                real0, real1 = cross_quarter(data[c, 0, 2 * i, s], data[c, 0, 2 * i + 1, s])
                imag0, imag1 = cross_quarter(data[c, 1, 2 * i, s], data[c, 1, 2 * i + 1, s])
                quad = [None] * 4
                quad[0], quad[2] = cross_half(real0, imag0)
                quad[1], quad[3] = cross_half(real1, imag1)
                for q in range(4):
                    ref[q * tile : (q + 1) * tile, lanes] = quad[q]
        return carry

    lax.fori_loop(0, 3, body, 0)


def curl_kernel(chunks, nx, ny, place, low_rim, high_rim, *refs):
    sources, outs = refs[: len(chunks)], refs[len(chunks) : 2 * len(chunks)]
    spectrum = refs[-1]
    _, _, nz, tile, _ = spectrum.shape
    slabs = sources[0].shape[3]
    planes = nz // slabs
    modes, half = LANES // 4, LANES // 2
    slab_at, pencil_at = place[0], place[1]
    spot = {}
    for n, chunk in enumerate(chunks):
        for i, pair in enumerate(chunk):
            spot[2 * pair], spot[2 * pair + 1] = (n, 2 * i), (n, 2 * i + 1)

    def across_planes(k, carry):
        for c in range(3):
            line = []
            for l in range(planes):
                n, i = spot[l]
                line.append((sources[n][c, 0, i, k], sources[n][c, 1, i, k]))
            for n, v in enumerate(fft(line, -1.0)):
                spectrum[c, 0, k + slabs * n], spectrum[c, 1, k + slabs * n] = v
        return carry

    reach = 2 * tile
    row = lax.broadcasted_iota(jnp.int32, (tile, LANES), 0)
    lane = lax.broadcasted_iota(jnp.int32, (tile, LANES), 1)
    number = slab_at * reach + (lane // modes) % 2 * tile + row
    ahead = lane < half
    mode = lane % modes + pencil_at * modes
    alone = number == 0
    number = number.astype(F32) * (2.0 * math.pi / nx)
    x_base = jnp.where(ahead, number, jnp.where(alone, math.pi, -number))
    x_trim = jnp.where(ahead, number, jnp.where(alone, 0.0, -number))
    wave_y = mode.astype(F32) * (2.0 * math.pi / ny)
    packed = mode == 0
    x_sq = x_base * x_base
    lateral = x_sq + wave_y * wave_y

    def curl_at(k, with_mirror):
        z_wave = jnp.where(k < nz // 2, k, k - nz).astype(F32) * (2.0 * math.pi / nz)
        z_trim = jnp.where(k == nz // 2, 0.0, z_wave)
        full = lateral + z_wave * z_wave
        empty = full == 0.0
        inverse = jnp.where(empty, 0.0, 1.0 / jnp.where(empty, 1.0, full))
        if with_mirror:
            other = 1.0 / (x_sq + (z_wave * z_wave + math.pi * math.pi))
            mirror = jnp.where(packed, 0.5 * (inverse - other), 0.0)
            inverse = jnp.where(packed, 0.5 * (inverse + other), inverse)
            opposite = lax.rem(nz - k, nz)
        stream = []
        for c in range(3):
            value = [spectrum[c, part, k] * inverse for part in range(2)]
            if with_mirror:
                for part, sign in enumerate((1.0, -1.0)):
                    there = spectrum[c, part, opposite]
                    there = jnp.where(alone, there, roll(there, half))
                    value[part] = value[part] + (mirror * sign) * there
            stream.append(value)
        made = []
        for part in range(2):
            s = [value[part] for value in stream]
            made.append(
                (
                    x_trim * s[2] - wave_y * s[1],
                    wave_y * s[0] - z_trim * s[2],
                    z_trim * s[1] - x_trim * s[0],
                )
            )
        return [(-made[1][c], made[0][c]) for c in range(3)]

    def curl_all(with_mirror):
        def body(k, carry):
            made = [curl_at(k + slabs * n, with_mirror) for n in range(planes)]
            for c in range(3):
                for l, v in enumerate(fft([m[c] for m in made], 1.0)):
                    n, i = spot[l]
                    outs[n][c, 0, i, k], outs[n][c, 1, i, k] = v
            return carry

        lax.fori_loop(0, slabs, body, 0)

    lax.fori_loop(0, slabs, across_planes, 0)

    @pl.when(pencil_at == 0)
    def _():
        curl_all(True)

    @pl.when(pencil_at != 0)
    def _():
        curl_all(False)


def planes_of(held, pairs, tables):
    pencils, rows, _ = held.shape
    groups = [(c, pair) for c in range(3) for pair in pairs]
    left = jnp.concatenate(
        [
            jnp.concatenate(
                [held[h, :, n * LANES : (n + 1) * LANES] for h in range(pencils)], axis=1
            )
            for n in range(len(groups))
        ],
        axis=0,
    )
    ny = tables[0].shape[1] // 2
    wide = table_right(left, tables[0][...], tables[1][...])
    made = {}
    for n, (c, pair) in enumerate(groups):
        for parity in range(2):
            made[c, 2 * pair + parity] = wide[
                n * rows : (n + 1) * rows, parity * ny : (parity + 1) * ny
            ]
    return made


def hold(tall, c, n, value):
    rows = value.shape[0]
    tall[c, n, RIM : RIM + rows] = value
    tall[c, n, 0:RIM] = value[rows - RIM : rows]


def edge_kernel(pairs, tables, place, *refs):
    tall, first, last, held = refs[-4:]
    gather_blocks(refs[:-4], held, place[1])
    listed = [2 * pair + parity for pair in pairs for parity in range(2)]
    cols = first.shape[1]
    values = planes_of(held, pairs, tables)
    for c in range(3):
        for n, z in enumerate(listed):
            hold(tall, c, n, values[c, z])
        first[c] = values[c, listed[0]][0:cols]
        last[c] = values[c, listed[-1]][0:cols]


def where_planes(chunks):
    spot = {}
    for n, chunk in enumerate(chunks):
        for i, pair in enumerate(chunk):
            spot[2 * pair], spot[2 * pair + 1] = (n, 2 * i), (n, 2 * i + 1)
    return spot


def rim_start(meshes, which, c, i):
    before = 6 * meshes[1].shape[1] if which == 0 else 0
    return before + 2 * (c * meshes[which].shape[1] + i)


def stretch_plane(out, mesh, rims, at, rows_of, above, below):
    cols, ny = out[0].shape
    low_rim, high_rim = rims
    for c in range(3):
        out[c][...] = mesh[c][...]
        out[c][0:2] += low_rim[at[c] : at[c] + 2]
        out[c][cols - 2 : cols] += high_rim[at[c] : at[c] + 2]
    omega = [ref[...] for ref in out]
    for c in range(3):
        value = rows_of(c, RIM)
        along_z = (above(c) - below(c)) * 0.5
        along_x = (rows_of(c, RIM + 1) - rows_of(c, RIM - 1)) * 0.5
        along_y = (pltpu.roll(value, ny - 1, 1) - pltpu.roll(value, 1, 1)) * 0.5
        stretch = omega[0] * along_z + omega[1] * along_x + omega[2] * along_y
        out[c][...] = omega[c] + TIME_STEP * stretch


def ends_kernel(_, __, edges, before, after, low_rim, high_rim, *refs):
    meshes, vorticity, out, sems = refs[:-4], refs[-3], refs[-2], refs[-1]
    cols = before.shape[1]
    size = edges.shape[1]
    copies = []

    def rows_of(i):
        return lambda c, start=RIM: edges[c, i, start : start + cols]

    for n, i in enumerate((0, size - 1)):
        stretch_plane(
            [out.at[c, n] for c in range(3)],
            [meshes[0].at[c, i] for c in range(3)],
            (low_rim, high_rim),
            [rim_start(meshes, 0, c, i) for c in range(3)],
            rows_of(i),
            (lambda c: after[c]) if i else rows_of(1),
            rows_of(size - 2) if i else (lambda c: before[c]),
        )
        copies.append(
            pltpu.make_async_copy(
                out.at[:, n], vorticity.at[:, n * (vorticity.shape[1] - 1)], sems.at[n]
            )
        )
        copies[-1].start()
    for copy in copies:
        copy.wait()


def stretch_kernel(chunks, tables, place, edges, low_rim, high_rim, *refs):
    meshes, refs = refs[:2], refs[2:]
    velocity, vorticity, held, inner, omega, sems = refs[-6:]
    _, planes, cols, ny = velocity.shape
    spot = where_planes(chunks)
    talls = (edges, inner)
    sent = []

    def send(source, target):
        sent.append(pltpu.make_async_copy(source, target, sems.at[len(sent)]))
        sent[-1].start()

    def rows_of(z):
        n, i = spot[z]
        return lambda c, start=RIM: talls[n][c, i, start : start + cols]

    def send_velocity(which):
        for z in range(planes):
            n, i = spot[z]
            if n == which:
                send(talls[n].at[:, i, pl.ds(RIM, cols)], velocity.at[:, z])

    send_velocity(0)
    gather_blocks(refs[:-6], held, place[1])
    for (c, z), value in planes_of(held, chunks[1], tables).items():
        hold(inner, c, spot[z][1], value)
    send_velocity(1)
    for z in range(1, planes - 1):
        which, i = spot[z]
        stretch_plane(
            [omega.at[c, z] for c in range(3)],
            [meshes[which].at[c, i] for c in range(3)],
            (low_rim, high_rim),
            [rim_start(meshes, which, c, i) for c in range(3)],
            rows_of(z),
            rows_of(z + 1),
            rows_of(z - 1),
        )
        send(omega.at[:, z], vorticity.at[:, z])
    for copy in sent:
        copy.wait()


VM = pl.BlockSpec(memory_space=pltpu.VMEM)
SM = pl.BlockSpec(memory_space=pltpu.SMEM)
AN = pl.BlockSpec(memory_space=pl.ANY)
HB = pl.BlockSpec(memory_space=pltpu.HBM)


def kept(values):
    return pltpu.with_memory_space_constraint(values, pltpu.HBM)


def loaded(kernel):
    def run(place, t_high, t_low, *refs):
        kernel((t_high, t_low), place, *refs)

    return run


def call(kernel, ins, outs, scratch=(), sems=0, micros=2.0, moved=None, aliases=None):
    extra = [pltpu.SemaphoreType.DMA((sems,))] if sems else []
    return pl.pallas_call(
        kernel,
        out_shape=[jax.ShapeDtypeStruct(shape, F32) for _, shape in outs],
        in_specs=[spec for spec, _ in ins],
        out_specs=[spec for spec, _ in outs],
        scratch_shapes=[pltpu.VMEM(shape, kind) for shape, kind in scratch] + extra,
        compiler_params=pltpu.CompilerParams(vmem_limit_bytes=VMEM),
        input_output_aliases=aliases or {},
        cost_estimate=pl.CostEstimate(
            flops=int(micros * 1.0e9),
            bytes_accessed=int(micros * 3.0e6) if moved is None else moved,
            transcendentals=0,
        ),
    )(*[value for _, value in ins])


def ring(axis, step):
    count = lax.axis_size(axis)
    return [(i, (i + step) % count) for i in range(count)]


def spread(axis):
    count = lax.axis_size(axis)
    return count <= 8 and count & (count - 1) == 0


def sent_shapes(axis, rows, width, whole=False):
    count = lax.axis_size(axis)
    return [(count, rows, width)] if whole or not spread(axis) else [(rows, width)] * count


def exchange(blocks, axis, start=0):
    if not spread(axis):
        return [lax.all_to_all(blocks[0], axis, split_axis=0, concat_axis=0, tiled=True)]
    count = lax.axis_size(axis)
    return [
        lax.ppermute(block, axis, [(i, i ^ k) for i in range(count)]) if k else block
        for k, block in zip(offset_order(count)[start:], blocks)
    ]


def on_device(strength, offsets, cell_index, migrate_count, ambient):
    _, planes, cols, ny = ambient.shape
    slabs, pencils = lax.axis_size("gz"), lax.axis_size("gx")
    nx, nz, rows = cols * pencils, planes * slabs, cols + RIM
    count = strength.shape[1]
    pair_count = planes // 2
    chunks = ((0, pair_count - 1), tuple(range(1, pair_count - 1)))
    widths = [3 * len(c) * LANES for c in chunks]
    block = nx // slabs

    y_ahead, y_back = [split_table(t) for t in y_tables(ny, pencils, 1.0 / (float(nx) * ny * nz))]
    x_ahead, x_back = [split_table(t) for t in x_tables(nx, cols, pencils, slabs)]
    place = jnp.stack([lax.axis_index("gz"), lax.axis_index("gx")]).astype(jnp.int32)
    here = (SM, place)

    packet, movers = call(
        packet_kernel,
        [
            (HB, kept(migrate_count.reshape(1, 2))),
            (HB, kept(strength)),
            (HB, kept(offsets)),
            (HB, kept(cell_index.reshape(1, count))),
        ],
        [(VM, (8, count)), (VM, (8, 2 * MIG))],
        [((1, 2), jnp.int32), ((1, count), jnp.int32)],
        sems=4,
        micros=1.0,
        moved=1000,
    )
    up1 = lax.ppermute(packet, "gz", ring("gz", -1))
    down1 = lax.ppermute(packet, "gz", ring("gz", 1))
    up2 = lax.ppermute(movers, "gz", ring("gz", -2))
    down2 = lax.ppermute(movers, "gz", ring("gz", 2))

    meshes, rims, parts = [None, None], [], [None, None]
    for n in (1, 0):
        chunk, width = chunks[n], widths[n]
        size = 2 * len(chunk)
        rim = (6 * size + (rims[0].shape[0] if rims else 0), ny)
        mesh, rim_high, rim_low, *part = call(
            functools.partial(deposit_kernel, chunk, len(rims)),
            [here]
            + [(VM, value) for value in (packet, up1, down1, up2, down2)]
            + [(VM, ambient), (VM, y_ahead[0]), (VM, y_ahead[1])]
            + [(VM, value) for value in rims],
            [(VM, (3, size, cols, ny)), (VM, rim), (VM, rim)]
            + [(VM, shape) for shape in sent_shapes("gx", rows, width)],
            [((3, size, rows, ny), F32), ((pencils, rows, width), F32)],
            micros=5.0,
        )
        meshes[n] = mesh
        rims = [rim_high, rim_low]
        parts[n] = exchange(part, "gx")
    low_rim = lax.ppermute(rims[0], "gx", ring("gx", 1))
    high_rim = lax.ppermute(rims[1], "gx", ring("gx", -1))

    tile = max(1, block // 4)
    data = [None, None]
    for n in (1, 0):
        chunk, part, width = chunks[n], parts[n], widths[n]
        shapes = sent_shapes("gz", block, width)
        part = call(
            functools.partial(x_ahead_kernel, len(shapes)),
            [here, (VM, x_ahead[0]), (VM, x_ahead[1])] + [(VM, p) for p in part],
            [(VM, shape) for shape in shapes],
            [((pencils, rows, width), F32), ((slabs, block, width), F32)],
        )
        (entered,) = call(
            functools.partial(enter_kernel, chunk, nz),
            [here] + [(VM, p) for p in exchange(part, "gz")],
            [(VM, (3, 2, 2 * len(chunk), slabs, tile, LANES))],
        )
        data[n] = entered
    data = call(
        functools.partial(curl_kernel, chunks, nx, ny),
        [here, (VM, low_rim), (VM, high_rim)] + [(VM, d) for d in data],
        [(VM, d.shape) for d in data],
        [((3, 2, nz, tile, LANES), F32)],
        micros=5.0,
    )
    plane = (3, cols, ny)
    tables = [(VM, t) for t in y_back]
    tall = [(3, 2 * len(chunk), cols + 2 * RIM, ny) for chunk in chunks]
    left = [
        call(
            functools.partial(leave_kernel, chunk, nz),
            [here, (VM, source)],
            [(VM, shape) for shape in sent_shapes("gz", block, width)],
            [(source.shape, F32)],
        )
        for chunk, source, width in zip(chunks, data, widths)
    ]

    def back(part, width):
        shapes = sent_shapes("gx", rows, width)
        part = call(
            loaded(functools.partial(x_back_kernel, len(shapes))),
            [here]
            + [(VM, t) for t in x_back]
            + [(VM, p) for p in part],
            [(VM, shape) for shape in shapes],
            [((slabs, block, width), F32), ((pencils, rows, width), F32)],
        )
        return exchange(part, "gx")

    early = max(1, len(left[1]) - LATE)
    second = exchange(left[1][:early], "gz")
    parts = [back(exchange(left[0], "gz"), widths[0])]
    edges, first, last = call(
        loaded(functools.partial(edge_kernel, chunks[0])),
        [here] + tables + [(VM, p) for p in parts[0]],
        [(VM, tall[0]), (VM, plane), (VM, plane)],
        [((pencils, rows, widths[0]), F32)],
    )
    if early < len(left[1]):
        late = call(
            pass_kernel,
            [(AN, parts[0][0])] + [(VM, p) for p in left[1][early:]],
            [(VM, p.shape) for p in left[1][early:]],
            micros=0.3,
        )
        second += exchange(late, "gz", early)
    parts.append(back(second, widths[1]))
    after = lax.ppermute(first, "gz", ring("gz", -1))
    before = lax.ppermute(last, "gz", ring("gz", 1))
    velocity, vorticity = call(
        loaded(functools.partial(stretch_kernel, chunks)),
        [here]
        + tables
        + [(VM, v) for v in (edges, low_rim, high_rim, *meshes)]
        + [(VM, p) for p in parts[1]],
        [(AN, ambient.shape), (AN, ambient.shape)],
        [
            ((pencils, rows, widths[1]), F32),
            (tall[1], F32),
            ((3, planes, cols, ny), F32),
        ],
        sems=2 * planes,
        micros=4.0,
    )
    return tuple(
        call(
            ends_kernel,
            [(AN, velocity), (AN, vorticity)]
            + [(VM, v) for v in (edges, before, after, low_rim, high_rim, *meshes)],
            [(AN, ambient.shape), (AN, ambient.shape)],
            [((3, 2, cols, ny), F32)],
            sems=2,
            micros=1.0,
            aliases={0: 0, 1: 1},
        )
    )


def solution(mesh):
    placed = (
        P(None, ("gz", "gx")),
        P(None, ("gz", "gx")),
        P(("gz", "gx")),
        P("gz", "gx", None),
        P(None, "gz", "gx", None),
    )
    return jax.shard_map(
        on_device,
        mesh=mesh,
        in_specs=placed,
        out_specs=(P(None, "gz", "gx", None), P(None, "gz", "gx", None)),
        check_vma=False,
    )
```

```python
import functools
import math

import jax
import jax.numpy as jnp
import ml_dtypes
import numpy as np
from jax import lax
from jax.experimental import pallas as pl
from jax.experimental.pallas import tpu as pltpu
from jax.sharding import PartitionSpec as P

MIG = 64
LANES = 128
RIM = 8
LATE = 3
TIME_STEP = 0.25
VMEM = 24 * 1024 * 1024
F32 = jnp.float32
BF16 = jnp.bfloat16


def split_table(table):
    high = table.astype(np.float32).astype(ml_dtypes.bfloat16)
    low = (table - high.astype(np.float64)).astype(np.float32).astype(ml_dtypes.bfloat16)
    return high, low


def angles(rows, columns, extent):
    return 2.0 * np.pi * (np.multiply.outer(rows, columns) % extent) / extent


def y_tables(ny, pencils, scale):
    modes = ny // (2 * pencils)
    position = np.arange(ny)
    angle = angles(position, np.arange(ny // 2), ny)
    real, imag = np.cos(angle), -np.sin(angle)
    imag[:, 0] = 1.0 - 2.0 * (position % 2)
    weight = np.where(np.arange(ny // 2) == 0, 1.0, 2.0) * scale
    ahead = np.zeros((2, ny, pencils, 2, 2, modes))
    back = np.zeros((pencils, 2, 2, modes, 2, ny))
    for parity in range(2):
        for part, values in enumerate((real, imag)):
            ahead[parity, :, :, part, parity] = values.reshape(ny, pencils, modes)
            back[:, part, parity, :, parity] = (values * weight).T.reshape(pencils, modes, ny)
    return ahead.reshape(2 * ny, -1), back.reshape(-1, 2 * ny)


def wave_order(nx, slabs):
    half = nx // 2
    ahead = np.arange(half).reshape(slabs, 1, half // slabs)
    behind = np.where(ahead == 0, half, (nx - ahead) % nx)
    return np.concatenate([ahead, behind], axis=1).reshape(-1)


def x_tables(nx, cols, pencils, slabs):
    order = wave_order(nx, slabs)
    angle = angles(order, np.arange(nx), nx)
    ahead = np.concatenate([np.cos(angle), np.sin(angle)], axis=0)
    row = np.arange(cols + RIM)
    offset = np.where(row <= cols, row, -1)
    used = ((row <= cols) | (row == cols + RIM - 1)).astype(np.float64)
    place = (np.arange(pencils)[:, None] * cols + offset[None, :]) % nx
    angle = angles(place.reshape(-1), order, nx)
    mask = np.tile(used, pencils)[:, None]
    back = np.concatenate([np.cos(angle) * mask, np.sin(angle) * mask], axis=0)
    return ahead, back


def split(values):
    high = values.astype(BF16)
    return high, (values - high.astype(F32)).astype(BF16)


def dot(left, right):
    return jnp.dot(left, right, preferred_element_type=F32)


def table_left(high, low, values):
    v_high, v_low = split(values)
    return dot(high, v_high) + (dot(high, v_low) + dot(low, v_high))


def table_right(values, high, low):
    v_high, v_low = split(values)
    return dot(v_high, high) + (dot(v_low, high) + dot(v_high, low))


def lane_of():
    return lax.broadcasted_iota(jnp.int32, (1, LANES), 1)


def times_i(values):
    half = LANES // 2
    sign = jnp.where(lane_of() < half, -1.0, 1.0).astype(F32)
    return pltpu.roll(values, half, 1) * sign


def kernel_weight(distance):
    radius = jnp.abs(distance)
    near = 1.0 + radius * radius * (1.5 * radius - 2.5)
    rest = jnp.maximum(2.0 - radius, 0.0)
    return jnp.where(radius < 1.0, near, 0.5 * rest * rest * (1.0 - radius))


def quotient(values, size):
    if size & (size - 1):
        return lax.div(values, size)
    return lax.shift_right_logical(values, size.bit_length() - 1)


def remainder(values, size):
    if size & (size - 1):
        return lax.rem(values, size)
    return values & (size - 1)


def turned(value, wave, extent, sign):
    wave = wave % extent
    real, imag = value
    if wave == 0:
        return value
    if 2 * wave == extent:
        return -real, -imag
    if 4 * wave == extent:
        return (-imag, real) if sign > 0 else (imag, -real)
    if 4 * wave == 3 * extent:
        return (imag, -real) if sign > 0 else (-imag, real)
    a = math.cos(2.0 * math.pi * wave / extent)
    b = sign * math.sin(2.0 * math.pi * wave / extent)
    return real * a - imag * b, real * b + imag * a


def fft(values, sign):
    count = len(values)
    if count == 1:
        return values
    even, odd = fft(values[::2], sign), fft(values[1::2], sign)
    odd = [turned(v, k, count, sign) for k, v in enumerate(odd)]
    plus = [(a[0] + b[0], a[1] + b[1]) for a, b in zip(even, odd)]
    minus = [(a[0] - b[0], a[1] - b[1]) for a, b in zip(even, odd)]
    return plus + minus


def offset_order(count, near_first=False):
    far, near = list(range(count // 2, count)), list(range(1, count // 2))
    if near_first:
        return [0] + near + far
    if count == 4:
        return [0] + far + near
    order = [0]
    while far or near:
        order += far[:1] + near[:1]
        far, near = far[1:], near[1:]
    return order


def blocks_of(refs, at, near_first=False):
    if len(refs) == 1:
        return [(d, refs[0].at[d]) for d in range(refs[0].shape[0])]
    return [(at ^ k, ref) for k, ref in zip(offset_order(len(refs), near_first), refs)]


def gather_blocks(refs, held, at, near_first=False):
    for d, ref in blocks_of(refs, at, near_first):
        held[d] = ref[...]


def packet_kernel(
    counts, strength, offsets, cells, packet, movers, near_counts, near_cells, sems
):
    copies = [
        pltpu.make_async_copy(counts, near_counts, sems.at[0]),
        pltpu.make_async_copy(cells, near_cells, sems.at[1]),
        pltpu.make_async_copy(strength, packet.at[pl.ds(0, 3)], sems.at[2]),
        pltpu.make_async_copy(offsets, packet.at[pl.ds(3, 3)], sems.at[3]),
    ]
    for copy in copies:
        copy.start()
    for copy in copies:
        copy.wait()
    slot = lax.broadcasted_iota(jnp.int32, (1, packet.shape[1]), 1)
    up = near_counts[0:1, 0:1]
    both = up + near_counts[0:1, 1:2]
    packet[6:7] = near_cells[...].astype(F32)
    packet[7:8] = jnp.where(slot < up, 1.0, jnp.where(slot < both, -1.0, 0.0))
    movers[...] = packet[:, : movers.shape[1]]


def deposit_kernel(
    pairs, rims_before, near_first, place, own, up1, down1, up2, down2, ambient, t_high, t_low, *refs
):
    rims, refs = refs[:rims_before], refs[rims_before:]
    mesh, rim_high, rim_low = refs[:3]
    total, made = refs[-2:]
    outs = refs[3:-2]
    _, planes, cols, ny = ambient.shape
    rows = cols + RIM
    movers = up2.shape[1]
    count = own.shape[1]
    listed = [2 * pair + parity for pair in pairs for parity in range(2)]

    def decode(ref, start, stop, shift):
        packet = ref[:, start:stop]
        cell = packet[6:7].astype(jnp.int32)
        move = packet[7:8].astype(jnp.int32)
        z_cell = quotient(cell, cols * ny) + planes * (move + shift)
        x_cell = remainder(quotient(cell, ny), cols)
        return packet[0:6], z_cell, x_cell, remainder(cell, ny)

    def joined(pieces):
        return [jnp.concatenate(p, axis=1) if len(p) > 1 else p[0] for p in zip(*pieces)]

    def add_block(pieces, wanted):
        values, z_cell, x_cell, y_cell = joined(pieces)
        width = values.shape[1]
        z_at = lax.broadcasted_iota(jnp.int32, (planes, width), 0)
        w_z = kernel_weight((z_at - z_cell).astype(F32) - values[3:4])
        row = lax.broadcasted_iota(jnp.int32, (rows, width), 0)
        x_at = jnp.where(row < cols + 2, row, jnp.where(row >= rows - 2, row - rows, 4 * rows))
        w_x = kernel_weight((x_at - x_cell).astype(F32) - values[4:5])
        y_at = lax.broadcasted_iota(jnp.int32, (ny, width), 0)
        y_off = remainder(y_at + (ny + ny // 2 - y_cell), ny) - ny // 2
        w_y = kernel_weight(y_off.astype(F32) - values[5:6])
        y_high, y_low = split(w_y)
        right = jnp.concatenate([y_high, y_high, y_low], axis=1)
        at = [listed.index(z) for z in wanted]
        for c in range(3):
            s_z = values[c : c + 1] * w_z
            left = jnp.concatenate([s_z[z : z + 1] * w_x for z in wanted], axis=0)
            l_high, l_low = split(left)
            left = jnp.concatenate([l_high, l_low, l_high], axis=1)
            added = lax.dot_general(
                left, right, (((1,), (1,)), ((), ())), preferred_element_type=F32
            )
            total[c, at[0] : at[-1] + 1] += added.reshape(len(wanted), rows, ny)

    for n, z in enumerate(listed):
        total[:, n, 0:cols] = ambient[:, z]
    total[:, :, cols:rows] = jnp.zeros((3, len(listed), RIM, ny), F32)
    step = 256
    for at in range(0, count, step):
        add_block([decode(own, at, min(at + step, count), 0)], listed)
    add_block([decode(up1, 0, movers, 1), decode(down1, 0, movers, -1)], listed)
    sides = ((up1, up2, 1, (planes - 2, planes - 1)), (down1, down2, -1, (0, 1)))
    for near, far, shift, wanted in sides:
        if not set(wanted) <= set(listed):
            continue
        whole = [decode(near, movers, count, shift), decode(far, 0, movers, 2 * shift)]
        values, z_cell, x_cell, y_cell = joined(whole)
        for at in range(0, count, step):
            to = min(at + step, count)
            block = (values[:, at:to], z_cell[:, at:to], x_cell[:, at:to], y_cell[:, at:to])
            add_block([block], wanted)

    mesh[...] = total[:, :, 0:cols]
    at = 0
    if rims:
        at = rims[0].shape[0]
        rim_high[0:at] = rims[0][...]
        rim_low[0:at] = rims[1][...]
    for n in range(3 * len(listed)):
        c, i = n // len(listed), n % len(listed)
        rim_high[at + 2 * n : at + 2 * n + 2] = total[c, i, cols : cols + 2]
        rim_low[at + 2 * n : at + 2 * n + 2] = total[c, i, rows - 2 : rows]
    groups = [(c, 2 * n) for c in range(3) for n in range(len(pairs))]
    left = jnp.concatenate(
        [jnp.concatenate([total[c, n], total[c, n + 1]], axis=1) for c, n in groups], axis=0
    )
    wide = table_right(left, t_high[...], t_low[...])
    for n in range(len(groups)):
        for g in range(made.shape[0]):
            made[g, :, n * LANES : (n + 1) * LANES] = wide[
                n * rows : (n + 1) * rows, g * LANES : (g + 1) * LANES
            ]
    for d, out in blocks_of(outs, place[1], near_first):
        out[...] = made[d]


def x_ahead_kernel(sends, near_first, place, t_high, t_low, *refs):
    held, made = refs[-2:]
    outs, parts = refs[-2 - sends : -2], refs[: -2 - sends]
    gather_blocks(parts, held, place[1], near_first)
    pencils, rows, width = held.shape
    cols = rows - RIM
    row = lax.broadcasted_iota(jnp.int32, (RIM, width), 0)
    pieces = []
    for h in range(pencils):
        from_low = held[(h - 1) % pencils, cols:rows]
        from_high = held[(h + 1) % pencils, cols:rows]
        pieces.append(held[h, 0:RIM] + jnp.where(row < 2, from_low, 0.0))
        pieces.append(held[h, RIM : cols - RIM])
        pieces.append(held[h, cols - RIM : cols] + jnp.where(row >= RIM - 2, from_high, 0.0))
    both = table_left(t_high[...], t_low[...], jnp.concatenate(pieces, axis=0))
    half = both.shape[0] // 2
    for n in range(width // LANES):
        lanes = slice(n * LANES, (n + 1) * LANES)
        value = both[:half, lanes] - times_i(both[half:, lanes])
        made[:, :, lanes] = value.reshape(made.shape[0], made.shape[1], LANES)
    for d, out in blocks_of(outs, place[0]):
        out[...] = made[d]


def x_back_kernel(sends, tables, place, *refs):
    held, made = refs[-2:]
    outs, parts = refs[-2 - sends : -2], refs[: -2 - sends]
    gather_blocks(parts, held, place[0])
    pencils, rows, width = made.shape
    both = table_left(tables[0][...], tables[1][...], held[...].reshape(-1, width))
    half = both.shape[0] // 2
    for n in range(width // LANES):
        lanes = slice(n * LANES, (n + 1) * LANES)
        value = both[:half, lanes] + times_i(both[half:, lanes])
        made[:, :, lanes] = value.reshape(pencils, rows, LANES)
    for d, out in blocks_of(outs, place[1]):
        out[...] = made[d]


def wave_lanes():
    lane = lane_of()
    return lane < LANES // 2, (lane // (LANES // 4)) % 2 == 0


def roll(values, shift):
    return pltpu.roll(values, shift, 1)


def cross_half(a, b):
    low, _ = wave_lanes()
    half = LANES // 2
    return jnp.where(low, a, roll(b, half)), jnp.where(low, roll(a, half), b)


def cross_quarter(a, b):
    _, first = wave_lanes()
    quarter = LANES // 4
    return (
        jnp.where(first, a, roll(b, quarter)),
        jnp.where(first, roll(a, LANES - quarter), b),
    )


def lanes_at(c, count, i):
    return pl.ds(pl.multiple_of((c * count + i) * LANES, LANES), LANES)


def enter_kernel(pairs, nz, place, *refs):
    parts, data = refs[:-1], refs[-1]
    _, _, _, slabs, tile, _ = data.shape

    def body(c, carry):
        for i, pair in enumerate(pairs):
            lanes = lanes_at(c, len(pairs), i)
            for s, ref in blocks_of(parts, place[0]):
                quad = [ref[q * tile : (q + 1) * tile, lanes] for q in range(4)]
                real0, imag0 = cross_half(quad[0], quad[2])
                real1, imag1 = cross_half(quad[1], quad[3])
                for part, (a, b) in enumerate(((real0, real1), (imag0, imag1))):
                    even, odd = cross_quarter(a, b)
                    data[c, part, 2 * i, s] = even
                    data[c, part, 2 * i + 1, s] = odd
            for parity in range(2):
                at = 2 * i + parity
                line = [(data[c, 0, at, s], data[c, 1, at, s]) for s in range(slabs)]
                for k, v in enumerate(fft(line, -1.0)):
                    v = turned(v, (2 * pair + parity) * k, nz, -1.0)
                    data[c, 0, at, k], data[c, 1, at, k] = v
        return carry

    lax.fori_loop(0, 3, body, 0)


def pass_kernel(before, *refs):
    for source, target in zip(refs[: len(refs) // 2], refs[len(refs) // 2 :]):
        target[...] = source[...]


def leave_kernel(pairs, nz, place, source, *refs):
    outs, data = refs[:-1], refs[-1]
    _, _, _, slabs, tile, _ = source.shape

    def body(c, carry):
        for i, pair in enumerate(pairs):
            lanes = lanes_at(c, len(pairs), i)
            for parity in range(2):
                at = 2 * i + parity
                line = [
                    turned(
                        (source[c, 0, at, k], source[c, 1, at, k]),
                        (2 * pair + parity) * k,
                        nz,
                        1.0,
                    )
                    for k in range(slabs)
                ]
                for s, v in enumerate(fft(line, 1.0)):
                    data[c, 0, at, s], data[c, 1, at, s] = v
            for s, ref in blocks_of(outs, place[0]):
                real0, real1 = cross_quarter(data[c, 0, 2 * i, s], data[c, 0, 2 * i + 1, s])
                imag0, imag1 = cross_quarter(data[c, 1, 2 * i, s], data[c, 1, 2 * i + 1, s])
                quad = [None] * 4
                quad[0], quad[2] = cross_half(real0, imag0)
                quad[1], quad[3] = cross_half(real1, imag1)
                for q in range(4):
                    ref[q * tile : (q + 1) * tile, lanes] = quad[q]
        return carry

    lax.fori_loop(0, 3, body, 0)


def curl_kernel(chunks, nx, ny, place, low_rim, high_rim, *refs):
    sources, outs = refs[: len(chunks)], refs[len(chunks) : 2 * len(chunks)]
    spectrum = refs[-1]
    _, _, nz, tile, _ = spectrum.shape
    slabs = sources[0].shape[3]
    planes = nz // slabs
    modes, half = LANES // 4, LANES // 2
    slab_at, pencil_at = place[0], place[1]
    spot = {}
    for n, chunk in enumerate(chunks):
        for i, pair in enumerate(chunk):
            spot[2 * pair], spot[2 * pair + 1] = (n, 2 * i), (n, 2 * i + 1)

    def across_planes(k, carry):
        for c in range(3):
            line = []
            for l in range(planes):
                n, i = spot[l]
                line.append((sources[n][c, 0, i, k], sources[n][c, 1, i, k]))
            for n, v in enumerate(fft(line, -1.0)):
                spectrum[c, 0, k + slabs * n], spectrum[c, 1, k + slabs * n] = v
        return carry

    reach = 2 * tile
    row = lax.broadcasted_iota(jnp.int32, (tile, LANES), 0)
    lane = lax.broadcasted_iota(jnp.int32, (tile, LANES), 1)
    number = slab_at * reach + (lane // modes) % 2 * tile + row
    ahead = lane < half
    mode = lane % modes + pencil_at * modes
    alone = number == 0
    number = number.astype(F32) * (2.0 * math.pi / nx)
    x_base = jnp.where(ahead, number, jnp.where(alone, math.pi, -number))
    x_trim = jnp.where(ahead, number, jnp.where(alone, 0.0, -number))
    wave_y = mode.astype(F32) * (2.0 * math.pi / ny)
    packed = mode == 0
    x_sq = x_base * x_base
    lateral = x_sq + wave_y * wave_y

    def curl_at(k, with_mirror):
        z_wave = jnp.where(k < nz // 2, k, k - nz).astype(F32) * (2.0 * math.pi / nz)
        z_trim = jnp.where(k == nz // 2, 0.0, z_wave)
        full = lateral + z_wave * z_wave
        empty = full == 0.0
        inverse = jnp.where(empty, 0.0, 1.0 / jnp.where(empty, 1.0, full))
        if with_mirror:
            other = 1.0 / (x_sq + (z_wave * z_wave + math.pi * math.pi))
            mirror = jnp.where(packed, 0.5 * (inverse - other), 0.0)
            inverse = jnp.where(packed, 0.5 * (inverse + other), inverse)
            opposite = lax.rem(nz - k, nz)
        stream = []
        for c in range(3):
            value = [spectrum[c, part, k] * inverse for part in range(2)]
            if with_mirror:
                for part, sign in enumerate((1.0, -1.0)):
                    there = spectrum[c, part, opposite]
                    there = jnp.where(alone, there, roll(there, half))
                    value[part] = value[part] + (mirror * sign) * there
            stream.append(value)
        made = []
        for part in range(2):
            s = [value[part] for value in stream]
            made.append(
                (
                    x_trim * s[2] - wave_y * s[1],
                    wave_y * s[0] - z_trim * s[2],
                    z_trim * s[1] - x_trim * s[0],
                )
            )
        return [(-made[1][c], made[0][c]) for c in range(3)]

    def curl_all(with_mirror):
        def body(k, carry):
            made = [curl_at(k + slabs * n, with_mirror) for n in range(planes)]
            for c in range(3):
                for l, v in enumerate(fft([m[c] for m in made], 1.0)):
                    n, i = spot[l]
                    outs[n][c, 0, i, k], outs[n][c, 1, i, k] = v
            return carry

        lax.fori_loop(0, slabs, body, 0)

    lax.fori_loop(0, slabs, across_planes, 0)

    @pl.when(pencil_at == 0)
    def _():
        curl_all(True)

    @pl.when(pencil_at != 0)
    def _():
        curl_all(False)


def planes_of(held, pairs, tables):
    pencils, rows, _ = held.shape
    groups = [(c, pair) for c in range(3) for pair in pairs]
    left = jnp.concatenate(
        [
            jnp.concatenate(
                [held[h, :, n * LANES : (n + 1) * LANES] for h in range(pencils)], axis=1
            )
            for n in range(len(groups))
        ],
        axis=0,
    )
    ny = tables[0].shape[1] // 2
    wide = table_right(left, tables[0][...], tables[1][...])
    made = {}
    for n, (c, pair) in enumerate(groups):
        for parity in range(2):
            made[c, 2 * pair + parity] = wide[
                n * rows : (n + 1) * rows, parity * ny : (parity + 1) * ny
            ]
    return made


def hold(tall, c, n, value):
    rows = value.shape[0]
    tall[c, n, RIM : RIM + rows] = value
    tall[c, n, 0:RIM] = value[rows - RIM : rows]


def edge_kernel(pairs, tables, place, *refs):
    tall, first, last, held = refs[-4:]
    gather_blocks(refs[:-4], held, place[1])
    listed = [2 * pair + parity for pair in pairs for parity in range(2)]
    cols = first.shape[1]
    values = planes_of(held, pairs, tables)
    for c in range(3):
        for n, z in enumerate(listed):
            hold(tall, c, n, values[c, z])
        first[c] = values[c, listed[0]][0:cols]
        last[c] = values[c, listed[-1]][0:cols]


def where_planes(chunks):
    spot = {}
    for n, chunk in enumerate(chunks):
        for i, pair in enumerate(chunk):
            spot[2 * pair], spot[2 * pair + 1] = (n, 2 * i), (n, 2 * i + 1)
    return spot


def rim_start(meshes, which, c, i):
    before = 6 * meshes[1].shape[1] if which == 0 else 0
    return before + 2 * (c * meshes[which].shape[1] + i)


def stretch_plane(out, mesh, rims, at, rows_of, above, below):
    cols, ny = out[0].shape
    low_rim, high_rim = rims
    for c in range(3):
        out[c][...] = mesh[c][...]
        out[c][0:2] += low_rim[at[c] : at[c] + 2]
        out[c][cols - 2 : cols] += high_rim[at[c] : at[c] + 2]
    omega = [ref[...] for ref in out]
    for c in range(3):
        value = rows_of(c, RIM)
        along_z = (above(c) - below(c)) * 0.5
        along_x = (rows_of(c, RIM + 1) - rows_of(c, RIM - 1)) * 0.5
        along_y = (pltpu.roll(value, ny - 1, 1) - pltpu.roll(value, 1, 1)) * 0.5
        stretch = omega[0] * along_z + omega[1] * along_x + omega[2] * along_y
        out[c][...] = omega[c] + TIME_STEP * stretch


def ends_kernel(_, __, edges, before, after, low_rim, high_rim, *refs):
    meshes, vorticity, out, sems = refs[:-4], refs[-3], refs[-2], refs[-1]
    cols = before.shape[1]
    size = edges.shape[1]
    copies = []

    def rows_of(i):
        return lambda c, start=RIM: edges[c, i, start : start + cols]

    for n, i in enumerate((0, size - 1)):
        stretch_plane(
            [out.at[c, n] for c in range(3)],
            [meshes[0].at[c, i] for c in range(3)],
            (low_rim, high_rim),
            [rim_start(meshes, 0, c, i) for c in range(3)],
            rows_of(i),
            (lambda c: after[c]) if i else rows_of(1),
            rows_of(size - 2) if i else (lambda c: before[c]),
        )
        copies.append(
            pltpu.make_async_copy(
                out.at[:, n], vorticity.at[:, n * (vorticity.shape[1] - 1)], sems.at[n]
            )
        )
        copies[-1].start()
    for copy in copies:
        copy.wait()


def stretch_kernel(chunks, tables, place, edges, low_rim, high_rim, *refs):
    meshes, refs = refs[:2], refs[2:]
    velocity, vorticity, held, inner, omega, sems = refs[-6:]
    _, planes, cols, ny = velocity.shape
    spot = where_planes(chunks)
    talls = (edges, inner)
    sent = []

    def send(source, target):
        sent.append(pltpu.make_async_copy(source, target, sems.at[len(sent)]))
        sent[-1].start()

    def rows_of(z):
        n, i = spot[z]
        return lambda c, start=RIM: talls[n][c, i, start : start + cols]

    def send_velocity(which):
        for z in range(planes):
            n, i = spot[z]
            if n == which:
                send(talls[n].at[:, i, pl.ds(RIM, cols)], velocity.at[:, z])

    send_velocity(0)
    gather_blocks(refs[:-6], held, place[1])
    for (c, z), value in planes_of(held, chunks[1], tables).items():
        hold(inner, c, spot[z][1], value)
    send_velocity(1)
    for z in range(1, planes - 1):
        which, i = spot[z]
        stretch_plane(
            [omega.at[c, z] for c in range(3)],
            [meshes[which].at[c, i] for c in range(3)],
            (low_rim, high_rim),
            [rim_start(meshes, which, c, i) for c in range(3)],
            rows_of(z),
            rows_of(z + 1),
            rows_of(z - 1),
        )
        send(omega.at[:, z], vorticity.at[:, z])
    for copy in sent:
        copy.wait()


VM = pl.BlockSpec(memory_space=pltpu.VMEM)
SM = pl.BlockSpec(memory_space=pltpu.SMEM)
AN = pl.BlockSpec(memory_space=pl.ANY)
HB = pl.BlockSpec(memory_space=pltpu.HBM)


def kept(values):
    return pltpu.with_memory_space_constraint(values, pltpu.HBM)


def loaded(kernel):
    def run(place, t_high, t_low, *refs):
        kernel((t_high, t_low), place, *refs)

    return run


def call(kernel, ins, outs, scratch=(), sems=0, micros=2.0, moved=None, aliases=None):
    extra = [pltpu.SemaphoreType.DMA((sems,))] if sems else []
    return pl.pallas_call(
        kernel,
        out_shape=[jax.ShapeDtypeStruct(shape, F32) for _, shape in outs],
        in_specs=[spec for spec, _ in ins],
        out_specs=[spec for spec, _ in outs],
        scratch_shapes=[pltpu.VMEM(shape, kind) for shape, kind in scratch] + extra,
        compiler_params=pltpu.CompilerParams(vmem_limit_bytes=VMEM),
        input_output_aliases=aliases or {},
        cost_estimate=pl.CostEstimate(
            flops=int(micros * 1.0e9),
            bytes_accessed=int(micros * 3.0e6) if moved is None else moved,
            transcendentals=0,
        ),
    )(*[value for _, value in ins])


def ring(axis, step):
    count = lax.axis_size(axis)
    return [(i, (i + step) % count) for i in range(count)]


def spread(axis):
    count = lax.axis_size(axis)
    return count <= 8 and count & (count - 1) == 0


def sent_shapes(axis, rows, width, whole=False):
    count = lax.axis_size(axis)
    return [(count, rows, width)] if whole or not spread(axis) else [(rows, width)] * count


def exchange(blocks, axis, start=0, near_first=False):
    if not spread(axis):
        return [lax.all_to_all(blocks[0], axis, split_axis=0, concat_axis=0, tiled=True)]
    count = lax.axis_size(axis)
    return [
        lax.ppermute(block, axis, [(i, i ^ k) for i in range(count)]) if k else block
        for k, block in zip(offset_order(count, near_first)[start:], blocks)
    ]


def on_device(strength, offsets, cell_index, migrate_count, ambient):
    _, planes, cols, ny = ambient.shape
    slabs, pencils = lax.axis_size("gz"), lax.axis_size("gx")
    nx, nz, rows = cols * pencils, planes * slabs, cols + RIM
    count = strength.shape[1]
    pair_count = planes // 2
    chunks = ((0, pair_count - 1), tuple(range(1, pair_count - 1)))
    widths = [3 * len(c) * LANES for c in chunks]
    block = nx // slabs

    y_ahead, y_back = [split_table(t) for t in y_tables(ny, pencils, 1.0 / (float(nx) * ny * nz))]
    x_ahead, x_back = [split_table(t) for t in x_tables(nx, cols, pencils, slabs)]
    place = jnp.stack([lax.axis_index("gz"), lax.axis_index("gx")]).astype(jnp.int32)
    here = (SM, place)

    packet, movers = call(
        packet_kernel,
        [
            (HB, kept(migrate_count.reshape(1, 2))),
            (HB, kept(strength)),
            (HB, kept(offsets)),
            (HB, kept(cell_index.reshape(1, count))),
        ],
        [(VM, (8, count)), (VM, (8, 2 * MIG))],
        [((1, 2), jnp.int32), ((1, count), jnp.int32)],
        sems=4,
        micros=1.0,
        moved=1000,
    )
    up1 = lax.ppermute(packet, "gz", ring("gz", -1))
    down1 = lax.ppermute(packet, "gz", ring("gz", 1))
    up2 = lax.ppermute(movers, "gz", ring("gz", -2))
    down2 = lax.ppermute(movers, "gz", ring("gz", 2))

    meshes, rims, parts = [None, None], [], [None, None]
    for n in (1, 0):
        chunk, width = chunks[n], widths[n]
        size = 2 * len(chunk)
        rim = (6 * size + (rims[0].shape[0] if rims else 0), ny)
        mesh, rim_high, rim_low, *part = call(
            functools.partial(deposit_kernel, chunk, len(rims), n == 0),
            [here]
            + [(VM, value) for value in (packet, up1, down1, up2, down2)]
            + [(VM, ambient), (VM, y_ahead[0]), (VM, y_ahead[1])]
            + [(VM, value) for value in rims],
            [(VM, (3, size, cols, ny)), (VM, rim), (VM, rim)]
            + [(VM, shape) for shape in sent_shapes("gx", rows, width)],
            [((3, size, rows, ny), F32), ((pencils, rows, width), F32)],
            micros=5.0,
        )
        meshes[n] = mesh
        rims = [rim_high, rim_low]
        parts[n] = exchange(part, "gx", near_first=n == 0)
    low_rim = lax.ppermute(rims[0], "gx", ring("gx", 1))
    high_rim = lax.ppermute(rims[1], "gx", ring("gx", -1))

    tile = max(1, block // 4)
    data = [None, None]
    for n in (1, 0):
        chunk, part, width = chunks[n], parts[n], widths[n]
        shapes = sent_shapes("gz", block, width)
        part = call(
            functools.partial(x_ahead_kernel, len(shapes), n == 0),
            [here, (VM, x_ahead[0]), (VM, x_ahead[1])] + [(VM, p) for p in part],
            [(VM, shape) for shape in shapes],
            [((pencils, rows, width), F32), ((slabs, block, width), F32)],
        )
        (entered,) = call(
            functools.partial(enter_kernel, chunk, nz),
            [here] + [(VM, p) for p in exchange(part, "gz")],
            [(VM, (3, 2, 2 * len(chunk), slabs, tile, LANES))],
        )
        data[n] = entered
    data = call(
        functools.partial(curl_kernel, chunks, nx, ny),
        [here, (VM, low_rim), (VM, high_rim)] + [(VM, d) for d in data],
        [(VM, d.shape) for d in data],
        [((3, 2, nz, tile, LANES), F32)],
        micros=5.0,
    )
    plane = (3, cols, ny)
    tables = [(VM, t) for t in y_back]
    tall = [(3, 2 * len(chunk), cols + 2 * RIM, ny) for chunk in chunks]
    left = [
        call(
            functools.partial(leave_kernel, chunk, nz),
            [here, (VM, source)],
            [(VM, shape) for shape in sent_shapes("gz", block, width)],
            [(source.shape, F32)],
        )
        for chunk, source, width in zip(chunks, data, widths)
    ]

    def back(part, width):
        shapes = sent_shapes("gx", rows, width)
        part = call(
            loaded(functools.partial(x_back_kernel, len(shapes))),
            [here]
            + [(VM, t) for t in x_back]
            + [(VM, p) for p in part],
            [(VM, shape) for shape in shapes],
            [((slabs, block, width), F32), ((pencils, rows, width), F32)],
        )
        return exchange(part, "gx")

    early = max(1, len(left[1]) - LATE)
    second = exchange(left[1][:early], "gz")
    parts = [back(exchange(left[0], "gz"), widths[0])]
    edges, first, last = call(
        loaded(functools.partial(edge_kernel, chunks[0])),
        [here] + tables + [(VM, p) for p in parts[0]],
        [(VM, tall[0]), (VM, plane), (VM, plane)],
        [((pencils, rows, widths[0]), F32)],
    )
    if early < len(left[1]):
        late = call(
            pass_kernel,
            [(AN, parts[0][0])] + [(VM, p) for p in left[1][early:]],
            [(VM, p.shape) for p in left[1][early:]],
            micros=0.3,
        )
        second += exchange(late, "gz", early)
    parts.append(back(second, widths[1]))
    after = lax.ppermute(first, "gz", ring("gz", -1))
    before = lax.ppermute(last, "gz", ring("gz", 1))
    velocity, vorticity = call(
        loaded(functools.partial(stretch_kernel, chunks)),
        [here]
        + tables
        + [(VM, v) for v in (edges, low_rim, high_rim, *meshes)]
        + [(VM, p) for p in parts[1]],
        [(AN, ambient.shape), (AN, ambient.shape)],
        [
            ((pencils, rows, widths[1]), F32),
            (tall[1], F32),
            ((3, planes, cols, ny), F32),
        ],
        sems=2 * planes,
        micros=4.0,
    )
    return tuple(
        call(
            ends_kernel,
            [(AN, velocity), (AN, vorticity)]
            + [(VM, v) for v in (edges, before, after, low_rim, high_rim, *meshes)],
            [(AN, ambient.shape), (AN, ambient.shape)],
            [((3, 2, cols, ny), F32)],
            sems=2,
            micros=1.0,
            aliases={0: 0, 1: 1},
        )
    )


def solution(mesh):
    placed = (
        P(None, ("gz", "gx")),
        P(None, ("gz", "gx")),
        P(("gz", "gx")),
        P("gz", "gx", None),
        P(None, "gz", "gx", None),
    )
    return jax.shard_map(
        on_device,
        mesh=mesh,
        in_specs=placed,
        out_specs=(P(None, "gz", "gx", None), P(None, "gz", "gx", None)),
        check_vma=False,
    )
```

```python
import functools
import math

import jax
import jax.numpy as jnp
import ml_dtypes
import numpy as np
from jax import lax
from jax.experimental import pallas as pl
from jax.experimental.pallas import tpu as pltpu
from jax.sharding import PartitionSpec as P

MIG = 64
LANES = 128
RIM = 8
LATE = 3
TIME_STEP = 0.25
VMEM = 24 * 1024 * 1024
F32 = jnp.float32
BF16 = jnp.bfloat16


def split_table(table):
    high = table.astype(np.float32).astype(ml_dtypes.bfloat16)
    low = (table - high.astype(np.float64)).astype(np.float32).astype(ml_dtypes.bfloat16)
    return high, low


def angles(rows, columns, extent):
    return 2.0 * np.pi * (np.multiply.outer(rows, columns) % extent) / extent


def y_tables(ny, pencils, scale):
    modes = ny // (2 * pencils)
    position = np.arange(ny)
    angle = angles(position, np.arange(ny // 2), ny)
    real, imag = np.cos(angle), -np.sin(angle)
    imag[:, 0] = 1.0 - 2.0 * (position % 2)
    weight = np.where(np.arange(ny // 2) == 0, 1.0, 2.0) * scale
    ahead = np.zeros((2, ny, pencils, 2, 2, modes))
    back = np.zeros((pencils, 2, 2, modes, 2, ny))
    for parity in range(2):
        for part, values in enumerate((real, imag)):
            ahead[parity, :, :, part, parity] = values.reshape(ny, pencils, modes)
            back[:, part, parity, :, parity] = (values * weight).T.reshape(pencils, modes, ny)
    return ahead.reshape(2 * ny, -1), back.reshape(-1, 2 * ny)


def wave_order(nx, slabs):
    half = nx // 2
    ahead = np.arange(half).reshape(slabs, 1, half // slabs)
    behind = np.where(ahead == 0, half, (nx - ahead) % nx)
    return np.concatenate([ahead, behind], axis=1).reshape(-1)


def x_tables(nx, cols, pencils, slabs):
    order = wave_order(nx, slabs)
    angle = angles(order, np.arange(nx), nx)
    ahead = np.concatenate([np.cos(angle), np.sin(angle)], axis=0)
    row = np.arange(cols + RIM)
    offset = np.where(row <= cols, row, -1)
    used = ((row <= cols) | (row == cols + RIM - 1)).astype(np.float64)
    place = (np.arange(pencils)[:, None] * cols + offset[None, :]) % nx
    angle = angles(place.reshape(-1), order, nx)
    mask = np.tile(used, pencils)[:, None]
    back = np.concatenate([np.cos(angle) * mask, np.sin(angle) * mask], axis=0)
    return ahead, back


def split(values):
    high = values.astype(BF16)
    return high, (values - high.astype(F32)).astype(BF16)


def dot(left, right):
    return jnp.dot(left, right, preferred_element_type=F32)


def table_left(high, low, values):
    v_high, v_low = split(values)
    return dot(high, v_high) + (dot(high, v_low) + dot(low, v_high))


def table_right(values, high, low):
    v_high, v_low = split(values)
    return dot(v_high, high) + (dot(v_low, high) + dot(v_high, low))


def lane_of():
    return lax.broadcasted_iota(jnp.int32, (1, LANES), 1)


def times_i(values):
    half = LANES // 2
    sign = jnp.where(lane_of() < half, -1.0, 1.0).astype(F32)
    return pltpu.roll(values, half, 1) * sign


def kernel_weight(distance):
    radius = jnp.abs(distance)
    near = 1.0 + radius * radius * (1.5 * radius - 2.5)
    rest = jnp.maximum(2.0 - radius, 0.0)
    return jnp.where(radius < 1.0, near, 0.5 * rest * rest * (1.0 - radius))


def quotient(values, size):
    if size & (size - 1):
        return lax.div(values, size)
    return lax.shift_right_logical(values, size.bit_length() - 1)


def remainder(values, size):
    if size & (size - 1):
        return lax.rem(values, size)
    return values & (size - 1)


def turned(value, wave, extent, sign):
    wave = wave % extent
    real, imag = value
    if wave == 0:
        return value
    if 2 * wave == extent:
        return -real, -imag
    if 4 * wave == extent:
        return (-imag, real) if sign > 0 else (imag, -real)
    if 4 * wave == 3 * extent:
        return (imag, -real) if sign > 0 else (-imag, real)
    a = math.cos(2.0 * math.pi * wave / extent)
    b = sign * math.sin(2.0 * math.pi * wave / extent)
    return real * a - imag * b, real * b + imag * a


def fft(values, sign):
    count = len(values)
    if count == 1:
        return values
    even, odd = fft(values[::2], sign), fft(values[1::2], sign)
    odd = [turned(v, k, count, sign) for k, v in enumerate(odd)]
    plus = [(a[0] + b[0], a[1] + b[1]) for a, b in zip(even, odd)]
    minus = [(a[0] - b[0], a[1] - b[1]) for a, b in zip(even, odd)]
    return plus + minus


def offset_order(count, first=None):
    far, near = list(range(count // 2, count)), list(range(1, count // 2))
    if first == "near":
        return [0] + near + far
    if first == "far":
        return [0] + far + near
    order = [0]
    while far or near:
        order += far[:1] + near[:1]
        far, near = far[1:], near[1:]
    return order


def blocks_of(refs, at, first=None):
    if len(refs) == 1:
        return [(d, refs[0].at[d]) for d in range(refs[0].shape[0])]
    return [(at ^ k, ref) for k, ref in zip(offset_order(len(refs), first), refs)]


def gather_blocks(refs, held, at, first=None):
    for d, ref in blocks_of(refs, at, first):
        held[d] = ref[...]


def packet_kernel(
    counts, strength, offsets, cells, packet, movers, near_counts, near_cells, sems
):
    copies = [
        pltpu.make_async_copy(counts, near_counts, sems.at[0]),
        pltpu.make_async_copy(cells, near_cells, sems.at[1]),
        pltpu.make_async_copy(strength, packet.at[pl.ds(0, 3)], sems.at[2]),
        pltpu.make_async_copy(offsets, packet.at[pl.ds(3, 3)], sems.at[3]),
    ]
    for copy in copies:
        copy.start()
    for copy in copies:
        copy.wait()
    slot = lax.broadcasted_iota(jnp.int32, (1, packet.shape[1]), 1)
    up = near_counts[0:1, 0:1]
    both = up + near_counts[0:1, 1:2]
    packet[6:7] = near_cells[...].astype(F32)
    packet[7:8] = jnp.where(slot < up, 1.0, jnp.where(slot < both, -1.0, 0.0))
    movers[...] = packet[:, : movers.shape[1]]


def deposit_kernel(
    pairs, rims_before, first, place, own, up1, down1, up2, down2, ambient, t_high, t_low, *refs
):
    rims, refs = refs[:rims_before], refs[rims_before:]
    mesh, rim_high, rim_low = refs[:3]
    total, made = refs[-2:]
    outs = refs[3:-2]
    _, planes, cols, ny = ambient.shape
    rows = cols + RIM
    movers = up2.shape[1]
    count = own.shape[1]
    listed = [2 * pair + parity for pair in pairs for parity in range(2)]

    def decode(ref, start, stop, shift):
        packet = ref[:, start:stop]
        cell = packet[6:7].astype(jnp.int32)
        move = packet[7:8].astype(jnp.int32)
        z_cell = quotient(cell, cols * ny) + planes * (move + shift)
        x_cell = remainder(quotient(cell, ny), cols)
        return packet[0:6], z_cell, x_cell, remainder(cell, ny)

    def joined(pieces):
        return [jnp.concatenate(p, axis=1) if len(p) > 1 else p[0] for p in zip(*pieces)]

    def add_block(pieces, wanted):
        values, z_cell, x_cell, y_cell = joined(pieces)
        width = values.shape[1]
        z_at = lax.broadcasted_iota(jnp.int32, (planes, width), 0)
        w_z = kernel_weight((z_at - z_cell).astype(F32) - values[3:4])
        row = lax.broadcasted_iota(jnp.int32, (rows, width), 0)
        x_at = jnp.where(row < cols + 2, row, jnp.where(row >= rows - 2, row - rows, 4 * rows))
        w_x = kernel_weight((x_at - x_cell).astype(F32) - values[4:5])
        y_at = lax.broadcasted_iota(jnp.int32, (ny, width), 0)
        y_off = remainder(y_at + (ny + ny // 2 - y_cell), ny) - ny // 2
        w_y = kernel_weight(y_off.astype(F32) - values[5:6])
        y_high, y_low = split(w_y)
        right = jnp.concatenate([y_high, y_high, y_low], axis=1)
        at = [listed.index(z) for z in wanted]
        for c in range(3):
            s_z = values[c : c + 1] * w_z
            left = jnp.concatenate([s_z[z : z + 1] * w_x for z in wanted], axis=0)
            l_high, l_low = split(left)
            left = jnp.concatenate([l_high, l_low, l_high], axis=1)
            added = lax.dot_general(
                left, right, (((1,), (1,)), ((), ())), preferred_element_type=F32
            )
            total[c, at[0] : at[-1] + 1] += added.reshape(len(wanted), rows, ny)

    for n, z in enumerate(listed):
        total[:, n, 0:cols] = ambient[:, z]
    total[:, :, cols:rows] = jnp.zeros((3, len(listed), RIM, ny), F32)
    step = 256
    for at in range(0, count, step):
        add_block([decode(own, at, min(at + step, count), 0)], listed)
    add_block([decode(up1, 0, movers, 1), decode(down1, 0, movers, -1)], listed)
    sides = ((up1, up2, 1, (planes - 2, planes - 1)), (down1, down2, -1, (0, 1)))
    for near, far, shift, wanted in sides:
        if not set(wanted) <= set(listed):
            continue
        whole = [decode(near, movers, count, shift), decode(far, 0, movers, 2 * shift)]
        values, z_cell, x_cell, y_cell = joined(whole)
        for at in range(0, count, step):
            to = min(at + step, count)
            block = (values[:, at:to], z_cell[:, at:to], x_cell[:, at:to], y_cell[:, at:to])
            add_block([block], wanted)

    mesh[...] = total[:, :, 0:cols]
    at = 0
    if rims:
        at = rims[0].shape[0]
        rim_high[0:at] = rims[0][...]
        rim_low[0:at] = rims[1][...]
    for n in range(3 * len(listed)):
        c, i = n // len(listed), n % len(listed)
        rim_high[at + 2 * n : at + 2 * n + 2] = total[c, i, cols : cols + 2]
        rim_low[at + 2 * n : at + 2 * n + 2] = total[c, i, rows - 2 : rows]
    groups = [(c, 2 * n) for c in range(3) for n in range(len(pairs))]
    left = jnp.concatenate(
        [jnp.concatenate([total[c, n], total[c, n + 1]], axis=1) for c, n in groups], axis=0
    )
    wide = table_right(left, t_high[...], t_low[...])
    for n in range(len(groups)):
        for g in range(made.shape[0]):
            made[g, :, n * LANES : (n + 1) * LANES] = wide[
                n * rows : (n + 1) * rows, g * LANES : (g + 1) * LANES
            ]
    for d, out in blocks_of(outs, place[1], first):
        out[...] = made[d]


def x_ahead_kernel(sends, first, place, t_high, t_low, *refs):
    held, made = refs[-2:]
    outs, parts = refs[-2 - sends : -2], refs[: -2 - sends]
    gather_blocks(parts, held, place[1], first)
    pencils, rows, width = held.shape
    cols = rows - RIM
    row = lax.broadcasted_iota(jnp.int32, (RIM, width), 0)
    pieces = []
    for h in range(pencils):
        from_low = held[(h - 1) % pencils, cols:rows]
        from_high = held[(h + 1) % pencils, cols:rows]
        pieces.append(held[h, 0:RIM] + jnp.where(row < 2, from_low, 0.0))
        pieces.append(held[h, RIM : cols - RIM])
        pieces.append(held[h, cols - RIM : cols] + jnp.where(row >= RIM - 2, from_high, 0.0))
    both = table_left(t_high[...], t_low[...], jnp.concatenate(pieces, axis=0))
    half = both.shape[0] // 2
    for n in range(width // LANES):
        lanes = slice(n * LANES, (n + 1) * LANES)
        value = both[:half, lanes] - times_i(both[half:, lanes])
        made[:, :, lanes] = value.reshape(made.shape[0], made.shape[1], LANES)
    for d, out in blocks_of(outs, place[0]):
        out[...] = made[d]


def x_back_kernel(sends, first, tables, place, *refs):
    held, made = refs[-2:]
    outs, parts = refs[-2 - sends : -2], refs[: -2 - sends]
    gather_blocks(parts, held, place[0])
    pencils, rows, width = made.shape
    both = table_left(tables[0][...], tables[1][...], held[...].reshape(-1, width))
    half = both.shape[0] // 2
    for n in range(width // LANES):
        lanes = slice(n * LANES, (n + 1) * LANES)
        value = both[:half, lanes] + times_i(both[half:, lanes])
        made[:, :, lanes] = value.reshape(pencils, rows, LANES)
    for d, out in blocks_of(outs, place[1], first):
        out[...] = made[d]


def wave_lanes():
    lane = lane_of()
    return lane < LANES // 2, (lane // (LANES // 4)) % 2 == 0


def roll(values, shift):
    return pltpu.roll(values, shift, 1)


def cross_half(a, b):
    low, _ = wave_lanes()
    half = LANES // 2
    return jnp.where(low, a, roll(b, half)), jnp.where(low, roll(a, half), b)


def cross_quarter(a, b):
    _, first = wave_lanes()
    quarter = LANES // 4
    return (
        jnp.where(first, a, roll(b, quarter)),
        jnp.where(first, roll(a, LANES - quarter), b),
    )


def lanes_at(c, count, i):
    return pl.ds(pl.multiple_of((c * count + i) * LANES, LANES), LANES)


def enter_kernel(pairs, nz, place, *refs):
    parts, data = refs[:-1], refs[-1]
    _, _, _, slabs, tile, _ = data.shape

    def body(c, carry):
        for i, pair in enumerate(pairs):
            lanes = lanes_at(c, len(pairs), i)
            for s, ref in blocks_of(parts, place[0]):
                quad = [ref[q * tile : (q + 1) * tile, lanes] for q in range(4)]
                real0, imag0 = cross_half(quad[0], quad[2])
                real1, imag1 = cross_half(quad[1], quad[3])
                for part, (a, b) in enumerate(((real0, real1), (imag0, imag1))):
                    even, odd = cross_quarter(a, b)
                    data[c, part, 2 * i, s] = even
                    data[c, part, 2 * i + 1, s] = odd
            for parity in range(2):
                at = 2 * i + parity
                line = [(data[c, 0, at, s], data[c, 1, at, s]) for s in range(slabs)]
                for k, v in enumerate(fft(line, -1.0)):
                    v = turned(v, (2 * pair + parity) * k, nz, -1.0)
                    data[c, 0, at, k], data[c, 1, at, k] = v
        return carry

    lax.fori_loop(0, 3, body, 0)


def pass_kernel(before, *refs):
    for source, target in zip(refs[: len(refs) // 2], refs[len(refs) // 2 :]):
        target[...] = source[...]


def leave_kernel(pairs, nz, place, source, *refs):
    outs, data = refs[:-1], refs[-1]
    _, _, _, slabs, tile, _ = source.shape

    def body(c, carry):
        for i, pair in enumerate(pairs):
            lanes = lanes_at(c, len(pairs), i)
            for parity in range(2):
                at = 2 * i + parity
                line = [
                    turned(
                        (source[c, 0, at, k], source[c, 1, at, k]),
                        (2 * pair + parity) * k,
                        nz,
                        1.0,
                    )
                    for k in range(slabs)
                ]
                for s, v in enumerate(fft(line, 1.0)):
                    data[c, 0, at, s], data[c, 1, at, s] = v
            for s, ref in blocks_of(outs, place[0]):
                real0, real1 = cross_quarter(data[c, 0, 2 * i, s], data[c, 0, 2 * i + 1, s])
                imag0, imag1 = cross_quarter(data[c, 1, 2 * i, s], data[c, 1, 2 * i + 1, s])
                quad = [None] * 4
                quad[0], quad[2] = cross_half(real0, imag0)
                quad[1], quad[3] = cross_half(real1, imag1)
                for q in range(4):
                    ref[q * tile : (q + 1) * tile, lanes] = quad[q]
        return carry

    lax.fori_loop(0, 3, body, 0)


def curl_kernel(chunks, nx, ny, place, low_rim, high_rim, *refs):
    sources, outs = refs[: len(chunks)], refs[len(chunks) : 2 * len(chunks)]
    spectrum = refs[-1]
    _, _, nz, tile, _ = spectrum.shape
    slabs = sources[0].shape[3]
    planes = nz // slabs
    modes, half = LANES // 4, LANES // 2
    slab_at, pencil_at = place[0], place[1]
    spot = {}
    for n, chunk in enumerate(chunks):
        for i, pair in enumerate(chunk):
            spot[2 * pair], spot[2 * pair + 1] = (n, 2 * i), (n, 2 * i + 1)

    def across_planes(k, carry):
        for c in range(3):
            line = []
            for l in range(planes):
                n, i = spot[l]
                line.append((sources[n][c, 0, i, k], sources[n][c, 1, i, k]))
            for n, v in enumerate(fft(line, -1.0)):
                spectrum[c, 0, k + slabs * n], spectrum[c, 1, k + slabs * n] = v
        return carry

    reach = 2 * tile
    row = lax.broadcasted_iota(jnp.int32, (tile, LANES), 0)
    lane = lax.broadcasted_iota(jnp.int32, (tile, LANES), 1)
    number = slab_at * reach + (lane // modes) % 2 * tile + row
    ahead = lane < half
    mode = lane % modes + pencil_at * modes
    alone = number == 0
    number = number.astype(F32) * (2.0 * math.pi / nx)
    x_base = jnp.where(ahead, number, jnp.where(alone, math.pi, -number))
    x_trim = jnp.where(ahead, number, jnp.where(alone, 0.0, -number))
    wave_y = mode.astype(F32) * (2.0 * math.pi / ny)
    packed = mode == 0
    x_sq = x_base * x_base
    lateral = x_sq + wave_y * wave_y

    def curl_at(k, with_mirror):
        z_wave = jnp.where(k < nz // 2, k, k - nz).astype(F32) * (2.0 * math.pi / nz)
        z_trim = jnp.where(k == nz // 2, 0.0, z_wave)
        full = lateral + z_wave * z_wave
        empty = full == 0.0
        inverse = jnp.where(empty, 0.0, 1.0 / jnp.where(empty, 1.0, full))
        if with_mirror:
            other = 1.0 / (x_sq + (z_wave * z_wave + math.pi * math.pi))
            mirror = jnp.where(packed, 0.5 * (inverse - other), 0.0)
            inverse = jnp.where(packed, 0.5 * (inverse + other), inverse)
            opposite = lax.rem(nz - k, nz)
        stream = []
        for c in range(3):
            value = [spectrum[c, part, k] * inverse for part in range(2)]
            if with_mirror:
                for part, sign in enumerate((1.0, -1.0)):
                    there = spectrum[c, part, opposite]
                    there = jnp.where(alone, there, roll(there, half))
                    value[part] = value[part] + (mirror * sign) * there
            stream.append(value)
        made = []
        for part in range(2):
            s = [value[part] for value in stream]
            made.append(
                (
                    x_trim * s[2] - wave_y * s[1],
                    wave_y * s[0] - z_trim * s[2],
                    z_trim * s[1] - x_trim * s[0],
                )
            )
        return [(-made[1][c], made[0][c]) for c in range(3)]

    def curl_all(with_mirror):
        def body(k, carry):
            made = [curl_at(k + slabs * n, with_mirror) for n in range(planes)]
            for c in range(3):
                for l, v in enumerate(fft([m[c] for m in made], 1.0)):
                    n, i = spot[l]
                    outs[n][c, 0, i, k], outs[n][c, 1, i, k] = v
            return carry

        lax.fori_loop(0, slabs, body, 0)

    lax.fori_loop(0, slabs, across_planes, 0)

    @pl.when(pencil_at == 0)
    def _():
        curl_all(True)

    @pl.when(pencil_at != 0)
    def _():
        curl_all(False)


def planes_of(held, pairs, tables):
    pencils, rows, _ = held.shape
    groups = [(c, pair) for c in range(3) for pair in pairs]
    left = jnp.concatenate(
        [
            jnp.concatenate(
                [held[h, :, n * LANES : (n + 1) * LANES] for h in range(pencils)], axis=1
            )
            for n in range(len(groups))
        ],
        axis=0,
    )
    ny = tables[0].shape[1] // 2
    wide = table_right(left, tables[0][...], tables[1][...])
    made = {}
    for n, (c, pair) in enumerate(groups):
        for parity in range(2):
            made[c, 2 * pair + parity] = wide[
                n * rows : (n + 1) * rows, parity * ny : (parity + 1) * ny
            ]
    return made


def hold(tall, c, n, value):
    rows = value.shape[0]
    tall[c, n, RIM : RIM + rows] = value
    tall[c, n, 0:RIM] = value[rows - RIM : rows]


def edge_kernel(pairs, tables, place, *refs):
    tall, first, last, held = refs[-4:]
    gather_blocks(refs[:-4], held, place[1])
    listed = [2 * pair + parity for pair in pairs for parity in range(2)]
    cols = first.shape[1]
    values = planes_of(held, pairs, tables)
    for c in range(3):
        for n, z in enumerate(listed):
            hold(tall, c, n, values[c, z])
        first[c] = values[c, listed[0]][0:cols]
        last[c] = values[c, listed[-1]][0:cols]


def where_planes(chunks):
    spot = {}
    for n, chunk in enumerate(chunks):
        for i, pair in enumerate(chunk):
            spot[2 * pair], spot[2 * pair + 1] = (n, 2 * i), (n, 2 * i + 1)
    return spot


def rim_start(meshes, which, c, i):
    before = 6 * meshes[1].shape[1] if which == 0 else 0
    return before + 2 * (c * meshes[which].shape[1] + i)


def stretch_plane(out, mesh, rims, at, rows_of, above, below):
    cols, ny = out[0].shape
    low_rim, high_rim = rims
    for c in range(3):
        out[c][...] = mesh[c][...]
        out[c][0:2] += low_rim[at[c] : at[c] + 2]
        out[c][cols - 2 : cols] += high_rim[at[c] : at[c] + 2]
    omega = [ref[...] for ref in out]
    for c in range(3):
        value = rows_of(c, RIM)
        along_z = (above(c) - below(c)) * 0.5
        along_x = (rows_of(c, RIM + 1) - rows_of(c, RIM - 1)) * 0.5
        along_y = (pltpu.roll(value, ny - 1, 1) - pltpu.roll(value, 1, 1)) * 0.5
        stretch = omega[0] * along_z + omega[1] * along_x + omega[2] * along_y
        out[c][...] = omega[c] + TIME_STEP * stretch


def ends_kernel(_, __, edges, before, after, low_rim, high_rim, *refs):
    meshes, vorticity, out, sems = refs[:-4], refs[-3], refs[-2], refs[-1]
    cols = before.shape[1]
    size = edges.shape[1]
    copies = []

    def rows_of(i):
        return lambda c, start=RIM: edges[c, i, start : start + cols]

    for n, i in enumerate((0, size - 1)):
        stretch_plane(
            [out.at[c, n] for c in range(3)],
            [meshes[0].at[c, i] for c in range(3)],
            (low_rim, high_rim),
            [rim_start(meshes, 0, c, i) for c in range(3)],
            rows_of(i),
            (lambda c: after[c]) if i else rows_of(1),
            rows_of(size - 2) if i else (lambda c: before[c]),
        )
        copies.append(
            pltpu.make_async_copy(
                out.at[:, n], vorticity.at[:, n * (vorticity.shape[1] - 1)], sems.at[n]
            )
        )
        copies[-1].start()
    for copy in copies:
        copy.wait()


def stretch_kernel(chunks, tables, place, edges, low_rim, high_rim, *refs):
    meshes, refs = refs[:2], refs[2:]
    velocity, vorticity, held, inner, omega, sems = refs[-6:]
    _, planes, cols, ny = velocity.shape
    spot = where_planes(chunks)
    talls = (edges, inner)
    sent = []

    def send(source, target):
        sent.append(pltpu.make_async_copy(source, target, sems.at[len(sent)]))
        sent[-1].start()

    def rows_of(z):
        n, i = spot[z]
        return lambda c, start=RIM: talls[n][c, i, start : start + cols]

    def send_velocity(which):
        for z in range(planes):
            n, i = spot[z]
            if n == which:
                send(talls[n].at[:, i, pl.ds(RIM, cols)], velocity.at[:, z])

    send_velocity(0)
    gather_blocks(refs[:-6], held, place[1], "far")
    for (c, z), value in planes_of(held, chunks[1], tables).items():
        hold(inner, c, spot[z][1], value)
    send_velocity(1)
    for z in range(1, planes - 1):
        which, i = spot[z]
        stretch_plane(
            [omega.at[c, z] for c in range(3)],
            [meshes[which].at[c, i] for c in range(3)],
            (low_rim, high_rim),
            [rim_start(meshes, which, c, i) for c in range(3)],
            rows_of(z),
            rows_of(z + 1),
            rows_of(z - 1),
        )
        send(omega.at[:, z], vorticity.at[:, z])
    for copy in sent:
        copy.wait()


VM = pl.BlockSpec(memory_space=pltpu.VMEM)
SM = pl.BlockSpec(memory_space=pltpu.SMEM)
AN = pl.BlockSpec(memory_space=pl.ANY)
HB = pl.BlockSpec(memory_space=pltpu.HBM)


def kept(values):
    return pltpu.with_memory_space_constraint(values, pltpu.HBM)


def loaded(kernel):
    def run(place, t_high, t_low, *refs):
        kernel((t_high, t_low), place, *refs)

    return run


def call(kernel, ins, outs, scratch=(), sems=0, micros=2.0, moved=None, aliases=None):
    extra = [pltpu.SemaphoreType.DMA((sems,))] if sems else []
    return pl.pallas_call(
        kernel,
        out_shape=[jax.ShapeDtypeStruct(shape, F32) for _, shape in outs],
        in_specs=[spec for spec, _ in ins],
        out_specs=[spec for spec, _ in outs],
        scratch_shapes=[pltpu.VMEM(shape, kind) for shape, kind in scratch] + extra,
        compiler_params=pltpu.CompilerParams(vmem_limit_bytes=VMEM),
        input_output_aliases=aliases or {},
        cost_estimate=pl.CostEstimate(
            flops=int(micros * 1.0e9),
            bytes_accessed=int(micros * 3.0e6) if moved is None else moved,
            transcendentals=0,
        ),
    )(*[value for _, value in ins])


def ring(axis, step):
    count = lax.axis_size(axis)
    return [(i, (i + step) % count) for i in range(count)]


def spread(axis):
    count = lax.axis_size(axis)
    return count <= 8 and count & (count - 1) == 0


def sent_shapes(axis, rows, width, whole=False):
    count = lax.axis_size(axis)
    return [(count, rows, width)] if whole or not spread(axis) else [(rows, width)] * count


def exchange(blocks, axis, start=0, first=None):
    if not spread(axis):
        return [lax.all_to_all(blocks[0], axis, split_axis=0, concat_axis=0, tiled=True)]
    count = lax.axis_size(axis)
    return [
        lax.ppermute(block, axis, [(i, i ^ k) for i in range(count)]) if k else block
        for k, block in zip(offset_order(count, first)[start:], blocks)
    ]


def on_device(strength, offsets, cell_index, migrate_count, ambient):
    _, planes, cols, ny = ambient.shape
    slabs, pencils = lax.axis_size("gz"), lax.axis_size("gx")
    nx, nz, rows = cols * pencils, planes * slabs, cols + RIM
    count = strength.shape[1]
    pair_count = planes // 2
    chunks = ((0, pair_count - 1), tuple(range(1, pair_count - 1)))
    widths = [3 * len(c) * LANES for c in chunks]
    block = nx // slabs

    y_ahead, y_back = [split_table(t) for t in y_tables(ny, pencils, 1.0 / (float(nx) * ny * nz))]
    x_ahead, x_back = [split_table(t) for t in x_tables(nx, cols, pencils, slabs)]
    place = jnp.stack([lax.axis_index("gz"), lax.axis_index("gx")]).astype(jnp.int32)
    here = (SM, place)

    packet, movers = call(
        packet_kernel,
        [
            (HB, kept(migrate_count.reshape(1, 2))),
            (HB, kept(strength)),
            (HB, kept(offsets)),
            (HB, kept(cell_index.reshape(1, count))),
        ],
        [(VM, (8, count)), (VM, (8, 2 * MIG))],
        [((1, 2), jnp.int32), ((1, count), jnp.int32)],
        sems=4,
        micros=1.0,
        moved=1000,
    )
    up1 = lax.ppermute(packet, "gz", ring("gz", -1))
    down1 = lax.ppermute(packet, "gz", ring("gz", 1))
    up2 = lax.ppermute(movers, "gz", ring("gz", -2))
    down2 = lax.ppermute(movers, "gz", ring("gz", 2))

    meshes, rims, parts = [None, None], [], [None, None]
    for n in (1, 0):
        chunk, width = chunks[n], widths[n]
        size = 2 * len(chunk)
        rim = (6 * size + (rims[0].shape[0] if rims else 0), ny)
        mesh, rim_high, rim_low, *part = call(
            functools.partial(deposit_kernel, chunk, len(rims), None if n else "near"),
            [here]
            + [(VM, value) for value in (packet, up1, down1, up2, down2)]
            + [(VM, ambient), (VM, y_ahead[0]), (VM, y_ahead[1])]
            + [(VM, value) for value in rims],
            [(VM, (3, size, cols, ny)), (VM, rim), (VM, rim)]
            + [(VM, shape) for shape in sent_shapes("gx", rows, width)],
            [((3, size, rows, ny), F32), ((pencils, rows, width), F32)],
            micros=5.0,
        )
        meshes[n] = mesh
        rims = [rim_high, rim_low]
        parts[n] = exchange(part, "gx", first="near" if n == 0 else None)
    low_rim = lax.ppermute(rims[0], "gx", ring("gx", 1))
    high_rim = lax.ppermute(rims[1], "gx", ring("gx", -1))

    tile = max(1, block // 4)
    data = [None, None]
    for n in (1, 0):
        chunk, part, width = chunks[n], parts[n], widths[n]
        shapes = sent_shapes("gz", block, width)
        part = call(
            functools.partial(x_ahead_kernel, len(shapes), None if n else "near"),
            [here, (VM, x_ahead[0]), (VM, x_ahead[1])] + [(VM, p) for p in part],
            [(VM, shape) for shape in shapes],
            [((pencils, rows, width), F32), ((slabs, block, width), F32)],
        )
        (entered,) = call(
            functools.partial(enter_kernel, chunk, nz),
            [here] + [(VM, p) for p in exchange(part, "gz")],
            [(VM, (3, 2, 2 * len(chunk), slabs, tile, LANES))],
        )
        data[n] = entered
    data = call(
        functools.partial(curl_kernel, chunks, nx, ny),
        [here, (VM, low_rim), (VM, high_rim)] + [(VM, d) for d in data],
        [(VM, d.shape) for d in data],
        [((3, 2, nz, tile, LANES), F32)],
        micros=5.0,
    )
    plane = (3, cols, ny)
    tables = [(VM, t) for t in y_back]
    tall = [(3, 2 * len(chunk), cols + 2 * RIM, ny) for chunk in chunks]
    left = [
        call(
            functools.partial(leave_kernel, chunk, nz),
            [here, (VM, source)],
            [(VM, shape) for shape in sent_shapes("gz", block, width)],
            [(source.shape, F32)],
        )
        for chunk, source, width in zip(chunks, data, widths)
    ]

    def back(part, width, first=None):
        shapes = sent_shapes("gx", rows, width)
        part = call(
            loaded(functools.partial(x_back_kernel, len(shapes), first)),
            [here]
            + [(VM, t) for t in x_back]
            + [(VM, p) for p in part],
            [(VM, shape) for shape in shapes],
            [((slabs, block, width), F32), ((pencils, rows, width), F32)],
        )
        return exchange(part, "gx", first=first)

    early = max(1, len(left[1]) - LATE)
    second = exchange(left[1][:early], "gz")
    parts = [back(exchange(left[0], "gz"), widths[0])]
    edges, first, last = call(
        loaded(functools.partial(edge_kernel, chunks[0])),
        [here] + tables + [(VM, p) for p in parts[0]],
        [(VM, tall[0]), (VM, plane), (VM, plane)],
        [((pencils, rows, widths[0]), F32)],
    )
    if early < len(left[1]):
        late = call(
            pass_kernel,
            [(AN, parts[0][0])] + [(VM, p) for p in left[1][early:]],
            [(VM, p.shape) for p in left[1][early:]],
            micros=0.3,
        )
        second += exchange(late, "gz", early)
    parts.append(back(second, widths[1], "far"))
    after = lax.ppermute(first, "gz", ring("gz", -1))
    before = lax.ppermute(last, "gz", ring("gz", 1))
    velocity, vorticity = call(
        loaded(functools.partial(stretch_kernel, chunks)),
        [here]
        + tables
        + [(VM, v) for v in (edges, low_rim, high_rim, *meshes)]
        + [(VM, p) for p in parts[1]],
        [(AN, ambient.shape), (AN, ambient.shape)],
        [
            ((pencils, rows, widths[1]), F32),
            (tall[1], F32),
            ((3, planes, cols, ny), F32),
        ],
        sems=2 * planes,
        micros=4.0,
    )
    return tuple(
        call(
            ends_kernel,
            [(AN, velocity), (AN, vorticity)]
            + [(VM, v) for v in (edges, before, after, low_rim, high_rim, *meshes)],
            [(AN, ambient.shape), (AN, ambient.shape)],
            [((3, 2, cols, ny), F32)],
            sems=2,
            micros=1.0,
            aliases={0: 0, 1: 1},
        )
    )


def solution(mesh):
    placed = (
        P(None, ("gz", "gx")),
        P(None, ("gz", "gx")),
        P(("gz", "gx")),
        P("gz", "gx", None),
        P(None, "gz", "gx", None),
    )
    return jax.shard_map(
        on_device,
        mesh=mesh,
        in_specs=placed,
        out_specs=(P(None, "gz", "gx", None), P(None, "gz", "gx", None)),
        check_vma=False,
    )
```

```python
import functools
import math

import jax
import jax.numpy as jnp
import ml_dtypes
import numpy as np
from jax import lax
from jax.experimental import pallas as pl
from jax.experimental.pallas import tpu as pltpu
from jax.sharding import PartitionSpec as P

MIG = 64
LANES = 128
RIM = 8
LATE = 1
TIME_STEP = 0.25
VMEM = 24 * 1024 * 1024
F32 = jnp.float32
BF16 = jnp.bfloat16


def split_table(table):
    high = table.astype(np.float32).astype(ml_dtypes.bfloat16)
    low = (table - high.astype(np.float64)).astype(np.float32).astype(ml_dtypes.bfloat16)
    return high, low


def angles(rows, columns, extent):
    return 2.0 * np.pi * (np.multiply.outer(rows, columns) % extent) / extent


def y_tables(ny, pencils, scale):
    modes = ny // (2 * pencils)
    position = np.arange(ny)
    angle = angles(position, np.arange(ny // 2), ny)
    real, imag = np.cos(angle), -np.sin(angle)
    imag[:, 0] = 1.0 - 2.0 * (position % 2)
    weight = np.where(np.arange(ny // 2) == 0, 1.0, 2.0) * scale
    ahead = np.zeros((2, ny, pencils, 2, 2, modes))
    back = np.zeros((pencils, 2, 2, modes, 2, ny))
    for parity in range(2):
        for part, values in enumerate((real, imag)):
            ahead[parity, :, :, part, parity] = values.reshape(ny, pencils, modes)
            back[:, part, parity, :, parity] = (values * weight).T.reshape(pencils, modes, ny)
    return ahead.reshape(2 * ny, -1), back.reshape(-1, 2 * ny)


def wave_order(nx, slabs):
    half = nx // 2
    ahead = np.arange(half).reshape(slabs, 1, half // slabs)
    behind = np.where(ahead == 0, half, (nx - ahead) % nx)
    return np.concatenate([ahead, behind], axis=1).reshape(-1)


def x_tables(nx, cols, pencils, slabs):
    order = wave_order(nx, slabs)
    angle = angles(order, np.arange(nx), nx)
    ahead = np.concatenate([np.cos(angle), np.sin(angle)], axis=0)
    row = np.arange(cols + RIM)
    offset = np.where(row <= cols, row, -1)
    used = ((row <= cols) | (row == cols + RIM - 1)).astype(np.float64)
    place = (np.arange(pencils)[:, None] * cols + offset[None, :]) % nx
    angle = angles(place.reshape(-1), order, nx)
    mask = np.tile(used, pencils)[:, None]
    back = np.concatenate([np.cos(angle) * mask, np.sin(angle) * mask], axis=0)
    return ahead, back


def split(values):
    high = values.astype(BF16)
    return high, (values - high.astype(F32)).astype(BF16)


def dot(left, right):
    return jnp.dot(left, right, preferred_element_type=F32)


def table_left(high, low, values):
    v_high, v_low = split(values)
    return dot(high, v_high) + (dot(high, v_low) + dot(low, v_high))


def table_right(values, high, low):
    v_high, v_low = split(values)
    return dot(v_high, high) + (dot(v_low, high) + dot(v_high, low))


def lane_of():
    return lax.broadcasted_iota(jnp.int32, (1, LANES), 1)


def times_i(values):
    half = LANES // 2
    sign = jnp.where(lane_of() < half, -1.0, 1.0).astype(F32)
    return pltpu.roll(values, half, 1) * sign


def kernel_weight(distance):
    radius = jnp.abs(distance)
    near = 1.0 + radius * radius * (1.5 * radius - 2.5)
    rest = jnp.maximum(2.0 - radius, 0.0)
    return jnp.where(radius < 1.0, near, 0.5 * rest * rest * (1.0 - radius))


def quotient(values, size):
    if size & (size - 1):
        return lax.div(values, size)
    return lax.shift_right_logical(values, size.bit_length() - 1)


def remainder(values, size):
    if size & (size - 1):
        return lax.rem(values, size)
    return values & (size - 1)


def turned(value, wave, extent, sign):
    wave = wave % extent
    real, imag = value
    if wave == 0:
        return value
    if 2 * wave == extent:
        return -real, -imag
    if 4 * wave == extent:
        return (-imag, real) if sign > 0 else (imag, -real)
    if 4 * wave == 3 * extent:
        return (imag, -real) if sign > 0 else (-imag, real)
    a = math.cos(2.0 * math.pi * wave / extent)
    b = sign * math.sin(2.0 * math.pi * wave / extent)
    return real * a - imag * b, real * b + imag * a


def fft(values, sign):
    count = len(values)
    if count == 1:
        return values
    even, odd = fft(values[::2], sign), fft(values[1::2], sign)
    odd = [turned(v, k, count, sign) for k, v in enumerate(odd)]
    plus = [(a[0] + b[0], a[1] + b[1]) for a, b in zip(even, odd)]
    minus = [(a[0] - b[0], a[1] - b[1]) for a, b in zip(even, odd)]
    return plus + minus


def offset_order(count, first=None):
    far, near = list(range(count // 2, count)), list(range(1, count // 2))
    if first == "near":
        return [0] + near + far
    if first == "far":
        return [0] + far + near
    order, last = [0], near[-1:]
    near = near[:-1]
    while far or near:
        order += far[:1] + near[:1]
        far, near = far[1:], near[1:]
    return order + last


def blocks_of(refs, at, first=None):
    if len(refs) == 1:
        return [(d, refs[0].at[d]) for d in range(refs[0].shape[0])]
    return [(at ^ k, ref) for k, ref in zip(offset_order(len(refs), first), refs)]


def gather_blocks(refs, held, at, first=None):
    for d, ref in blocks_of(refs, at, first):
        held[d] = ref[...]


def packet_kernel(
    counts, strength, offsets, cells, packet, movers, near_counts, near_cells, sems
):
    copies = [
        pltpu.make_async_copy(counts, near_counts, sems.at[0]),
        pltpu.make_async_copy(cells, near_cells, sems.at[1]),
        pltpu.make_async_copy(strength, packet.at[pl.ds(0, 3)], sems.at[2]),
        pltpu.make_async_copy(offsets, packet.at[pl.ds(3, 3)], sems.at[3]),
    ]
    for copy in copies:
        copy.start()
    for copy in copies:
        copy.wait()
    slot = lax.broadcasted_iota(jnp.int32, (1, packet.shape[1]), 1)
    up = near_counts[0:1, 0:1]
    both = up + near_counts[0:1, 1:2]
    packet[6:7] = near_cells[...].astype(F32)
    packet[7:8] = jnp.where(slot < up, 1.0, jnp.where(slot < both, -1.0, 0.0))
    movers[...] = packet[:, : movers.shape[1]]


def deposit_kernel(
    pairs, rims_before, first, place, own, up1, down1, up2, down2, ambient, t_high, t_low, *refs
):
    rims, refs = refs[:rims_before], refs[rims_before:]
    mesh, rim_high, rim_low = refs[:3]
    total, made = refs[-2:]
    outs = refs[3:-2]
    _, planes, cols, ny = ambient.shape
    rows = cols + RIM
    movers = up2.shape[1]
    count = own.shape[1]
    listed = [2 * pair + parity for pair in pairs for parity in range(2)]

    def decode(ref, start, stop, shift):
        packet = ref[:, start:stop]
        cell = packet[6:7].astype(jnp.int32)
        move = packet[7:8].astype(jnp.int32)
        z_cell = quotient(cell, cols * ny) + planes * (move + shift)
        x_cell = remainder(quotient(cell, ny), cols)
        return packet[0:6], z_cell, x_cell, remainder(cell, ny)

    def joined(pieces):
        return [jnp.concatenate(p, axis=1) if len(p) > 1 else p[0] for p in zip(*pieces)]

    def add_block(pieces, wanted):
        values, z_cell, x_cell, y_cell = joined(pieces)
        width = values.shape[1]
        z_at = lax.broadcasted_iota(jnp.int32, (planes, width), 0)
        w_z = kernel_weight((z_at - z_cell).astype(F32) - values[3:4])
        row = lax.broadcasted_iota(jnp.int32, (rows, width), 0)
        x_at = jnp.where(row < cols + 2, row, jnp.where(row >= rows - 2, row - rows, 4 * rows))
        w_x = kernel_weight((x_at - x_cell).astype(F32) - values[4:5])
        y_at = lax.broadcasted_iota(jnp.int32, (ny, width), 0)
        y_off = remainder(y_at + (ny + ny // 2 - y_cell), ny) - ny // 2
        w_y = kernel_weight(y_off.astype(F32) - values[5:6])
        y_high, y_low = split(w_y)
        right = jnp.concatenate([y_high, y_high, y_low], axis=1)
        at = [listed.index(z) for z in wanted]
        for c in range(3):
            s_z = values[c : c + 1] * w_z
            left = jnp.concatenate([s_z[z : z + 1] * w_x for z in wanted], axis=0)
            l_high, l_low = split(left)
            left = jnp.concatenate([l_high, l_low, l_high], axis=1)
            added = lax.dot_general(
                left, right, (((1,), (1,)), ((), ())), preferred_element_type=F32
            )
            total[c, at[0] : at[-1] + 1] += added.reshape(len(wanted), rows, ny)

    for n, z in enumerate(listed):
        total[:, n, 0:cols] = ambient[:, z]
    total[:, :, cols:rows] = jnp.zeros((3, len(listed), RIM, ny), F32)
    step = 256
    for at in range(0, count, step):
        add_block([decode(own, at, min(at + step, count), 0)], listed)
    add_block([decode(up1, 0, movers, 1), decode(down1, 0, movers, -1)], listed)
    sides = ((up1, up2, 1, (planes - 2, planes - 1)), (down1, down2, -1, (0, 1)))
    for near, far, shift, wanted in sides:
        if not set(wanted) <= set(listed):
            continue
        whole = [decode(near, movers, count, shift), decode(far, 0, movers, 2 * shift)]
        values, z_cell, x_cell, y_cell = joined(whole)
        for at in range(0, count, step):
            to = min(at + step, count)
            block = (values[:, at:to], z_cell[:, at:to], x_cell[:, at:to], y_cell[:, at:to])
            add_block([block], wanted)

    mesh[...] = total[:, :, 0:cols]
    at = 0
    if rims:
        at = rims[0].shape[0]
        rim_high[0:at] = rims[0][...]
        rim_low[0:at] = rims[1][...]
    for n in range(3 * len(listed)):
        c, i = n // len(listed), n % len(listed)
        rim_high[at + 2 * n : at + 2 * n + 2] = total[c, i, cols : cols + 2]
        rim_low[at + 2 * n : at + 2 * n + 2] = total[c, i, rows - 2 : rows]
    groups = [(c, 2 * n) for c in range(3) for n in range(len(pairs))]
    left = jnp.concatenate(
        [jnp.concatenate([total[c, n], total[c, n + 1]], axis=1) for c, n in groups], axis=0
    )
    wide = table_right(left, t_high[...], t_low[...])
    for n in range(len(groups)):
        for g in range(made.shape[0]):
            made[g, :, n * LANES : (n + 1) * LANES] = wide[
                n * rows : (n + 1) * rows, g * LANES : (g + 1) * LANES
            ]
    for d, out in blocks_of(outs, place[1], first):
        out[...] = made[d]


def x_ahead_kernel(sends, first, place, t_high, t_low, *refs):
    held, made = refs[-2:]
    outs, parts = refs[-2 - sends : -2], refs[: -2 - sends]
    gather_blocks(parts, held, place[1], first)
    pencils, rows, width = held.shape
    cols = rows - RIM
    row = lax.broadcasted_iota(jnp.int32, (RIM, width), 0)
    pieces = []
    for h in range(pencils):
        from_low = held[(h - 1) % pencils, cols:rows]
        from_high = held[(h + 1) % pencils, cols:rows]
        pieces.append(held[h, 0:RIM] + jnp.where(row < 2, from_low, 0.0))
        pieces.append(held[h, RIM : cols - RIM])
        pieces.append(held[h, cols - RIM : cols] + jnp.where(row >= RIM - 2, from_high, 0.0))
    both = table_left(t_high[...], t_low[...], jnp.concatenate(pieces, axis=0))
    half = both.shape[0] // 2
    for n in range(width // LANES):
        lanes = slice(n * LANES, (n + 1) * LANES)
        value = both[:half, lanes] - times_i(both[half:, lanes])
        made[:, :, lanes] = value.reshape(made.shape[0], made.shape[1], LANES)
    for d, out in blocks_of(outs, place[0]):
        out[...] = made[d]


def x_back_kernel(sends, first, passed, tables, place, *refs):
    held, made = refs[-2:]
    outs, parts = refs[-2 - sends : -2], refs[passed : -2 - sends]
    gather_blocks(parts, held, place[0])
    pencils, rows, width = made.shape
    both = table_left(tables[0][...], tables[1][...], held[...].reshape(-1, width))
    half = both.shape[0] // 2
    for n in range(width // LANES):
        lanes = slice(n * LANES, (n + 1) * LANES)
        value = both[:half, lanes] + times_i(both[half:, lanes])
        made[:, :, lanes] = value.reshape(pencils, rows, LANES)
    for d, out in blocks_of(outs, place[1], first):
        out[...] = made[d]


def wave_lanes():
    lane = lane_of()
    return lane < LANES // 2, (lane // (LANES // 4)) % 2 == 0


def roll(values, shift):
    return pltpu.roll(values, shift, 1)


def cross_half(a, b):
    low, _ = wave_lanes()
    half = LANES // 2
    return jnp.where(low, a, roll(b, half)), jnp.where(low, roll(a, half), b)


def cross_quarter(a, b):
    _, first = wave_lanes()
    quarter = LANES // 4
    return (
        jnp.where(first, a, roll(b, quarter)),
        jnp.where(first, roll(a, LANES - quarter), b),
    )


def lanes_at(c, count, i):
    return pl.ds(pl.multiple_of((c * count + i) * LANES, LANES), LANES)


def enter_kernel(pairs, nz, place, *refs):
    parts, data = refs[:-1], refs[-1]
    _, _, _, slabs, tile, _ = data.shape

    def body(c, carry):
        for i, pair in enumerate(pairs):
            lanes = lanes_at(c, len(pairs), i)
            for s, ref in blocks_of(parts, place[0]):
                quad = [ref[q * tile : (q + 1) * tile, lanes] for q in range(4)]
                real0, imag0 = cross_half(quad[0], quad[2])
                real1, imag1 = cross_half(quad[1], quad[3])
                for part, (a, b) in enumerate(((real0, real1), (imag0, imag1))):
                    even, odd = cross_quarter(a, b)
                    data[c, part, 2 * i, s] = even
                    data[c, part, 2 * i + 1, s] = odd
            for parity in range(2):
                at = 2 * i + parity
                line = [(data[c, 0, at, s], data[c, 1, at, s]) for s in range(slabs)]
                for k, v in enumerate(fft(line, -1.0)):
                    v = turned(v, (2 * pair + parity) * k, nz, -1.0)
                    data[c, 0, at, k], data[c, 1, at, k] = v
        return carry

    lax.fori_loop(0, 3, body, 0)


def pass_kernel(before, *refs):
    half = LATE
    for source, target in zip(refs[-2 * half : -half], refs[-half:]):
        target[...] = source[...]


def leave_kernel(pairs, nz, place, source, *refs):
    outs, data = refs[:-1], refs[-1]
    _, _, _, slabs, tile, _ = source.shape

    def body(c, carry):
        for i, pair in enumerate(pairs):
            lanes = lanes_at(c, len(pairs), i)
            for parity in range(2):
                at = 2 * i + parity
                line = [
                    turned(
                        (source[c, 0, at, k], source[c, 1, at, k]),
                        (2 * pair + parity) * k,
                        nz,
                        1.0,
                    )
                    for k in range(slabs)
                ]
                for s, v in enumerate(fft(line, 1.0)):
                    data[c, 0, at, s], data[c, 1, at, s] = v
            for s, ref in blocks_of(outs, place[0]):
                real0, real1 = cross_quarter(data[c, 0, 2 * i, s], data[c, 0, 2 * i + 1, s])
                imag0, imag1 = cross_quarter(data[c, 1, 2 * i, s], data[c, 1, 2 * i + 1, s])
                quad = [None] * 4
                quad[0], quad[2] = cross_half(real0, imag0)
                quad[1], quad[3] = cross_half(real1, imag1)
                for q in range(4):
                    ref[q * tile : (q + 1) * tile, lanes] = quad[q]
        return carry

    lax.fori_loop(0, 3, body, 0)


def curl_kernel(chunks, nx, ny, place, low_rim, high_rim, *refs):
    sources, outs = refs[: len(chunks)], refs[len(chunks) : 2 * len(chunks)]
    spectrum = refs[-1]
    _, _, nz, tile, _ = spectrum.shape
    slabs = sources[0].shape[3]
    planes = nz // slabs
    modes, half = LANES // 4, LANES // 2
    slab_at, pencil_at = place[0], place[1]
    spot = {}
    for n, chunk in enumerate(chunks):
        for i, pair in enumerate(chunk):
            spot[2 * pair], spot[2 * pair + 1] = (n, 2 * i), (n, 2 * i + 1)

    def across_planes(k, carry):
        for c in range(3):
            line = []
            for l in range(planes):
                n, i = spot[l]
                line.append((sources[n][c, 0, i, k], sources[n][c, 1, i, k]))
            for n, v in enumerate(fft(line, -1.0)):
                spectrum[c, 0, k + slabs * n], spectrum[c, 1, k + slabs * n] = v
        return carry

    reach = 2 * tile
    row = lax.broadcasted_iota(jnp.int32, (tile, LANES), 0)
    lane = lax.broadcasted_iota(jnp.int32, (tile, LANES), 1)
    number = slab_at * reach + (lane // modes) % 2 * tile + row
    ahead = lane < half
    mode = lane % modes + pencil_at * modes
    alone = number == 0
    number = number.astype(F32) * (2.0 * math.pi / nx)
    x_base = jnp.where(ahead, number, jnp.where(alone, math.pi, -number))
    x_trim = jnp.where(ahead, number, jnp.where(alone, 0.0, -number))
    wave_y = mode.astype(F32) * (2.0 * math.pi / ny)
    packed = mode == 0
    x_sq = x_base * x_base
    lateral = x_sq + wave_y * wave_y

    def curl_at(k, with_mirror):
        z_wave = jnp.where(k < nz // 2, k, k - nz).astype(F32) * (2.0 * math.pi / nz)
        z_trim = jnp.where(k == nz // 2, 0.0, z_wave)
        full = lateral + z_wave * z_wave
        empty = full == 0.0
        inverse = jnp.where(empty, 0.0, 1.0 / jnp.where(empty, 1.0, full))
        if with_mirror:
            other = 1.0 / (x_sq + (z_wave * z_wave + math.pi * math.pi))
            mirror = jnp.where(packed, 0.5 * (inverse - other), 0.0)
            inverse = jnp.where(packed, 0.5 * (inverse + other), inverse)
            opposite = lax.rem(nz - k, nz)
        stream = []
        for c in range(3):
            value = [spectrum[c, part, k] * inverse for part in range(2)]
            if with_mirror:
                for part, sign in enumerate((1.0, -1.0)):
                    there = spectrum[c, part, opposite]
                    there = jnp.where(alone, there, roll(there, half))
                    value[part] = value[part] + (mirror * sign) * there
            stream.append(value)
        made = []
        for part in range(2):
            s = [value[part] for value in stream]
            made.append(
                (
                    x_trim * s[2] - wave_y * s[1],
                    wave_y * s[0] - z_trim * s[2],
                    z_trim * s[1] - x_trim * s[0],
                )
            )
        return [(-made[1][c], made[0][c]) for c in range(3)]

    def curl_all(with_mirror):
        def body(k, carry):
            made = [curl_at(k + slabs * n, with_mirror) for n in range(planes)]
            for c in range(3):
                for l, v in enumerate(fft([m[c] for m in made], 1.0)):
                    n, i = spot[l]
                    outs[n][c, 0, i, k], outs[n][c, 1, i, k] = v
            return carry

        lax.fori_loop(0, slabs, body, 0)

    lax.fori_loop(0, slabs, across_planes, 0)

    @pl.when(pencil_at == 0)
    def _():
        curl_all(True)

    @pl.when(pencil_at != 0)
    def _():
        curl_all(False)


def planes_of(held, pairs, tables):
    pencils, rows, _ = held.shape
    groups = [(c, pair) for c in range(3) for pair in pairs]
    left = jnp.concatenate(
        [
            jnp.concatenate(
                [held[h, :, n * LANES : (n + 1) * LANES] for h in range(pencils)], axis=1
            )
            for n in range(len(groups))
        ],
        axis=0,
    )
    ny = tables[0].shape[1] // 2
    wide = table_right(left, tables[0][...], tables[1][...])
    made = {}
    for n, (c, pair) in enumerate(groups):
        for parity in range(2):
            made[c, 2 * pair + parity] = wide[
                n * rows : (n + 1) * rows, parity * ny : (parity + 1) * ny
            ]
    return made


def hold(tall, c, n, value):
    rows = value.shape[0]
    tall[c, n, RIM : RIM + rows] = value
    tall[c, n, 0:RIM] = value[rows - RIM : rows]


def edge_kernel(pairs, tables, place, *refs):
    tall, first, last, held = refs[-4:]
    gather_blocks(refs[:-4], held, place[1])
    listed = [2 * pair + parity for pair in pairs for parity in range(2)]
    cols = first.shape[1]
    values = planes_of(held, pairs, tables)
    for c in range(3):
        for n, z in enumerate(listed):
            hold(tall, c, n, values[c, z])
        first[c] = values[c, listed[0]][0:cols]
        last[c] = values[c, listed[-1]][0:cols]


def where_planes(chunks):
    spot = {}
    for n, chunk in enumerate(chunks):
        for i, pair in enumerate(chunk):
            spot[2 * pair], spot[2 * pair + 1] = (n, 2 * i), (n, 2 * i + 1)
    return spot


def rim_start(meshes, which, c, i):
    before = 6 * meshes[1].shape[1] if which == 0 else 0
    return before + 2 * (c * meshes[which].shape[1] + i)


def stretch_plane(out, mesh, rims, at, rows_of, above, below):
    cols, ny = out[0].shape
    low_rim, high_rim = rims
    for c in range(3):
        out[c][...] = mesh[c][...]
        out[c][0:2] += low_rim[at[c] : at[c] + 2]
        out[c][cols - 2 : cols] += high_rim[at[c] : at[c] + 2]
    omega = [ref[...] for ref in out]
    for c in range(3):
        value = rows_of(c, RIM)
        along_z = (above(c) - below(c)) * 0.5
        along_x = (rows_of(c, RIM + 1) - rows_of(c, RIM - 1)) * 0.5
        along_y = (pltpu.roll(value, ny - 1, 1) - pltpu.roll(value, 1, 1)) * 0.5
        stretch = omega[0] * along_z + omega[1] * along_x + omega[2] * along_y
        out[c][...] = omega[c] + TIME_STEP * stretch


def ends_kernel(_, __, edges, before, after, low_rim, high_rim, *refs):
    meshes, vorticity, out, sems = refs[:-4], refs[-3], refs[-2], refs[-1]
    cols = before.shape[1]
    size = edges.shape[1]
    copies = []

    def rows_of(i):
        return lambda c, start=RIM: edges[c, i, start : start + cols]

    for n, i in enumerate((0, size - 1)):
        stretch_plane(
            [out.at[c, n] for c in range(3)],
            [meshes[0].at[c, i] for c in range(3)],
            (low_rim, high_rim),
            [rim_start(meshes, 0, c, i) for c in range(3)],
            rows_of(i),
            (lambda c: after[c]) if i else rows_of(1),
            rows_of(size - 2) if i else (lambda c: before[c]),
        )
        copies.append(
            pltpu.make_async_copy(
                out.at[:, n], vorticity.at[:, n * (vorticity.shape[1] - 1)], sems.at[n]
            )
        )
        copies[-1].start()
    for copy in copies:
        copy.wait()


def stretch_kernel(chunks, tables, place, edges, low_rim, high_rim, *refs):
    meshes, refs = refs[:2], refs[2:]
    velocity, vorticity, held, inner, omega, sems = refs[-6:]
    _, planes, cols, ny = velocity.shape
    spot = where_planes(chunks)
    talls = (edges, inner)
    sent = []

    def send(source, target):
        sent.append(pltpu.make_async_copy(source, target, sems.at[len(sent)]))
        sent[-1].start()

    def rows_of(z):
        n, i = spot[z]
        return lambda c, start=RIM: talls[n][c, i, start : start + cols]

    def send_velocity(which):
        for z in range(planes):
            n, i = spot[z]
            if n == which:
                send(talls[n].at[:, i, pl.ds(RIM, cols)], velocity.at[:, z])

    send_velocity(0)
    gather_blocks(refs[:-6], held, place[1], "far")
    for (c, z), value in planes_of(held, chunks[1], tables).items():
        hold(inner, c, spot[z][1], value)
    send_velocity(1)
    for z in range(1, planes - 1):
        which, i = spot[z]
        stretch_plane(
            [omega.at[c, z] for c in range(3)],
            [meshes[which].at[c, i] for c in range(3)],
            (low_rim, high_rim),
            [rim_start(meshes, which, c, i) for c in range(3)],
            rows_of(z),
            rows_of(z + 1),
            rows_of(z - 1),
        )
        send(omega.at[:, z], vorticity.at[:, z])
    for copy in sent:
        copy.wait()


VM = pl.BlockSpec(memory_space=pltpu.VMEM)
SM = pl.BlockSpec(memory_space=pltpu.SMEM)
AN = pl.BlockSpec(memory_space=pl.ANY)
HB = pl.BlockSpec(memory_space=pltpu.HBM)


def kept(values):
    return pltpu.with_memory_space_constraint(values, pltpu.HBM)


def loaded(kernel):
    def run(place, t_high, t_low, *refs):
        kernel((t_high, t_low), place, *refs)

    return run


def call(kernel, ins, outs, scratch=(), sems=0, micros=2.0, moved=None, aliases=None):
    extra = [pltpu.SemaphoreType.DMA((sems,))] if sems else []
    return pl.pallas_call(
        kernel,
        out_shape=[jax.ShapeDtypeStruct(shape, F32) for _, shape in outs],
        in_specs=[spec for spec, _ in ins],
        out_specs=[spec for spec, _ in outs],
        scratch_shapes=[pltpu.VMEM(shape, kind) for shape, kind in scratch] + extra,
        compiler_params=pltpu.CompilerParams(vmem_limit_bytes=VMEM),
        input_output_aliases=aliases or {},
        cost_estimate=pl.CostEstimate(
            flops=int(micros * 1.0e9),
            bytes_accessed=int(micros * 3.0e6) if moved is None else moved,
            transcendentals=0,
        ),
    )(*[value for _, value in ins])


def ring(axis, step):
    count = lax.axis_size(axis)
    return [(i, (i + step) % count) for i in range(count)]


def spread(axis):
    count = lax.axis_size(axis)
    return count <= 8 and count & (count - 1) == 0


def sent_shapes(axis, rows, width, whole=False):
    count = lax.axis_size(axis)
    return [(count, rows, width)] if whole or not spread(axis) else [(rows, width)] * count


def exchange(blocks, axis, start=0, first=None):
    if not spread(axis):
        return [lax.all_to_all(blocks[0], axis, split_axis=0, concat_axis=0, tiled=True)]
    count = lax.axis_size(axis)
    return [
        lax.ppermute(block, axis, [(i, i ^ k) for i in range(count)]) if k else block
        for k, block in zip(offset_order(count, first)[start:], blocks)
    ]


def on_device(strength, offsets, cell_index, migrate_count, ambient):
    _, planes, cols, ny = ambient.shape
    slabs, pencils = lax.axis_size("gz"), lax.axis_size("gx")
    nx, nz, rows = cols * pencils, planes * slabs, cols + RIM
    count = strength.shape[1]
    pair_count = planes // 2
    chunks = ((0, pair_count - 1), tuple(range(1, pair_count - 1)))
    widths = [3 * len(c) * LANES for c in chunks]
    block = nx // slabs

    y_ahead, y_back = [split_table(t) for t in y_tables(ny, pencils, 1.0 / (float(nx) * ny * nz))]
    x_ahead, x_back = [split_table(t) for t in x_tables(nx, cols, pencils, slabs)]
    place = jnp.stack([lax.axis_index("gz"), lax.axis_index("gx")]).astype(jnp.int32)
    here = (SM, place)

    packet, movers = call(
        packet_kernel,
        [
            (HB, kept(migrate_count.reshape(1, 2))),
            (HB, kept(strength)),
            (HB, kept(offsets)),
            (HB, kept(cell_index.reshape(1, count))),
        ],
        [(VM, (8, count)), (VM, (8, 2 * MIG))],
        [((1, 2), jnp.int32), ((1, count), jnp.int32)],
        sems=4,
        micros=1.0,
        moved=1000,
    )
    up1 = lax.ppermute(packet, "gz", ring("gz", -1))
    down1 = lax.ppermute(packet, "gz", ring("gz", 1))
    up2 = lax.ppermute(movers, "gz", ring("gz", -2))
    down2 = lax.ppermute(movers, "gz", ring("gz", 2))

    meshes, rims, parts = [None, None], [], [None, None]
    for n in (1, 0):
        chunk, width = chunks[n], widths[n]
        size = 2 * len(chunk)
        rim = (6 * size + (rims[0].shape[0] if rims else 0), ny)
        mesh, rim_high, rim_low, *part = call(
            functools.partial(deposit_kernel, chunk, len(rims), None if n else "near"),
            [here]
            + [(VM, value) for value in (packet, up1, down1, up2, down2)]
            + [(VM, ambient), (VM, y_ahead[0]), (VM, y_ahead[1])]
            + [(VM, value) for value in rims],
            [(VM, (3, size, cols, ny)), (VM, rim), (VM, rim)]
            + [(VM, shape) for shape in sent_shapes("gx", rows, width)],
            [((3, size, rows, ny), F32), ((pencils, rows, width), F32)],
            micros=5.0,
        )
        meshes[n] = mesh
        rims = [rim_high, rim_low]
        parts[n] = exchange(part, "gx", first="near" if n == 0 else None)
    low_rim = lax.ppermute(rims[0], "gx", ring("gx", 1))
    high_rim = lax.ppermute(rims[1], "gx", ring("gx", -1))

    tile = max(1, block // 4)
    data = [None, None]
    for n in (1, 0):
        chunk, part, width = chunks[n], parts[n], widths[n]
        shapes = sent_shapes("gz", block, width)
        part = call(
            functools.partial(x_ahead_kernel, len(shapes), None if n else "near"),
            [here, (VM, x_ahead[0]), (VM, x_ahead[1])] + [(VM, p) for p in part],
            [(VM, shape) for shape in shapes],
            [((pencils, rows, width), F32), ((slabs, block, width), F32)],
        )
        (entered,) = call(
            functools.partial(enter_kernel, chunk, nz),
            [here] + [(VM, p) for p in exchange(part, "gz")],
            [(VM, (3, 2, 2 * len(chunk), slabs, tile, LANES))],
        )
        data[n] = entered
    data = call(
        functools.partial(curl_kernel, chunks, nx, ny),
        [here, (VM, low_rim), (VM, high_rim)] + [(VM, d) for d in data],
        [(VM, d.shape) for d in data],
        [((3, 2, nz, tile, LANES), F32)],
        micros=5.0,
    )
    plane = (3, cols, ny)
    tables = [(VM, t) for t in y_back]
    tall = [(3, 2 * len(chunk), cols + 2 * RIM, ny) for chunk in chunks]
    left = [
        call(
            functools.partial(leave_kernel, chunk, nz),
            [here, (VM, source)],
            [(VM, shape) for shape in sent_shapes("gz", block, width)],
            [(source.shape, F32)],
        )
        for chunk, source, width in zip(chunks, data, widths)
    ]

    def back(part, width, first=None, before=()):
        shapes = sent_shapes("gx", rows, width)
        part = call(
            loaded(functools.partial(x_back_kernel, len(shapes), first, len(before))),
            [here]
            + [(VM, t) for t in x_back]
            + [(AN, b) for b in before]
            + [(VM, p) for p in part],
            [(VM, shape) for shape in shapes],
            [((slabs, block, width), F32), ((pencils, rows, width), F32)],
        )
        return exchange(part, "gx", first=first)

    early = max(1, len(left[1]) - LATE)
    second = exchange(left[1][:early], "gz")
    parts = [back(exchange(left[0], "gz"), widths[0])]
    edges, first, last = call(
        loaded(functools.partial(edge_kernel, chunks[0])),
        [here] + tables + [(VM, p) for p in parts[0]],
        [(VM, tall[0]), (VM, plane), (VM, plane)],
        [((pencils, rows, widths[0]), F32)],
    )
    if early < len(left[1]):
        late = call(
            pass_kernel,
            [(AN, parts[0][0])] + [(AN, p) for p in second[1:]] + [(VM, p) for p in left[1][early:]],
            [(VM, p.shape) for p in left[1][early:]],
            micros=0.3,
        )
        second += exchange(late, "gz", early)
    parts.append(back(second, widths[1], "far", [first]))
    after = lax.ppermute(first, "gz", ring("gz", -1))
    before = lax.ppermute(last, "gz", ring("gz", 1))
    velocity, vorticity = call(
        loaded(functools.partial(stretch_kernel, chunks)),
        [here]
        + tables
        + [(VM, v) for v in (edges, low_rim, high_rim, *meshes)]
        + [(VM, p) for p in parts[1]],
        [(AN, ambient.shape), (AN, ambient.shape)],
        [
            ((pencils, rows, widths[1]), F32),
            (tall[1], F32),
            ((3, planes, cols, ny), F32),
        ],
        sems=2 * planes,
        micros=4.0,
    )
    return tuple(
        call(
            ends_kernel,
            [(AN, velocity), (AN, vorticity)]
            + [(VM, v) for v in (edges, before, after, low_rim, high_rim, *meshes)],
            [(AN, ambient.shape), (AN, ambient.shape)],
            [((3, 2, cols, ny), F32)],
            sems=2,
            micros=1.0,
            aliases={0: 0, 1: 1},
        )
    )


def solution(mesh):
    placed = (
        P(None, ("gz", "gx")),
        P(None, ("gz", "gx")),
        P(("gz", "gx")),
        P("gz", "gx", None),
        P(None, "gz", "gx", None),
    )
    return jax.shard_map(
        on_device,
        mesh=mesh,
        in_specs=placed,
        out_specs=(P(None, "gz", "gx", None), P(None, "gz", "gx", None)),
        check_vma=False,
    )
```

```python
import functools
import math

import jax
import jax.numpy as jnp
import ml_dtypes
import numpy as np
from jax import lax
from jax.experimental import pallas as pl
from jax.experimental.pallas import tpu as pltpu
from jax.sharding import PartitionSpec as P

MIG = 64
LANES = 128
RIM = 8
LATE = 3
TIME_STEP = 0.25
VMEM = 24 * 1024 * 1024
F32 = jnp.float32
BF16 = jnp.bfloat16


def split_table(table):
    high = table.astype(np.float32).astype(ml_dtypes.bfloat16)
    low = (table - high.astype(np.float64)).astype(np.float32).astype(ml_dtypes.bfloat16)
    return high, low


def angles(rows, columns, extent):
    return 2.0 * np.pi * (np.multiply.outer(rows, columns) % extent) / extent


def y_tables(ny, pencils, scale):
    modes = ny // (2 * pencils)
    position = np.arange(ny)
    angle = angles(position, np.arange(ny // 2), ny)
    real, imag = np.cos(angle), -np.sin(angle)
    imag[:, 0] = 1.0 - 2.0 * (position % 2)
    weight = np.where(np.arange(ny // 2) == 0, 1.0, 2.0) * scale
    ahead = np.zeros((2, ny, pencils, 2, 2, modes))
    back = np.zeros((pencils, 2, 2, modes, 2, ny))
    for parity in range(2):
        for part, values in enumerate((real, imag)):
            ahead[parity, :, :, part, parity] = values.reshape(ny, pencils, modes)
            back[:, part, parity, :, parity] = (values * weight).T.reshape(pencils, modes, ny)
    return ahead.reshape(2 * ny, -1), back.reshape(-1, 2 * ny)


def wave_order(nx, slabs):
    half = nx // 2
    ahead = np.arange(half).reshape(slabs, 1, half // slabs)
    behind = np.where(ahead == 0, half, (nx - ahead) % nx)
    return np.concatenate([ahead, behind], axis=1).reshape(-1)


def x_tables(nx, cols, pencils, slabs):
    order = wave_order(nx, slabs)
    angle = angles(order, np.arange(nx), nx)
    ahead = np.concatenate([np.cos(angle), np.sin(angle)], axis=0)
    row = np.arange(cols + RIM)
    offset = np.where(row <= cols, row, -1)
    used = ((row <= cols) | (row == cols + RIM - 1)).astype(np.float64)
    place = (np.arange(pencils)[:, None] * cols + offset[None, :]) % nx
    angle = angles(place.reshape(-1), order, nx)
    mask = np.tile(used, pencils)[:, None]
    back = np.concatenate([np.cos(angle) * mask, np.sin(angle) * mask], axis=0)
    return ahead, back


def split(values):
    high = values.astype(BF16)
    return high, (values - high.astype(F32)).astype(BF16)


def dot(left, right):
    return jnp.dot(left, right, preferred_element_type=F32)


def table_left(high, low, values):
    v_high, v_low = split(values)
    return dot(high, v_high) + (dot(high, v_low) + dot(low, v_high))


def table_right(values, high, low):
    v_high, v_low = split(values)
    return dot(v_high, high) + (dot(v_low, high) + dot(v_high, low))


def lane_of():
    return lax.broadcasted_iota(jnp.int32, (1, LANES), 1)


def times_i(values):
    half = LANES // 2
    sign = jnp.where(lane_of() < half, -1.0, 1.0).astype(F32)
    return pltpu.roll(values, half, 1) * sign


def kernel_weight(distance):
    radius = jnp.abs(distance)
    near = 1.0 + radius * radius * (1.5 * radius - 2.5)
    rest = jnp.maximum(2.0 - radius, 0.0)
    return jnp.where(radius < 1.0, near, 0.5 * rest * rest * (1.0 - radius))


def quotient(values, size):
    if size & (size - 1):
        return lax.div(values, size)
    return lax.shift_right_logical(values, size.bit_length() - 1)


def remainder(values, size):
    if size & (size - 1):
        return lax.rem(values, size)
    return values & (size - 1)


def turned(value, wave, extent, sign):
    wave = wave % extent
    real, imag = value
    if wave == 0:
        return value
    if 2 * wave == extent:
        return -real, -imag
    if 4 * wave == extent:
        return (-imag, real) if sign > 0 else (imag, -real)
    if 4 * wave == 3 * extent:
        return (imag, -real) if sign > 0 else (-imag, real)
    a = math.cos(2.0 * math.pi * wave / extent)
    b = sign * math.sin(2.0 * math.pi * wave / extent)
    return real * a - imag * b, real * b + imag * a


def fft(values, sign):
    count = len(values)
    if count == 1:
        return values
    even, odd = fft(values[::2], sign), fft(values[1::2], sign)
    odd = [turned(v, k, count, sign) for k, v in enumerate(odd)]
    plus = [(a[0] + b[0], a[1] + b[1]) for a, b in zip(even, odd)]
    minus = [(a[0] - b[0], a[1] - b[1]) for a, b in zip(even, odd)]
    return plus + minus


def offset_order(count, first=None):
    far, near = list(range(count // 2, count)), list(range(1, count // 2))
    if first == "near":
        return [0] + near + far
    if first == "far":
        return [0] + far + near
    order, last = [0], near[2:]
    near = near[:2]
    while far or near:
        order += far[:1] + near[:1]
        far, near = far[1:], near[1:]
    return order + last


def blocks_of(refs, at, first=None):
    if len(refs) == 1:
        return [(d, refs[0].at[d]) for d in range(refs[0].shape[0])]
    return [(at ^ k, ref) for k, ref in zip(offset_order(len(refs), first), refs)]


def gather_blocks(refs, held, at, first=None):
    for d, ref in blocks_of(refs, at, first):
        held[d] = ref[...]


def packet_kernel(
    counts, strength, offsets, cells, packet, movers, near_counts, near_cells, sems
):
    copies = [
        pltpu.make_async_copy(counts, near_counts, sems.at[0]),
        pltpu.make_async_copy(cells, near_cells, sems.at[1]),
        pltpu.make_async_copy(strength, packet.at[pl.ds(0, 3)], sems.at[2]),
        pltpu.make_async_copy(offsets, packet.at[pl.ds(3, 3)], sems.at[3]),
    ]
    for copy in copies:
        copy.start()
    for copy in copies:
        copy.wait()
    slot = lax.broadcasted_iota(jnp.int32, (1, packet.shape[1]), 1)
    up = near_counts[0:1, 0:1]
    both = up + near_counts[0:1, 1:2]
    packet[6:7] = near_cells[...].astype(F32)
    packet[7:8] = jnp.where(slot < up, 1.0, jnp.where(slot < both, -1.0, 0.0))
    movers[...] = packet[:, : movers.shape[1]]


def deposit_kernel(
    pairs, rims_before, first, place, own, up1, down1, up2, down2, ambient, t_high, t_low, *refs
):
    rims, refs = refs[:rims_before], refs[rims_before:]
    mesh, rim_high, rim_low = refs[:3]
    total, made = refs[-2:]
    outs = refs[3:-2]
    _, planes, cols, ny = ambient.shape
    rows = cols + RIM
    movers = up2.shape[1]
    count = own.shape[1]
    listed = [2 * pair + parity for pair in pairs for parity in range(2)]

    def decode(ref, start, stop, shift):
        packet = ref[:, start:stop]
        cell = packet[6:7].astype(jnp.int32)
        move = packet[7:8].astype(jnp.int32)
        z_cell = quotient(cell, cols * ny) + planes * (move + shift)
        x_cell = remainder(quotient(cell, ny), cols)
        return packet[0:6], z_cell, x_cell, remainder(cell, ny)

    def joined(pieces):
        return [jnp.concatenate(p, axis=1) if len(p) > 1 else p[0] for p in zip(*pieces)]

    def add_block(pieces, wanted):
        values, z_cell, x_cell, y_cell = joined(pieces)
        width = values.shape[1]
        z_at = lax.broadcasted_iota(jnp.int32, (planes, width), 0)
        w_z = kernel_weight((z_at - z_cell).astype(F32) - values[3:4])
        row = lax.broadcasted_iota(jnp.int32, (rows, width), 0)
        x_at = jnp.where(row < cols + 2, row, jnp.where(row >= rows - 2, row - rows, 4 * rows))
        w_x = kernel_weight((x_at - x_cell).astype(F32) - values[4:5])
        y_at = lax.broadcasted_iota(jnp.int32, (ny, width), 0)
        y_off = remainder(y_at + (ny + ny // 2 - y_cell), ny) - ny // 2
        w_y = kernel_weight(y_off.astype(F32) - values[5:6])
        y_high, y_low = split(w_y)
        right = jnp.concatenate([y_high, y_high, y_low], axis=1)
        at = [listed.index(z) for z in wanted]
        for c in range(3):
            s_z = values[c : c + 1] * w_z
            left = jnp.concatenate([s_z[z : z + 1] * w_x for z in wanted], axis=0)
            l_high, l_low = split(left)
            left = jnp.concatenate([l_high, l_low, l_high], axis=1)
            added = lax.dot_general(
                left, right, (((1,), (1,)), ((), ())), preferred_element_type=F32
            )
            total[c, at[0] : at[-1] + 1] += added.reshape(len(wanted), rows, ny)

    for n, z in enumerate(listed):
        total[:, n, 0:cols] = ambient[:, z]
    total[:, :, cols:rows] = jnp.zeros((3, len(listed), RIM, ny), F32)
    step = 256
    for at in range(0, count, step):
        add_block([decode(own, at, min(at + step, count), 0)], listed)
    add_block([decode(up1, 0, movers, 1), decode(down1, 0, movers, -1)], listed)
    sides = ((up1, up2, 1, (planes - 2, planes - 1)), (down1, down2, -1, (0, 1)))
    for near, far, shift, wanted in sides:
        if not set(wanted) <= set(listed):
            continue
        whole = [decode(near, movers, count, shift), decode(far, 0, movers, 2 * shift)]
        values, z_cell, x_cell, y_cell = joined(whole)
        for at in range(0, count, step):
            to = min(at + step, count)
            block = (values[:, at:to], z_cell[:, at:to], x_cell[:, at:to], y_cell[:, at:to])
            add_block([block], wanted)

    mesh[...] = total[:, :, 0:cols]
    at = 0
    if rims:
        at = rims[0].shape[0]
        rim_high[0:at] = rims[0][...]
        rim_low[0:at] = rims[1][...]
    for n in range(3 * len(listed)):
        c, i = n // len(listed), n % len(listed)
        rim_high[at + 2 * n : at + 2 * n + 2] = total[c, i, cols : cols + 2]
        rim_low[at + 2 * n : at + 2 * n + 2] = total[c, i, rows - 2 : rows]
    groups = [(c, 2 * n) for c in range(3) for n in range(len(pairs))]
    left = jnp.concatenate(
        [jnp.concatenate([total[c, n], total[c, n + 1]], axis=1) for c, n in groups], axis=0
    )
    wide = table_right(left, t_high[...], t_low[...])
    for n in range(len(groups)):
        for g in range(made.shape[0]):
            made[g, :, n * LANES : (n + 1) * LANES] = wide[
                n * rows : (n + 1) * rows, g * LANES : (g + 1) * LANES
            ]
    for d, out in blocks_of(outs, place[1], first):
        out[...] = made[d]


def x_ahead_kernel(sends, first, place, t_high, t_low, *refs):
    held, made = refs[-2:]
    outs, parts = refs[-2 - sends : -2], refs[: -2 - sends]
    gather_blocks(parts, held, place[1], first)
    pencils, rows, width = held.shape
    cols = rows - RIM
    row = lax.broadcasted_iota(jnp.int32, (RIM, width), 0)
    pieces = []
    for h in range(pencils):
        from_low = held[(h - 1) % pencils, cols:rows]
        from_high = held[(h + 1) % pencils, cols:rows]
        pieces.append(held[h, 0:RIM] + jnp.where(row < 2, from_low, 0.0))
        pieces.append(held[h, RIM : cols - RIM])
        pieces.append(held[h, cols - RIM : cols] + jnp.where(row >= RIM - 2, from_high, 0.0))
    both = table_left(t_high[...], t_low[...], jnp.concatenate(pieces, axis=0))
    half = both.shape[0] // 2
    for n in range(width // LANES):
        lanes = slice(n * LANES, (n + 1) * LANES)
        value = both[:half, lanes] - times_i(both[half:, lanes])
        made[:, :, lanes] = value.reshape(made.shape[0], made.shape[1], LANES)
    for d, out in blocks_of(outs, place[0]):
        out[...] = made[d]


def x_back_kernel(sends, first, tables, place, *refs):
    held, made = refs[-2:]
    outs, parts = refs[-2 - sends : -2], refs[: -2 - sends]
    gather_blocks(parts, held, place[0])
    pencils, rows, width = made.shape
    both = table_left(tables[0][...], tables[1][...], held[...].reshape(-1, width))
    half = both.shape[0] // 2
    for n in range(width // LANES):
        lanes = slice(n * LANES, (n + 1) * LANES)
        value = both[:half, lanes] + times_i(both[half:, lanes])
        made[:, :, lanes] = value.reshape(pencils, rows, LANES)
    for d, out in blocks_of(outs, place[1], first):
        out[...] = made[d]


def wave_lanes():
    lane = lane_of()
    return lane < LANES // 2, (lane // (LANES // 4)) % 2 == 0


def roll(values, shift):
    return pltpu.roll(values, shift, 1)


def cross_half(a, b):
    low, _ = wave_lanes()
    half = LANES // 2
    return jnp.where(low, a, roll(b, half)), jnp.where(low, roll(a, half), b)


def cross_quarter(a, b):
    _, first = wave_lanes()
    quarter = LANES // 4
    return (
        jnp.where(first, a, roll(b, quarter)),
        jnp.where(first, roll(a, LANES - quarter), b),
    )


def lanes_at(c, count, i):
    return pl.ds(pl.multiple_of((c * count + i) * LANES, LANES), LANES)


def enter_kernel(pairs, nz, place, *refs):
    parts, data = refs[:-1], refs[-1]
    _, _, _, slabs, tile, _ = data.shape

    def body(c, carry):
        for i, pair in enumerate(pairs):
            lanes = lanes_at(c, len(pairs), i)
            for s, ref in blocks_of(parts, place[0]):
                quad = [ref[q * tile : (q + 1) * tile, lanes] for q in range(4)]
                real0, imag0 = cross_half(quad[0], quad[2])
                real1, imag1 = cross_half(quad[1], quad[3])
                for part, (a, b) in enumerate(((real0, real1), (imag0, imag1))):
                    even, odd = cross_quarter(a, b)
                    data[c, part, 2 * i, s] = even
                    data[c, part, 2 * i + 1, s] = odd
            for parity in range(2):
                at = 2 * i + parity
                line = [(data[c, 0, at, s], data[c, 1, at, s]) for s in range(slabs)]
                for k, v in enumerate(fft(line, -1.0)):
                    v = turned(v, (2 * pair + parity) * k, nz, -1.0)
                    data[c, 0, at, k], data[c, 1, at, k] = v
        return carry

    lax.fori_loop(0, 3, body, 0)


def pass_kernel(before, *refs):
    for source, target in zip(refs[: len(refs) // 2], refs[len(refs) // 2 :]):
        target[...] = source[...]


def leave_kernel(pairs, nz, place, source, *refs):
    outs, data = refs[:-1], refs[-1]
    _, _, _, slabs, tile, _ = source.shape

    def body(c, carry):
        for i, pair in enumerate(pairs):
            lanes = lanes_at(c, len(pairs), i)
            for parity in range(2):
                at = 2 * i + parity
                line = [
                    turned(
                        (source[c, 0, at, k], source[c, 1, at, k]),
                        (2 * pair + parity) * k,
                        nz,
                        1.0,
                    )
                    for k in range(slabs)
                ]
                for s, v in enumerate(fft(line, 1.0)):
                    data[c, 0, at, s], data[c, 1, at, s] = v
            for s, ref in blocks_of(outs, place[0]):
                real0, real1 = cross_quarter(data[c, 0, 2 * i, s], data[c, 0, 2 * i + 1, s])
                imag0, imag1 = cross_quarter(data[c, 1, 2 * i, s], data[c, 1, 2 * i + 1, s])
                quad = [None] * 4
                quad[0], quad[2] = cross_half(real0, imag0)
                quad[1], quad[3] = cross_half(real1, imag1)
                for q in range(4):
                    ref[q * tile : (q + 1) * tile, lanes] = quad[q]
        return carry

    lax.fori_loop(0, 3, body, 0)


def curl_kernel(chunks, nx, ny, place, low_rim, high_rim, *refs):
    sources, outs = refs[: len(chunks)], refs[len(chunks) : 2 * len(chunks)]
    spectrum = refs[-1]
    _, _, nz, tile, _ = spectrum.shape
    slabs = sources[0].shape[3]
    planes = nz // slabs
    modes, half = LANES // 4, LANES // 2
    slab_at, pencil_at = place[0], place[1]
    spot = {}
    for n, chunk in enumerate(chunks):
        for i, pair in enumerate(chunk):
            spot[2 * pair], spot[2 * pair + 1] = (n, 2 * i), (n, 2 * i + 1)

    def across_planes(k, carry):
        for c in range(3):
            line = []
            for l in range(planes):
                n, i = spot[l]
                line.append((sources[n][c, 0, i, k], sources[n][c, 1, i, k]))
            for n, v in enumerate(fft(line, -1.0)):
                spectrum[c, 0, k + slabs * n], spectrum[c, 1, k + slabs * n] = v
        return carry

    reach = 2 * tile
    row = lax.broadcasted_iota(jnp.int32, (tile, LANES), 0)
    lane = lax.broadcasted_iota(jnp.int32, (tile, LANES), 1)
    number = slab_at * reach + (lane // modes) % 2 * tile + row
    ahead = lane < half
    mode = lane % modes + pencil_at * modes
    alone = number == 0
    number = number.astype(F32) * (2.0 * math.pi / nx)
    x_base = jnp.where(ahead, number, jnp.where(alone, math.pi, -number))
    x_trim = jnp.where(ahead, number, jnp.where(alone, 0.0, -number))
    wave_y = mode.astype(F32) * (2.0 * math.pi / ny)
    packed = mode == 0
    x_sq = x_base * x_base
    lateral = x_sq + wave_y * wave_y

    def curl_at(k, with_mirror):
        z_wave = jnp.where(k < nz // 2, k, k - nz).astype(F32) * (2.0 * math.pi / nz)
        z_trim = jnp.where(k == nz // 2, 0.0, z_wave)
        full = lateral + z_wave * z_wave
        empty = full == 0.0
        inverse = jnp.where(empty, 0.0, 1.0 / jnp.where(empty, 1.0, full))
        if with_mirror:
            other = 1.0 / (x_sq + (z_wave * z_wave + math.pi * math.pi))
            mirror = jnp.where(packed, 0.5 * (inverse - other), 0.0)
            inverse = jnp.where(packed, 0.5 * (inverse + other), inverse)
            opposite = lax.rem(nz - k, nz)
        stream = []
        for c in range(3):
            value = [spectrum[c, part, k] * inverse for part in range(2)]
            if with_mirror:
                for part, sign in enumerate((1.0, -1.0)):
                    there = spectrum[c, part, opposite]
                    there = jnp.where(alone, there, roll(there, half))
                    value[part] = value[part] + (mirror * sign) * there
            stream.append(value)
        made = []
        for part in range(2):
            s = [value[part] for value in stream]
            made.append(
                (
                    x_trim * s[2] - wave_y * s[1],
                    wave_y * s[0] - z_trim * s[2],
                    z_trim * s[1] - x_trim * s[0],
                )
            )
        return [(-made[1][c], made[0][c]) for c in range(3)]

    def curl_all(with_mirror):
        def body(k, carry):
            made = [curl_at(k + slabs * n, with_mirror) for n in range(planes)]
            for c in range(3):
                for l, v in enumerate(fft([m[c] for m in made], 1.0)):
                    n, i = spot[l]
                    outs[n][c, 0, i, k], outs[n][c, 1, i, k] = v
            return carry

        lax.fori_loop(0, slabs, body, 0)

    lax.fori_loop(0, slabs, across_planes, 0)

    @pl.when(pencil_at == 0)
    def _():
        curl_all(True)

    @pl.when(pencil_at != 0)
    def _():
        curl_all(False)


def planes_of(held, pairs, tables):
    pencils, rows, _ = held.shape
    groups = [(c, pair) for c in range(3) for pair in pairs]
    left = jnp.concatenate(
        [
            jnp.concatenate(
                [held[h, :, n * LANES : (n + 1) * LANES] for h in range(pencils)], axis=1
            )
            for n in range(len(groups))
        ],
        axis=0,
    )
    ny = tables[0].shape[1] // 2
    wide = table_right(left, tables[0][...], tables[1][...])
    made = {}
    for n, (c, pair) in enumerate(groups):
        for parity in range(2):
            made[c, 2 * pair + parity] = wide[
                n * rows : (n + 1) * rows, parity * ny : (parity + 1) * ny
            ]
    return made


def hold(tall, c, n, value):
    rows = value.shape[0]
    tall[c, n, RIM : RIM + rows] = value
    tall[c, n, 0:RIM] = value[rows - RIM : rows]


def edge_kernel(pairs, tables, place, *refs):
    tall, first, last, held = refs[-4:]
    gather_blocks(refs[:-4], held, place[1])
    listed = [2 * pair + parity for pair in pairs for parity in range(2)]
    cols = first.shape[1]
    values = planes_of(held, pairs, tables)
    for c in range(3):
        for n, z in enumerate(listed):
            hold(tall, c, n, values[c, z])
        first[c] = values[c, listed[0]][0:cols]
        last[c] = values[c, listed[-1]][0:cols]


def where_planes(chunks):
    spot = {}
    for n, chunk in enumerate(chunks):
        for i, pair in enumerate(chunk):
            spot[2 * pair], spot[2 * pair + 1] = (n, 2 * i), (n, 2 * i + 1)
    return spot


def rim_start(meshes, which, c, i):
    before = 6 * meshes[1].shape[1] if which == 0 else 0
    return before + 2 * (c * meshes[which].shape[1] + i)


def stretch_plane(out, mesh, rims, at, rows_of, above, below):
    cols, ny = out[0].shape
    low_rim, high_rim = rims
    for c in range(3):
        out[c][...] = mesh[c][...]
        out[c][0:2] += low_rim[at[c] : at[c] + 2]
        out[c][cols - 2 : cols] += high_rim[at[c] : at[c] + 2]
    omega = [ref[...] for ref in out]
    for c in range(3):
        value = rows_of(c, RIM)
        along_z = (above(c) - below(c)) * 0.5
        along_x = (rows_of(c, RIM + 1) - rows_of(c, RIM - 1)) * 0.5
        along_y = (pltpu.roll(value, ny - 1, 1) - pltpu.roll(value, 1, 1)) * 0.5
        stretch = omega[0] * along_z + omega[1] * along_x + omega[2] * along_y
        out[c][...] = omega[c] + TIME_STEP * stretch


def ends_kernel(_, __, edges, before, after, low_rim, high_rim, *refs):
    meshes, vorticity, out, sems = refs[:-4], refs[-3], refs[-2], refs[-1]
    cols = before.shape[1]
    size = edges.shape[1]
    copies = []

    def rows_of(i):
        return lambda c, start=RIM: edges[c, i, start : start + cols]

    for n, i in enumerate((0, size - 1)):
        stretch_plane(
            [out.at[c, n] for c in range(3)],
            [meshes[0].at[c, i] for c in range(3)],
            (low_rim, high_rim),
            [rim_start(meshes, 0, c, i) for c in range(3)],
            rows_of(i),
            (lambda c: after[c]) if i else rows_of(1),
            rows_of(size - 2) if i else (lambda c: before[c]),
        )
        copies.append(
            pltpu.make_async_copy(
                out.at[:, n], vorticity.at[:, n * (vorticity.shape[1] - 1)], sems.at[n]
            )
        )
        copies[-1].start()
    for copy in copies:
        copy.wait()


def stretch_kernel(chunks, tables, place, edges, low_rim, high_rim, *refs):
    meshes, refs = refs[:2], refs[2:]
    velocity, vorticity, held, inner, omega, sems = refs[-6:]
    _, planes, cols, ny = velocity.shape
    spot = where_planes(chunks)
    talls = (edges, inner)
    sent = []

    def send(source, target):
        sent.append(pltpu.make_async_copy(source, target, sems.at[len(sent)]))
        sent[-1].start()

    def rows_of(z):
        n, i = spot[z]
        return lambda c, start=RIM: talls[n][c, i, start : start + cols]

    def send_velocity(which):
        for z in range(planes):
            n, i = spot[z]
            if n == which:
                send(talls[n].at[:, i, pl.ds(RIM, cols)], velocity.at[:, z])

    send_velocity(0)
    gather_blocks(refs[:-6], held, place[1], "far")
    for (c, z), value in planes_of(held, chunks[1], tables).items():
        hold(inner, c, spot[z][1], value)
    send_velocity(1)
    for z in range(1, planes - 1):
        which, i = spot[z]
        stretch_plane(
            [omega.at[c, z] for c in range(3)],
            [meshes[which].at[c, i] for c in range(3)],
            (low_rim, high_rim),
            [rim_start(meshes, which, c, i) for c in range(3)],
            rows_of(z),
            rows_of(z + 1),
            rows_of(z - 1),
        )
        send(omega.at[:, z], vorticity.at[:, z])
    for copy in sent:
        copy.wait()


VM = pl.BlockSpec(memory_space=pltpu.VMEM)
SM = pl.BlockSpec(memory_space=pltpu.SMEM)
AN = pl.BlockSpec(memory_space=pl.ANY)
HB = pl.BlockSpec(memory_space=pltpu.HBM)


def kept(values):
    return pltpu.with_memory_space_constraint(values, pltpu.HBM)


def loaded(kernel):
    def run(place, t_high, t_low, *refs):
        kernel((t_high, t_low), place, *refs)

    return run


def call(kernel, ins, outs, scratch=(), sems=0, micros=2.0, moved=None, aliases=None):
    extra = [pltpu.SemaphoreType.DMA((sems,))] if sems else []
    return pl.pallas_call(
        kernel,
        out_shape=[jax.ShapeDtypeStruct(shape, F32) for _, shape in outs],
        in_specs=[spec for spec, _ in ins],
        out_specs=[spec for spec, _ in outs],
        scratch_shapes=[pltpu.VMEM(shape, kind) for shape, kind in scratch] + extra,
        compiler_params=pltpu.CompilerParams(vmem_limit_bytes=VMEM),
        input_output_aliases=aliases or {},
        cost_estimate=pl.CostEstimate(
            flops=int(micros * 1.0e9),
            bytes_accessed=int(micros * 3.0e6) if moved is None else moved,
            transcendentals=0,
        ),
    )(*[value for _, value in ins])


def ring(axis, step):
    count = lax.axis_size(axis)
    return [(i, (i + step) % count) for i in range(count)]


def spread(axis):
    count = lax.axis_size(axis)
    return count <= 8 and count & (count - 1) == 0


def sent_shapes(axis, rows, width, whole=False):
    count = lax.axis_size(axis)
    return [(count, rows, width)] if whole or not spread(axis) else [(rows, width)] * count


def exchange(blocks, axis, start=0, first=None):
    if not spread(axis):
        return [lax.all_to_all(blocks[0], axis, split_axis=0, concat_axis=0, tiled=True)]
    count = lax.axis_size(axis)
    return [
        lax.ppermute(block, axis, [(i, i ^ k) for i in range(count)]) if k else block
        for k, block in zip(offset_order(count, first)[start:], blocks)
    ]


def on_device(strength, offsets, cell_index, migrate_count, ambient):
    _, planes, cols, ny = ambient.shape
    slabs, pencils = lax.axis_size("gz"), lax.axis_size("gx")
    nx, nz, rows = cols * pencils, planes * slabs, cols + RIM
    count = strength.shape[1]
    pair_count = planes // 2
    chunks = ((0, pair_count - 1), tuple(range(1, pair_count - 1)))
    widths = [3 * len(c) * LANES for c in chunks]
    block = nx // slabs

    y_ahead, y_back = [split_table(t) for t in y_tables(ny, pencils, 1.0 / (float(nx) * ny * nz))]
    x_ahead, x_back = [split_table(t) for t in x_tables(nx, cols, pencils, slabs)]
    place = jnp.stack([lax.axis_index("gz"), lax.axis_index("gx")]).astype(jnp.int32)
    here = (SM, place)

    packet, movers = call(
        packet_kernel,
        [
            (HB, kept(migrate_count.reshape(1, 2))),
            (HB, kept(strength)),
            (HB, kept(offsets)),
            (HB, kept(cell_index.reshape(1, count))),
        ],
        [(VM, (8, count)), (VM, (8, 2 * MIG))],
        [((1, 2), jnp.int32), ((1, count), jnp.int32)],
        sems=4,
        micros=1.0,
        moved=1000,
    )
    up1 = lax.ppermute(packet, "gz", ring("gz", -1))
    down1 = lax.ppermute(packet, "gz", ring("gz", 1))
    up2 = lax.ppermute(movers, "gz", ring("gz", -2))
    down2 = lax.ppermute(movers, "gz", ring("gz", 2))

    meshes, rims, parts = [None, None], [], [None, None]
    for n in (1, 0):
        chunk, width = chunks[n], widths[n]
        size = 2 * len(chunk)
        rim = (6 * size + (rims[0].shape[0] if rims else 0), ny)
        mesh, rim_high, rim_low, *part = call(
            functools.partial(deposit_kernel, chunk, len(rims), None if n else "near"),
            [here]
            + [(VM, value) for value in (packet, up1, down1, up2, down2)]
            + [(VM, ambient), (VM, y_ahead[0]), (VM, y_ahead[1])]
            + [(VM, value) for value in rims],
            [(VM, (3, size, cols, ny)), (VM, rim), (VM, rim)]
            + [(VM, shape) for shape in sent_shapes("gx", rows, width)],
            [((3, size, rows, ny), F32), ((pencils, rows, width), F32)],
            micros=5.0,
        )
        meshes[n] = mesh
        rims = [rim_high, rim_low]
        parts[n] = exchange(part, "gx", first="near" if n == 0 else None)
    low_rim = lax.ppermute(rims[0], "gx", ring("gx", 1))
    high_rim = lax.ppermute(rims[1], "gx", ring("gx", -1))

    tile = max(1, block // 4)
    data = [None, None]
    for n in (1, 0):
        chunk, part, width = chunks[n], parts[n], widths[n]
        shapes = sent_shapes("gz", block, width)
        part = call(
            functools.partial(x_ahead_kernel, len(shapes), None if n else "near"),
            [here, (VM, x_ahead[0]), (VM, x_ahead[1])] + [(VM, p) for p in part],
            [(VM, shape) for shape in shapes],
            [((pencils, rows, width), F32), ((slabs, block, width), F32)],
        )
        (entered,) = call(
            functools.partial(enter_kernel, chunk, nz),
            [here] + [(VM, p) for p in exchange(part, "gz")],
            [(VM, (3, 2, 2 * len(chunk), slabs, tile, LANES))],
        )
        data[n] = entered
    data = call(
        functools.partial(curl_kernel, chunks, nx, ny),
        [here, (VM, low_rim), (VM, high_rim)] + [(VM, d) for d in data],
        [(VM, d.shape) for d in data],
        [((3, 2, nz, tile, LANES), F32)],
        micros=5.0,
    )
    plane = (3, cols, ny)
    tables = [(VM, t) for t in y_back]
    tall = [(3, 2 * len(chunk), cols + 2 * RIM, ny) for chunk in chunks]
    left = [
        call(
            functools.partial(leave_kernel, chunk, nz),
            [here, (VM, source)],
            [(VM, shape) for shape in sent_shapes("gz", block, width)],
            [(source.shape, F32)],
        )
        for chunk, source, width in zip(chunks, data, widths)
    ]

    def back(part, width, first=None):
        shapes = sent_shapes("gx", rows, width)
        part = call(
            loaded(functools.partial(x_back_kernel, len(shapes), first)),
            [here]
            + [(VM, t) for t in x_back]
            + [(VM, p) for p in part],
            [(VM, shape) for shape in shapes],
            [((slabs, block, width), F32), ((pencils, rows, width), F32)],
        )
        return exchange(part, "gx", first=first)

    early = max(1, len(left[1]) - LATE)
    second = exchange(left[1][:early], "gz")
    parts = [back(exchange(left[0], "gz"), widths[0])]
    edges, first, last = call(
        loaded(functools.partial(edge_kernel, chunks[0])),
        [here] + tables + [(VM, p) for p in parts[0]],
        [(VM, tall[0]), (VM, plane), (VM, plane)],
        [((pencils, rows, widths[0]), F32)],
    )
    if early < len(left[1]):
        late = call(
            pass_kernel,
            [(AN, parts[0][0])] + [(VM, p) for p in left[1][early:]],
            [(VM, p.shape) for p in left[1][early:]],
            micros=0.3,
        )
        second += exchange(late, "gz", early)
    parts.append(back(second, widths[1], "far"))
    after = lax.ppermute(first, "gz", ring("gz", -1))
    before = lax.ppermute(last, "gz", ring("gz", 1))
    velocity, vorticity = call(
        loaded(functools.partial(stretch_kernel, chunks)),
        [here]
        + tables
        + [(VM, v) for v in (edges, low_rim, high_rim, *meshes)]
        + [(VM, p) for p in parts[1]],
        [(AN, ambient.shape), (AN, ambient.shape)],
        [
            ((pencils, rows, widths[1]), F32),
            (tall[1], F32),
            ((3, planes, cols, ny), F32),
        ],
        sems=2 * planes,
        micros=4.0,
    )
    return tuple(
        call(
            ends_kernel,
            [(AN, velocity), (AN, vorticity)]
            + [(VM, v) for v in (edges, before, after, low_rim, high_rim, *meshes)],
            [(AN, ambient.shape), (AN, ambient.shape)],
            [((3, 2, cols, ny), F32)],
            sems=2,
            micros=1.0,
            aliases={0: 0, 1: 1},
        )
    )


def solution(mesh):
    placed = (
        P(None, ("gz", "gx")),
        P(None, ("gz", "gx")),
        P(("gz", "gx")),
        P("gz", "gx", None),
        P(None, "gz", "gx", None),
    )
    return jax.shard_map(
        on_device,
        mesh=mesh,
        in_specs=placed,
        out_specs=(P(None, "gz", "gx", None), P(None, "gz", "gx", None)),
        check_vma=False,
    )
```

```python
import functools
import math

import jax
import jax.numpy as jnp
import ml_dtypes
import numpy as np
from jax import lax
from jax.experimental import pallas as pl
from jax.experimental.pallas import tpu as pltpu
from jax.sharding import PartitionSpec as P

MIG = 64
LANES = 128
RIM = 8
LATE = 3
TIME_STEP = 0.25
VMEM = 24 * 1024 * 1024
F32 = jnp.float32
BF16 = jnp.bfloat16


def split_table(table):
    high = table.astype(np.float32).astype(ml_dtypes.bfloat16)
    low = (table - high.astype(np.float64)).astype(np.float32).astype(ml_dtypes.bfloat16)
    return high, low


def angles(rows, columns, extent):
    return 2.0 * np.pi * (np.multiply.outer(rows, columns) % extent) / extent


def y_tables(ny, pencils, scale):
    modes = ny // (2 * pencils)
    position = np.arange(ny)
    angle = angles(position, np.arange(ny // 2), ny)
    real, imag = np.cos(angle), -np.sin(angle)
    imag[:, 0] = 1.0 - 2.0 * (position % 2)
    weight = np.where(np.arange(ny // 2) == 0, 1.0, 2.0) * scale
    ahead = np.zeros((2, ny, pencils, 2, 2, modes))
    back = np.zeros((pencils, 2, 2, modes, 2, ny))
    for parity in range(2):
        for part, values in enumerate((real, imag)):
            ahead[parity, :, :, part, parity] = values.reshape(ny, pencils, modes)
            back[:, part, parity, :, parity] = (values * weight).T.reshape(pencils, modes, ny)
    return ahead.reshape(2 * ny, -1), back.reshape(-1, 2 * ny)


def wave_order(nx, slabs):
    half = nx // 2
    ahead = np.arange(half).reshape(slabs, 1, half // slabs)
    behind = np.where(ahead == 0, half, (nx - ahead) % nx)
    return np.concatenate([ahead, behind], axis=1).reshape(-1)


def x_tables(nx, cols, pencils, slabs):
    order = wave_order(nx, slabs)
    angle = angles(order, np.arange(nx), nx)
    ahead = np.concatenate([np.cos(angle), np.sin(angle)], axis=0)
    row = np.arange(cols + RIM)
    offset = np.where(row <= cols, row, -1)
    used = ((row <= cols) | (row == cols + RIM - 1)).astype(np.float64)
    place = (np.arange(pencils)[:, None] * cols + offset[None, :]) % nx
    angle = angles(place.reshape(-1), order, nx)
    mask = np.tile(used, pencils)[:, None]
    back = np.concatenate([np.cos(angle) * mask, np.sin(angle) * mask], axis=0)
    return ahead, back


def split(values):
    high = values.astype(BF16)
    return high, (values - high.astype(F32)).astype(BF16)


def dot(left, right):
    return jnp.dot(left, right, preferred_element_type=F32)


def table_left(high, low, values):
    v_high, v_low = split(values)
    return dot(high, v_high) + (dot(high, v_low) + dot(low, v_high))


def table_right(values, high, low):
    v_high, v_low = split(values)
    return dot(v_high, high) + (dot(v_low, high) + dot(v_high, low))


def lane_of():
    return lax.broadcasted_iota(jnp.int32, (1, LANES), 1)


def times_i(values):
    half = LANES // 2
    sign = jnp.where(lane_of() < half, -1.0, 1.0).astype(F32)
    return pltpu.roll(values, half, 1) * sign


def kernel_weight(distance):
    radius = jnp.abs(distance)
    near = 1.0 + radius * radius * (1.5 * radius - 2.5)
    rest = jnp.maximum(2.0 - radius, 0.0)
    return jnp.where(radius < 1.0, near, 0.5 * rest * rest * (1.0 - radius))


def quotient(values, size):
    if size & (size - 1):
        return lax.div(values, size)
    return lax.shift_right_logical(values, size.bit_length() - 1)


def remainder(values, size):
    if size & (size - 1):
        return lax.rem(values, size)
    return values & (size - 1)


def turned(value, wave, extent, sign):
    wave = wave % extent
    real, imag = value
    if wave == 0:
        return value
    if 2 * wave == extent:
        return -real, -imag
    if 4 * wave == extent:
        return (-imag, real) if sign > 0 else (imag, -real)
    if 4 * wave == 3 * extent:
        return (imag, -real) if sign > 0 else (-imag, real)
    a = math.cos(2.0 * math.pi * wave / extent)
    b = sign * math.sin(2.0 * math.pi * wave / extent)
    return real * a - imag * b, real * b + imag * a


def fft(values, sign):
    count = len(values)
    if count == 1:
        return values
    even, odd = fft(values[::2], sign), fft(values[1::2], sign)
    odd = [turned(v, k, count, sign) for k, v in enumerate(odd)]
    plus = [(a[0] + b[0], a[1] + b[1]) for a, b in zip(even, odd)]
    minus = [(a[0] - b[0], a[1] - b[1]) for a, b in zip(even, odd)]
    return plus + minus


def offset_order(count, first=None):
    far, near = list(range(count // 2, count)), list(range(1, count // 2))
    if first == "near":
        return [0] + near + far
    if count == 4 and first is None:
        return [0, 2, 1, 3]
    if first == "far":
        return [0] + far + near
    order, last = [0], near[1:]
    near = near[:1]
    while far or near:
        order += far[:2] + near[:1]
        far, near = far[2:], near[1:]
    return order + last


def blocks_of(refs, at, first=None):
    if len(refs) == 1:
        return [(d, refs[0].at[d]) for d in range(refs[0].shape[0])]
    return [(at ^ k, ref) for k, ref in zip(offset_order(len(refs), first), refs)]


def gather_blocks(refs, held, at, first=None):
    for d, ref in blocks_of(refs, at, first):
        held[d] = ref[...]


def packet_kernel(
    counts, strength, offsets, cells, packet, movers, near_counts, near_cells, sems
):
    copies = [
        pltpu.make_async_copy(counts, near_counts, sems.at[0]),
        pltpu.make_async_copy(cells, near_cells, sems.at[1]),
        pltpu.make_async_copy(strength, packet.at[pl.ds(0, 3)], sems.at[2]),
        pltpu.make_async_copy(offsets, packet.at[pl.ds(3, 3)], sems.at[3]),
    ]
    for copy in copies:
        copy.start()
    for copy in copies:
        copy.wait()
    slot = lax.broadcasted_iota(jnp.int32, (1, packet.shape[1]), 1)
    up = near_counts[0:1, 0:1]
    both = up + near_counts[0:1, 1:2]
    packet[6:7] = near_cells[...].astype(F32)
    packet[7:8] = jnp.where(slot < up, 1.0, jnp.where(slot < both, -1.0, 0.0))
    movers[...] = packet[:, : movers.shape[1]]


def deposit_kernel(
    pairs, rims_before, first, place, own, up1, down1, up2, down2, ambient, t_high, t_low, *refs
):
    rims, refs = refs[:rims_before], refs[rims_before:]
    mesh, rim_high, rim_low = refs[:3]
    total, made = refs[-2:]
    outs = refs[3:-2]
    _, planes, cols, ny = ambient.shape
    rows = cols + RIM
    movers = up2.shape[1]
    count = own.shape[1]
    listed = [2 * pair + parity for pair in pairs for parity in range(2)]

    def decode(ref, start, stop, shift):
        packet = ref[:, start:stop]
        cell = packet[6:7].astype(jnp.int32)
        move = packet[7:8].astype(jnp.int32)
        z_cell = quotient(cell, cols * ny) + planes * (move + shift)
        x_cell = remainder(quotient(cell, ny), cols)
        return packet[0:6], z_cell, x_cell, remainder(cell, ny)

    def joined(pieces):
        return [jnp.concatenate(p, axis=1) if len(p) > 1 else p[0] for p in zip(*pieces)]

    def add_block(pieces, wanted):
        values, z_cell, x_cell, y_cell = joined(pieces)
        width = values.shape[1]
        z_at = lax.broadcasted_iota(jnp.int32, (planes, width), 0)
        w_z = kernel_weight((z_at - z_cell).astype(F32) - values[3:4])
        row = lax.broadcasted_iota(jnp.int32, (rows, width), 0)
        x_at = jnp.where(row < cols + 2, row, jnp.where(row >= rows - 2, row - rows, 4 * rows))
        w_x = kernel_weight((x_at - x_cell).astype(F32) - values[4:5])
        y_at = lax.broadcasted_iota(jnp.int32, (ny, width), 0)
        y_off = remainder(y_at + (ny + ny // 2 - y_cell), ny) - ny // 2
        w_y = kernel_weight(y_off.astype(F32) - values[5:6])
        y_high, y_low = split(w_y)
        right = jnp.concatenate([y_high, y_high, y_low], axis=1)
        at = [listed.index(z) for z in wanted]
        for c in range(3):
            s_z = values[c : c + 1] * w_z
            left = jnp.concatenate([s_z[z : z + 1] * w_x for z in wanted], axis=0)
            l_high, l_low = split(left)
            left = jnp.concatenate([l_high, l_low, l_high], axis=1)
            added = lax.dot_general(
                left, right, (((1,), (1,)), ((), ())), preferred_element_type=F32
            )
            total[c, at[0] : at[-1] + 1] += added.reshape(len(wanted), rows, ny)

    for n, z in enumerate(listed):
        total[:, n, 0:cols] = ambient[:, z]
    total[:, :, cols:rows] = jnp.zeros((3, len(listed), RIM, ny), F32)
    step = 256
    for at in range(0, count, step):
        add_block([decode(own, at, min(at + step, count), 0)], listed)
    add_block([decode(up1, 0, movers, 1), decode(down1, 0, movers, -1)], listed)
    sides = ((up1, up2, 1, (planes - 2, planes - 1)), (down1, down2, -1, (0, 1)))
    for near, far, shift, wanted in sides:
        if not set(wanted) <= set(listed):
            continue
        whole = [decode(near, movers, count, shift), decode(far, 0, movers, 2 * shift)]
        values, z_cell, x_cell, y_cell = joined(whole)
        for at in range(0, count, step):
            to = min(at + step, count)
            block = (values[:, at:to], z_cell[:, at:to], x_cell[:, at:to], y_cell[:, at:to])
            add_block([block], wanted)

    mesh[...] = total[:, :, 0:cols]
    at = 0
    if rims:
        at = rims[0].shape[0]
        rim_high[0:at] = rims[0][...]
        rim_low[0:at] = rims[1][...]
    for n in range(3 * len(listed)):
        c, i = n // len(listed), n % len(listed)
        rim_high[at + 2 * n : at + 2 * n + 2] = total[c, i, cols : cols + 2]
        rim_low[at + 2 * n : at + 2 * n + 2] = total[c, i, rows - 2 : rows]
    groups = [(c, 2 * n) for c in range(3) for n in range(len(pairs))]
    left = jnp.concatenate(
        [jnp.concatenate([total[c, n], total[c, n + 1]], axis=1) for c, n in groups], axis=0
    )
    wide = table_right(left, t_high[...], t_low[...])
    for n in range(len(groups)):
        for g in range(made.shape[0]):
            made[g, :, n * LANES : (n + 1) * LANES] = wide[
                n * rows : (n + 1) * rows, g * LANES : (g + 1) * LANES
            ]
    for d, out in blocks_of(outs, place[1], first):
        out[...] = made[d]


def x_ahead_kernel(sends, first, place, t_high, t_low, *refs):
    held, made = refs[-2:]
    outs, parts = refs[-2 - sends : -2], refs[: -2 - sends]
    gather_blocks(parts, held, place[1], first)
    pencils, rows, width = held.shape
    cols = rows - RIM
    row = lax.broadcasted_iota(jnp.int32, (RIM, width), 0)
    pieces = []
    for h in range(pencils):
        from_low = held[(h - 1) % pencils, cols:rows]
        from_high = held[(h + 1) % pencils, cols:rows]
        pieces.append(held[h, 0:RIM] + jnp.where(row < 2, from_low, 0.0))
        pieces.append(held[h, RIM : cols - RIM])
        pieces.append(held[h, cols - RIM : cols] + jnp.where(row >= RIM - 2, from_high, 0.0))
    both = table_left(t_high[...], t_low[...], jnp.concatenate(pieces, axis=0))
    half = both.shape[0] // 2
    for n in range(width // LANES):
        lanes = slice(n * LANES, (n + 1) * LANES)
        value = both[:half, lanes] - times_i(both[half:, lanes])
        made[:, :, lanes] = value.reshape(made.shape[0], made.shape[1], LANES)
    for d, out in blocks_of(outs, place[0]):
        out[...] = made[d]


def x_back_kernel(sends, first, tables, place, *refs):
    held, made = refs[-2:]
    outs, parts = refs[-2 - sends : -2], refs[: -2 - sends]
    gather_blocks(parts, held, place[0])
    pencils, rows, width = made.shape
    both = table_left(tables[0][...], tables[1][...], held[...].reshape(-1, width))
    half = both.shape[0] // 2
    for n in range(width // LANES):
        lanes = slice(n * LANES, (n + 1) * LANES)
        value = both[:half, lanes] + times_i(both[half:, lanes])
        made[:, :, lanes] = value.reshape(pencils, rows, LANES)
    for d, out in blocks_of(outs, place[1], first):
        out[...] = made[d]


def wave_lanes():
    lane = lane_of()
    return lane < LANES // 2, (lane // (LANES // 4)) % 2 == 0


def roll(values, shift):
    return pltpu.roll(values, shift, 1)


def cross_half(a, b):
    low, _ = wave_lanes()
    half = LANES // 2
    return jnp.where(low, a, roll(b, half)), jnp.where(low, roll(a, half), b)


def cross_quarter(a, b):
    _, first = wave_lanes()
    quarter = LANES // 4
    return (
        jnp.where(first, a, roll(b, quarter)),
        jnp.where(first, roll(a, LANES - quarter), b),
    )


def lanes_at(c, count, i):
    return pl.ds(pl.multiple_of((c * count + i) * LANES, LANES), LANES)


def enter_kernel(pairs, nz, place, *refs):
    parts, data = refs[:-1], refs[-1]
    _, _, _, slabs, tile, _ = data.shape

    def body(c, carry):
        for i, pair in enumerate(pairs):
            lanes = lanes_at(c, len(pairs), i)
            for s, ref in blocks_of(parts, place[0]):
                quad = [ref[q * tile : (q + 1) * tile, lanes] for q in range(4)]
                real0, imag0 = cross_half(quad[0], quad[2])
                real1, imag1 = cross_half(quad[1], quad[3])
                for part, (a, b) in enumerate(((real0, real1), (imag0, imag1))):
                    even, odd = cross_quarter(a, b)
                    data[c, part, 2 * i, s] = even
                    data[c, part, 2 * i + 1, s] = odd
            for parity in range(2):
                at = 2 * i + parity
                line = [(data[c, 0, at, s], data[c, 1, at, s]) for s in range(slabs)]
                for k, v in enumerate(fft(line, -1.0)):
                    v = turned(v, (2 * pair + parity) * k, nz, -1.0)
                    data[c, 0, at, k], data[c, 1, at, k] = v
        return carry

    lax.fori_loop(0, 3, body, 0)


def pass_kernel(before, *refs):
    for source, target in zip(refs[: len(refs) // 2], refs[len(refs) // 2 :]):
        target[...] = source[...]


def leave_kernel(pairs, nz, place, source, *refs):
    outs, data = refs[:-1], refs[-1]
    _, _, _, slabs, tile, _ = source.shape

    def body(c, carry):
        for i, pair in enumerate(pairs):
            lanes = lanes_at(c, len(pairs), i)
            for parity in range(2):
                at = 2 * i + parity
                line = [
                    turned(
                        (source[c, 0, at, k], source[c, 1, at, k]),
                        (2 * pair + parity) * k,
                        nz,
                        1.0,
                    )
                    for k in range(slabs)
                ]
                for s, v in enumerate(fft(line, 1.0)):
                    data[c, 0, at, s], data[c, 1, at, s] = v
            for s, ref in blocks_of(outs, place[0]):
                real0, real1 = cross_quarter(data[c, 0, 2 * i, s], data[c, 0, 2 * i + 1, s])
                imag0, imag1 = cross_quarter(data[c, 1, 2 * i, s], data[c, 1, 2 * i + 1, s])
                quad = [None] * 4
                quad[0], quad[2] = cross_half(real0, imag0)
                quad[1], quad[3] = cross_half(real1, imag1)
                for q in range(4):
                    ref[q * tile : (q + 1) * tile, lanes] = quad[q]
        return carry

    lax.fori_loop(0, 3, body, 0)


def curl_kernel(chunks, nx, ny, place, low_rim, high_rim, *refs):
    sources, outs = refs[: len(chunks)], refs[len(chunks) : 2 * len(chunks)]
    spectrum = refs[-1]
    _, _, nz, tile, _ = spectrum.shape
    slabs = sources[0].shape[3]
    planes = nz // slabs
    modes, half = LANES // 4, LANES // 2
    slab_at, pencil_at = place[0], place[1]
    spot = {}
    for n, chunk in enumerate(chunks):
        for i, pair in enumerate(chunk):
            spot[2 * pair], spot[2 * pair + 1] = (n, 2 * i), (n, 2 * i + 1)

    def across_planes(k, carry):
        for c in range(3):
            line = []
            for l in range(planes):
                n, i = spot[l]
                line.append((sources[n][c, 0, i, k], sources[n][c, 1, i, k]))
            for n, v in enumerate(fft(line, -1.0)):
                spectrum[c, 0, k + slabs * n], spectrum[c, 1, k + slabs * n] = v
        return carry

    reach = 2 * tile
    row = lax.broadcasted_iota(jnp.int32, (tile, LANES), 0)
    lane = lax.broadcasted_iota(jnp.int32, (tile, LANES), 1)
    number = slab_at * reach + (lane // modes) % 2 * tile + row
    ahead = lane < half
    mode = lane % modes + pencil_at * modes
    alone = number == 0
    number = number.astype(F32) * (2.0 * math.pi / nx)
    x_base = jnp.where(ahead, number, jnp.where(alone, math.pi, -number))
    x_trim = jnp.where(ahead, number, jnp.where(alone, 0.0, -number))
    wave_y = mode.astype(F32) * (2.0 * math.pi / ny)
    packed = mode == 0
    x_sq = x_base * x_base
    lateral = x_sq + wave_y * wave_y

    def curl_at(k, with_mirror):
        z_wave = jnp.where(k < nz // 2, k, k - nz).astype(F32) * (2.0 * math.pi / nz)
        z_trim = jnp.where(k == nz // 2, 0.0, z_wave)
        full = lateral + z_wave * z_wave
        empty = full == 0.0
        inverse = jnp.where(empty, 0.0, 1.0 / jnp.where(empty, 1.0, full))
        if with_mirror:
            other = 1.0 / (x_sq + (z_wave * z_wave + math.pi * math.pi))
            mirror = jnp.where(packed, 0.5 * (inverse - other), 0.0)
            inverse = jnp.where(packed, 0.5 * (inverse + other), inverse)
            opposite = lax.rem(nz - k, nz)
        stream = []
        for c in range(3):
            value = [spectrum[c, part, k] * inverse for part in range(2)]
            if with_mirror:
                for part, sign in enumerate((1.0, -1.0)):
                    there = spectrum[c, part, opposite]
                    there = jnp.where(alone, there, roll(there, half))
                    value[part] = value[part] + (mirror * sign) * there
            stream.append(value)
        made = []
        for part in range(2):
            s = [value[part] for value in stream]
            made.append(
                (
                    x_trim * s[2] - wave_y * s[1],
                    wave_y * s[0] - z_trim * s[2],
                    z_trim * s[1] - x_trim * s[0],
                )
            )
        return [(-made[1][c], made[0][c]) for c in range(3)]

    def curl_all(with_mirror):
        def body(k, carry):
            made = [curl_at(k + slabs * n, with_mirror) for n in range(planes)]
            for c in range(3):
                for l, v in enumerate(fft([m[c] for m in made], 1.0)):
                    n, i = spot[l]
                    outs[n][c, 0, i, k], outs[n][c, 1, i, k] = v
            return carry

        lax.fori_loop(0, slabs, body, 0)

    lax.fori_loop(0, slabs, across_planes, 0)

    @pl.when(pencil_at == 0)
    def _():
        curl_all(True)

    @pl.when(pencil_at != 0)
    def _():
        curl_all(False)


def planes_of(held, pairs, tables):
    pencils, rows, _ = held.shape
    groups = [(c, pair) for c in range(3) for pair in pairs]
    left = jnp.concatenate(
        [
            jnp.concatenate(
                [held[h, :, n * LANES : (n + 1) * LANES] for h in range(pencils)], axis=1
            )
            for n in range(len(groups))
        ],
        axis=0,
    )
    ny = tables[0].shape[1] // 2
    wide = table_right(left, tables[0][...], tables[1][...])
    made = {}
    for n, (c, pair) in enumerate(groups):
        for parity in range(2):
            made[c, 2 * pair + parity] = wide[
                n * rows : (n + 1) * rows, parity * ny : (parity + 1) * ny
            ]
    return made


def hold(tall, c, n, value):
    rows = value.shape[0]
    tall[c, n, RIM : RIM + rows] = value
    tall[c, n, 0:RIM] = value[rows - RIM : rows]


def edge_kernel(pairs, tables, place, *refs):
    tall, first, last, held = refs[-4:]
    gather_blocks(refs[:-4], held, place[1])
    listed = [2 * pair + parity for pair in pairs for parity in range(2)]
    cols = first.shape[1]
    values = planes_of(held, pairs, tables)
    for c in range(3):
        for n, z in enumerate(listed):
            hold(tall, c, n, values[c, z])
        first[c] = values[c, listed[0]][0:cols]
        last[c] = values[c, listed[-1]][0:cols]


def where_planes(chunks):
    spot = {}
    for n, chunk in enumerate(chunks):
        for i, pair in enumerate(chunk):
            spot[2 * pair], spot[2 * pair + 1] = (n, 2 * i), (n, 2 * i + 1)
    return spot


def rim_start(meshes, which, c, i):
    before = 6 * meshes[1].shape[1] if which == 0 else 0
    return before + 2 * (c * meshes[which].shape[1] + i)


def stretch_plane(out, mesh, rims, at, rows_of, above, below):
    cols, ny = out[0].shape
    low_rim, high_rim = rims
    for c in range(3):
        out[c][...] = mesh[c][...]
        out[c][0:2] += low_rim[at[c] : at[c] + 2]
        out[c][cols - 2 : cols] += high_rim[at[c] : at[c] + 2]
    omega = [ref[...] for ref in out]
    for c in range(3):
        value = rows_of(c, RIM)
        along_z = (above(c) - below(c)) * 0.5
        along_x = (rows_of(c, RIM + 1) - rows_of(c, RIM - 1)) * 0.5
        along_y = (pltpu.roll(value, ny - 1, 1) - pltpu.roll(value, 1, 1)) * 0.5
        stretch = omega[0] * along_z + omega[1] * along_x + omega[2] * along_y
        out[c][...] = omega[c] + TIME_STEP * stretch


def ends_kernel(_, __, edges, before, after, low_rim, high_rim, *refs):
    meshes, vorticity, out, sems = refs[:-4], refs[-3], refs[-2], refs[-1]
    cols = before.shape[1]
    size = edges.shape[1]
    copies = []

    def rows_of(i):
        return lambda c, start=RIM: edges[c, i, start : start + cols]

    for n, i in enumerate((0, size - 1)):
        stretch_plane(
            [out.at[c, n] for c in range(3)],
            [meshes[0].at[c, i] for c in range(3)],
            (low_rim, high_rim),
            [rim_start(meshes, 0, c, i) for c in range(3)],
            rows_of(i),
            (lambda c: after[c]) if i else rows_of(1),
            rows_of(size - 2) if i else (lambda c: before[c]),
        )
        copies.append(
            pltpu.make_async_copy(
                out.at[:, n], vorticity.at[:, n * (vorticity.shape[1] - 1)], sems.at[n]
            )
        )
        copies[-1].start()
    for copy in copies:
        copy.wait()


def stretch_kernel(chunks, tables, place, edges, low_rim, high_rim, *refs):
    meshes, refs = refs[:2], refs[2:]
    velocity, vorticity, held, inner, omega, sems = refs[-6:]
    _, planes, cols, ny = velocity.shape
    spot = where_planes(chunks)
    talls = (edges, inner)
    sent = []

    def send(source, target):
        sent.append(pltpu.make_async_copy(source, target, sems.at[len(sent)]))
        sent[-1].start()

    def rows_of(z):
        n, i = spot[z]
        return lambda c, start=RIM: talls[n][c, i, start : start + cols]

    def send_velocity(which):
        for z in range(planes):
            n, i = spot[z]
            if n == which:
                send(talls[n].at[:, i, pl.ds(RIM, cols)], velocity.at[:, z])

    send_velocity(0)
    gather_blocks(refs[:-6], held, place[1], "far")
    for (c, z), value in planes_of(held, chunks[1], tables).items():
        hold(inner, c, spot[z][1], value)
    send_velocity(1)
    for z in range(1, planes - 1):
        which, i = spot[z]
        stretch_plane(
            [omega.at[c, z] for c in range(3)],
            [meshes[which].at[c, i] for c in range(3)],
            (low_rim, high_rim),
            [rim_start(meshes, which, c, i) for c in range(3)],
            rows_of(z),
            rows_of(z + 1),
            rows_of(z - 1),
        )
        send(omega.at[:, z], vorticity.at[:, z])
    for copy in sent:
        copy.wait()


VM = pl.BlockSpec(memory_space=pltpu.VMEM)
SM = pl.BlockSpec(memory_space=pltpu.SMEM)
AN = pl.BlockSpec(memory_space=pl.ANY)
HB = pl.BlockSpec(memory_space=pltpu.HBM)


def kept(values):
    return pltpu.with_memory_space_constraint(values, pltpu.HBM)


def loaded(kernel):
    def run(place, t_high, t_low, *refs):
        kernel((t_high, t_low), place, *refs)

    return run


def call(kernel, ins, outs, scratch=(), sems=0, micros=2.0, moved=None, aliases=None):
    extra = [pltpu.SemaphoreType.DMA((sems,))] if sems else []
    return pl.pallas_call(
        kernel,
        out_shape=[jax.ShapeDtypeStruct(shape, F32) for _, shape in outs],
        in_specs=[spec for spec, _ in ins],
        out_specs=[spec for spec, _ in outs],
        scratch_shapes=[pltpu.VMEM(shape, kind) for shape, kind in scratch] + extra,
        compiler_params=pltpu.CompilerParams(vmem_limit_bytes=VMEM),
        input_output_aliases=aliases or {},
        cost_estimate=pl.CostEstimate(
            flops=int(micros * 1.0e9),
            bytes_accessed=int(micros * 3.0e6) if moved is None else moved,
            transcendentals=0,
        ),
    )(*[value for _, value in ins])


def ring(axis, step):
    count = lax.axis_size(axis)
    return [(i, (i + step) % count) for i in range(count)]


def spread(axis):
    count = lax.axis_size(axis)
    return count <= 8 and count & (count - 1) == 0


def sent_shapes(axis, rows, width, whole=False):
    count = lax.axis_size(axis)
    return [(count, rows, width)] if whole or not spread(axis) else [(rows, width)] * count


def exchange(blocks, axis, start=0, first=None):
    if not spread(axis):
        return [lax.all_to_all(blocks[0], axis, split_axis=0, concat_axis=0, tiled=True)]
    count = lax.axis_size(axis)
    return [
        lax.ppermute(block, axis, [(i, i ^ k) for i in range(count)]) if k else block
        for k, block in zip(offset_order(count, first)[start:], blocks)
    ]


def on_device(strength, offsets, cell_index, migrate_count, ambient):
    _, planes, cols, ny = ambient.shape
    slabs, pencils = lax.axis_size("gz"), lax.axis_size("gx")
    nx, nz, rows = cols * pencils, planes * slabs, cols + RIM
    count = strength.shape[1]
    pair_count = planes // 2
    chunks = ((0, pair_count - 1), tuple(range(1, pair_count - 1)))
    widths = [3 * len(c) * LANES for c in chunks]
    block = nx // slabs

    y_ahead, y_back = [split_table(t) for t in y_tables(ny, pencils, 1.0 / (float(nx) * ny * nz))]
    x_ahead, x_back = [split_table(t) for t in x_tables(nx, cols, pencils, slabs)]
    place = jnp.stack([lax.axis_index("gz"), lax.axis_index("gx")]).astype(jnp.int32)
    here = (SM, place)

    packet, movers = call(
        packet_kernel,
        [
            (HB, kept(migrate_count.reshape(1, 2))),
            (HB, kept(strength)),
            (HB, kept(offsets)),
            (HB, kept(cell_index.reshape(1, count))),
        ],
        [(VM, (8, count)), (VM, (8, 2 * MIG))],
        [((1, 2), jnp.int32), ((1, count), jnp.int32)],
        sems=4,
        micros=1.0,
        moved=1000,
    )
    up1 = lax.ppermute(packet, "gz", ring("gz", -1))
    down1 = lax.ppermute(packet, "gz", ring("gz", 1))
    up2 = lax.ppermute(movers, "gz", ring("gz", -2))
    down2 = lax.ppermute(movers, "gz", ring("gz", 2))

    meshes, rims, parts = [None, None], [], [None, None]
    for n in (1, 0):
        chunk, width = chunks[n], widths[n]
        size = 2 * len(chunk)
        rim = (6 * size + (rims[0].shape[0] if rims else 0), ny)
        mesh, rim_high, rim_low, *part = call(
            functools.partial(deposit_kernel, chunk, len(rims), None if n else "near"),
            [here]
            + [(VM, value) for value in (packet, up1, down1, up2, down2)]
            + [(VM, ambient), (VM, y_ahead[0]), (VM, y_ahead[1])]
            + [(VM, value) for value in rims],
            [(VM, (3, size, cols, ny)), (VM, rim), (VM, rim)]
            + [(VM, shape) for shape in sent_shapes("gx", rows, width)],
            [((3, size, rows, ny), F32), ((pencils, rows, width), F32)],
            micros=5.0,
        )
        meshes[n] = mesh
        rims = [rim_high, rim_low]
        parts[n] = exchange(part, "gx", first="near" if n == 0 else None)
    low_rim = lax.ppermute(rims[0], "gx", ring("gx", 1))
    high_rim = lax.ppermute(rims[1], "gx", ring("gx", -1))

    tile = max(1, block // 4)
    data = [None, None]
    for n in (1, 0):
        chunk, part, width = chunks[n], parts[n], widths[n]
        shapes = sent_shapes("gz", block, width)
        part = call(
            functools.partial(x_ahead_kernel, len(shapes), None if n else "near"),
            [here, (VM, x_ahead[0]), (VM, x_ahead[1])] + [(VM, p) for p in part],
            [(VM, shape) for shape in shapes],
            [((pencils, rows, width), F32), ((slabs, block, width), F32)],
        )
        (entered,) = call(
            functools.partial(enter_kernel, chunk, nz),
            [here] + [(VM, p) for p in exchange(part, "gz")],
            [(VM, (3, 2, 2 * len(chunk), slabs, tile, LANES))],
        )
        data[n] = entered
    data = call(
        functools.partial(curl_kernel, chunks, nx, ny),
        [here, (VM, low_rim), (VM, high_rim)] + [(VM, d) for d in data],
        [(VM, d.shape) for d in data],
        [((3, 2, nz, tile, LANES), F32)],
        micros=5.0,
    )
    plane = (3, cols, ny)
    tables = [(VM, t) for t in y_back]
    tall = [(3, 2 * len(chunk), cols + 2 * RIM, ny) for chunk in chunks]
    left = [
        call(
            functools.partial(leave_kernel, chunk, nz),
            [here, (VM, source)],
            [(VM, shape) for shape in sent_shapes("gz", block, width)],
            [(source.shape, F32)],
        )
        for chunk, source, width in zip(chunks, data, widths)
    ]

    def back(part, width, first=None):
        shapes = sent_shapes("gx", rows, width)
        part = call(
            loaded(functools.partial(x_back_kernel, len(shapes), first)),
            [here]
            + [(VM, t) for t in x_back]
            + [(VM, p) for p in part],
            [(VM, shape) for shape in shapes],
            [((slabs, block, width), F32), ((pencils, rows, width), F32)],
        )
        return exchange(part, "gx", first=first)

    early = max(1, len(left[1]) - LATE)
    second = exchange(left[1][:early], "gz")
    parts = [back(exchange(left[0], "gz"), widths[0])]
    edges, first, last = call(
        loaded(functools.partial(edge_kernel, chunks[0])),
        [here] + tables + [(VM, p) for p in parts[0]],
        [(VM, tall[0]), (VM, plane), (VM, plane)],
        [((pencils, rows, widths[0]), F32)],
    )
    if early < len(left[1]):
        late = call(
            pass_kernel,
            [(AN, parts[0][0])] + [(VM, p) for p in left[1][early:]],
            [(VM, p.shape) for p in left[1][early:]],
            micros=0.3,
        )
        second += exchange(late, "gz", early)
    parts.append(back(second, widths[1], "far"))
    after = lax.ppermute(first, "gz", ring("gz", -1))
    before = lax.ppermute(last, "gz", ring("gz", 1))
    velocity, vorticity = call(
        loaded(functools.partial(stretch_kernel, chunks)),
        [here]
        + tables
        + [(VM, v) for v in (edges, low_rim, high_rim, *meshes)]
        + [(VM, p) for p in parts[1]],
        [(AN, ambient.shape), (AN, ambient.shape)],
        [
            ((pencils, rows, widths[1]), F32),
            (tall[1], F32),
            ((3, planes, cols, ny), F32),
        ],
        sems=2 * planes,
        micros=4.0,
    )
    return tuple(
        call(
            ends_kernel,
            [(AN, velocity), (AN, vorticity)]
            + [(VM, v) for v in (edges, before, after, low_rim, high_rim, *meshes)],
            [(AN, ambient.shape), (AN, ambient.shape)],
            [((3, 2, cols, ny), F32)],
            sems=2,
            micros=1.0,
            aliases={0: 0, 1: 1},
        )
    )


def solution(mesh):
    placed = (
        P(None, ("gz", "gx")),
        P(None, ("gz", "gx")),
        P(("gz", "gx")),
        P("gz", "gx", None),
        P(None, "gz", "gx", None),
    )
    return jax.shard_map(
        on_device,
        mesh=mesh,
        in_specs=placed,
        out_specs=(P(None, "gz", "gx", None), P(None, "gz", "gx", None)),
        check_vma=False,
    )
```

```python
import functools
import math

import jax
import jax.numpy as jnp
import ml_dtypes
import numpy as np
from jax import lax
from jax.experimental import pallas as pl
from jax.experimental.pallas import tpu as pltpu
from jax.sharding import PartitionSpec as P

MIG = 64
LANES = 128
RIM = 8
LATE = 2
TIME_STEP = 0.25
VMEM = 24 * 1024 * 1024
F32 = jnp.float32
BF16 = jnp.bfloat16


def split_table(table):
    high = table.astype(np.float32).astype(ml_dtypes.bfloat16)
    low = (table - high.astype(np.float64)).astype(np.float32).astype(ml_dtypes.bfloat16)
    return high, low


def angles(rows, columns, extent):
    return 2.0 * np.pi * (np.multiply.outer(rows, columns) % extent) / extent


def y_tables(ny, pencils, scale):
    modes = ny // (2 * pencils)
    position = np.arange(ny)
    angle = angles(position, np.arange(ny // 2), ny)
    real, imag = np.cos(angle), -np.sin(angle)
    imag[:, 0] = 1.0 - 2.0 * (position % 2)
    weight = np.where(np.arange(ny // 2) == 0, 1.0, 2.0) * scale
    ahead = np.zeros((2, ny, pencils, 2, 2, modes))
    back = np.zeros((pencils, 2, 2, modes, 2, ny))
    for parity in range(2):
        for part, values in enumerate((real, imag)):
            ahead[parity, :, :, part, parity] = values.reshape(ny, pencils, modes)
            back[:, part, parity, :, parity] = (values * weight).T.reshape(pencils, modes, ny)
    return ahead.reshape(2 * ny, -1), back.reshape(-1, 2 * ny)


def wave_order(nx, slabs):
    half = nx // 2
    ahead = np.arange(half).reshape(slabs, 1, half // slabs)
    behind = np.where(ahead == 0, half, (nx - ahead) % nx)
    return np.concatenate([ahead, behind], axis=1).reshape(-1)


def x_tables(nx, cols, pencils, slabs):
    order = wave_order(nx, slabs)
    angle = angles(order, np.arange(nx), nx)
    ahead = np.concatenate([np.cos(angle), np.sin(angle)], axis=0)
    row = np.arange(cols + RIM)
    offset = np.where(row <= cols, row, -1)
    used = ((row <= cols) | (row == cols + RIM - 1)).astype(np.float64)
    place = (np.arange(pencils)[:, None] * cols + offset[None, :]) % nx
    angle = angles(place.reshape(-1), order, nx)
    mask = np.tile(used, pencils)[:, None]
    back = np.concatenate([np.cos(angle) * mask, np.sin(angle) * mask], axis=0)
    return ahead, back


def split(values):
    high = values.astype(BF16)
    return high, (values - high.astype(F32)).astype(BF16)


def dot(left, right):
    return jnp.dot(left, right, preferred_element_type=F32)


def table_left(high, low, values):
    v_high, v_low = split(values)
    return dot(high, v_high) + (dot(high, v_low) + dot(low, v_high))


def table_right(values, high, low):
    v_high, v_low = split(values)
    return dot(v_high, high) + (dot(v_low, high) + dot(v_high, low))


def lane_of():
    return lax.broadcasted_iota(jnp.int32, (1, LANES), 1)


def times_i(values):
    half = LANES // 2
    sign = jnp.where(lane_of() < half, -1.0, 1.0).astype(F32)
    return pltpu.roll(values, half, 1) * sign


def kernel_weight(distance):
    radius = jnp.abs(distance)
    near = 1.0 + radius * radius * (1.5 * radius - 2.5)
    rest = jnp.maximum(2.0 - radius, 0.0)
    return jnp.where(radius < 1.0, near, 0.5 * rest * rest * (1.0 - radius))


def quotient(values, size):
    if size & (size - 1):
        return lax.div(values, size)
    return lax.shift_right_logical(values, size.bit_length() - 1)


def remainder(values, size):
    if size & (size - 1):
        return lax.rem(values, size)
    return values & (size - 1)


def turned(value, wave, extent, sign):
    wave = wave % extent
    real, imag = value
    if wave == 0:
        return value
    if 2 * wave == extent:
        return -real, -imag
    if 4 * wave == extent:
        return (-imag, real) if sign > 0 else (imag, -real)
    if 4 * wave == 3 * extent:
        return (imag, -real) if sign > 0 else (-imag, real)
    a = math.cos(2.0 * math.pi * wave / extent)
    b = sign * math.sin(2.0 * math.pi * wave / extent)
    return real * a - imag * b, real * b + imag * a


def fft(values, sign):
    count = len(values)
    if count == 1:
        return values
    even, odd = fft(values[::2], sign), fft(values[1::2], sign)
    odd = [turned(v, k, count, sign) for k, v in enumerate(odd)]
    plus = [(a[0] + b[0], a[1] + b[1]) for a, b in zip(even, odd)]
    minus = [(a[0] - b[0], a[1] - b[1]) for a, b in zip(even, odd)]
    return plus + minus


def offset_order(count, first=None):
    far, near = list(range(count // 2, count)), list(range(1, count // 2))
    if first == "near":
        return [0] + near + far
    if first == "far":
        return [0] + far + near
    order, last = [0], near[2:]
    near = near[:2]
    while far or near:
        order += far[:1] + near[:1]
        far, near = far[1:], near[1:]
    return order + last


def blocks_of(refs, at, first=None):
    if len(refs) == 1:
        return [(d, refs[0].at[d]) for d in range(refs[0].shape[0])]
    return [(at ^ k, ref) for k, ref in zip(offset_order(len(refs), first), refs)]


def gather_blocks(refs, held, at, first=None):
    for d, ref in blocks_of(refs, at, first):
        held[d] = ref[...]


def packet_kernel(
    counts, strength, offsets, cells, packet, movers, near_counts, near_cells, sems
):
    copies = [
        pltpu.make_async_copy(counts, near_counts, sems.at[0]),
        pltpu.make_async_copy(cells, near_cells, sems.at[1]),
        pltpu.make_async_copy(strength, packet.at[pl.ds(0, 3)], sems.at[2]),
        pltpu.make_async_copy(offsets, packet.at[pl.ds(3, 3)], sems.at[3]),
    ]
    for copy in copies:
        copy.start()
    for copy in copies:
        copy.wait()
    slot = lax.broadcasted_iota(jnp.int32, (1, packet.shape[1]), 1)
    up = near_counts[0:1, 0:1]
    both = up + near_counts[0:1, 1:2]
    packet[6:7] = near_cells[...].astype(F32)
    packet[7:8] = jnp.where(slot < up, 1.0, jnp.where(slot < both, -1.0, 0.0))
    movers[...] = packet[:, : movers.shape[1]]


def deposit_kernel(
    pairs, rims_before, first, place, own, up1, down1, up2, down2, ambient, t_high, t_low, *refs
):
    rims, refs = refs[:rims_before], refs[rims_before:]
    mesh, rim_high, rim_low = refs[:3]
    total, made = refs[-2:]
    outs = refs[3:-2]
    _, planes, cols, ny = ambient.shape
    rows = cols + RIM
    movers = up2.shape[1]
    count = own.shape[1]
    listed = [2 * pair + parity for pair in pairs for parity in range(2)]

    def decode(ref, start, stop, shift):
        packet = ref[:, start:stop]
        cell = packet[6:7].astype(jnp.int32)
        move = packet[7:8].astype(jnp.int32)
        z_cell = quotient(cell, cols * ny) + planes * (move + shift)
        x_cell = remainder(quotient(cell, ny), cols)
        return packet[0:6], z_cell, x_cell, remainder(cell, ny)

    def joined(pieces):
        return [jnp.concatenate(p, axis=1) if len(p) > 1 else p[0] for p in zip(*pieces)]

    def add_block(pieces, wanted):
        values, z_cell, x_cell, y_cell = joined(pieces)
        width = values.shape[1]
        z_at = lax.broadcasted_iota(jnp.int32, (planes, width), 0)
        w_z = kernel_weight((z_at - z_cell).astype(F32) - values[3:4])
        row = lax.broadcasted_iota(jnp.int32, (rows, width), 0)
        x_at = jnp.where(row < cols + 2, row, jnp.where(row >= rows - 2, row - rows, 4 * rows))
        w_x = kernel_weight((x_at - x_cell).astype(F32) - values[4:5])
        y_at = lax.broadcasted_iota(jnp.int32, (ny, width), 0)
        y_off = remainder(y_at + (ny + ny // 2 - y_cell), ny) - ny // 2
        w_y = kernel_weight(y_off.astype(F32) - values[5:6])
        y_high, y_low = split(w_y)
        right = jnp.concatenate([y_high, y_high, y_low], axis=1)
        at = [listed.index(z) for z in wanted]
        for c in range(3):
            s_z = values[c : c + 1] * w_z
            left = jnp.concatenate([s_z[z : z + 1] * w_x for z in wanted], axis=0)
            l_high, l_low = split(left)
            left = jnp.concatenate([l_high, l_low, l_high], axis=1)
            added = lax.dot_general(
                left, right, (((1,), (1,)), ((), ())), preferred_element_type=F32
            )
            total[c, at[0] : at[-1] + 1] += added.reshape(len(wanted), rows, ny)

    for n, z in enumerate(listed):
        total[:, n, 0:cols] = ambient[:, z]
    total[:, :, cols:rows] = jnp.zeros((3, len(listed), RIM, ny), F32)
    step = 256
    for at in range(0, count, step):
        add_block([decode(own, at, min(at + step, count), 0)], listed)
    add_block([decode(up1, 0, movers, 1), decode(down1, 0, movers, -1)], listed)
    sides = ((up1, up2, 1, (planes - 2, planes - 1)), (down1, down2, -1, (0, 1)))
    for near, far, shift, wanted in sides:
        if not set(wanted) <= set(listed):
            continue
        whole = [decode(near, movers, count, shift), decode(far, 0, movers, 2 * shift)]
        values, z_cell, x_cell, y_cell = joined(whole)
        for at in range(0, count, step):
            to = min(at + step, count)
            block = (values[:, at:to], z_cell[:, at:to], x_cell[:, at:to], y_cell[:, at:to])
            add_block([block], wanted)

    mesh[...] = total[:, :, 0:cols]
    at = 0
    if rims:
        at = rims[0].shape[0]
        rim_high[0:at] = rims[0][...]
        rim_low[0:at] = rims[1][...]
    for n in range(3 * len(listed)):
        c, i = n // len(listed), n % len(listed)
        rim_high[at + 2 * n : at + 2 * n + 2] = total[c, i, cols : cols + 2]
        rim_low[at + 2 * n : at + 2 * n + 2] = total[c, i, rows - 2 : rows]
    groups = [(c, 2 * n) for c in range(3) for n in range(len(pairs))]
    left = jnp.concatenate(
        [jnp.concatenate([total[c, n], total[c, n + 1]], axis=1) for c, n in groups], axis=0
    )
    wide = table_right(left, t_high[...], t_low[...])
    for n in range(len(groups)):
        for g in range(made.shape[0]):
            made[g, :, n * LANES : (n + 1) * LANES] = wide[
                n * rows : (n + 1) * rows, g * LANES : (g + 1) * LANES
            ]
    for d, out in blocks_of(outs, place[1], first):
        out[...] = made[d]


def x_ahead_kernel(sends, first, place, t_high, t_low, *refs):
    held, made = refs[-2:]
    outs, parts = refs[-2 - sends : -2], refs[: -2 - sends]
    gather_blocks(parts, held, place[1], first)
    pencils, rows, width = held.shape
    cols = rows - RIM
    row = lax.broadcasted_iota(jnp.int32, (RIM, width), 0)
    pieces = []
    for h in range(pencils):
        from_low = held[(h - 1) % pencils, cols:rows]
        from_high = held[(h + 1) % pencils, cols:rows]
        pieces.append(held[h, 0:RIM] + jnp.where(row < 2, from_low, 0.0))
        pieces.append(held[h, RIM : cols - RIM])
        pieces.append(held[h, cols - RIM : cols] + jnp.where(row >= RIM - 2, from_high, 0.0))
    both = table_left(t_high[...], t_low[...], jnp.concatenate(pieces, axis=0))
    half = both.shape[0] // 2
    for n in range(width // LANES):
        lanes = slice(n * LANES, (n + 1) * LANES)
        value = both[:half, lanes] - times_i(both[half:, lanes])
        made[:, :, lanes] = value.reshape(made.shape[0], made.shape[1], LANES)
    for d, out in blocks_of(outs, place[0]):
        out[...] = made[d]


def x_back_kernel(sends, first, tables, place, *refs):
    held, made = refs[-2:]
    outs, parts = refs[-2 - sends : -2], refs[: -2 - sends]
    gather_blocks(parts, held, place[0])
    pencils, rows, width = made.shape
    both = table_left(tables[0][...], tables[1][...], held[...].reshape(-1, width))
    half = both.shape[0] // 2
    for n in range(width // LANES):
        lanes = slice(n * LANES, (n + 1) * LANES)
        value = both[:half, lanes] + times_i(both[half:, lanes])
        made[:, :, lanes] = value.reshape(pencils, rows, LANES)
    for d, out in blocks_of(outs, place[1], first):
        out[...] = made[d]


def wave_lanes():
    lane = lane_of()
    return lane < LANES // 2, (lane // (LANES // 4)) % 2 == 0


def roll(values, shift):
    return pltpu.roll(values, shift, 1)


def cross_half(a, b):
    low, _ = wave_lanes()
    half = LANES // 2
    return jnp.where(low, a, roll(b, half)), jnp.where(low, roll(a, half), b)


def cross_quarter(a, b):
    _, first = wave_lanes()
    quarter = LANES // 4
    return (
        jnp.where(first, a, roll(b, quarter)),
        jnp.where(first, roll(a, LANES - quarter), b),
    )


def lanes_at(c, count, i):
    return pl.ds(pl.multiple_of((c * count + i) * LANES, LANES), LANES)


def enter_kernel(pairs, nz, place, *refs):
    parts, data = refs[:-1], refs[-1]
    _, _, _, slabs, tile, _ = data.shape

    def body(c, carry):
        for i, pair in enumerate(pairs):
            lanes = lanes_at(c, len(pairs), i)
            for s, ref in blocks_of(parts, place[0]):
                quad = [ref[q * tile : (q + 1) * tile, lanes] for q in range(4)]
                real0, imag0 = cross_half(quad[0], quad[2])
                real1, imag1 = cross_half(quad[1], quad[3])
                for part, (a, b) in enumerate(((real0, real1), (imag0, imag1))):
                    even, odd = cross_quarter(a, b)
                    data[c, part, 2 * i, s] = even
                    data[c, part, 2 * i + 1, s] = odd
            for parity in range(2):
                at = 2 * i + parity
                line = [(data[c, 0, at, s], data[c, 1, at, s]) for s in range(slabs)]
                for k, v in enumerate(fft(line, -1.0)):
                    v = turned(v, (2 * pair + parity) * k, nz, -1.0)
                    data[c, 0, at, k], data[c, 1, at, k] = v
        return carry

    lax.fori_loop(0, 3, body, 0)


def pass_kernel(before, *refs):
    for source, target in zip(refs[: len(refs) // 2], refs[len(refs) // 2 :]):
        target[...] = source[...]


def leave_kernel(pairs, nz, place, source, *refs):
    outs, data = refs[:-1], refs[-1]
    _, _, _, slabs, tile, _ = source.shape

    def body(c, carry):
        for i, pair in enumerate(pairs):
            lanes = lanes_at(c, len(pairs), i)
            for parity in range(2):
                at = 2 * i + parity
                line = [
                    turned(
                        (source[c, 0, at, k], source[c, 1, at, k]),
                        (2 * pair + parity) * k,
                        nz,
                        1.0,
                    )
                    for k in range(slabs)
                ]
                for s, v in enumerate(fft(line, 1.0)):
                    data[c, 0, at, s], data[c, 1, at, s] = v
            for s, ref in blocks_of(outs, place[0]):
                real0, real1 = cross_quarter(data[c, 0, 2 * i, s], data[c, 0, 2 * i + 1, s])
                imag0, imag1 = cross_quarter(data[c, 1, 2 * i, s], data[c, 1, 2 * i + 1, s])
                quad = [None] * 4
                quad[0], quad[2] = cross_half(real0, imag0)
                quad[1], quad[3] = cross_half(real1, imag1)
                for q in range(4):
                    ref[q * tile : (q + 1) * tile, lanes] = quad[q]
        return carry

    lax.fori_loop(0, 3, body, 0)


def curl_kernel(chunks, nx, ny, place, low_rim, high_rim, *refs):
    sources, outs = refs[: len(chunks)], refs[len(chunks) : 2 * len(chunks)]
    spectrum = refs[-1]
    _, _, nz, tile, _ = spectrum.shape
    slabs = sources[0].shape[3]
    planes = nz // slabs
    modes, half = LANES // 4, LANES // 2
    slab_at, pencil_at = place[0], place[1]
    spot = {}
    for n, chunk in enumerate(chunks):
        for i, pair in enumerate(chunk):
            spot[2 * pair], spot[2 * pair + 1] = (n, 2 * i), (n, 2 * i + 1)

    def across_planes(k, carry):
        for c in range(3):
            line = []
            for l in range(planes):
                n, i = spot[l]
                line.append((sources[n][c, 0, i, k], sources[n][c, 1, i, k]))
            for n, v in enumerate(fft(line, -1.0)):
                spectrum[c, 0, k + slabs * n], spectrum[c, 1, k + slabs * n] = v
        return carry

    reach = 2 * tile
    row = lax.broadcasted_iota(jnp.int32, (tile, LANES), 0)
    lane = lax.broadcasted_iota(jnp.int32, (tile, LANES), 1)
    number = slab_at * reach + (lane // modes) % 2 * tile + row
    ahead = lane < half
    mode = lane % modes + pencil_at * modes
    alone = number == 0
    number = number.astype(F32) * (2.0 * math.pi / nx)
    x_base = jnp.where(ahead, number, jnp.where(alone, math.pi, -number))
    x_trim = jnp.where(ahead, number, jnp.where(alone, 0.0, -number))
    wave_y = mode.astype(F32) * (2.0 * math.pi / ny)
    packed = mode == 0
    x_sq = x_base * x_base
    lateral = x_sq + wave_y * wave_y

    def curl_at(k, with_mirror):
        z_wave = jnp.where(k < nz // 2, k, k - nz).astype(F32) * (2.0 * math.pi / nz)
        z_trim = jnp.where(k == nz // 2, 0.0, z_wave)
        full = lateral + z_wave * z_wave
        empty = full == 0.0
        inverse = jnp.where(empty, 0.0, 1.0 / jnp.where(empty, 1.0, full))
        if with_mirror:
            other = 1.0 / (x_sq + (z_wave * z_wave + math.pi * math.pi))
            mirror = jnp.where(packed, 0.5 * (inverse - other), 0.0)
            inverse = jnp.where(packed, 0.5 * (inverse + other), inverse)
            opposite = lax.rem(nz - k, nz)
        stream = []
        for c in range(3):
            value = [spectrum[c, part, k] * inverse for part in range(2)]
            if with_mirror:
                for part, sign in enumerate((1.0, -1.0)):
                    there = spectrum[c, part, opposite]
                    there = jnp.where(alone, there, roll(there, half))
                    value[part] = value[part] + (mirror * sign) * there
            stream.append(value)
        made = []
        for part in range(2):
            s = [value[part] for value in stream]
            made.append(
                (
                    x_trim * s[2] - wave_y * s[1],
                    wave_y * s[0] - z_trim * s[2],
                    z_trim * s[1] - x_trim * s[0],
                )
            )
        return [(-made[1][c], made[0][c]) for c in range(3)]

    def curl_all(with_mirror):
        def body(k, carry):
            made = [curl_at(k + slabs * n, with_mirror) for n in range(planes)]
            for c in range(3):
                for l, v in enumerate(fft([m[c] for m in made], 1.0)):
                    n, i = spot[l]
                    outs[n][c, 0, i, k], outs[n][c, 1, i, k] = v
            return carry

        lax.fori_loop(0, slabs, body, 0)

    lax.fori_loop(0, slabs, across_planes, 0)

    @pl.when(pencil_at == 0)
    def _():
        curl_all(True)

    @pl.when(pencil_at != 0)
    def _():
        curl_all(False)


def planes_of(held, pairs, tables):
    pencils, rows, _ = held.shape
    groups = [(c, pair) for c in range(3) for pair in pairs]
    left = jnp.concatenate(
        [
            jnp.concatenate(
                [held[h, :, n * LANES : (n + 1) * LANES] for h in range(pencils)], axis=1
            )
            for n in range(len(groups))
        ],
        axis=0,
    )
    ny = tables[0].shape[1] // 2
    wide = table_right(left, tables[0][...], tables[1][...])
    made = {}
    for n, (c, pair) in enumerate(groups):
        for parity in range(2):
            made[c, 2 * pair + parity] = wide[
                n * rows : (n + 1) * rows, parity * ny : (parity + 1) * ny
            ]
    return made


def hold(tall, c, n, value):
    rows = value.shape[0]
    tall[c, n, RIM : RIM + rows] = value
    tall[c, n, 0:RIM] = value[rows - RIM : rows]


def edge_kernel(pairs, tables, place, *refs):
    tall, first, last, held = refs[-4:]
    gather_blocks(refs[:-4], held, place[1])
    listed = [2 * pair + parity for pair in pairs for parity in range(2)]
    cols = first.shape[1]
    values = planes_of(held, pairs, tables)
    for c in range(3):
        for n, z in enumerate(listed):
            hold(tall, c, n, values[c, z])
        first[c] = values[c, listed[0]][0:cols]
        last[c] = values[c, listed[-1]][0:cols]


def where_planes(chunks):
    spot = {}
    for n, chunk in enumerate(chunks):
        for i, pair in enumerate(chunk):
            spot[2 * pair], spot[2 * pair + 1] = (n, 2 * i), (n, 2 * i + 1)
    return spot


def rim_start(meshes, which, c, i):
    before = 6 * meshes[1].shape[1] if which == 0 else 0
    return before + 2 * (c * meshes[which].shape[1] + i)


def stretch_plane(out, mesh, rims, at, rows_of, above, below):
    cols, ny = out[0].shape
    low_rim, high_rim = rims
    for c in range(3):
        out[c][...] = mesh[c][...]
        out[c][0:2] += low_rim[at[c] : at[c] + 2]
        out[c][cols - 2 : cols] += high_rim[at[c] : at[c] + 2]
    omega = [ref[...] for ref in out]
    for c in range(3):
        value = rows_of(c, RIM)
        along_z = (above(c) - below(c)) * 0.5
        along_x = (rows_of(c, RIM + 1) - rows_of(c, RIM - 1)) * 0.5
        along_y = (pltpu.roll(value, ny - 1, 1) - pltpu.roll(value, 1, 1)) * 0.5
        stretch = omega[0] * along_z + omega[1] * along_x + omega[2] * along_y
        out[c][...] = omega[c] + TIME_STEP * stretch


def ends_kernel(_, __, edges, before, after, low_rim, high_rim, *refs):
    meshes, vorticity, out, sems = refs[:-4], refs[-3], refs[-2], refs[-1]
    cols = before.shape[1]
    size = edges.shape[1]
    copies = []

    def rows_of(i):
        return lambda c, start=RIM: edges[c, i, start : start + cols]

    for n, i in enumerate((0, size - 1)):
        stretch_plane(
            [out.at[c, n] for c in range(3)],
            [meshes[0].at[c, i] for c in range(3)],
            (low_rim, high_rim),
            [rim_start(meshes, 0, c, i) for c in range(3)],
            rows_of(i),
            (lambda c: after[c]) if i else rows_of(1),
            rows_of(size - 2) if i else (lambda c: before[c]),
        )
        copies.append(
            pltpu.make_async_copy(
                out.at[:, n], vorticity.at[:, n * (vorticity.shape[1] - 1)], sems.at[n]
            )
        )
        copies[-1].start()
    for copy in copies:
        copy.wait()


def stretch_kernel(chunks, tables, place, edges, low_rim, high_rim, *refs):
    meshes, refs = refs[:2], refs[2:]
    velocity, vorticity, held, inner, omega, sems = refs[-6:]
    _, planes, cols, ny = velocity.shape
    spot = where_planes(chunks)
    talls = (edges, inner)
    sent = []

    def send(source, target):
        sent.append(pltpu.make_async_copy(source, target, sems.at[len(sent)]))
        sent[-1].start()

    def rows_of(z):
        n, i = spot[z]
        return lambda c, start=RIM: talls[n][c, i, start : start + cols]

    def send_velocity(which):
        for z in range(planes):
            n, i = spot[z]
            if n == which:
                send(talls[n].at[:, i, pl.ds(RIM, cols)], velocity.at[:, z])

    send_velocity(0)
    gather_blocks(refs[:-6], held, place[1], "far")
    for (c, z), value in planes_of(held, chunks[1], tables).items():
        hold(inner, c, spot[z][1], value)
    send_velocity(1)
    for z in range(1, planes - 1):
        which, i = spot[z]
        stretch_plane(
            [omega.at[c, z] for c in range(3)],
            [meshes[which].at[c, i] for c in range(3)],
            (low_rim, high_rim),
            [rim_start(meshes, which, c, i) for c in range(3)],
            rows_of(z),
            rows_of(z + 1),
            rows_of(z - 1),
        )
        send(omega.at[:, z], vorticity.at[:, z])
    for copy in sent:
        copy.wait()


VM = pl.BlockSpec(memory_space=pltpu.VMEM)
SM = pl.BlockSpec(memory_space=pltpu.SMEM)
AN = pl.BlockSpec(memory_space=pl.ANY)
HB = pl.BlockSpec(memory_space=pltpu.HBM)


def kept(values):
    return pltpu.with_memory_space_constraint(values, pltpu.HBM)


def loaded(kernel):
    def run(place, t_high, t_low, *refs):
        kernel((t_high, t_low), place, *refs)

    return run


def call(kernel, ins, outs, scratch=(), sems=0, micros=2.0, moved=None, aliases=None):
    extra = [pltpu.SemaphoreType.DMA((sems,))] if sems else []
    return pl.pallas_call(
        kernel,
        out_shape=[jax.ShapeDtypeStruct(shape, F32) for _, shape in outs],
        in_specs=[spec for spec, _ in ins],
        out_specs=[spec for spec, _ in outs],
        scratch_shapes=[pltpu.VMEM(shape, kind) for shape, kind in scratch] + extra,
        compiler_params=pltpu.CompilerParams(vmem_limit_bytes=VMEM),
        input_output_aliases=aliases or {},
        cost_estimate=pl.CostEstimate(
            flops=int(micros * 1.0e9),
            bytes_accessed=int(micros * 3.0e6) if moved is None else moved,
            transcendentals=0,
        ),
    )(*[value for _, value in ins])


def ring(axis, step):
    count = lax.axis_size(axis)
    return [(i, (i + step) % count) for i in range(count)]


def spread(axis):
    count = lax.axis_size(axis)
    return count <= 8 and count & (count - 1) == 0


def sent_shapes(axis, rows, width, whole=False):
    count = lax.axis_size(axis)
    return [(count, rows, width)] if whole or not spread(axis) else [(rows, width)] * count


def exchange(blocks, axis, start=0, first=None):
    if not spread(axis):
        return [lax.all_to_all(blocks[0], axis, split_axis=0, concat_axis=0, tiled=True)]
    count = lax.axis_size(axis)
    return [
        lax.ppermute(block, axis, [(i, i ^ k) for i in range(count)]) if k else block
        for k, block in zip(offset_order(count, first)[start:], blocks)
    ]


def on_device(strength, offsets, cell_index, migrate_count, ambient):
    _, planes, cols, ny = ambient.shape
    slabs, pencils = lax.axis_size("gz"), lax.axis_size("gx")
    nx, nz, rows = cols * pencils, planes * slabs, cols + RIM
    count = strength.shape[1]
    pair_count = planes // 2
    chunks = ((0, pair_count - 1), tuple(range(1, pair_count - 1)))
    widths = [3 * len(c) * LANES for c in chunks]
    block = nx // slabs

    y_ahead, y_back = [split_table(t) for t in y_tables(ny, pencils, 1.0 / (float(nx) * ny * nz))]
    x_ahead, x_back = [split_table(t) for t in x_tables(nx, cols, pencils, slabs)]
    place = jnp.stack([lax.axis_index("gz"), lax.axis_index("gx")]).astype(jnp.int32)
    here = (SM, place)

    packet, movers = call(
        packet_kernel,
        [
            (HB, kept(migrate_count.reshape(1, 2))),
            (HB, kept(strength)),
            (HB, kept(offsets)),
            (HB, kept(cell_index.reshape(1, count))),
        ],
        [(VM, (8, count)), (VM, (8, 2 * MIG))],
        [((1, 2), jnp.int32), ((1, count), jnp.int32)],
        sems=4,
        micros=1.0,
        moved=1000,
    )
    up1 = lax.ppermute(packet, "gz", ring("gz", -1))
    down1 = lax.ppermute(packet, "gz", ring("gz", 1))
    up2 = lax.ppermute(movers, "gz", ring("gz", -2))
    down2 = lax.ppermute(movers, "gz", ring("gz", 2))

    meshes, rims, parts = [None, None], [], [None, None]
    for n in (1, 0):
        chunk, width = chunks[n], widths[n]
        size = 2 * len(chunk)
        rim = (6 * size + (rims[0].shape[0] if rims else 0), ny)
        mesh, rim_high, rim_low, *part = call(
            functools.partial(deposit_kernel, chunk, len(rims), None if n else "near"),
            [here]
            + [(VM, value) for value in (packet, up1, down1, up2, down2)]
            + [(VM, ambient), (VM, y_ahead[0]), (VM, y_ahead[1])]
            + [(VM, value) for value in rims],
            [(VM, (3, size, cols, ny)), (VM, rim), (VM, rim)]
            + [(VM, shape) for shape in sent_shapes("gx", rows, width)],
            [((3, size, rows, ny), F32), ((pencils, rows, width), F32)],
            micros=5.0,
        )
        meshes[n] = mesh
        rims = [rim_high, rim_low]
        parts[n] = exchange(part, "gx", first="near" if n == 0 else None)
    low_rim = lax.ppermute(rims[0], "gx", ring("gx", 1))
    high_rim = lax.ppermute(rims[1], "gx", ring("gx", -1))

    tile = max(1, block // 4)
    data = [None, None]
    for n in (1, 0):
        chunk, part, width = chunks[n], parts[n], widths[n]
        shapes = sent_shapes("gz", block, width)
        part = call(
            functools.partial(x_ahead_kernel, len(shapes), None if n else "near"),
            [here, (VM, x_ahead[0]), (VM, x_ahead[1])] + [(VM, p) for p in part],
            [(VM, shape) for shape in shapes],
            [((pencils, rows, width), F32), ((slabs, block, width), F32)],
        )
        (entered,) = call(
            functools.partial(enter_kernel, chunk, nz),
            [here] + [(VM, p) for p in exchange(part, "gz")],
            [(VM, (3, 2, 2 * len(chunk), slabs, tile, LANES))],
        )
        data[n] = entered
    data = call(
        functools.partial(curl_kernel, chunks, nx, ny),
        [here, (VM, low_rim), (VM, high_rim)] + [(VM, d) for d in data],
        [(VM, d.shape) for d in data],
        [((3, 2, nz, tile, LANES), F32)],
        micros=5.0,
    )
    plane = (3, cols, ny)
    tables = [(VM, t) for t in y_back]
    tall = [(3, 2 * len(chunk), cols + 2 * RIM, ny) for chunk in chunks]
    left = [
        call(
            functools.partial(leave_kernel, chunk, nz),
            [here, (VM, source)],
            [(VM, shape) for shape in sent_shapes("gz", block, width)],
            [(source.shape, F32)],
        )
        for chunk, source, width in zip(chunks, data, widths)
    ]

    def back(part, width, first=None):
        shapes = sent_shapes("gx", rows, width)
        part = call(
            loaded(functools.partial(x_back_kernel, len(shapes), first)),
            [here]
            + [(VM, t) for t in x_back]
            + [(VM, p) for p in part],
            [(VM, shape) for shape in shapes],
            [((slabs, block, width), F32), ((pencils, rows, width), F32)],
        )
        return exchange(part, "gx", first=first)

    early = max(1, len(left[1]) - LATE)
    second = exchange(left[1][:early], "gz")
    parts = [back(exchange(left[0], "gz"), widths[0])]
    edges, first, last = call(
        loaded(functools.partial(edge_kernel, chunks[0])),
        [here] + tables + [(VM, p) for p in parts[0]],
        [(VM, tall[0]), (VM, plane), (VM, plane)],
        [((pencils, rows, widths[0]), F32)],
    )
    if early < len(left[1]):
        late = call(
            pass_kernel,
            [(AN, parts[0][0])] + [(VM, p) for p in left[1][early:]],
            [(VM, p.shape) for p in left[1][early:]],
            micros=0.3,
        )
        second += exchange(late, "gz", early)
    parts.append(back(second, widths[1], "far"))
    after = lax.ppermute(first, "gz", ring("gz", -1))
    before = lax.ppermute(last, "gz", ring("gz", 1))
    velocity, vorticity = call(
        loaded(functools.partial(stretch_kernel, chunks)),
        [here]
        + tables
        + [(VM, v) for v in (edges, low_rim, high_rim, *meshes)]
        + [(VM, p) for p in parts[1]],
        [(AN, ambient.shape), (AN, ambient.shape)],
        [
            ((pencils, rows, widths[1]), F32),
            (tall[1], F32),
            ((3, planes, cols, ny), F32),
        ],
        sems=2 * planes,
        micros=4.0,
    )
    return tuple(
        call(
            ends_kernel,
            [(AN, velocity), (AN, vorticity)]
            + [(VM, v) for v in (edges, before, after, low_rim, high_rim, *meshes)],
            [(AN, ambient.shape), (AN, ambient.shape)],
            [((3, 2, cols, ny), F32)],
            sems=2,
            micros=1.0,
            aliases={0: 0, 1: 1},
        )
    )


def solution(mesh):
    placed = (
        P(None, ("gz", "gx")),
        P(None, ("gz", "gx")),
        P(("gz", "gx")),
        P("gz", "gx", None),
        P(None, "gz", "gx", None),
    )
    return jax.shard_map(
        on_device,
        mesh=mesh,
        in_specs=placed,
        out_specs=(P(None, "gz", "gx", None), P(None, "gz", "gx", None)),
        check_vma=False,
    )
```

```python
import functools
import math

import jax
import jax.numpy as jnp
import ml_dtypes
import numpy as np
from jax import lax
from jax.experimental import pallas as pl
from jax.experimental.pallas import tpu as pltpu
from jax.sharding import PartitionSpec as P

MIG = 64
LANES = 128
RIM = 8
LATE = 3
TIME_STEP = 0.25
VMEM = 24 * 1024 * 1024
F32 = jnp.float32
BF16 = jnp.bfloat16


def split_table(table):
    high = table.astype(np.float32).astype(ml_dtypes.bfloat16)
    low = (table - high.astype(np.float64)).astype(np.float32).astype(ml_dtypes.bfloat16)
    return high, low


def angles(rows, columns, extent):
    return 2.0 * np.pi * (np.multiply.outer(rows, columns) % extent) / extent


def y_tables(ny, pencils, scale):
    modes = ny // (2 * pencils)
    position = np.arange(ny)
    angle = angles(position, np.arange(ny // 2), ny)
    real, imag = np.cos(angle), -np.sin(angle)
    imag[:, 0] = 1.0 - 2.0 * (position % 2)
    weight = np.where(np.arange(ny // 2) == 0, 1.0, 2.0) * scale
    ahead = np.zeros((2, ny, pencils, 2, 2, modes))
    back = np.zeros((pencils, 2, 2, modes, 2, ny))
    for parity in range(2):
        for part, values in enumerate((real, imag)):
            ahead[parity, :, :, part, parity] = values.reshape(ny, pencils, modes)
            back[:, part, parity, :, parity] = (values * weight).T.reshape(pencils, modes, ny)
    return ahead.reshape(2 * ny, -1), back.reshape(-1, 2 * ny)


def wave_order(nx, slabs):
    half = nx // 2
    ahead = np.arange(half).reshape(slabs, 1, half // slabs)
    behind = np.where(ahead == 0, half, (nx - ahead) % nx)
    return np.concatenate([ahead, behind], axis=1).reshape(-1)


def x_tables(nx, cols, pencils, slabs):
    order = wave_order(nx, slabs)
    angle = angles(order, np.arange(nx), nx)
    ahead = np.concatenate([np.cos(angle), np.sin(angle)], axis=0)
    row = np.arange(cols + RIM)
    offset = np.where(row <= cols, row, -1)
    used = ((row <= cols) | (row == cols + RIM - 1)).astype(np.float64)
    place = (np.arange(pencils)[:, None] * cols + offset[None, :]) % nx
    angle = angles(place.reshape(-1), order, nx)
    mask = np.tile(used, pencils)[:, None]
    back = np.concatenate([np.cos(angle) * mask, np.sin(angle) * mask], axis=0)
    return ahead, back


def split(values):
    high = values.astype(BF16)
    return high, (values - high.astype(F32)).astype(BF16)


def dot(left, right):
    return jnp.dot(left, right, preferred_element_type=F32)


def table_left(high, low, values):
    v_high, v_low = split(values)
    return dot(high, v_high) + (dot(high, v_low) + dot(low, v_high))


def table_right(values, high, low):
    v_high, v_low = split(values)
    return dot(v_high, high) + (dot(v_low, high) + dot(v_high, low))


def lane_of():
    return lax.broadcasted_iota(jnp.int32, (1, LANES), 1)


def times_i(values):
    half = LANES // 2
    sign = jnp.where(lane_of() < half, -1.0, 1.0).astype(F32)
    return pltpu.roll(values, half, 1) * sign


def kernel_weight(distance):
    radius = jnp.abs(distance)
    near = 1.0 + radius * radius * (1.5 * radius - 2.5)
    rest = jnp.maximum(2.0 - radius, 0.0)
    return jnp.where(radius < 1.0, near, 0.5 * rest * rest * (1.0 - radius))


def quotient(values, size):
    if size & (size - 1):
        return lax.div(values, size)
    return lax.shift_right_logical(values, size.bit_length() - 1)


def remainder(values, size):
    if size & (size - 1):
        return lax.rem(values, size)
    return values & (size - 1)


def turned(value, wave, extent, sign):
    wave = wave % extent
    real, imag = value
    if wave == 0:
        return value
    if 2 * wave == extent:
        return -real, -imag
    if 4 * wave == extent:
        return (-imag, real) if sign > 0 else (imag, -real)
    if 4 * wave == 3 * extent:
        return (imag, -real) if sign > 0 else (-imag, real)
    a = math.cos(2.0 * math.pi * wave / extent)
    b = sign * math.sin(2.0 * math.pi * wave / extent)
    return real * a - imag * b, real * b + imag * a


def fft(values, sign):
    count = len(values)
    if count == 1:
        return values
    even, odd = fft(values[::2], sign), fft(values[1::2], sign)
    odd = [turned(v, k, count, sign) for k, v in enumerate(odd)]
    plus = [(a[0] + b[0], a[1] + b[1]) for a, b in zip(even, odd)]
    minus = [(a[0] - b[0], a[1] - b[1]) for a, b in zip(even, odd)]
    return plus + minus


def offset_order(count, first=None):
    far, near = list(range(count // 2, count)), list(range(1, count // 2))
    if first == "near":
        return [0] + near + far
    if first == "far":
        return [0] + far + near
    order, last = [0], near[2:]
    near = near[:2]
    while far or near:
        order += far[:1] + near[:1]
        far, near = far[1:], near[1:]
    return order + last


def blocks_of(refs, at, first=None):
    if len(refs) == 1:
        return [(d, refs[0].at[d]) for d in range(refs[0].shape[0])]
    return [(at ^ k, ref) for k, ref in zip(offset_order(len(refs), first), refs)]


def gather_blocks(refs, held, at, first=None):
    for d, ref in blocks_of(refs, at, first):
        held[d] = ref[...]


def packet_kernel(
    counts, strength, offsets, cells, packet, movers, near_counts, near_cells, sems
):
    copies = [
        pltpu.make_async_copy(counts, near_counts, sems.at[0]),
        pltpu.make_async_copy(cells, near_cells, sems.at[1]),
        pltpu.make_async_copy(strength, packet.at[pl.ds(0, 3)], sems.at[2]),
        pltpu.make_async_copy(offsets, packet.at[pl.ds(3, 3)], sems.at[3]),
    ]
    for copy in copies:
        copy.start()
    for copy in copies:
        copy.wait()
    slot = lax.broadcasted_iota(jnp.int32, (1, packet.shape[1]), 1)
    up = near_counts[0:1, 0:1]
    both = up + near_counts[0:1, 1:2]
    packet[6:7] = near_cells[...].astype(F32)
    packet[7:8] = jnp.where(slot < up, 1.0, jnp.where(slot < both, -1.0, 0.0))
    movers[...] = packet[:, : movers.shape[1]]


def deposit_kernel(
    pairs, rims_before, first, place, own, up1, down1, up2, down2, ambient, t_high, t_low, *refs
):
    rims, refs = refs[:rims_before], refs[rims_before:]
    mesh, rim_high, rim_low = refs[:3]
    total, made = refs[-2:]
    outs = refs[3:-2]
    _, planes, cols, ny = ambient.shape
    rows = cols + RIM
    movers = up2.shape[1]
    count = own.shape[1]
    listed = [2 * pair + parity for pair in pairs for parity in range(2)]

    def decode(ref, start, stop, shift):
        packet = ref[:, start:stop]
        cell = packet[6:7].astype(jnp.int32)
        move = packet[7:8].astype(jnp.int32)
        z_cell = quotient(cell, cols * ny) + planes * (move + shift)
        x_cell = remainder(quotient(cell, ny), cols)
        return packet[0:6], z_cell, x_cell, remainder(cell, ny)

    def joined(pieces):
        return [jnp.concatenate(p, axis=1) if len(p) > 1 else p[0] for p in zip(*pieces)]

    def add_block(pieces, wanted):
        values, z_cell, x_cell, y_cell = joined(pieces)
        width = values.shape[1]
        z_at = lax.broadcasted_iota(jnp.int32, (planes, width), 0)
        w_z = kernel_weight((z_at - z_cell).astype(F32) - values[3:4])
        row = lax.broadcasted_iota(jnp.int32, (rows, width), 0)
        x_at = jnp.where(row < cols + 2, row, jnp.where(row >= rows - 2, row - rows, 4 * rows))
        w_x = kernel_weight((x_at - x_cell).astype(F32) - values[4:5])
        y_at = lax.broadcasted_iota(jnp.int32, (ny, width), 0)
        y_off = remainder(y_at + (ny + ny // 2 - y_cell), ny) - ny // 2
        w_y = kernel_weight(y_off.astype(F32) - values[5:6])
        y_high, y_low = split(w_y)
        right = jnp.concatenate([y_high, y_high, y_low], axis=1)
        at = [listed.index(z) for z in wanted]
        left = []
        for c in range(3):
            s_z = values[c : c + 1] * w_z
            left += [s_z[z : z + 1] * w_x for z in wanted]
        l_high, l_low = split(jnp.concatenate(left, axis=0))
        added = lax.dot_general(
            jnp.concatenate([l_high, l_low, l_high], axis=1),
            right,
            (((1,), (1,)), ((), ())),
            preferred_element_type=F32,
        )
        total[:, at[0] : at[-1] + 1] += added.reshape(3, len(wanted), rows, ny)

    for n, z in enumerate(listed):
        total[:, n, 0:cols] = ambient[:, z]
    total[:, :, cols:rows] = jnp.zeros((3, len(listed), RIM, ny), F32)
    step = 256
    for at in range(0, count, step):
        add_block([decode(own, at, min(at + step, count), 0)], listed)
    add_block([decode(up1, 0, movers, 1), decode(down1, 0, movers, -1)], listed)
    sides = ((up1, up2, 1, (planes - 2, planes - 1)), (down1, down2, -1, (0, 1)))
    for near, far, shift, wanted in sides:
        if not set(wanted) <= set(listed):
            continue
        whole = [decode(near, movers, count, shift), decode(far, 0, movers, 2 * shift)]
        values, z_cell, x_cell, y_cell = joined(whole)
        for at in range(0, count, step):
            to = min(at + step, count)
            block = (values[:, at:to], z_cell[:, at:to], x_cell[:, at:to], y_cell[:, at:to])
            add_block([block], wanted)

    mesh[...] = total[:, :, 0:cols]
    at = 0
    if rims:
        at = rims[0].shape[0]
        rim_high[0:at] = rims[0][...]
        rim_low[0:at] = rims[1][...]
    for n in range(3 * len(listed)):
        c, i = n // len(listed), n % len(listed)
        rim_high[at + 2 * n : at + 2 * n + 2] = total[c, i, cols : cols + 2]
        rim_low[at + 2 * n : at + 2 * n + 2] = total[c, i, rows - 2 : rows]
    groups = [(c, 2 * n) for c in range(3) for n in range(len(pairs))]
    left = jnp.concatenate(
        [jnp.concatenate([total[c, n], total[c, n + 1]], axis=1) for c, n in groups], axis=0
    )
    wide = table_right(left, t_high[...], t_low[...])
    for n in range(len(groups)):
        for g in range(made.shape[0]):
            made[g, :, n * LANES : (n + 1) * LANES] = wide[
                n * rows : (n + 1) * rows, g * LANES : (g + 1) * LANES
            ]
    for d, out in blocks_of(outs, place[1], first):
        out[...] = made[d]


def x_ahead_kernel(sends, first, place, t_high, t_low, *refs):
    held, made = refs[-2:]
    outs, parts = refs[-2 - sends : -2], refs[: -2 - sends]
    gather_blocks(parts, held, place[1], first)
    pencils, rows, width = held.shape
    cols = rows - RIM
    row = lax.broadcasted_iota(jnp.int32, (RIM, width), 0)
    pieces = []
    for h in range(pencils):
        from_low = held[(h - 1) % pencils, cols:rows]
        from_high = held[(h + 1) % pencils, cols:rows]
        pieces.append(held[h, 0:RIM] + jnp.where(row < 2, from_low, 0.0))
        pieces.append(held[h, RIM : cols - RIM])
        pieces.append(held[h, cols - RIM : cols] + jnp.where(row >= RIM - 2, from_high, 0.0))
    both = table_left(t_high[...], t_low[...], jnp.concatenate(pieces, axis=0))
    half = both.shape[0] // 2
    for n in range(width // LANES):
        lanes = slice(n * LANES, (n + 1) * LANES)
        value = both[:half, lanes] - times_i(both[half:, lanes])
        made[:, :, lanes] = value.reshape(made.shape[0], made.shape[1], LANES)
    for d, out in blocks_of(outs, place[0]):
        out[...] = made[d]


def x_back_kernel(sends, first, tables, place, *refs):
    held, made = refs[-2:]
    outs, parts = refs[-2 - sends : -2], refs[: -2 - sends]
    gather_blocks(parts, held, place[0])
    pencils, rows, width = made.shape
    both = table_left(tables[0][...], tables[1][...], held[...].reshape(-1, width))
    half = both.shape[0] // 2
    for n in range(width // LANES):
        lanes = slice(n * LANES, (n + 1) * LANES)
        value = both[:half, lanes] + times_i(both[half:, lanes])
        made[:, :, lanes] = value.reshape(pencils, rows, LANES)
    for d, out in blocks_of(outs, place[1], first):
        out[...] = made[d]


def wave_lanes():
    lane = lane_of()
    return lane < LANES // 2, (lane // (LANES // 4)) % 2 == 0


def roll(values, shift):
    return pltpu.roll(values, shift, 1)


def cross_half(a, b):
    low, _ = wave_lanes()
    half = LANES // 2
    return jnp.where(low, a, roll(b, half)), jnp.where(low, roll(a, half), b)


def cross_quarter(a, b):
    _, first = wave_lanes()
    quarter = LANES // 4
    return (
        jnp.where(first, a, roll(b, quarter)),
        jnp.where(first, roll(a, LANES - quarter), b),
    )


def lanes_at(c, count, i):
    return pl.ds(pl.multiple_of((c * count + i) * LANES, LANES), LANES)


def enter_kernel(pairs, nz, place, *refs):
    parts, data = refs[:-1], refs[-1]
    _, _, _, slabs, tile, _ = data.shape

    def body(c, carry):
        for i, pair in enumerate(pairs):
            lanes = lanes_at(c, len(pairs), i)
            for s, ref in blocks_of(parts, place[0]):
                quad = [ref[q * tile : (q + 1) * tile, lanes] for q in range(4)]
                real0, imag0 = cross_half(quad[0], quad[2])
                real1, imag1 = cross_half(quad[1], quad[3])
                for part, (a, b) in enumerate(((real0, real1), (imag0, imag1))):
                    even, odd = cross_quarter(a, b)
                    data[c, part, 2 * i, s] = even
                    data[c, part, 2 * i + 1, s] = odd
            for parity in range(2):
                at = 2 * i + parity
                line = [(data[c, 0, at, s], data[c, 1, at, s]) for s in range(slabs)]
                for k, v in enumerate(fft(line, -1.0)):
                    v = turned(v, (2 * pair + parity) * k, nz, -1.0)
                    data[c, 0, at, k], data[c, 1, at, k] = v
        return carry

    lax.fori_loop(0, 3, body, 0)


def pass_kernel(before, *refs):
    for source, target in zip(refs[: len(refs) // 2], refs[len(refs) // 2 :]):
        target[...] = source[...]


def leave_kernel(pairs, nz, place, source, *refs):
    outs, data = refs[:-1], refs[-1]
    _, _, _, slabs, tile, _ = source.shape

    def body(c, carry):
        for i, pair in enumerate(pairs):
            lanes = lanes_at(c, len(pairs), i)
            for parity in range(2):
                at = 2 * i + parity
                line = [
                    turned(
                        (source[c, 0, at, k], source[c, 1, at, k]),
                        (2 * pair + parity) * k,
                        nz,
                        1.0,
                    )
                    for k in range(slabs)
                ]
                for s, v in enumerate(fft(line, 1.0)):
                    data[c, 0, at, s], data[c, 1, at, s] = v
            for s, ref in blocks_of(outs, place[0]):
                real0, real1 = cross_quarter(data[c, 0, 2 * i, s], data[c, 0, 2 * i + 1, s])
                imag0, imag1 = cross_quarter(data[c, 1, 2 * i, s], data[c, 1, 2 * i + 1, s])
                quad = [None] * 4
                quad[0], quad[2] = cross_half(real0, imag0)
                quad[1], quad[3] = cross_half(real1, imag1)
                for q in range(4):
                    ref[q * tile : (q + 1) * tile, lanes] = quad[q]
        return carry

    lax.fori_loop(0, 3, body, 0)


def curl_kernel(chunks, nx, ny, place, low_rim, high_rim, *refs):
    sources, outs = refs[: len(chunks)], refs[len(chunks) : 2 * len(chunks)]
    spectrum = refs[-1]
    _, _, nz, tile, _ = spectrum.shape
    slabs = sources[0].shape[3]
    planes = nz // slabs
    modes, half = LANES // 4, LANES // 2
    slab_at, pencil_at = place[0], place[1]
    spot = {}
    for n, chunk in enumerate(chunks):
        for i, pair in enumerate(chunk):
            spot[2 * pair], spot[2 * pair + 1] = (n, 2 * i), (n, 2 * i + 1)

    def across_planes(k, carry):
        for c in range(3):
            line = []
            for l in range(planes):
                n, i = spot[l]
                line.append((sources[n][c, 0, i, k], sources[n][c, 1, i, k]))
            for n, v in enumerate(fft(line, -1.0)):
                spectrum[c, 0, k + slabs * n], spectrum[c, 1, k + slabs * n] = v
        return carry

    reach = 2 * tile
    row = lax.broadcasted_iota(jnp.int32, (tile, LANES), 0)
    lane = lax.broadcasted_iota(jnp.int32, (tile, LANES), 1)
    number = slab_at * reach + (lane // modes) % 2 * tile + row
    ahead = lane < half
    mode = lane % modes + pencil_at * modes
    alone = number == 0
    number = number.astype(F32) * (2.0 * math.pi / nx)
    x_base = jnp.where(ahead, number, jnp.where(alone, math.pi, -number))
    x_trim = jnp.where(ahead, number, jnp.where(alone, 0.0, -number))
    wave_y = mode.astype(F32) * (2.0 * math.pi / ny)
    packed = mode == 0
    x_sq = x_base * x_base
    lateral = x_sq + wave_y * wave_y

    def curl_at(k, with_mirror):
        z_wave = jnp.where(k < nz // 2, k, k - nz).astype(F32) * (2.0 * math.pi / nz)
        z_trim = jnp.where(k == nz // 2, 0.0, z_wave)
        full = lateral + z_wave * z_wave
        empty = full == 0.0
        inverse = jnp.where(empty, 0.0, 1.0 / jnp.where(empty, 1.0, full))
        if with_mirror:
            other = 1.0 / (x_sq + (z_wave * z_wave + math.pi * math.pi))
            mirror = jnp.where(packed, 0.5 * (inverse - other), 0.0)
            inverse = jnp.where(packed, 0.5 * (inverse + other), inverse)
            opposite = lax.rem(nz - k, nz)
        stream = []
        for c in range(3):
            value = [spectrum[c, part, k] * inverse for part in range(2)]
            if with_mirror:
                for part, sign in enumerate((1.0, -1.0)):
                    there = spectrum[c, part, opposite]
                    there = jnp.where(alone, there, roll(there, half))
                    value[part] = value[part] + (mirror * sign) * there
            stream.append(value)
        made = []
        for part in range(2):
            s = [value[part] for value in stream]
            made.append(
                (
                    x_trim * s[2] - wave_y * s[1],
                    wave_y * s[0] - z_trim * s[2],
                    z_trim * s[1] - x_trim * s[0],
                )
            )
        return [(-made[1][c], made[0][c]) for c in range(3)]

    def curl_all(with_mirror):
        def body(k, carry):
            made = [curl_at(k + slabs * n, with_mirror) for n in range(planes)]
            for c in range(3):
                for l, v in enumerate(fft([m[c] for m in made], 1.0)):
                    n, i = spot[l]
                    outs[n][c, 0, i, k], outs[n][c, 1, i, k] = v
            return carry

        lax.fori_loop(0, slabs, body, 0)

    lax.fori_loop(0, slabs, across_planes, 0)

    @pl.when(pencil_at == 0)
    def _():
        curl_all(True)

    @pl.when(pencil_at != 0)
    def _():
        curl_all(False)


def planes_of(held, pairs, tables):
    pencils, rows, _ = held.shape
    groups = [(c, pair) for c in range(3) for pair in pairs]
    left = jnp.concatenate(
        [
            jnp.concatenate(
                [held[h, :, n * LANES : (n + 1) * LANES] for h in range(pencils)], axis=1
            )
            for n in range(len(groups))
        ],
        axis=0,
    )
    ny = tables[0].shape[1] // 2
    wide = table_right(left, tables[0][...], tables[1][...])
    made = {}
    for n, (c, pair) in enumerate(groups):
        for parity in range(2):
            made[c, 2 * pair + parity] = wide[
                n * rows : (n + 1) * rows, parity * ny : (parity + 1) * ny
            ]
    return made


def hold(tall, c, n, value):
    rows = value.shape[0]
    tall[c, n, RIM : RIM + rows] = value
    tall[c, n, 0:RIM] = value[rows - RIM : rows]


def edge_kernel(pairs, tables, place, *refs):
    tall, first, last, held = refs[-4:]
    gather_blocks(refs[:-4], held, place[1])
    listed = [2 * pair + parity for pair in pairs for parity in range(2)]
    cols = first.shape[1]
    values = planes_of(held, pairs, tables)
    for c in range(3):
        for n, z in enumerate(listed):
            hold(tall, c, n, values[c, z])
        first[c] = values[c, listed[0]][0:cols]
        last[c] = values[c, listed[-1]][0:cols]


def where_planes(chunks):
    spot = {}
    for n, chunk in enumerate(chunks):
        for i, pair in enumerate(chunk):
            spot[2 * pair], spot[2 * pair + 1] = (n, 2 * i), (n, 2 * i + 1)
    return spot


def rim_start(meshes, which, c, i):
    before = 6 * meshes[1].shape[1] if which == 0 else 0
    return before + 2 * (c * meshes[which].shape[1] + i)


def stretch_plane(out, mesh, rims, at, rows_of, above, below):
    cols, ny = out[0].shape
    low_rim, high_rim = rims
    for c in range(3):
        out[c][...] = mesh[c][...]
        out[c][0:2] += low_rim[at[c] : at[c] + 2]
        out[c][cols - 2 : cols] += high_rim[at[c] : at[c] + 2]
    omega = [ref[...] for ref in out]
    for c in range(3):
        value = rows_of(c, RIM)
        along_z = (above(c) - below(c)) * 0.5
        along_x = (rows_of(c, RIM + 1) - rows_of(c, RIM - 1)) * 0.5
        along_y = (pltpu.roll(value, ny - 1, 1) - pltpu.roll(value, 1, 1)) * 0.5
        stretch = omega[0] * along_z + omega[1] * along_x + omega[2] * along_y
        out[c][...] = omega[c] + TIME_STEP * stretch


def ends_kernel(_, __, edges, before, after, low_rim, high_rim, *refs):
    meshes, vorticity, out, sems = refs[:-4], refs[-3], refs[-2], refs[-1]
    cols = before.shape[1]
    size = edges.shape[1]
    copies = []

    def rows_of(i):
        return lambda c, start=RIM: edges[c, i, start : start + cols]

    for n, i in enumerate((0, size - 1)):
        stretch_plane(
            [out.at[c, n] for c in range(3)],
            [meshes[0].at[c, i] for c in range(3)],
            (low_rim, high_rim),
            [rim_start(meshes, 0, c, i) for c in range(3)],
            rows_of(i),
            (lambda c: after[c]) if i else rows_of(1),
            rows_of(size - 2) if i else (lambda c: before[c]),
        )
        copies.append(
            pltpu.make_async_copy(
                out.at[:, n], vorticity.at[:, n * (vorticity.shape[1] - 1)], sems.at[n]
            )
        )
        copies[-1].start()
    for copy in copies:
        copy.wait()


def stretch_kernel(chunks, tables, place, edges, low_rim, high_rim, *refs):
    meshes, refs = refs[:2], refs[2:]
    velocity, vorticity, held, inner, omega, sems = refs[-6:]
    _, planes, cols, ny = velocity.shape
    spot = where_planes(chunks)
    talls = (edges, inner)
    sent = []

    def send(source, target):
        sent.append(pltpu.make_async_copy(source, target, sems.at[len(sent)]))
        sent[-1].start()

    def rows_of(z):
        n, i = spot[z]
        return lambda c, start=RIM: talls[n][c, i, start : start + cols]

    def send_velocity(which):
        for z in range(planes):
            n, i = spot[z]
            if n == which:
                send(talls[n].at[:, i, pl.ds(RIM, cols)], velocity.at[:, z])

    send_velocity(0)
    gather_blocks(refs[:-6], held, place[1], "far")
    for (c, z), value in planes_of(held, chunks[1], tables).items():
        hold(inner, c, spot[z][1], value)
    send_velocity(1)
    for z in range(1, planes - 1):
        which, i = spot[z]
        stretch_plane(
            [omega.at[c, z] for c in range(3)],
            [meshes[which].at[c, i] for c in range(3)],
            (low_rim, high_rim),
            [rim_start(meshes, which, c, i) for c in range(3)],
            rows_of(z),
            rows_of(z + 1),
            rows_of(z - 1),
        )
        send(omega.at[:, z], vorticity.at[:, z])
    for copy in sent:
        copy.wait()


VM = pl.BlockSpec(memory_space=pltpu.VMEM)
SM = pl.BlockSpec(memory_space=pltpu.SMEM)
AN = pl.BlockSpec(memory_space=pl.ANY)
HB = pl.BlockSpec(memory_space=pltpu.HBM)


def kept(values):
    return pltpu.with_memory_space_constraint(values, pltpu.HBM)


def loaded(kernel):
    def run(place, t_high, t_low, *refs):
        kernel((t_high, t_low), place, *refs)

    return run


def call(kernel, ins, outs, scratch=(), sems=0, micros=2.0, moved=None, aliases=None):
    extra = [pltpu.SemaphoreType.DMA((sems,))] if sems else []
    return pl.pallas_call(
        kernel,
        out_shape=[jax.ShapeDtypeStruct(shape, F32) for _, shape in outs],
        in_specs=[spec for spec, _ in ins],
        out_specs=[spec for spec, _ in outs],
        scratch_shapes=[pltpu.VMEM(shape, kind) for shape, kind in scratch] + extra,
        compiler_params=pltpu.CompilerParams(vmem_limit_bytes=VMEM),
        input_output_aliases=aliases or {},
        cost_estimate=pl.CostEstimate(
            flops=int(micros * 1.0e9),
            bytes_accessed=int(micros * 3.0e6) if moved is None else moved,
            transcendentals=0,
        ),
    )(*[value for _, value in ins])


def ring(axis, step):
    count = lax.axis_size(axis)
    return [(i, (i + step) % count) for i in range(count)]


def spread(axis):
    count = lax.axis_size(axis)
    return count <= 8 and count & (count - 1) == 0


def sent_shapes(axis, rows, width, whole=False):
    count = lax.axis_size(axis)
    return [(count, rows, width)] if whole or not spread(axis) else [(rows, width)] * count


def exchange(blocks, axis, start=0, first=None):
    if not spread(axis):
        return [lax.all_to_all(blocks[0], axis, split_axis=0, concat_axis=0, tiled=True)]
    count = lax.axis_size(axis)
    return [
        lax.ppermute(block, axis, [(i, i ^ k) for i in range(count)]) if k else block
        for k, block in zip(offset_order(count, first)[start:], blocks)
    ]


def on_device(strength, offsets, cell_index, migrate_count, ambient):
    _, planes, cols, ny = ambient.shape
    slabs, pencils = lax.axis_size("gz"), lax.axis_size("gx")
    nx, nz, rows = cols * pencils, planes * slabs, cols + RIM
    count = strength.shape[1]
    pair_count = planes // 2
    chunks = ((0, pair_count - 1), tuple(range(1, pair_count - 1)))
    widths = [3 * len(c) * LANES for c in chunks]
    block = nx // slabs

    y_ahead, y_back = [split_table(t) for t in y_tables(ny, pencils, 1.0 / (float(nx) * ny * nz))]
    x_ahead, x_back = [split_table(t) for t in x_tables(nx, cols, pencils, slabs)]
    place = jnp.stack([lax.axis_index("gz"), lax.axis_index("gx")]).astype(jnp.int32)
    here = (SM, place)

    packet, movers = call(
        packet_kernel,
        [
            (HB, kept(migrate_count.reshape(1, 2))),
            (HB, kept(strength)),
            (HB, kept(offsets)),
            (HB, kept(cell_index.reshape(1, count))),
        ],
        [(VM, (8, count)), (VM, (8, 2 * MIG))],
        [((1, 2), jnp.int32), ((1, count), jnp.int32)],
        sems=4,
        micros=1.0,
        moved=1000,
    )
    up1 = lax.ppermute(packet, "gz", ring("gz", -1))
    down1 = lax.ppermute(packet, "gz", ring("gz", 1))
    up2 = lax.ppermute(movers, "gz", ring("gz", -2))
    down2 = lax.ppermute(movers, "gz", ring("gz", 2))

    meshes, rims, parts = [None, None], [], [None, None]
    for n in (1, 0):
        chunk, width = chunks[n], widths[n]
        size = 2 * len(chunk)
        rim = (6 * size + (rims[0].shape[0] if rims else 0), ny)
        mesh, rim_high, rim_low, *part = call(
            functools.partial(deposit_kernel, chunk, len(rims), None if n else "near"),
            [here]
            + [(VM, value) for value in (packet, up1, down1, up2, down2)]
            + [(VM, ambient), (VM, y_ahead[0]), (VM, y_ahead[1])]
            + [(VM, value) for value in rims],
            [(VM, (3, size, cols, ny)), (VM, rim), (VM, rim)]
            + [(VM, shape) for shape in sent_shapes("gx", rows, width)],
            [((3, size, rows, ny), F32), ((pencils, rows, width), F32)],
            micros=5.0,
        )
        meshes[n] = mesh
        rims = [rim_high, rim_low]
        parts[n] = exchange(part, "gx", first="near" if n == 0 else None)
    low_rim = lax.ppermute(rims[0], "gx", ring("gx", 1))
    high_rim = lax.ppermute(rims[1], "gx", ring("gx", -1))

    tile = max(1, block // 4)
    data = [None, None]
    for n in (1, 0):
        chunk, part, width = chunks[n], parts[n], widths[n]
        shapes = sent_shapes("gz", block, width)
        part = call(
            functools.partial(x_ahead_kernel, len(shapes), None if n else "near"),
            [here, (VM, x_ahead[0]), (VM, x_ahead[1])] + [(VM, p) for p in part],
            [(VM, shape) for shape in shapes],
            [((pencils, rows, width), F32), ((slabs, block, width), F32)],
        )
        (entered,) = call(
            functools.partial(enter_kernel, chunk, nz),
            [here] + [(VM, p) for p in exchange(part, "gz")],
            [(VM, (3, 2, 2 * len(chunk), slabs, tile, LANES))],
        )
        data[n] = entered
    data = call(
        functools.partial(curl_kernel, chunks, nx, ny),
        [here, (VM, low_rim), (VM, high_rim)] + [(VM, d) for d in data],
        [(VM, d.shape) for d in data],
        [((3, 2, nz, tile, LANES), F32)],
        micros=5.0,
    )
    plane = (3, cols, ny)
    tables = [(VM, t) for t in y_back]
    tall = [(3, 2 * len(chunk), cols + 2 * RIM, ny) for chunk in chunks]
    left = [
        call(
            functools.partial(leave_kernel, chunk, nz),
            [here, (VM, source)],
            [(VM, shape) for shape in sent_shapes("gz", block, width)],
            [(source.shape, F32)],
        )
        for chunk, source, width in zip(chunks, data, widths)
    ]

    def back(part, width, first=None):
        shapes = sent_shapes("gx", rows, width)
        part = call(
            loaded(functools.partial(x_back_kernel, len(shapes), first)),
            [here]
            + [(VM, t) for t in x_back]
            + [(VM, p) for p in part],
            [(VM, shape) for shape in shapes],
            [((slabs, block, width), F32), ((pencils, rows, width), F32)],
        )
        return exchange(part, "gx", first=first)

    early = max(1, len(left[1]) - LATE)
    second = exchange(left[1][:early], "gz")
    parts = [back(exchange(left[0], "gz"), widths[0])]
    edges, first, last = call(
        loaded(functools.partial(edge_kernel, chunks[0])),
        [here] + tables + [(VM, p) for p in parts[0]],
        [(VM, tall[0]), (VM, plane), (VM, plane)],
        [((pencils, rows, widths[0]), F32)],
    )
    if early < len(left[1]):
        late = call(
            pass_kernel,
            [(AN, parts[0][0])] + [(VM, p) for p in left[1][early:]],
            [(VM, p.shape) for p in left[1][early:]],
            micros=0.3,
        )
        second += exchange(late, "gz", early)
    parts.append(back(second, widths[1], "far"))
    after = lax.ppermute(first, "gz", ring("gz", -1))
    before = lax.ppermute(last, "gz", ring("gz", 1))
    velocity, vorticity = call(
        loaded(functools.partial(stretch_kernel, chunks)),
        [here]
        + tables
        + [(VM, v) for v in (edges, low_rim, high_rim, *meshes)]
        + [(VM, p) for p in parts[1]],
        [(AN, ambient.shape), (AN, ambient.shape)],
        [
            ((pencils, rows, widths[1]), F32),
            (tall[1], F32),
            ((3, planes, cols, ny), F32),
        ],
        sems=2 * planes,
        micros=4.0,
    )
    return tuple(
        call(
            ends_kernel,
            [(AN, velocity), (AN, vorticity)]
            + [(VM, v) for v in (edges, before, after, low_rim, high_rim, *meshes)],
            [(AN, ambient.shape), (AN, ambient.shape)],
            [((3, 2, cols, ny), F32)],
            sems=2,
            micros=1.0,
            aliases={0: 0, 1: 1},
        )
    )


def solution(mesh):
    placed = (
        P(None, ("gz", "gx")),
        P(None, ("gz", "gx")),
        P(("gz", "gx")),
        P("gz", "gx", None),
        P(None, "gz", "gx", None),
    )
    return jax.shard_map(
        on_device,
        mesh=mesh,
        in_specs=placed,
        out_specs=(P(None, "gz", "gx", None), P(None, "gz", "gx", None)),
        check_vma=False,
    )
```

```python
import functools
import math

import jax
import jax.numpy as jnp
import ml_dtypes
import numpy as np
from jax import lax
from jax.experimental import pallas as pl
from jax.experimental.pallas import tpu as pltpu
from jax.sharding import PartitionSpec as P

MIG = 64
LANES = 128
RIM = 8
LATE = 3
TIME_STEP = 0.25
VMEM = 24 * 1024 * 1024
F32 = jnp.float32
BF16 = jnp.bfloat16


def split_table(table):
    high = table.astype(np.float32).astype(ml_dtypes.bfloat16)
    low = (table - high.astype(np.float64)).astype(np.float32).astype(ml_dtypes.bfloat16)
    return high, low


def angles(rows, columns, extent):
    return 2.0 * np.pi * (np.multiply.outer(rows, columns) % extent) / extent


def y_tables(ny, pencils, scale):
    modes = ny // (2 * pencils)
    position = np.arange(ny)
    angle = angles(position, np.arange(ny // 2), ny)
    real, imag = np.cos(angle), -np.sin(angle)
    imag[:, 0] = 1.0 - 2.0 * (position % 2)
    weight = np.where(np.arange(ny // 2) == 0, 1.0, 2.0) * scale
    ahead = np.zeros((2, ny, pencils, 2, 2, modes))
    back = np.zeros((pencils, 2, 2, modes, 2, ny))
    for parity in range(2):
        for part, values in enumerate((real, imag)):
            ahead[parity, :, :, part, parity] = values.reshape(ny, pencils, modes)
            back[:, part, parity, :, parity] = (values * weight).T.reshape(pencils, modes, ny)
    return ahead.reshape(2 * ny, -1), back.reshape(-1, 2 * ny)


def wave_order(nx, slabs):
    half = nx // 2
    ahead = np.arange(half).reshape(slabs, 1, half // slabs)
    behind = np.where(ahead == 0, half, (nx - ahead) % nx)
    return np.concatenate([ahead, behind], axis=1).reshape(-1)


def x_tables(nx, cols, pencils, slabs):
    order = wave_order(nx, slabs)
    angle = angles(order, np.arange(nx), nx)
    ahead = np.concatenate([np.cos(angle), np.sin(angle)], axis=0)
    row = np.arange(cols + RIM)
    offset = np.where(row <= cols, row, -1)
    used = ((row <= cols) | (row == cols + RIM - 1)).astype(np.float64)
    place = (np.arange(pencils)[:, None] * cols + offset[None, :]) % nx
    angle = angles(place.reshape(-1), order, nx)
    mask = np.tile(used, pencils)[:, None]
    back = np.concatenate([np.cos(angle) * mask, np.sin(angle) * mask], axis=0)
    return ahead, back


def split(values):
    high = values.astype(BF16)
    return high, (values - high.astype(F32)).astype(BF16)


def dot(left, right):
    return jnp.dot(left, right, preferred_element_type=F32)


def table_left(high, low, values):
    v_high, v_low = split(values)
    return dot(high, v_high) + (dot(high, v_low) + dot(low, v_high))


def table_right(values, high, low):
    v_high, v_low = split(values)
    return dot(v_high, high) + (dot(v_low, high) + dot(v_high, low))


def lane_of():
    return lax.broadcasted_iota(jnp.int32, (1, LANES), 1)


def times_i(values):
    half = LANES // 2
    sign = jnp.where(lane_of() < half, -1.0, 1.0).astype(F32)
    return pltpu.roll(values, half, 1) * sign


def kernel_weight(distance):
    radius = jnp.abs(distance)
    near = 1.0 + radius * radius * (1.5 * radius - 2.5)
    rest = jnp.maximum(2.0 - radius, 0.0)
    return jnp.where(radius < 1.0, near, 0.5 * rest * rest * (1.0 - radius))


def quotient(values, size):
    if size & (size - 1):
        return lax.div(values, size)
    return lax.shift_right_logical(values, size.bit_length() - 1)


def remainder(values, size):
    if size & (size - 1):
        return lax.rem(values, size)
    return values & (size - 1)


def turned(value, wave, extent, sign):
    wave = wave % extent
    real, imag = value
    if wave == 0:
        return value
    if 2 * wave == extent:
        return -real, -imag
    if 4 * wave == extent:
        return (-imag, real) if sign > 0 else (imag, -real)
    if 4 * wave == 3 * extent:
        return (imag, -real) if sign > 0 else (-imag, real)
    a = math.cos(2.0 * math.pi * wave / extent)
    b = sign * math.sin(2.0 * math.pi * wave / extent)
    return real * a - imag * b, real * b + imag * a


def fft(values, sign):
    count = len(values)
    if count == 1:
        return values
    even, odd = fft(values[::2], sign), fft(values[1::2], sign)
    odd = [turned(v, k, count, sign) for k, v in enumerate(odd)]
    plus = [(a[0] + b[0], a[1] + b[1]) for a, b in zip(even, odd)]
    minus = [(a[0] - b[0], a[1] - b[1]) for a, b in zip(even, odd)]
    return plus + minus


def offset_order(count, first=None):
    far, near = list(range(count // 2, count)), list(range(1, count // 2))
    if first == "near":
        return [0] + near + far
    if first == "far":
        return [0] + far + near
    order, last = [0], near[2:]
    near, far = near[:2], far[::2] + far[1::2]
    while far or near:
        order += far[:1] + near[:1]
        far, near = far[1:], near[1:]
    return order + last


def blocks_of(refs, at, first=None):
    if len(refs) == 1:
        return [(d, refs[0].at[d]) for d in range(refs[0].shape[0])]
    return [(at ^ k, ref) for k, ref in zip(offset_order(len(refs), first), refs)]


def gather_blocks(refs, held, at, first=None):
    for d, ref in blocks_of(refs, at, first):
        held[d] = ref[...]


def packet_kernel(
    counts, strength, offsets, cells, packet, movers, near_counts, near_cells, sems
):
    copies = [
        pltpu.make_async_copy(counts, near_counts, sems.at[0]),
        pltpu.make_async_copy(cells, near_cells, sems.at[1]),
        pltpu.make_async_copy(strength, packet.at[pl.ds(0, 3)], sems.at[2]),
        pltpu.make_async_copy(offsets, packet.at[pl.ds(3, 3)], sems.at[3]),
    ]
    for copy in copies:
        copy.start()
    for copy in copies:
        copy.wait()
    slot = lax.broadcasted_iota(jnp.int32, (1, packet.shape[1]), 1)
    up = near_counts[0:1, 0:1]
    both = up + near_counts[0:1, 1:2]
    packet[6:7] = near_cells[...].astype(F32)
    packet[7:8] = jnp.where(slot < up, 1.0, jnp.where(slot < both, -1.0, 0.0))
    movers[...] = packet[:, : movers.shape[1]]


def deposit_kernel(
    pairs, rims_before, first, place, own, up1, down1, up2, down2, ambient, t_high, t_low, *refs
):
    rims, refs = refs[:rims_before], refs[rims_before:]
    mesh, rim_high, rim_low = refs[:3]
    total, made = refs[-2:]
    outs = refs[3:-2]
    _, planes, cols, ny = ambient.shape
    rows = cols + RIM
    movers = up2.shape[1]
    count = own.shape[1]
    listed = [2 * pair + parity for pair in pairs for parity in range(2)]

    def decode(ref, start, stop, shift):
        packet = ref[:, start:stop]
        cell = packet[6:7].astype(jnp.int32)
        move = packet[7:8].astype(jnp.int32)
        z_cell = quotient(cell, cols * ny) + planes * (move + shift)
        x_cell = remainder(quotient(cell, ny), cols)
        return packet[0:6], z_cell, x_cell, remainder(cell, ny)

    def joined(pieces):
        return [jnp.concatenate(p, axis=1) if len(p) > 1 else p[0] for p in zip(*pieces)]

    def add_block(pieces, wanted):
        values, z_cell, x_cell, y_cell = joined(pieces)
        width = values.shape[1]
        z_at = lax.broadcasted_iota(jnp.int32, (planes, width), 0)
        w_z = kernel_weight((z_at - z_cell).astype(F32) - values[3:4])
        row = lax.broadcasted_iota(jnp.int32, (rows, width), 0)
        x_at = jnp.where(row < cols + 2, row, jnp.where(row >= rows - 2, row - rows, 4 * rows))
        w_x = kernel_weight((x_at - x_cell).astype(F32) - values[4:5])
        y_at = lax.broadcasted_iota(jnp.int32, (ny, width), 0)
        y_off = remainder(y_at + (ny + ny // 2 - y_cell), ny) - ny // 2
        w_y = kernel_weight(y_off.astype(F32) - values[5:6])
        y_high, y_low = split(w_y)
        right = jnp.concatenate([y_high, y_high, y_low], axis=1)
        at = [listed.index(z) for z in wanted]
        for c in range(3):
            s_z = values[c : c + 1] * w_z
            left = jnp.concatenate([s_z[z : z + 1] * w_x for z in wanted], axis=0)
            l_high, l_low = split(left)
            left = jnp.concatenate([l_high, l_low, l_high], axis=1)
            added = lax.dot_general(
                left, right, (((1,), (1,)), ((), ())), preferred_element_type=F32
            )
            total[c, at[0] : at[-1] + 1] += added.reshape(len(wanted), rows, ny)

    for n, z in enumerate(listed):
        total[:, n, 0:cols] = ambient[:, z]
    total[:, :, cols:rows] = jnp.zeros((3, len(listed), RIM, ny), F32)
    step = 256
    for at in range(0, count, step):
        add_block([decode(own, at, min(at + step, count), 0)], listed)
    add_block([decode(up1, 0, movers, 1), decode(down1, 0, movers, -1)], listed)
    sides = ((up1, up2, 1, (planes - 2, planes - 1)), (down1, down2, -1, (0, 1)))
    for near, far, shift, wanted in sides:
        if not set(wanted) <= set(listed):
            continue
        whole = [decode(near, movers, count, shift), decode(far, 0, movers, 2 * shift)]
        values, z_cell, x_cell, y_cell = joined(whole)
        for at in range(0, count, step):
            to = min(at + step, count)
            block = (values[:, at:to], z_cell[:, at:to], x_cell[:, at:to], y_cell[:, at:to])
            add_block([block], wanted)

    mesh[...] = total[:, :, 0:cols]
    at = 0
    if rims:
        at = rims[0].shape[0]
        rim_high[0:at] = rims[0][...]
        rim_low[0:at] = rims[1][...]
    for n in range(3 * len(listed)):
        c, i = n // len(listed), n % len(listed)
        rim_high[at + 2 * n : at + 2 * n + 2] = total[c, i, cols : cols + 2]
        rim_low[at + 2 * n : at + 2 * n + 2] = total[c, i, rows - 2 : rows]
    groups = [(c, 2 * n) for c in range(3) for n in range(len(pairs))]
    left = jnp.concatenate(
        [jnp.concatenate([total[c, n], total[c, n + 1]], axis=1) for c, n in groups], axis=0
    )
    wide = table_right(left, t_high[...], t_low[...])
    for n in range(len(groups)):
        for g in range(made.shape[0]):
            made[g, :, n * LANES : (n + 1) * LANES] = wide[
                n * rows : (n + 1) * rows, g * LANES : (g + 1) * LANES
            ]
    for d, out in blocks_of(outs, place[1], first):
        out[...] = made[d]


def x_ahead_kernel(sends, first, place, t_high, t_low, *refs):
    held, made = refs[-2:]
    outs, parts = refs[-2 - sends : -2], refs[: -2 - sends]
    gather_blocks(parts, held, place[1], first)
    pencils, rows, width = held.shape
    cols = rows - RIM
    row = lax.broadcasted_iota(jnp.int32, (RIM, width), 0)
    pieces = []
    for h in range(pencils):
        from_low = held[(h - 1) % pencils, cols:rows]
        from_high = held[(h + 1) % pencils, cols:rows]
        pieces.append(held[h, 0:RIM] + jnp.where(row < 2, from_low, 0.0))
        pieces.append(held[h, RIM : cols - RIM])
        pieces.append(held[h, cols - RIM : cols] + jnp.where(row >= RIM - 2, from_high, 0.0))
    both = table_left(t_high[...], t_low[...], jnp.concatenate(pieces, axis=0))
    half = both.shape[0] // 2
    for n in range(width // LANES):
        lanes = slice(n * LANES, (n + 1) * LANES)
        value = both[:half, lanes] - times_i(both[half:, lanes])
        made[:, :, lanes] = value.reshape(made.shape[0], made.shape[1], LANES)
    for d, out in blocks_of(outs, place[0]):
        out[...] = made[d]


def x_back_kernel(sends, first, tables, place, *refs):
    held, made = refs[-2:]
    outs, parts = refs[-2 - sends : -2], refs[: -2 - sends]
    gather_blocks(parts, held, place[0])
    pencils, rows, width = made.shape
    both = table_left(tables[0][...], tables[1][...], held[...].reshape(-1, width))
    half = both.shape[0] // 2
    for n in range(width // LANES):
        lanes = slice(n * LANES, (n + 1) * LANES)
        value = both[:half, lanes] + times_i(both[half:, lanes])
        made[:, :, lanes] = value.reshape(pencils, rows, LANES)
    for d, out in blocks_of(outs, place[1], first):
        out[...] = made[d]


def wave_lanes():
    lane = lane_of()
    return lane < LANES // 2, (lane // (LANES // 4)) % 2 == 0


def roll(values, shift):
    return pltpu.roll(values, shift, 1)


def cross_half(a, b):
    low, _ = wave_lanes()
    half = LANES // 2
    return jnp.where(low, a, roll(b, half)), jnp.where(low, roll(a, half), b)


def cross_quarter(a, b):
    _, first = wave_lanes()
    quarter = LANES // 4
    return (
        jnp.where(first, a, roll(b, quarter)),
        jnp.where(first, roll(a, LANES - quarter), b),
    )


def lanes_at(c, count, i):
    return pl.ds(pl.multiple_of((c * count + i) * LANES, LANES), LANES)


def enter_kernel(pairs, nz, place, *refs):
    parts, data = refs[:-1], refs[-1]
    _, _, _, slabs, tile, _ = data.shape

    def body(c, carry):
        for i, pair in enumerate(pairs):
            lanes = lanes_at(c, len(pairs), i)
            for s, ref in blocks_of(parts, place[0]):
                quad = [ref[q * tile : (q + 1) * tile, lanes] for q in range(4)]
                real0, imag0 = cross_half(quad[0], quad[2])
                real1, imag1 = cross_half(quad[1], quad[3])
                for part, (a, b) in enumerate(((real0, real1), (imag0, imag1))):
                    even, odd = cross_quarter(a, b)
                    data[c, part, 2 * i, s] = even
                    data[c, part, 2 * i + 1, s] = odd
            for parity in range(2):
                at = 2 * i + parity
                line = [(data[c, 0, at, s], data[c, 1, at, s]) for s in range(slabs)]
                for k, v in enumerate(fft(line, -1.0)):
                    v = turned(v, (2 * pair + parity) * k, nz, -1.0)
                    data[c, 0, at, k], data[c, 1, at, k] = v
        return carry

    lax.fori_loop(0, 3, body, 0)


def pass_kernel(before, *refs):
    for source, target in zip(refs[: len(refs) // 2], refs[len(refs) // 2 :]):
        target[...] = source[...]


def leave_kernel(pairs, nz, place, source, *refs):
    outs, data = refs[:-1], refs[-1]
    _, _, _, slabs, tile, _ = source.shape

    def body(c, carry):
        for i, pair in enumerate(pairs):
            lanes = lanes_at(c, len(pairs), i)
            for parity in range(2):
                at = 2 * i + parity
                line = [
                    turned(
                        (source[c, 0, at, k], source[c, 1, at, k]),
                        (2 * pair + parity) * k,
                        nz,
                        1.0,
                    )
                    for k in range(slabs)
                ]
                for s, v in enumerate(fft(line, 1.0)):
                    data[c, 0, at, s], data[c, 1, at, s] = v
            for s, ref in blocks_of(outs, place[0]):
                real0, real1 = cross_quarter(data[c, 0, 2 * i, s], data[c, 0, 2 * i + 1, s])
                imag0, imag1 = cross_quarter(data[c, 1, 2 * i, s], data[c, 1, 2 * i + 1, s])
                quad = [None] * 4
                quad[0], quad[2] = cross_half(real0, imag0)
                quad[1], quad[3] = cross_half(real1, imag1)
                for q in range(4):
                    ref[q * tile : (q + 1) * tile, lanes] = quad[q]
        return carry

    lax.fori_loop(0, 3, body, 0)


def curl_kernel(chunks, nx, ny, place, low_rim, high_rim, *refs):
    sources, outs = refs[: len(chunks)], refs[len(chunks) : 2 * len(chunks)]
    spectrum = refs[-1]
    _, _, nz, tile, _ = spectrum.shape
    slabs = sources[0].shape[3]
    planes = nz // slabs
    modes, half = LANES // 4, LANES // 2
    slab_at, pencil_at = place[0], place[1]
    spot = {}
    for n, chunk in enumerate(chunks):
        for i, pair in enumerate(chunk):
            spot[2 * pair], spot[2 * pair + 1] = (n, 2 * i), (n, 2 * i + 1)

    def across_planes(k, carry):
        for c in range(3):
            line = []
            for l in range(planes):
                n, i = spot[l]
                line.append((sources[n][c, 0, i, k], sources[n][c, 1, i, k]))
            for n, v in enumerate(fft(line, -1.0)):
                spectrum[c, 0, k + slabs * n], spectrum[c, 1, k + slabs * n] = v
        return carry

    reach = 2 * tile
    row = lax.broadcasted_iota(jnp.int32, (tile, LANES), 0)
    lane = lax.broadcasted_iota(jnp.int32, (tile, LANES), 1)
    number = slab_at * reach + (lane // modes) % 2 * tile + row
    ahead = lane < half
    mode = lane % modes + pencil_at * modes
    alone = number == 0
    number = number.astype(F32) * (2.0 * math.pi / nx)
    x_base = jnp.where(ahead, number, jnp.where(alone, math.pi, -number))
    x_trim = jnp.where(ahead, number, jnp.where(alone, 0.0, -number))
    wave_y = mode.astype(F32) * (2.0 * math.pi / ny)
    packed = mode == 0
    x_sq = x_base * x_base
    lateral = x_sq + wave_y * wave_y

    def curl_at(k, with_mirror):
        z_wave = jnp.where(k < nz // 2, k, k - nz).astype(F32) * (2.0 * math.pi / nz)
        z_trim = jnp.where(k == nz // 2, 0.0, z_wave)
        full = lateral + z_wave * z_wave
        empty = full == 0.0
        inverse = jnp.where(empty, 0.0, 1.0 / jnp.where(empty, 1.0, full))
        if with_mirror:
            other = 1.0 / (x_sq + (z_wave * z_wave + math.pi * math.pi))
            mirror = jnp.where(packed, 0.5 * (inverse - other), 0.0)
            inverse = jnp.where(packed, 0.5 * (inverse + other), inverse)
            opposite = lax.rem(nz - k, nz)
        stream = []
        for c in range(3):
            value = [spectrum[c, part, k] * inverse for part in range(2)]
            if with_mirror:
                for part, sign in enumerate((1.0, -1.0)):
                    there = spectrum[c, part, opposite]
                    there = jnp.where(alone, there, roll(there, half))
                    value[part] = value[part] + (mirror * sign) * there
            stream.append(value)
        made = []
        for part in range(2):
            s = [value[part] for value in stream]
            made.append(
                (
                    x_trim * s[2] - wave_y * s[1],
                    wave_y * s[0] - z_trim * s[2],
                    z_trim * s[1] - x_trim * s[0],
                )
            )
        return [(-made[1][c], made[0][c]) for c in range(3)]

    def curl_all(with_mirror):
        def body(k, carry):
            made = [curl_at(k + slabs * n, with_mirror) for n in range(planes)]
            for c in range(3):
                for l, v in enumerate(fft([m[c] for m in made], 1.0)):
                    n, i = spot[l]
                    outs[n][c, 0, i, k], outs[n][c, 1, i, k] = v
            return carry

        lax.fori_loop(0, slabs, body, 0)

    lax.fori_loop(0, slabs, across_planes, 0)

    @pl.when(pencil_at == 0)
    def _():
        curl_all(True)

    @pl.when(pencil_at != 0)
    def _():
        curl_all(False)


def planes_of(held, pairs, tables):
    pencils, rows, _ = held.shape
    groups = [(c, pair) for c in range(3) for pair in pairs]
    left = jnp.concatenate(
        [
            jnp.concatenate(
                [held[h, :, n * LANES : (n + 1) * LANES] for h in range(pencils)], axis=1
            )
            for n in range(len(groups))
        ],
        axis=0,
    )
    ny = tables[0].shape[1] // 2
    wide = table_right(left, tables[0][...], tables[1][...])
    made = {}
    for n, (c, pair) in enumerate(groups):
        for parity in range(2):
            made[c, 2 * pair + parity] = wide[
                n * rows : (n + 1) * rows, parity * ny : (parity + 1) * ny
            ]
    return made


def hold(tall, c, n, value):
    rows = value.shape[0]
    tall[c, n, RIM : RIM + rows] = value
    tall[c, n, 0:RIM] = value[rows - RIM : rows]


def edge_kernel(pairs, tables, place, *refs):
    tall, first, last, held = refs[-4:]
    gather_blocks(refs[:-4], held, place[1])
    listed = [2 * pair + parity for pair in pairs for parity in range(2)]
    cols = first.shape[1]
    values = planes_of(held, pairs, tables)
    for c in range(3):
        for n, z in enumerate(listed):
            hold(tall, c, n, values[c, z])
        first[c] = values[c, listed[0]][0:cols]
        last[c] = values[c, listed[-1]][0:cols]


def where_planes(chunks):
    spot = {}
    for n, chunk in enumerate(chunks):
        for i, pair in enumerate(chunk):
            spot[2 * pair], spot[2 * pair + 1] = (n, 2 * i), (n, 2 * i + 1)
    return spot


def rim_start(meshes, which, c, i):
    before = 6 * meshes[1].shape[1] if which == 0 else 0
    return before + 2 * (c * meshes[which].shape[1] + i)


def stretch_plane(out, mesh, rims, at, rows_of, above, below):
    cols, ny = out[0].shape
    low_rim, high_rim = rims
    for c in range(3):
        out[c][...] = mesh[c][...]
        out[c][0:2] += low_rim[at[c] : at[c] + 2]
        out[c][cols - 2 : cols] += high_rim[at[c] : at[c] + 2]
    omega = [ref[...] for ref in out]
    for c in range(3):
        value = rows_of(c, RIM)
        along_z = (above(c) - below(c)) * 0.5
        along_x = (rows_of(c, RIM + 1) - rows_of(c, RIM - 1)) * 0.5
        along_y = (pltpu.roll(value, ny - 1, 1) - pltpu.roll(value, 1, 1)) * 0.5
        stretch = omega[0] * along_z + omega[1] * along_x + omega[2] * along_y
        out[c][...] = omega[c] + TIME_STEP * stretch


def ends_kernel(_, __, edges, before, after, low_rim, high_rim, *refs):
    meshes, vorticity, out, sems = refs[:-4], refs[-3], refs[-2], refs[-1]
    cols = before.shape[1]
    size = edges.shape[1]
    copies = []

    def rows_of(i):
        return lambda c, start=RIM: edges[c, i, start : start + cols]

    for n, i in enumerate((0, size - 1)):
        stretch_plane(
            [out.at[c, n] for c in range(3)],
            [meshes[0].at[c, i] for c in range(3)],
            (low_rim, high_rim),
            [rim_start(meshes, 0, c, i) for c in range(3)],
            rows_of(i),
            (lambda c: after[c]) if i else rows_of(1),
            rows_of(size - 2) if i else (lambda c: before[c]),
        )
        copies.append(
            pltpu.make_async_copy(
                out.at[:, n], vorticity.at[:, n * (vorticity.shape[1] - 1)], sems.at[n]
            )
        )
        copies[-1].start()
    for copy in copies:
        copy.wait()


def stretch_kernel(chunks, tables, place, edges, low_rim, high_rim, *refs):
    meshes, refs = refs[:2], refs[2:]
    velocity, vorticity, held, inner, omega, sems = refs[-6:]
    _, planes, cols, ny = velocity.shape
    spot = where_planes(chunks)
    talls = (edges, inner)
    sent = []

    def send(source, target):
        sent.append(pltpu.make_async_copy(source, target, sems.at[len(sent)]))
        sent[-1].start()

    def rows_of(z):
        n, i = spot[z]
        return lambda c, start=RIM: talls[n][c, i, start : start + cols]

    def send_velocity(which):
        for z in range(planes):
            n, i = spot[z]
            if n == which:
                send(talls[n].at[:, i, pl.ds(RIM, cols)], velocity.at[:, z])

    send_velocity(0)
    gather_blocks(refs[:-6], held, place[1], "far")
    for (c, z), value in planes_of(held, chunks[1], tables).items():
        hold(inner, c, spot[z][1], value)
    send_velocity(1)
    for z in range(1, planes - 1):
        which, i = spot[z]
        stretch_plane(
            [omega.at[c, z] for c in range(3)],
            [meshes[which].at[c, i] for c in range(3)],
            (low_rim, high_rim),
            [rim_start(meshes, which, c, i) for c in range(3)],
            rows_of(z),
            rows_of(z + 1),
            rows_of(z - 1),
        )
        send(omega.at[:, z], vorticity.at[:, z])
    for copy in sent:
        copy.wait()


VM = pl.BlockSpec(memory_space=pltpu.VMEM)
SM = pl.BlockSpec(memory_space=pltpu.SMEM)
AN = pl.BlockSpec(memory_space=pl.ANY)
HB = pl.BlockSpec(memory_space=pltpu.HBM)


def kept(values):
    return pltpu.with_memory_space_constraint(values, pltpu.HBM)


def loaded(kernel):
    def run(place, t_high, t_low, *refs):
        kernel((t_high, t_low), place, *refs)

    return run


def call(kernel, ins, outs, scratch=(), sems=0, micros=2.0, moved=None, aliases=None):
    extra = [pltpu.SemaphoreType.DMA((sems,))] if sems else []
    return pl.pallas_call(
        kernel,
        out_shape=[jax.ShapeDtypeStruct(shape, F32) for _, shape in outs],
        in_specs=[spec for spec, _ in ins],
        out_specs=[spec for spec, _ in outs],
        scratch_shapes=[pltpu.VMEM(shape, kind) for shape, kind in scratch] + extra,
        compiler_params=pltpu.CompilerParams(vmem_limit_bytes=VMEM),
        input_output_aliases=aliases or {},
        cost_estimate=pl.CostEstimate(
            flops=int(micros * 1.0e9),
            bytes_accessed=int(micros * 3.0e6) if moved is None else moved,
            transcendentals=0,
        ),
    )(*[value for _, value in ins])


def ring(axis, step):
    count = lax.axis_size(axis)
    return [(i, (i + step) % count) for i in range(count)]


def spread(axis):
    count = lax.axis_size(axis)
    return count <= 8 and count & (count - 1) == 0


def sent_shapes(axis, rows, width, whole=False):
    count = lax.axis_size(axis)
    return [(count, rows, width)] if whole or not spread(axis) else [(rows, width)] * count


def exchange(blocks, axis, start=0, first=None):
    if not spread(axis):
        return [lax.all_to_all(blocks[0], axis, split_axis=0, concat_axis=0, tiled=True)]
    count = lax.axis_size(axis)
    return [
        lax.ppermute(block, axis, [(i, i ^ k) for i in range(count)]) if k else block
        for k, block in zip(offset_order(count, first)[start:], blocks)
    ]


def on_device(strength, offsets, cell_index, migrate_count, ambient):
    _, planes, cols, ny = ambient.shape
    slabs, pencils = lax.axis_size("gz"), lax.axis_size("gx")
    nx, nz, rows = cols * pencils, planes * slabs, cols + RIM
    count = strength.shape[1]
    pair_count = planes // 2
    chunks = ((0, pair_count - 1), tuple(range(1, pair_count - 1)))
    widths = [3 * len(c) * LANES for c in chunks]
    block = nx // slabs

    y_ahead, y_back = [split_table(t) for t in y_tables(ny, pencils, 1.0 / (float(nx) * ny * nz))]
    x_ahead, x_back = [split_table(t) for t in x_tables(nx, cols, pencils, slabs)]
    place = jnp.stack([lax.axis_index("gz"), lax.axis_index("gx")]).astype(jnp.int32)
    here = (SM, place)

    packet, movers = call(
        packet_kernel,
        [
            (HB, kept(migrate_count.reshape(1, 2))),
            (HB, kept(strength)),
            (HB, kept(offsets)),
            (HB, kept(cell_index.reshape(1, count))),
        ],
        [(VM, (8, count)), (VM, (8, 2 * MIG))],
        [((1, 2), jnp.int32), ((1, count), jnp.int32)],
        sems=4,
        micros=1.0,
        moved=1000,
    )
    up1 = lax.ppermute(packet, "gz", ring("gz", -1))
    down1 = lax.ppermute(packet, "gz", ring("gz", 1))
    up2 = lax.ppermute(movers, "gz", ring("gz", -2))
    down2 = lax.ppermute(movers, "gz", ring("gz", 2))

    meshes, rims, parts = [None, None], [], [None, None]
    for n in (1, 0):
        chunk, width = chunks[n], widths[n]
        size = 2 * len(chunk)
        rim = (6 * size + (rims[0].shape[0] if rims else 0), ny)
        mesh, rim_high, rim_low, *part = call(
            functools.partial(deposit_kernel, chunk, len(rims), None if n else "near"),
            [here]
            + [(VM, value) for value in (packet, up1, down1, up2, down2)]
            + [(VM, ambient), (VM, y_ahead[0]), (VM, y_ahead[1])]
            + [(VM, value) for value in rims],
            [(VM, (3, size, cols, ny)), (VM, rim), (VM, rim)]
            + [(VM, shape) for shape in sent_shapes("gx", rows, width)],
            [((3, size, rows, ny), F32), ((pencils, rows, width), F32)],
            micros=5.0,
        )
        meshes[n] = mesh
        rims = [rim_high, rim_low]
        parts[n] = exchange(part, "gx", first="near" if n == 0 else None)
    low_rim = lax.ppermute(rims[0], "gx", ring("gx", 1))
    high_rim = lax.ppermute(rims[1], "gx", ring("gx", -1))

    tile = max(1, block // 4)
    data = [None, None]
    for n in (1, 0):
        chunk, part, width = chunks[n], parts[n], widths[n]
        shapes = sent_shapes("gz", block, width)
        part = call(
            functools.partial(x_ahead_kernel, len(shapes), None if n else "near"),
            [here, (VM, x_ahead[0]), (VM, x_ahead[1])] + [(VM, p) for p in part],
            [(VM, shape) for shape in shapes],
            [((pencils, rows, width), F32), ((slabs, block, width), F32)],
        )
        (entered,) = call(
            functools.partial(enter_kernel, chunk, nz),
            [here] + [(VM, p) for p in exchange(part, "gz")],
            [(VM, (3, 2, 2 * len(chunk), slabs, tile, LANES))],
        )
        data[n] = entered
    data = call(
        functools.partial(curl_kernel, chunks, nx, ny),
        [here, (VM, low_rim), (VM, high_rim)] + [(VM, d) for d in data],
        [(VM, d.shape) for d in data],
        [((3, 2, nz, tile, LANES), F32)],
        micros=5.0,
    )
    plane = (3, cols, ny)
    tables = [(VM, t) for t in y_back]
    tall = [(3, 2 * len(chunk), cols + 2 * RIM, ny) for chunk in chunks]
    left = [
        call(
            functools.partial(leave_kernel, chunk, nz),
            [here, (VM, source)],
            [(VM, shape) for shape in sent_shapes("gz", block, width)],
            [(source.shape, F32)],
        )
        for chunk, source, width in zip(chunks, data, widths)
    ]

    def back(part, width, first=None):
        shapes = sent_shapes("gx", rows, width)
        part = call(
            loaded(functools.partial(x_back_kernel, len(shapes), first)),
            [here]
            + [(VM, t) for t in x_back]
            + [(VM, p) for p in part],
            [(VM, shape) for shape in shapes],
            [((slabs, block, width), F32), ((pencils, rows, width), F32)],
        )
        return exchange(part, "gx", first=first)

    early = max(1, len(left[1]) - LATE)
    second = exchange(left[1][:early], "gz")
    parts = [back(exchange(left[0], "gz"), widths[0])]
    edges, first, last = call(
        loaded(functools.partial(edge_kernel, chunks[0])),
        [here] + tables + [(VM, p) for p in parts[0]],
        [(VM, tall[0]), (VM, plane), (VM, plane)],
        [((pencils, rows, widths[0]), F32)],
    )
    if early < len(left[1]):
        late = call(
            pass_kernel,
            [(AN, parts[0][0])] + [(VM, p) for p in left[1][early:]],
            [(VM, p.shape) for p in left[1][early:]],
            micros=0.3,
        )
        second += exchange(late, "gz", early)
    parts.append(back(second, widths[1], "far"))
    after = lax.ppermute(first, "gz", ring("gz", -1))
    before = lax.ppermute(last, "gz", ring("gz", 1))
    velocity, vorticity = call(
        loaded(functools.partial(stretch_kernel, chunks)),
        [here]
        + tables
        + [(VM, v) for v in (edges, low_rim, high_rim, *meshes)]
        + [(VM, p) for p in parts[1]],
        [(AN, ambient.shape), (AN, ambient.shape)],
        [
            ((pencils, rows, widths[1]), F32),
            (tall[1], F32),
            ((3, planes, cols, ny), F32),
        ],
        sems=2 * planes,
        micros=4.0,
    )
    return tuple(
        call(
            ends_kernel,
            [(AN, velocity), (AN, vorticity)]
            + [(VM, v) for v in (edges, before, after, low_rim, high_rim, *meshes)],
            [(AN, ambient.shape), (AN, ambient.shape)],
            [((3, 2, cols, ny), F32)],
            sems=2,
            micros=1.0,
            aliases={0: 0, 1: 1},
        )
    )


def solution(mesh):
    placed = (
        P(None, ("gz", "gx")),
        P(None, ("gz", "gx")),
        P(("gz", "gx")),
        P("gz", "gx", None),
        P(None, "gz", "gx", None),
    )
    return jax.shard_map(
        on_device,
        mesh=mesh,
        in_specs=placed,
        out_specs=(P(None, "gz", "gx", None), P(None, "gz", "gx", None)),
        check_vma=False,
    )
```
